32 devices in a mesh: gx: 4 (over y, x), gy: 2 (over core), gz: 4 (over z).
Axes of the slice: x: 2, y: 2, z: 4, core: 2. Of those that a mesh axis runs over, the one named last changes fastest.
Arguments:
- point_data: float32 [32, 32, 7, 32], P(('gx', 'gy', 'gz')), may hold values from -2.8 to 2.8, as said below
- point_cells: int32 [32, 32, 3, 32], P(('gx', 'gy', 'gz')), may hold values from 0 to 127, as said below
- send_counts: int32 [32, 32], P(('gx', 'gy', 'gz')), may hold values from 0 to 32, as said below
Outputs:
- indicator: float32 [64, 32, 512], P('gx', 'gy', 'gz')
- point_values: float32 [32, 32, 32], P(('gx', 'gy', 'gz'))
The draws below stay inside these ranges and needn't reach their ends.
Inputs may be any that keep to these rules, and one draw needn't show every extreme that they name: `point_data`: channels 0 to 2 of a slot are an oriented normal, channel 3 a confidence between 0.05 and 1, channels 4 to 6 offsets inside the cell between 0 and 1. `point_cells`: channel 0 lies below 16, channel 1 below 16, channel 2 below 128. Slot j from block s to brick d is live where j < send_counts[s, d]. In every draw some brick receives 32 live slots from every block.
All inputs are finite; a program needn't handle non-finite values.
Results may differ from the reference program's by a relative error of at most 0.00002.
Values sent between devices are 32-bit elements; how exact they have to be, the bound alone decides.
No kernel may reach another device: no remote copies, remote signals or barrier semaphores. Data moves between devices by JAX's collectives and lax.ppermute only.
A program may use at most 128 MiB of HBM per device.

```python
import jax
import jax.numpy as jnp

CX = 16
CY = 16
CZ = 128
CAP = 32
ITERS = 6
BRICKS = 32
NX = 64
NY = 32
NZ = 512
N_GY = 2
N_GZ = 4


def draw_point_data(key, part):
    key_normal, key_conf, key_offset = jax.random.split(key, 3)
    shape_normal = (BRICKS, BRICKS, 3, CAP)
    normal = jnp.clip(0.7 * jax.random.normal(key_normal, shape_normal, jnp.float32), -2.8, 2.8)
    confidence = jax.random.uniform(key_conf, (BRICKS, BRICKS, 1, CAP), jnp.float32, 0.2, 1.0)
    offsets = jax.random.uniform(key_offset, shape_normal, jnp.float32, 0.0, 1.0)
    return jnp.concatenate([normal, confidence, offsets], axis=2).astype(jnp.float32)


def draw_point_cells(key, part):
    limits = jnp.array([CX, CY, CZ], jnp.int32)[None, None, :, None]
    raw_bits = jax.random.randint(key, (BRICKS, BRICKS, 3, CAP), 0, 1048576)
    return (raw_bits % limits).astype(jnp.int32)


def draw_send_counts(key, part):
    key_heavy, key_level, key_count = jax.random.split(jax.random.fold_in(key, 7), 3)
    heavy = jax.random.randint(key_heavy, (), 0, BRICKS)
    levels = jax.random.randint(key_level, (BRICKS,), 1, 5)
    raw_count = jax.random.randint(key_count, (BRICKS, BRICKS), 0, CAP + 1)
    counts = jnp.minimum(CAP, raw_count * levels[None, :] // 4)
    dest_ids = jnp.arange(BRICKS, dtype=jnp.int32)
    return jnp.where(dest_ids[None, :] == heavy, CAP, counts).astype(jnp.int32)


def setup_inputs(seed: int = 0) -> dict:
    key_list = jax.random.split(jax.random.key(seed), 4)
    return {
        "point_data": draw_point_data(jax.random.fold_in(key_list[3], 71), 0),
        "point_cells": draw_point_cells(jax.random.fold_in(key_list[3], 71), 0),
        "send_counts": draw_send_counts(jax.random.fold_in(key_list[3], 71), 0),
    }


base_screen = 0.25
point_screen = 4.0


def trilinear(offsets, corner_x, corner_y, corner_z):
    along_x = offsets[..., 0, :] if corner_x else 1.0 - offsets[..., 0, :]
    along_y = offsets[..., 1, :] if corner_y else 1.0 - offsets[..., 1, :]
    along_z = offsets[..., 2, :] if corner_z else 1.0 - offsets[..., 2, :]
    return along_x * along_y * along_z


def six_sum(padded):
    total = padded[2:, 1:-1, 1:-1] + padded[:-2, 1:-1, 1:-1]
    total = total + padded[1:-1, 2:, 1:-1] + padded[1:-1, :-2, 1:-1]
    return total + padded[1:-1, 1:-1, 2:] + padded[1:-1, 1:-1, :-2]


def divergence(padded):
    total = padded[0, 2:, 1:-1, 1:-1] - padded[0, :-2, 1:-1, 1:-1]
    total = total + padded[1, 1:-1, 2:, 1:-1] - padded[1, 1:-1, :-2, 1:-1]
    return total + padded[2, 1:-1, 1:-1, 2:] - padded[2, 1:-1, 1:-1, :-2]


def chebyshev(source_term, diagonal, operate):
    half_width = 6.0 / (6.0 + base_screen)
    sigma_ratio = 1.0 / half_width
    rho_prev = half_width
    solution = jnp.zeros_like(source_term)
    residual = source_term
    direction = source_term / diagonal
    for sweep in range(ITERS):
        solution = solution + direction
        residual = residual - operate(direction)
        if sweep + 1 < ITERS:
            rho_next = 1.0 / (2.0 * sigma_ratio - rho_prev)
            direction = (rho_next * rho_prev) * direction + (2.0 * rho_next / half_width) * residual / diagonal
            rho_prev = rho_next
    return solution


def reference(point_data, point_cells, send_counts):
    slot_index = jnp.arange(CAP, dtype=jnp.int32)
    live_mask = (slot_index[None, None, :] < send_counts[:, :, None]).astype(jnp.float32)
    weight = point_data[:, :, 3, :] * live_mask
    offsets = point_data[:, :, 4:7, :]
    brick_ids = jnp.arange(BRICKS, dtype=jnp.int32)
    cell_x = point_cells[:, :, 0, :] + ((brick_ids // (N_GY * N_GZ)) * CX)[None, :, None]
    cell_y = point_cells[:, :, 1, :] + (((brick_ids // N_GZ) % N_GY) * CY)[None, :, None]
    cell_z = point_cells[:, :, 2, :] + ((brick_ids % N_GZ) * CZ)[None, :, None]
    volume = jnp.zeros((4, (NX + 1) * (NY + 1) * (NZ + 1)), jnp.float32)
    for corner_x in (0, 1):
        for corner_y in (0, 1):
            for corner_z in (0, 1):
                point_mass = weight * trilinear(offsets, corner_x, corner_y, corner_z)
                contrib = jnp.stack([point_data[:, :, 0, :] * point_mass, point_data[:, :, 1, :] * point_mass,
                                     point_data[:, :, 2, :] * point_mass, point_mass]).reshape(4, -1)
                linear_at = ((cell_x + corner_x) * (NY + 1) + cell_y + corner_y) * (NZ + 1) + cell_z + corner_z
                volume = volume.at[:, linear_at.reshape(-1)].add(contrib)
    splat = volume.reshape(4, NX + 1, NY + 1, NZ + 1)[:, :NX, :NY, :NZ]
    padded = jnp.pad(splat[:3], ((0, 0), (1, 1), (1, 1), (1, 1)))
    source_term = -0.5 * divergence(padded)
    diagonal = 6.0 + base_screen + point_screen * splat[3]

    def operate(field):
        return diagonal * field - six_sum(jnp.pad(field, 1))

    indicator = chebyshev(source_term, diagonal, operate)
    top_padded = jnp.pad(indicator, ((0, 1), (0, 1), (0, 1))).reshape(-1)
    values = jnp.zeros(live_mask.shape, jnp.float32)
    for corner_x in (0, 1):
        for corner_y in (0, 1):
            for corner_z in (0, 1):
                linear_at = ((cell_x + corner_x) * (NY + 1) + cell_y + corner_y) * (NZ + 1) + cell_z + corner_z
                values = values + trilinear(offsets, corner_x, corner_y, corner_z) * top_padded[linear_at]
    return indicator, values * live_mask
```

```python
import functools

import jax
import jax.numpy as jnp
from jax import lax
from jax.experimental import pallas as pl
from jax.experimental.pallas import tpu as pltpu
from jax.sharding import PartitionSpec as P

CX = 16
CY = 16
CZ = 128
ITERS = 6

base_screen = 0.25
point_screen = 4.0

AXES = ("gx", "gy", "gz")
REACH = ITERS - 1
XO = REACH
YO = 9
ZO = 8
YS = 32
XPT = 128 // YS
XTILES = -(-(CX + 2 * REACH + 1) // XPT)
LANES = XTILES * 128
ROWS = CZ + 16
CENTER = tuple(range((XO - 1) // XPT, (XO + CX + 1) // XPT + 1))
LOWER = tuple(range(0, (XO + 1) // XPT + 1))
UPPER = tuple(range((XO + CX - 1) // XPT, XTILES))
WINDOW_LOW = YO - REACH
WINDOW_HIGH = YO + CY - 1
UP_AT = ZO + CZ - REACH
DOWN_AT = ZO - 1
HALO = 8
GROUPS = 8
VMEM_LIMIT = 56 * 1024 * 1024

f32 = jnp.float32
bf16 = jnp.bfloat16


def split(value):
    high = value.astype(bf16)
    return high, (value - high.astype(f32)).astype(bf16)


def dot_nt(lhs, rhs):
    return lax.dot_general(lhs, rhs, (((1,), (1,)), ((), ())), preferred_element_type=f32)


def dot_nn(lhs, rhs):
    return lax.dot_general(lhs, rhs, (((1,), (0,)), ((), ())), preferred_element_type=f32)


def other_count(gy):
    return min(gy - 1, 2)


def extra_place(brick, bricks):
    return bricks + brick // 4, 2 * (brick % 4)


def pack_kernel(shape, data_ref, cells_ref, counts_ref, out_ref, main, extra):
    gx, gy, gz = shape
    slots = data_ref.shape[3]
    lane = lax.broadcasted_iota(jnp.int32, (1, slots), 1)
    others = other_count(gy)
    bricks = 3 * (1 + others)
    for d in range(gx * gy * gz):
        block = data_ref[0, d]
        cell = cells_ref[0, d].astype(f32)
        weight = jnp.where(lane < counts_ref[0, d], block[3:4], 0.0)
        main[d, 0:3] = block[0:3] * (-0.5 * weight)
        main[d, 3:4] = weight
        main[d, 4:7] = block[4:7]
        main[d, 7:8] = cell[0:1]
        extra[d] = cell[1:3]
    out_ref[...] = jnp.zeros_like(out_ref)
    for d in range(gx * gy * gz):
        x, y, z = d // (gy * gz), (d // gz) % gy, d % gz
        if others == 0:
            ys = (y,)
        elif others == 1:
            ys = (y, 1 - y)
        else:
            ys = (y, y - 1, y + 1)
        for e, by in enumerate(ys):
            for o, bx in enumerate((x, x - 1, x + 1)):
                if not (0 <= bx < gx and 0 <= by < gy):
                    continue
                b = e * 3 + o
                source = (bx * gy + by) * gz + z
                tile, part = b // 4, b % 4
                out_ref[d, 8 * tile : 8 * tile + 8, slots * part : slots * part + slots] = main[source]
                place, row = extra_place(b, bricks)
                tile, part = place // 4, place % 4
                out_ref[
                    d, 8 * tile + row : 8 * tile + row + 2, slots * part : slots * part + slots
                ] = extra[source]


def hat(coordinate, cell, low, high):
    away = coordinate - cell
    return jnp.where(away == 0.0, low, jnp.where(away == 1.0, high, 0.0))


def hat_slope(coordinate, cell, low, high):
    away = coordinate - cell
    rising = jnp.where(away == -1.0, low, jnp.where(away == 0.0, high, 0.0))
    return rising - jnp.where(away == 1.0, low, jnp.where(away == 2.0, high, 0.0))


def row_iota(rows):
    return lax.broadcasted_iota(jnp.int32, (rows, 128), 0).astype(f32)


def splat_kernel(
    shape, recv_ref, rhs_ref, density_ref, up_ref, down_ref, own_ref,
    points, high_ref, low_ref, hz_ref, hx_ref, wide,
):
    gx, gy, gz = shape
    mx, my, mz = lax.axis_index("gx"), lax.axis_index("gy"), lax.axis_index("gz")
    step = pl.program_id(0)
    others = other_count(gy)
    bricks = 3 * (1 + others)
    tiles = recv_ref.shape[2] // 8
    lane = lax.broadcasted_iota(jnp.int32, (8, 128), 1)
    lane_part = lane // 32

    @pl.when(step == 0)
    def _():
        wide[...] = jnp.zeros_like(wide)

    for t in range(tiles):
        for g in range(GROUPS):
            given = [recv_ref[q, g, 8 * t : 8 * t + 8, :] for q in range(4)]
            for k in range(4):
                if 4 * t + k >= bricks + -(-bricks // 4):
                    continue
                merged = None
                for q in range(4):
                    moved = given[q] if q == k else pltpu.roll(given[q], (32 * (q - k)) % 128, 1)
                    merged = moved if merged is None else jnp.where(lane_part == q, moved, merged)
                points[4 * t + k, g] = merged
    own_ref[0] = points[0]
    own_ref[1] = points[bricks]

    z_limit = jnp.where(mz == gz - 1, CZ, CZ + 1).astype(f32)
    z_row = row_iota(ROWS) - float(ZO)
    own_row = row_iota(24) + float(8 - YO)

    for e in range(1 + others):
        if e == 0:
            y_limit = jnp.where(my == gy - 1, CY, CY + 1).astype(f32)
            y_row = own_row
        else:
            if others == 1:
                above = my == 0
            else:
                above = e == 2
            y_limit = jnp.where(
                jnp.logical_and(above, my + 1 == gy - 1), CY, CY + 1
            ).astype(f32)
            window = jnp.where(above, WINDOW_HIGH, WINDOW_LOW)
            first = jnp.where(above, WINDOW_HIGH - YO - CY, WINDOW_LOW - YO + CY)
            y_row = row_iota(8) + first.astype(f32)
        for o, (shift, x_tiles) in enumerate(((0, CENTER), (-1, LOWER), (1, UPPER))):
            b = e * 3 + o
            place, row = extra_place(b, bricks)
            x_limit = jnp.where(mx + shift == gx - 1, CX, CX + 1).astype(f32)
            cell_x = points[b, :, 7, :]
            off_x = points[b, :, 6 - 2, :]
            low_x = 1.0 - off_x
            high_x = jnp.where(cell_x + 1.0 < x_limit, off_x, 0.0)
            planes = [XPT * t + i for t in x_tiles for i in range(XPT)]
            for n, plane in enumerate(planes):
                at = float(plane - XO - CX * shift)
                hx_ref[0, n] = hat(at, cell_x, low_x, high_x)
                hx_ref[1, n] = hat_slope(at, cell_x, low_x, high_x)
            y_parts = []
            for g in range(GROUPS):
                main = points[b, g]
                more = points[place, g]
                cell_y, cell_z = more[row : row + 1], more[row + 1 : row + 2]
                off_y, off_z = main[5:6], main[6:7]
                high_z = jnp.where(cell_z + 1.0 < z_limit, off_z, 0.0)
                hz_high, hz_low = split(hat(z_row, cell_z, 1.0 - off_z, high_z))
                hz_ref[0:ROWS, 128 * g : 128 * g + 128] = hz_high
                hz_ref[ROWS : 2 * ROWS, 128 * g : 128 * g + 128] = hz_low
                high_y = jnp.where(cell_y + 1.0 < y_limit, off_y, 0.0)
                hy = hat(y_row, cell_y, 1.0 - off_y, high_y)
                dy = hat_slope(y_row, cell_y, 1.0 - off_y, high_y)
                y_parts.append((main[0:1] * hy, main[1:2] * dy, main[2:3] * hy, main[3:4] * hy))
            if e == 0:
                blocks = [(t,) for t in x_tiles]
            else:
                blocks = [x_tiles[i : i + 4] for i in range(0, len(x_tiles), 4)]
            for n, block in enumerate(blocks):
                base = 384 * n
                for g in range(GROUPS):
                    part_x0, part_y1, part_z, part_w = y_parts[g]
                    at = slice(128 * g, 128 * g + 128)
                    for i in range(XPT):
                        rows = ([], [], [])
                        for t in block:
                            plane = planes.index(XPT * t + i)
                            hx = hx_ref[0, plane, g : g + 1, :]
                            dx = hx_ref[1, plane, g : g + 1, :]
                            rows[0].append(dx * part_x0 + hx * part_y1)
                            rows[1].append(hx * part_z)
                            rows[2].append(hx * part_w)
                        for c in range(3):
                            have = sum(v.shape[0] for v in rows[c])
                            pad = [jnp.zeros((YS - have, 128), f32)] if have < YS else []
                            full = pad + rows[c] if e == 0 else rows[c] + pad
                            full = jnp.concatenate(full, axis=0) if len(full) > 1 else full[0]
                            high, low = split(full)
                            start = base + 128 * c + YS * i
                            high_ref[start : start + YS, at] = high
                            low_ref[start : start + YS, at] = low
            for n, block in enumerate(blocks):
                span = slice(384 * n, 384 * n + 384)
                both = dot_nt(hz_ref[...], high_ref[span, :])
                got = both[:ROWS] + both[ROWS:] + dot_nt(hz_ref[0:ROWS, :], low_ref[span, :])
                for k, t in enumerate(block):
                    for c in range(3):
                        value = got[:, 128 * c : 128 * c + 128]
                        if e > 0:
                            value = pltpu.roll(value, window + (128 - 8 * k), 1)
                            in_group = lax.broadcasted_iota(jnp.int32, (ROWS, 128), 1) % YS
                            inside = jnp.logical_and(in_group >= window, in_group < window + 8)
                            value = jnp.where(inside, value, 0.0)
                        wide[c, :, 128 * t : 128 * t + 128] += value

    @pl.when(step == pl.num_programs(0) - 1)
    def _():
        for t in range(XTILES):
            at = slice(128 * t, 128 * t + 128)
            along_z = wide[1, :, at]
            rhs_ref[:, at] = (
                wide[0, :, at]
                + pltpu.roll(along_z, ROWS - 1, 0)
                - pltpu.roll(along_z, 1, 0)
            )
            density_ref[:, at] = wide[2, :, at]
        up_ref[0] = rhs_ref[UP_AT : UP_AT + HALO, :]
        up_ref[1] = density_ref[UP_AT : UP_AT + HALO, :]
        down_ref[0] = rhs_ref[DOWN_AT : DOWN_AT + HALO, :]
        down_ref[1] = density_ref[DOWN_AT : DOWN_AT + HALO, :]


def chebyshev_factors():
    half_width = 6.0 / (6.0 + base_screen)
    sigma_ratio = 1.0 / half_width
    rho_prev = half_width
    factors = []
    for _ in range(ITERS - 1):
        rho_next = 1.0 / (2.0 * sigma_ratio - rho_prev)
        factors.append((rho_next * rho_prev, 2.0 * rho_next / half_width))
        rho_prev = rho_next
    return factors


def solve_kernel(
    shape, rhs_ref, density_ref, from_low_ref, from_high_ref, own_ref,
    indicator_ref, values_ref,
    first, second, scaled, inverse, total, edge, high_ref, low_ref,
):
    gx, gy, gz = shape
    mx, my, mz = lax.axis_index("gx"), lax.axis_index("gy"), lax.axis_index("gz")
    edge[...] = jnp.zeros_like(edge)
    low_at, high_at = UP_AT - CZ, DOWN_AT + CZ - (ROWS - 16)
    edge[0, :, low_at : low_at + HALO, :] = from_low_ref[...]
    edge[1, :, high_at : high_at + HALO, :] = from_high_ref[...]

    def with_edge(ref, channel, i):
        value = ref[8 * i : 8 * i + 8, :]
        if i < 2:
            return value + edge[0, channel, 8 * i : 8 * i + 8, :]
        if i >= ROWS // 8 - 2:
            at = 8 * (i - ROWS // 8 + 2)
            return value + edge[1, channel, at : at + 8, :]
        return value

    lane = lax.broadcasted_iota(jnp.int32, (8, LANES), 1)
    x, y = lane // YS - XO + mx * CX, lane % YS - YO + my * CY
    inside_xy = (x >= 0) & (x < gx * CX) & (y >= 0) & (y < gy * CY)
    zero = jnp.zeros((8, LANES), f32)
    first[0:8, :] = zero
    first[ROWS + 8 : ROWS + 16, :] = zero
    second[0:8, :] = zero
    second[ROWS + 8 : ROWS + 16, :] = zero
    for i in range(ROWS // 8):
        at = slice(8 * i, 8 * i + 8)
        z = lax.broadcasted_iota(jnp.int32, (8, LANES), 0) + (8 * i - ZO) + mz * CZ
        inside = inside_xy & (z >= 0) & (z < gz * CZ)
        diagonal = 6.0 + base_screen + point_screen * with_edge(density_ref, 1, i)
        inv = jnp.where(inside, 1.0 / diagonal, 0.0)
        start = with_edge(rhs_ref, 0, i) * inv
        inverse[at, :] = inv
        scaled[at, :] = start
        total[at, :] = start
        first[8 * i + 8 : 8 * i + 16, :] = start

    now, later = first, second
    factors = chebyshev_factors()
    for k, (keep, gain) in enumerate(factors):
        last = k + 1 == len(factors)
        for i in range(ROWS // 8):
            at = slice(8 * i, 8 * i + 8)
            here = now[8 * i + 8 : 8 * i + 16, :]
            near = now[8 * i + 7 : 8 * i + 15, :] + now[8 * i + 9 : 8 * i + 17, :]
            near = near + pltpu.roll(here, 1, 1) + pltpu.roll(here, LANES - 1, 1)
            near = near + pltpu.roll(here, YS, 1) + pltpu.roll(here, LANES - YS, 1)
            left = scaled[at, :] - here + inverse[at, :] * near
            ahead = keep * here + gain * left
            total[at, :] += ahead
            if not last:
                scaled[at, :] = left
                later[8 * i + 8 : 8 * i + 16, :] = ahead
        now, later = later, now

    for t in CENTER:
        turned = total[ZO : ZO + CZ, 128 * t : 128 * t + 128].T
        for i in range(XPT):
            plane = XPT * t + i - XO
            if 0 <= plane < CX:
                indicator_ref[plane] = turned[YS * i + YO : YS * i + YO + CY, :]

    groups = own_ref.shape[1]
    first_lane, end_lane = 128 * CENTER[0], 128 * CENTER[-1] + 128
    depth = end_lane - first_lane
    u_high, u_low = split(total[:, first_lane:end_lane])
    z_row = row_iota(ROWS) - float(ZO)
    y_row = row_iota(24) + float(8 - YO)
    blank = jnp.zeros((8, 128), f32)
    for chunk in range(groups // GROUPS):
        for g in range(GROUPS):
            main = own_ref[0, chunk * GROUPS + g]
            more = own_ref[1, chunk * GROUPS + g]
            off_x, off_y = main[4:5], main[5:6]
            hy = hat(y_row, more[0:1], 1.0 - off_y, off_y)
            at = slice(128 * g, 128 * g + 128)
            for plane in range(XPT * CENTER[0], XPT * CENTER[-1] + XPT):
                start = YS * plane - first_lane
                if 0 <= plane - XO <= CX:
                    hx = hat(float(plane - XO), main[7:8], 1.0 - off_x, off_x)
                    high, low = split(jnp.concatenate([blank, hx * hy], axis=0))
                else:
                    high = jnp.zeros((YS, 128), bf16)
                    low = high
                high_ref[start : start + YS, at] = high
                low_ref[start : start + YS, at] = low
        got = dot_nn(u_high, high_ref[...]) + dot_nn(u_low, high_ref[...])
        got = got + dot_nn(u_high, low_ref[...])
        rows = []
        for g in range(GROUPS):
            main = own_ref[0, chunk * GROUPS + g]
            more = own_ref[1, chunk * GROUPS + g]
            off_z = main[6:7]
            hz = hat(z_row, more[1:2], 1.0 - off_z, off_z)
            value = jnp.sum(hz * got[:, 128 * g : 128 * g + 128], axis=0, keepdims=True)
            rows.append(jnp.where(main[3:4] > 0.0, value, 0.0))
        values = jnp.concatenate(rows, axis=0)
        for q in range(4):
            moved = values if q == 0 else pltpu.roll(values, 128 - 32 * q, 1)
            start = q * groups + chunk * GROUPS
            values_ref[start : start + GROUPS, :] = moved[:, 0:32]


def on_device(shape, point_data, point_cells, send_counts):
    gx, gy, gz = shape
    sources = gx * gy * gz
    slots = point_data.shape[3]
    bricks = 3 * (1 + other_count(gy))
    rows = 8 * -(-(bricks + -(-bricks // 4)) // 4)
    groups = sources // 4
    params = pltpu.CompilerParams(vmem_limit_bytes=VMEM_LIMIT)
    whole = pl.BlockSpec(memory_space=pltpu.VMEM)

    outgoing = pl.pallas_call(
        functools.partial(pack_kernel, shape),
        out_shape=jax.ShapeDtypeStruct((sources, rows, 128), f32),
        in_specs=[whole, whole, pl.BlockSpec(memory_space=pltpu.SMEM)],
        out_specs=whole,
        scratch_shapes=[
            pltpu.VMEM((sources, 8, slots), f32),
            pltpu.VMEM((sources, 2, slots), f32),
        ],
        compiler_params=params,
        name="pack_points",
    )(point_data, point_cells, send_counts)

    arrived = lax.all_to_all(outgoing, AXES, split_axis=0, concat_axis=0, tiled=True)
    arrived = arrived.reshape(4, groups, rows, 128)

    most = 384 * len(CENTER)
    wide_shape = jax.ShapeDtypeStruct((ROWS, LANES), f32)
    edge_shape = jax.ShapeDtypeStruct((2, HALO, LANES), f32)
    steps = groups // GROUPS
    rhs, density, up, down, own = pl.pallas_call(
        functools.partial(splat_kernel, shape),
        grid=(steps,),
        out_shape=(
            wide_shape, wide_shape, edge_shape, edge_shape,
            jax.ShapeDtypeStruct((2, groups, 8, 128), f32),
        ),
        in_specs=[pl.BlockSpec((4, GROUPS, rows, 128), lambda s: (0, s, 0, 0))],
        out_specs=(
            pl.BlockSpec((ROWS, LANES), lambda s: (0, 0)),
            pl.BlockSpec((ROWS, LANES), lambda s: (0, 0)),
            pl.BlockSpec((2, HALO, LANES), lambda s: (0, 0, 0)),
            pl.BlockSpec((2, HALO, LANES), lambda s: (0, 0, 0)),
            pl.BlockSpec((2, GROUPS, 8, 128), lambda s: (0, s, 0, 0)),
        ),
        scratch_shapes=[
            pltpu.VMEM((rows // 2, GROUPS, 8, 128), f32),
            pltpu.VMEM((most, 128 * GROUPS), bf16),
            pltpu.VMEM((most, 128 * GROUPS), bf16),
            pltpu.VMEM((2 * ROWS, 128 * GROUPS), bf16),
            pltpu.VMEM((2, XPT * len(CENTER), GROUPS, 128), f32),
            pltpu.VMEM((3, ROWS, LANES), f32),
        ],
        compiler_params=params,
        name="splat_points",
    )(arrived)

    from_low = lax.ppermute(up, "gz", [(i, i + 1) for i in range(gz - 1)])
    from_high = lax.ppermute(down, "gz", [(i + 1, i) for i in range(gz - 1)])

    depth = 128 * len(CENTER)
    indicator, values = pl.pallas_call(
        functools.partial(solve_kernel, shape),
        out_shape=(
            jax.ShapeDtypeStruct((CX, CY, CZ), f32),
            jax.ShapeDtypeStruct((sources, slots), f32),
        ),
        in_specs=[whole] * 5,
        out_specs=(whole, whole),
        scratch_shapes=[
            pltpu.VMEM((ROWS + 16, LANES), f32),
            pltpu.VMEM((ROWS + 16, LANES), f32),
            pltpu.VMEM((ROWS, LANES), f32),
            pltpu.VMEM((ROWS, LANES), f32),
            pltpu.VMEM((ROWS, LANES), f32),
            pltpu.VMEM((2, 2, 16, LANES), f32),
            pltpu.VMEM((depth, 128 * GROUPS), bf16),
            pltpu.VMEM((depth, 128 * GROUPS), bf16),
        ],
        compiler_params=params,
        name="solve_and_read",
    )(rhs, density, from_low, from_high, own)

    returned = lax.all_to_all(values, AXES, split_axis=0, concat_axis=0, tiled=True)
    return indicator, returned.reshape(1, sources, slots)


def solution(mesh):
    shape = tuple(mesh.shape[axis] for axis in AXES)
    in_specs = (
        P(AXES, None, None, None),
        P(AXES, None, None, None),
        P(AXES, None),
    )
    out_specs = (P("gx", "gy", "gz"), P(AXES, None, None))
    return jax.shard_map(
        functools.partial(on_device, shape),
        mesh=mesh,
        in_specs=in_specs,
        out_specs=out_specs,
        check_vma=False,
    )
```

```python
import functools

import jax
import jax.numpy as jnp
from jax import lax
from jax.experimental import pallas as pl
from jax.experimental.pallas import tpu as pltpu
from jax.sharding import PartitionSpec as P

CX = 16
CY = 16
CZ = 128
ITERS = 6

base_screen = 0.25
point_screen = 4.0

AXES = ("gx", "gy", "gz")
REACH = ITERS - 1
XO = REACH
YO = 9
ZO = 8
YS = 32
XPT = 128 // YS
XTILES = -(-(CX + 2 * REACH + 1) // XPT)
LANES = XTILES * 128
ROWS = CZ + 16
CENTER = tuple(range(XO - 1, XO + CX + 2))
LOWER = tuple(range(0, XO + 2))
UPPER = tuple(range(XO + CX - 1, XO + CX + REACH + 1))
FIRST_TILE, END_TILE = XO // XPT, (XO + CX) // XPT + 1
WINDOW_LOW = YO - REACH
WINDOW_HIGH = YO + CY - 1
UP_AT = ZO + CZ - REACH
DOWN_AT = ZO - 1
HALO = 8
GROUPS = 8
VMEM_LIMIT = 56 * 1024 * 1024

f32 = jnp.float32
bf16 = jnp.bfloat16


def split(value):
    high = value.astype(bf16)
    return high, (value - high.astype(f32)).astype(bf16)


def dot_nt(lhs, rhs):
    return lax.dot_general(lhs, rhs, (((1,), (1,)), ((), ())), preferred_element_type=f32)


def dot_nn(lhs, rhs):
    return lax.dot_general(lhs, rhs, (((1,), (0,)), ((), ())), preferred_element_type=f32)


def other_count(gy):
    return min(gy - 1, 2)


def extra_place(brick, bricks):
    return bricks + brick // 4, 2 * (brick % 4)


def pack_kernel(shape, data_ref, cells_ref, counts_ref, out_ref, main, extra):
    gx, gy, gz = shape
    slots = data_ref.shape[3]
    lane = lax.broadcasted_iota(jnp.int32, (gx * gy * gz, slots), 1)
    others = other_count(gy)
    bricks = 3 * (1 + others)
    weight = jnp.where(lane < counts_ref[...], data_ref[0, 3], 0.0)
    for c in range(3):
        main[:, c, :] = data_ref[0, c] * (-0.5 * weight)
    main[:, 3, :] = weight
    for c in range(4, 7):
        main[:, c, :] = data_ref[0, c]
    main[:, 7, :] = cells_ref[0, 0].astype(f32)
    extra[:, 0, :] = cells_ref[0, 1].astype(f32)
    extra[:, 1, :] = cells_ref[0, 2].astype(f32)
    out_ref[...] = jnp.zeros_like(out_ref)
    for d in range(gx * gy * gz):
        x, y, z = d // (gy * gz), (d // gz) % gy, d % gz
        if others == 0:
            ys = (y,)
        elif others == 1:
            ys = (y, 1 - y)
        else:
            ys = (y, y - 1, y + 1)
        for e, by in enumerate(ys):
            for o, bx in enumerate((x, x - 1, x + 1)):
                if not (0 <= bx < gx and 0 <= by < gy):
                    continue
                b = e * 3 + o
                source = (bx * gy + by) * gz + z
                tile, part = b // 4, b % 4
                out_ref[d, 8 * tile : 8 * tile + 8, slots * part : slots * part + slots] = main[source]
                place, row = extra_place(b, bricks)
                tile, part = place // 4, place % 4
                out_ref[
                    d, 8 * tile + row : 8 * tile + row + 2, slots * part : slots * part + slots
                ] = extra[source]


def hat(coordinate, cell, low, high):
    away = coordinate - cell
    return jnp.where(away == 0.0, low, jnp.where(away == 1.0, high, 0.0))


def hat_slope(coordinate, cell, low, high):
    away = coordinate - cell
    rising = jnp.where(away == -1.0, low, jnp.where(away == 0.0, high, 0.0))
    return rising - jnp.where(away == 1.0, low, jnp.where(away == 2.0, high, 0.0))


def row_iota(rows):
    return lax.broadcasted_iota(jnp.int32, (rows, 128), 0).astype(f32)


def stack_rows(parts, multiple):
    have = sum(part.shape[0] for part in parts)
    if have % multiple:
        parts = parts + [jnp.zeros((multiple - have % multiple, 128), f32)]
    return jnp.concatenate(parts, axis=0) if len(parts) > 1 else parts[0]


def splat_kernel(
    shape, recv_ref, rhs_ref, density_ref, up_ref, down_ref, own_ref,
    points, left_ref, right_ref, hx_ref, near, beside,
):
    gx, gy, gz = shape
    mx, my, mz = lax.axis_index("gx"), lax.axis_index("gy"), lax.axis_index("gz")
    step = pl.program_id(0)
    single = recv_ref.shape[1] * 4 == gx * gy * gz
    others = other_count(gy)
    bricks = 3 * (1 + others)
    tiles = recv_ref.shape[2] // 8
    lane_part = lax.broadcasted_iota(jnp.int32, (8, 128), 1) // 32
    span = 128 * GROUPS
    written = set()

    def add(ref, place, value):
        if single and place not in written:
            written.add(place)
            ref[place + (slice(None), slice(0, ROWS))] = value
        else:
            ref[place + (slice(None), slice(0, ROWS))] += value

    if not single:
        @pl.when(step == 0)
        def _():
            near[...] = jnp.zeros_like(near)
            beside[...] = jnp.zeros_like(beside)

    for t in range(tiles):
        for g in range(GROUPS):
            given = [recv_ref[q, g, 8 * t : 8 * t + 8, :] for q in range(4)]
            for k in range(4):
                if 4 * t + k >= bricks + -(-bricks // 4):
                    continue
                merged = None
                for q in range(4):
                    moved = given[q] if q == k else pltpu.roll(given[q], (32 * (q - k)) % 128, 1)
                    merged = moved if merged is None else jnp.where(lane_part == q, moved, merged)
                points[4 * t + k, g] = merged
    own_ref[0] = points[0]
    own_ref[1] = points[bricks]

    z_limit = jnp.where(mz == gz - 1, CZ, CZ + 1).astype(f32)
    z_row = row_iota(ROWS) - float(ZO)
    own_row = row_iota(24) + float(8 - YO)

    row_at = 0
    for e in range(1 + others):
        if e == 0:
            y_limit = jnp.where(my == gy - 1, CY, CY + 1).astype(f32)
            y_row = own_row
        else:
            above = my == 0 if others == 1 else jnp.bool_(e == 2)
            y_limit = jnp.where(
                jnp.logical_and(above, my + 1 == gy - 1), CY, CY + 1
            ).astype(f32)
            first = jnp.where(above, WINDOW_HIGH - YO - CY, WINDOW_LOW - YO + CY)
            y_row = row_iota(8) + first.astype(f32)
        high = y_row.shape[0]
        for o, (shift, planes) in enumerate(((0, CENTER), (-1, LOWER), (1, UPPER))):
            b = e * 3 + o
            place, row = extra_place(b, bricks)
            x_limit = jnp.where(mx + shift == gx - 1, CX, CX + 1).astype(f32)
            cell_x = points[b, :, 7, :]
            off_x = points[b, :, 4, :]
            low_x = 1.0 - off_x
            high_x = jnp.where(cell_x + 1.0 < x_limit, off_x, 0.0)
            for n, plane in enumerate(planes):
                at = float(plane - XO - CX * shift)
                hx_ref[b, 0, n] = hat(at, cell_x, low_x, high_x)
                hx_ref[b, 1, n] = hat_slope(at, cell_x, low_x, high_x)
            y_parts = []
            for g in range(GROUPS):
                main = points[b, g]
                more = points[place, g]
                cell_y, cell_z = more[row : row + 1], more[row + 1 : row + 2]
                off_y, off_z = main[5:6], main[6:7]
                high_z = jnp.where(cell_z + 1.0 < z_limit, off_z, 0.0)
                hz_high, hz_low = split(hat(z_row, cell_z, 1.0 - off_z, high_z))
                at = slice(128 * g, 128 * g + 128)
                right_ref[b, 0, :, at] = hz_high
                right_ref[b, 1, :, at] = hz_low
                high_y = jnp.where(cell_y + 1.0 < y_limit, off_y, 0.0)
                hy = hat(y_row, cell_y, 1.0 - off_y, high_y)
                dy = hat_slope(y_row, cell_y, 1.0 - off_y, high_y)
                y_parts.append((main[0:1] * hy, main[1:2] * dy, main[2:3] * hy, main[3:4] * hy))
            size = 4 if e == 0 else 12
            for start in range(0, len(planes), size):
                block = range(start, min(start + size, len(planes)))
                count = -(-len(block) * high // 16) * 16
                for g in range(GROUPS):
                    part_x0, part_y1, part_z, part_w = y_parts[g]
                    at = slice(128 * g, 128 * g + 128)
                    rows = ([], [], [])
                    for n in block:
                        hx = hx_ref[b, 0, n, g : g + 1, :]
                        dx = hx_ref[b, 1, n, g : g + 1, :]
                        rows[0].append(dx * part_x0 + hx * part_y1)
                        rows[1].append(hx * part_z)
                        rows[2].append(hx * part_w)
                    for c in range(3):
                        main_part, rest = split(stack_rows(rows[c], 16))
                        lines = slice(row_at + c * count, row_at + c * count + count)
                        left_ref[0, lines, at] = main_part
                        left_ref[1, lines, at] = rest
                lines = slice(row_at, row_at + 3 * count)
                got = dot_nt(left_ref[0, lines, :], right_ref[b, 0])
                got = got + dot_nt(left_ref[1, lines, :], right_ref[b, 0])
                got = got + dot_nt(left_ref[0, lines, :], right_ref[b, 1])
                for c in range(3):
                    for i, n in enumerate(block):
                        begin = c * count + i * high
                        value = got[begin : begin + high]
                        if e == 0:
                            add(near, (c, planes[n]), value)
                        else:
                            add(beside, (e - 1, c, planes[n]), value)
                row_at += 3 * count

    @pl.when(step == pl.num_programs(0) - 1)
    def _():
        row8 = lax.broadcasted_iota(jnp.int32, (8, 2 * 128), 0)
        zero = jnp.zeros((8, 2 * 128), f32)
        for t in range(XTILES):
            turned = []
            for c in range(3):
                pieces = []
                for plane in range(XPT * t, XPT * t + XPT):
                    if plane > UPPER[-1]:
                        pieces.append(jnp.zeros((YS, 2 * 128), f32))
                        continue
                    parts = [zero] + [near[c, plane, 8 * i : 8 * i + 8, :] for i in range(3)]
                    if others:
                        if others == 1:
                            value = beside[0, c, plane]
                            low_part = jnp.where(my == 0, 0.0, value)
                            high_part = jnp.where(my == 0, value, 0.0)
                        else:
                            low_part, high_part = beside[0, c, plane], beside[1, c, plane]
                        moved = pltpu.roll(low_part, 4, 0)
                        parts[0] = jnp.where(row8 >= 4, moved, 0.0)
                        parts[1] = parts[1] + jnp.where(row8 < 4, moved, 0.0)
                        parts[3] = parts[3] + high_part
                    pieces.extend(parts)
                stacked = jnp.concatenate(pieces, axis=0)
                turned.append(
                    jnp.concatenate([stacked[:, :128].T, stacked[:, 128:].T[: ROWS - 128]], axis=0)
                )
            at = slice(128 * t, 128 * t + 128)
            rhs_ref[:, at] = (
                turned[0]
                + pltpu.roll(turned[1], ROWS - 1, 0)
                - pltpu.roll(turned[1], 1, 0)
            )
            density_ref[:, at] = turned[2]
        up_ref[0] = rhs_ref[UP_AT : UP_AT + HALO, :]
        up_ref[1] = density_ref[UP_AT : UP_AT + HALO, :]
        down_ref[0] = rhs_ref[DOWN_AT : DOWN_AT + HALO, :]
        down_ref[1] = density_ref[DOWN_AT : DOWN_AT + HALO, :]


def chebyshev_factors():
    half_width = 6.0 / (6.0 + base_screen)
    sigma_ratio = 1.0 / half_width
    rho_prev = half_width
    factors = []
    for _ in range(ITERS - 1):
        rho_next = 1.0 / (2.0 * sigma_ratio - rho_prev)
        factors.append((rho_next * rho_prev, 2.0 * rho_next / half_width))
        rho_prev = rho_next
    return factors


def solve_kernel(
    shape, rhs_ref, density_ref, from_low_ref, from_high_ref, own_ref,
    indicator_ref, values_ref,
    first, second, scaled, inverse, total, edge, high_ref, low_ref,
):
    gx, gy, gz = shape
    mx, my, mz = lax.axis_index("gx"), lax.axis_index("gy"), lax.axis_index("gz")
    edge[...] = jnp.zeros_like(edge)
    low_at, high_at = UP_AT - CZ, DOWN_AT + CZ - (ROWS - 16)
    edge[0, :, low_at : low_at + HALO, :] = from_low_ref[...]
    edge[1, :, high_at : high_at + HALO, :] = from_high_ref[...]

    def with_edge(ref, channel, i):
        value = ref[8 * i : 8 * i + 8, :]
        if i < 2:
            return value + edge[0, channel, 8 * i : 8 * i + 8, :]
        if i >= ROWS // 8 - 2:
            at = 8 * (i - ROWS // 8 + 2)
            return value + edge[1, channel, at : at + 8, :]
        return value

    lane = lax.broadcasted_iota(jnp.int32, (8, LANES), 1)
    x, y = lane // YS - XO + mx * CX, lane % YS - YO + my * CY
    inside_xy = (x >= 0) & (x < gx * CX) & (y >= 0) & (y < gy * CY)
    zero = jnp.zeros((8, LANES), f32)
    first[0:8, :] = zero
    first[ROWS + 8 : ROWS + 16, :] = zero
    second[0:8, :] = zero
    second[ROWS + 8 : ROWS + 16, :] = zero
    for i in range(ROWS // 8):
        at = slice(8 * i, 8 * i + 8)
        z = lax.broadcasted_iota(jnp.int32, (8, LANES), 0) + (8 * i - ZO) + mz * CZ
        inside = inside_xy & (z >= 0) & (z < gz * CZ)
        diagonal = 6.0 + base_screen + point_screen * with_edge(density_ref, 1, i)
        inv = jnp.where(inside, 1.0 / diagonal, 0.0)
        start = with_edge(rhs_ref, 0, i) * inv
        inverse[at, :] = inv
        scaled[at, :] = start
        total[at, :] = start
        first[8 * i + 8 : 8 * i + 16, :] = start

    now, later = first, second
    factors = chebyshev_factors()
    for k, (keep, gain) in enumerate(factors):
        last = k + 1 == len(factors)
        for i in range(ROWS // 8):
            at = slice(8 * i, 8 * i + 8)
            here = now[8 * i + 8 : 8 * i + 16, :]
            near = now[8 * i + 7 : 8 * i + 15, :] + now[8 * i + 9 : 8 * i + 17, :]
            near = near + pltpu.roll(here, 1, 1) + pltpu.roll(here, LANES - 1, 1)
            near = near + pltpu.roll(here, YS, 1) + pltpu.roll(here, LANES - YS, 1)
            left = scaled[at, :] - here + inverse[at, :] * near
            ahead = keep * here + gain * left
            total[at, :] += ahead
            if not last:
                scaled[at, :] = left
                later[8 * i + 8 : 8 * i + 16, :] = ahead
        now, later = later, now

    for t in range(FIRST_TILE, END_TILE):
        turned = total[ZO : ZO + CZ, 128 * t : 128 * t + 128].T
        for i in range(XPT):
            plane = XPT * t + i - XO
            if 0 <= plane < CX:
                indicator_ref[plane] = turned[YS * i + YO : YS * i + YO + CY, :]

    groups = own_ref.shape[1]
    first_lane, end_lane = 128 * FIRST_TILE, 128 * END_TILE
    u_high, u_low = split(total[:, first_lane:end_lane])
    z_row = row_iota(ROWS) - float(ZO)
    y_row = row_iota(24) + float(8 - YO)
    blank = jnp.zeros((8, 128), f32)
    for chunk in range(groups // GROUPS):
        for g in range(GROUPS):
            main = own_ref[0, chunk * GROUPS + g]
            more = own_ref[1, chunk * GROUPS + g]
            off_x, off_y = main[4:5], main[5:6]
            hy = hat(y_row, more[0:1], 1.0 - off_y, off_y)
            at = slice(128 * g, 128 * g + 128)
            for plane in range(XPT * FIRST_TILE, XPT * END_TILE):
                start = YS * plane - first_lane
                if 0 <= plane - XO <= CX:
                    hx = hat(float(plane - XO), main[7:8], 1.0 - off_x, off_x)
                    high, low = split(jnp.concatenate([blank, hx * hy], axis=0))
                else:
                    high = jnp.zeros((YS, 128), bf16)
                    low = high
                high_ref[start : start + YS, at] = high
                low_ref[start : start + YS, at] = low
        got = dot_nn(u_high, high_ref[...]) + dot_nn(u_low, high_ref[...])
        got = got + dot_nn(u_high, low_ref[...])
        rows = []
        for g in range(GROUPS):
            main = own_ref[0, chunk * GROUPS + g]
            more = own_ref[1, chunk * GROUPS + g]
            off_z = main[6:7]
            hz = hat(z_row, more[1:2], 1.0 - off_z, off_z)
            value = jnp.sum(hz * got[:, 128 * g : 128 * g + 128], axis=0, keepdims=True)
            rows.append(jnp.where(main[3:4] > 0.0, value, 0.0))
        values = jnp.concatenate(rows, axis=0)
        for q in range(4):
            moved = values if q == 0 else pltpu.roll(values, 128 - 32 * q, 1)
            start = q * groups + chunk * GROUPS
            values_ref[start : start + GROUPS, :] = moved[:, 0:32]


def on_device(shape, point_data, point_cells, send_counts):
    gx, gy, gz = shape
    sources = gx * gy * gz
    slots = point_data.shape[3]
    bricks = 3 * (1 + other_count(gy))
    rows = 8 * -(-(bricks + -(-bricks // 4)) // 4)
    groups = sources // 4
    params = pltpu.CompilerParams(vmem_limit_bytes=VMEM_LIMIT)
    whole = pl.BlockSpec(memory_space=pltpu.VMEM)

    outgoing = pl.pallas_call(
        functools.partial(pack_kernel, shape),
        out_shape=jax.ShapeDtypeStruct((sources, rows, 128), f32),
        in_specs=[whole, whole, whole],
        out_specs=whole,
        scratch_shapes=[
            pltpu.VMEM((sources, 8, slots), f32),
            pltpu.VMEM((sources, 2, slots), f32),
        ],
        compiler_params=params,
        name="pack_points",
    )(
        jnp.transpose(point_data, (0, 2, 1, 3)),
        jnp.transpose(point_cells, (0, 2, 1, 3)),
        send_counts.reshape(sources, 1),
    )

    arrived = lax.all_to_all(outgoing, AXES, split_axis=0, concat_axis=0, tiled=True)
    arrived = arrived.reshape(4, groups, rows, 128)

    others = other_count(gy)
    lines = 0
    for planes in (CENTER, LOWER, UPPER):
        for high, size in ((24, 4),) + ((8, 12),) * others:
            for start in range(0, len(planes), size):
                count = min(size, len(planes) - start)
                lines += 3 * 16 * -(-count * high // 16)
    wide_shape = jax.ShapeDtypeStruct((ROWS, LANES), f32)
    edge_shape = jax.ShapeDtypeStruct((2, HALO, LANES), f32)
    steps = groups // GROUPS
    rhs, density, up, down, own = pl.pallas_call(
        functools.partial(splat_kernel, shape),
        grid=(steps,),
        out_shape=(
            wide_shape, wide_shape, edge_shape, edge_shape,
            jax.ShapeDtypeStruct((2, groups, 8, 128), f32),
        ),
        in_specs=[pl.BlockSpec((4, GROUPS, rows, 128), lambda s: (0, s, 0, 0))],
        out_specs=(
            pl.BlockSpec((ROWS, LANES), lambda s: (0, 0)),
            pl.BlockSpec((ROWS, LANES), lambda s: (0, 0)),
            pl.BlockSpec((2, HALO, LANES), lambda s: (0, 0, 0)),
            pl.BlockSpec((2, HALO, LANES), lambda s: (0, 0, 0)),
            pl.BlockSpec((2, GROUPS, 8, 128), lambda s: (0, s, 0, 0)),
        ),
        scratch_shapes=[
            pltpu.VMEM((rows // 2, GROUPS, 8, 128), f32),
            pltpu.VMEM((2, lines, 128 * GROUPS), bf16),
            pltpu.VMEM((bricks, 2, ROWS, 128 * GROUPS), bf16),
            pltpu.VMEM((bricks, 2, len(CENTER), GROUPS, 128), f32),
            pltpu.VMEM((3, XPT * XTILES, 24, 2 * 128), f32),
            pltpu.VMEM((max(others, 1), 3, XPT * XTILES, 8, 2 * 128), f32),
        ],
        compiler_params=params,
        name="splat_points",
    )(arrived)

    from_low = lax.ppermute(up, "gz", [(i, i + 1) for i in range(gz - 1)])
    from_high = lax.ppermute(down, "gz", [(i + 1, i) for i in range(gz - 1)])

    depth = 128 * (END_TILE - FIRST_TILE)
    indicator, values = pl.pallas_call(
        functools.partial(solve_kernel, shape),
        out_shape=(
            jax.ShapeDtypeStruct((CX, CY, CZ), f32),
            jax.ShapeDtypeStruct((sources, slots), f32),
        ),
        in_specs=[whole] * 5,
        out_specs=(whole, whole),
        scratch_shapes=[
            pltpu.VMEM((ROWS + 16, LANES), f32),
            pltpu.VMEM((ROWS + 16, LANES), f32),
            pltpu.VMEM((ROWS, LANES), f32),
            pltpu.VMEM((ROWS, LANES), f32),
            pltpu.VMEM((ROWS, LANES), f32),
            pltpu.VMEM((2, 2, 16, LANES), f32),
            pltpu.VMEM((depth, 128 * GROUPS), bf16),
            pltpu.VMEM((depth, 128 * GROUPS), bf16),
        ],
        compiler_params=params,
        name="solve_and_read",
    )(rhs, density, from_low, from_high, own)

    returned = lax.all_to_all(values, AXES, split_axis=0, concat_axis=0, tiled=True)
    return indicator, returned.reshape(1, sources, slots)


def solution(mesh):
    shape = tuple(mesh.shape[axis] for axis in AXES)
    in_specs = (
        P(AXES, None, None, None),
        P(AXES, None, None, None),
        P(AXES, None),
    )
    out_specs = (P("gx", "gy", "gz"), P(AXES, None, None))
    return jax.shard_map(
        functools.partial(on_device, shape),
        mesh=mesh,
        in_specs=in_specs,
        out_specs=out_specs,
        check_vma=False,
    )
```

```python
import functools

import jax
import jax.numpy as jnp
from jax import lax
from jax.experimental import pallas as pl
from jax.experimental.pallas import tpu as pltpu
from jax.sharding import PartitionSpec as P

CX = 16
CY = 16
CZ = 128
ITERS = 6

base_screen = 0.25
point_screen = 4.0

AXES = ("gx", "gy", "gz")
REACH = ITERS - 1
XO = REACH
YO = 9
ZO = 8
YS = 32
XPT = 128 // YS
XTILES = -(-(CX + 2 * REACH + 1) // XPT)
LANES = XTILES * 128
ROWS = CZ + 16
CENTER = tuple(range(XO - 1, XO + CX + 2))
LOWER = tuple(range(0, XO + 2))
UPPER = tuple(range(XO + CX - 1, XO + CX + REACH + 1))
FIRST_TILE, END_TILE = XO // XPT, (XO + CX) // XPT + 1
WINDOW_LOW = YO - REACH
WINDOW_HIGH = YO + CY - 1
UP_AT = ZO + CZ - REACH
DOWN_AT = ZO - 1
HALO = 8
GROUPS = 8
VMEM_LIMIT = 56 * 1024 * 1024

f32 = jnp.float32
bf16 = jnp.bfloat16


def split(value):
    high = value.astype(bf16)
    return high, (value - high.astype(f32)).astype(bf16)


def dot_nt(lhs, rhs):
    return lax.dot_general(lhs, rhs, (((1,), (1,)), ((), ())), preferred_element_type=f32)


def dot_nn(lhs, rhs):
    return lax.dot_general(lhs, rhs, (((1,), (0,)), ((), ())), preferred_element_type=f32)


def other_count(gy):
    return min(gy - 1, 2)


def extra_place(brick, bricks):
    return bricks + brick // 4, 2 * (brick % 4)


def pack_kernel(shape, data_ref, cells_ref, counts_ref, out_ref, main, extra):
    gx, gy, gz = shape
    slots = data_ref.shape[3]
    sources = gx * gy * gz
    lane = lax.broadcasted_iota(jnp.int32, (sources, slots), 1)
    at_row = lax.broadcasted_iota(jnp.int32, (sources, sources), 0)
    at_lane = lax.broadcasted_iota(jnp.int32, (sources, sources), 1)
    counts = jnp.where(at_row == at_lane, counts_ref[...], 0).astype(f32)
    counts = jnp.sum(counts, axis=1, keepdims=True).astype(jnp.int32)
    others = other_count(gy)
    bricks = 3 * (1 + others)
    weight = jnp.where(lane < counts, data_ref[0, 3], 0.0)
    for c in range(3):
        main[:, c, :] = data_ref[0, c] * (-0.5 * weight)
    main[:, 3, :] = weight
    for c in range(4, 7):
        main[:, c, :] = data_ref[0, c]
    main[:, 7, :] = cells_ref[0, 0].astype(f32)
    extra[:, 0, :] = cells_ref[0, 1].astype(f32)
    extra[:, 1, :] = cells_ref[0, 2].astype(f32)
    out_ref[...] = jnp.zeros_like(out_ref)
    for d in range(gx * gy * gz):
        x, y, z = d // (gy * gz), (d // gz) % gy, d % gz
        if others == 0:
            ys = (y,)
        elif others == 1:
            ys = (y, 1 - y)
        else:
            ys = (y, y - 1, y + 1)
        for e, by in enumerate(ys):
            for o, bx in enumerate((x, x - 1, x + 1)):
                if not (0 <= bx < gx and 0 <= by < gy):
                    continue
                b = e * 3 + o
                source = (bx * gy + by) * gz + z
                tile, part = b // 4, b % 4
                out_ref[d, 8 * tile : 8 * tile + 8, slots * part : slots * part + slots] = main[source]
                place, row = extra_place(b, bricks)
                tile, part = place // 4, place % 4
                out_ref[
                    d, 8 * tile + row : 8 * tile + row + 2, slots * part : slots * part + slots
                ] = extra[source]


def hat(coordinate, cell, low, high):
    away = coordinate - cell
    return jnp.where(away == 0.0, low, jnp.where(away == 1.0, high, 0.0))


def hat_slope(coordinate, cell, low, high):
    away = coordinate - cell
    rising = jnp.where(away == -1.0, low, jnp.where(away == 0.0, high, 0.0))
    return rising - jnp.where(away == 1.0, low, jnp.where(away == 2.0, high, 0.0))


def row_iota(rows):
    return lax.broadcasted_iota(jnp.int32, (rows, 128), 0).astype(f32)


def stack_rows(parts, multiple):
    have = sum(part.shape[0] for part in parts)
    if have % multiple:
        parts = parts + [jnp.zeros((multiple - have % multiple, 128), f32)]
    return jnp.concatenate(parts, axis=0) if len(parts) > 1 else parts[0]


def splat_kernel(
    shape, recv_ref, rhs_ref, density_ref, up_ref, down_ref, own_ref,
    points, left_ref, right_ref, hx_ref, near, beside,
):
    gx, gy, gz = shape
    mx, my, mz = lax.axis_index("gx"), lax.axis_index("gy"), lax.axis_index("gz")
    step = pl.program_id(0)
    single = recv_ref.shape[1] * 4 == gx * gy * gz
    others = other_count(gy)
    bricks = 3 * (1 + others)
    tiles = recv_ref.shape[2] // 8
    lane_part = lax.broadcasted_iota(jnp.int32, (8, 128), 1) // 32
    span = 128 * GROUPS
    written = set()

    def add(ref, place, value):
        if single and place not in written:
            written.add(place)
            ref[place + (slice(None), slice(0, ROWS))] = value
        else:
            ref[place + (slice(None), slice(0, ROWS))] += value

    if not single:
        @pl.when(step == 0)
        def _():
            near[...] = jnp.zeros_like(near)
            beside[...] = jnp.zeros_like(beside)

    for t in range(tiles):
        for g in range(GROUPS):
            given = [recv_ref[q, g, 8 * t : 8 * t + 8, :] for q in range(4)]
            for k in range(4):
                if 4 * t + k >= bricks + -(-bricks // 4):
                    continue
                merged = None
                for q in range(4):
                    moved = given[q] if q == k else pltpu.roll(given[q], (32 * (q - k)) % 128, 1)
                    merged = moved if merged is None else jnp.where(lane_part == q, moved, merged)
                points[4 * t + k, g] = merged
    own_ref[0] = points[0]
    own_ref[1] = points[bricks]

    z_limit = jnp.where(mz == gz - 1, CZ, CZ + 1).astype(f32)
    z_row = row_iota(ROWS) - float(ZO)
    own_row = row_iota(24) + float(8 - YO)

    row_at = 0
    for e in reversed(range(1 + others)):
        if e == 0:
            y_limit = jnp.where(my == gy - 1, CY, CY + 1).astype(f32)
            y_row = own_row
        else:
            above = my == 0 if others == 1 else jnp.bool_(e == 2)
            y_limit = jnp.where(
                jnp.logical_and(above, my + 1 == gy - 1), CY, CY + 1
            ).astype(f32)
            first = jnp.where(above, WINDOW_HIGH - YO - CY, WINDOW_LOW - YO + CY)
            y_row = row_iota(8) + first.astype(f32)
        high = y_row.shape[0]
        for o, shift, planes in ((1, -1, LOWER), (0, 0, CENTER), (2, 1, UPPER)):
            b = e * 3 + o
            place, row = extra_place(b, bricks)
            x_limit = jnp.where(mx + shift == gx - 1, CX, CX + 1).astype(f32)
            cell_x = points[b, :, 7, :]
            off_x = points[b, :, 4, :]
            low_x = 1.0 - off_x
            high_x = jnp.where(cell_x + 1.0 < x_limit, off_x, 0.0)
            for n, plane in enumerate(planes):
                at = float(plane - XO - CX * shift)
                hx_ref[b, 0, n] = hat(at, cell_x, low_x, high_x)
                hx_ref[b, 1, n] = hat_slope(at, cell_x, low_x, high_x)
            y_parts = []
            for g in range(GROUPS):
                main = points[b, g]
                more = points[place, g]
                cell_y, cell_z = more[row : row + 1], more[row + 1 : row + 2]
                off_y, off_z = main[5:6], main[6:7]
                high_z = jnp.where(cell_z + 1.0 < z_limit, off_z, 0.0)
                hz_high, hz_low = split(hat(z_row, cell_z, 1.0 - off_z, high_z))
                at = slice(128 * g, 128 * g + 128)
                right_ref[b, 0, at, 0:ROWS] = hz_high.T
                right_ref[b, 1, at, 0:ROWS] = hz_low.T
                high_y = jnp.where(cell_y + 1.0 < y_limit, off_y, 0.0)
                hy = hat(y_row, cell_y, 1.0 - off_y, high_y)
                dy = hat_slope(y_row, cell_y, 1.0 - off_y, high_y)
                y_parts.append((main[0:1] * hy, main[1:2] * dy, main[2:3] * hy, main[3:4] * hy))
            count = -(-len(planes) * high // 16) * 16
            for c in range(3):
                for g in range(GROUPS):
                    part_x0, part_y1, part_z, part_w = y_parts[g]
                    at = slice(128 * g, 128 * g + 128)
                    for start in range(0, len(planes), 2):
                        rows = []
                        for n in range(start, min(start + 2, len(planes))):
                            hx = hx_ref[b, 0, n, g : g + 1, :]
                            if c == 0:
                                dx = hx_ref[b, 1, n, g : g + 1, :]
                                rows.append(dx * part_x0 + hx * part_y1)
                            else:
                                rows.append(hx * (part_z if c == 1 else part_w))
                        main_part, rest = split(stack_rows(rows, 16))
                        begin = row_at + c * count + start * high
                        lines = slice(begin, begin + main_part.shape[0])
                        left_ref[0, lines, at] = main_part
                        left_ref[1, lines, at] = rest
            lines = slice(row_at, row_at + 3 * count)
            got = dot_nn(left_ref[0, lines, :], right_ref[b, 0, :, 0:ROWS])
            got = got + dot_nn(left_ref[1, lines, :], right_ref[b, 0, :, 0:ROWS])
            got = got + dot_nn(left_ref[0, lines, :], right_ref[b, 1, :, 0:ROWS])
            for c in range(3):
                for n, plane in enumerate(planes):
                    begin = c * count + n * high
                    value = got[begin : begin + high]
                    if e == 0:
                        add(near, (c, plane), value)
                    else:
                        add(beside, (e - 1, c, plane), value)
            row_at += 3 * count

    @pl.when(step == pl.num_programs(0) - 1)
    def _():
        row8 = lax.broadcasted_iota(jnp.int32, (8, 2 * 128), 0)
        zero = jnp.zeros((8, 2 * 128), f32)
        for t in range(XTILES):
            turned = []
            for c in range(3):
                pieces = []
                for plane in range(XPT * t, XPT * t + XPT):
                    if plane > UPPER[-1]:
                        pieces.append(jnp.zeros((YS, 2 * 128), f32))
                        continue
                    parts = [zero] + [near[c, plane, 8 * i : 8 * i + 8, :] for i in range(3)]
                    if others:
                        if others == 1:
                            value = beside[0, c, plane]
                            low_part = jnp.where(my == 0, 0.0, value)
                            high_part = jnp.where(my == 0, value, 0.0)
                        else:
                            low_part, high_part = beside[0, c, plane], beside[1, c, plane]
                        moved = pltpu.roll(low_part, 4, 0)
                        parts[0] = jnp.where(row8 >= 4, moved, 0.0)
                        parts[1] = parts[1] + jnp.where(row8 < 4, moved, 0.0)
                        parts[3] = parts[3] + high_part
                    pieces.extend(parts)
                stacked = jnp.concatenate(pieces, axis=0)
                turned.append(
                    jnp.concatenate([stacked[:, :128].T, stacked[:, 128:].T[: ROWS - 128]], axis=0)
                )
            at = slice(128 * t, 128 * t + 128)
            rhs_ref[:, at] = (
                turned[0]
                + pltpu.roll(turned[1], ROWS - 1, 0)
                - pltpu.roll(turned[1], 1, 0)
            )
            density_ref[:, at] = turned[2]
        up_ref[0] = rhs_ref[UP_AT : UP_AT + HALO, :]
        up_ref[1] = density_ref[UP_AT : UP_AT + HALO, :]
        down_ref[0] = rhs_ref[DOWN_AT : DOWN_AT + HALO, :]
        down_ref[1] = density_ref[DOWN_AT : DOWN_AT + HALO, :]


def chebyshev_factors():
    half_width = 6.0 / (6.0 + base_screen)
    sigma_ratio = 1.0 / half_width
    rho_prev = half_width
    factors = []
    for _ in range(ITERS - 1):
        rho_next = 1.0 / (2.0 * sigma_ratio - rho_prev)
        factors.append((rho_next * rho_prev, 2.0 * rho_next / half_width))
        rho_prev = rho_next
    return factors


def solve_kernel(
    shape, rhs_ref, density_ref, from_low_ref, from_high_ref, own_ref,
    indicator_ref, values_ref,
    first, second, scaled, inverse, total, edge, high_ref, low_ref,
):
    gx, gy, gz = shape
    mx, my, mz = lax.axis_index("gx"), lax.axis_index("gy"), lax.axis_index("gz")
    edge[...] = jnp.zeros_like(edge)
    low_at, high_at = UP_AT - CZ, DOWN_AT + CZ - (ROWS - 16)
    edge[0, :, low_at : low_at + HALO, :] = from_low_ref[...]
    edge[1, :, high_at : high_at + HALO, :] = from_high_ref[...]

    def with_edge(ref, channel, i):
        value = ref[8 * i : 8 * i + 8, :]
        if i < 2:
            return value + edge[0, channel, 8 * i : 8 * i + 8, :]
        if i >= ROWS // 8 - 2:
            at = 8 * (i - ROWS // 8 + 2)
            return value + edge[1, channel, at : at + 8, :]
        return value

    lane = lax.broadcasted_iota(jnp.int32, (8, LANES), 1)
    x, y = lane // YS - XO + mx * CX, lane % YS - YO + my * CY
    inside_xy = (x >= 0) & (x < gx * CX) & (y >= 0) & (y < gy * CY)
    zero = jnp.zeros((8, LANES), f32)
    first[0:8, :] = zero
    first[ROWS + 8 : ROWS + 16, :] = zero
    second[0:8, :] = zero
    second[ROWS + 8 : ROWS + 16, :] = zero
    for i in range(ROWS // 8):
        at = slice(8 * i, 8 * i + 8)
        z = lax.broadcasted_iota(jnp.int32, (8, LANES), 0) + (8 * i - ZO) + mz * CZ
        inside = inside_xy & (z >= 0) & (z < gz * CZ)
        diagonal = 6.0 + base_screen + point_screen * with_edge(density_ref, 1, i)
        inv = jnp.where(inside, 1.0 / diagonal, 0.0)
        start = with_edge(rhs_ref, 0, i) * inv
        inverse[at, :] = inv
        scaled[at, :] = start
        total[at, :] = start
        first[8 * i + 8 : 8 * i + 16, :] = start

    now, later = first, second
    factors = chebyshev_factors()
    for k, (keep, gain) in enumerate(factors):
        last = k + 1 == len(factors)
        for i in range(ROWS // 8):
            at = slice(8 * i, 8 * i + 8)
            here = now[8 * i + 8 : 8 * i + 16, :]
            near = now[8 * i + 7 : 8 * i + 15, :] + now[8 * i + 9 : 8 * i + 17, :]
            near = near + pltpu.roll(here, 1, 1) + pltpu.roll(here, LANES - 1, 1)
            near = near + pltpu.roll(here, YS, 1) + pltpu.roll(here, LANES - YS, 1)
            left = scaled[at, :] - here + inverse[at, :] * near
            ahead = keep * here + gain * left
            total[at, :] += ahead
            if not last:
                scaled[at, :] = left
                later[8 * i + 8 : 8 * i + 16, :] = ahead
        now, later = later, now

    for t in range(FIRST_TILE, END_TILE):
        turned = total[ZO : ZO + CZ, 128 * t : 128 * t + 128].T
        for i in range(XPT):
            plane = XPT * t + i - XO
            if 0 <= plane < CX:
                indicator_ref[plane] = turned[YS * i + YO : YS * i + YO + CY, :]

    groups = own_ref.shape[1]
    first_lane, end_lane = 128 * FIRST_TILE, 128 * END_TILE
    u_high, u_low = split(total[:, first_lane:end_lane])
    z_row = row_iota(ROWS) - float(ZO)
    y_row = row_iota(24) + float(8 - YO)
    blank = jnp.zeros((8, 128), f32)
    for chunk in range(groups // GROUPS):
        for g in range(GROUPS):
            main = own_ref[0, chunk * GROUPS + g]
            more = own_ref[1, chunk * GROUPS + g]
            off_x, off_y = main[4:5], main[5:6]
            hy = hat(y_row, more[0:1], 1.0 - off_y, off_y)
            at = slice(128 * g, 128 * g + 128)
            for plane in range(XPT * FIRST_TILE, XPT * END_TILE):
                start = YS * plane - first_lane
                if 0 <= plane - XO <= CX:
                    hx = hat(float(plane - XO), main[7:8], 1.0 - off_x, off_x)
                    high, low = split(jnp.concatenate([blank, hx * hy], axis=0))
                else:
                    high = jnp.zeros((YS, 128), bf16)
                    low = high
                high_ref[start : start + YS, at] = high
                low_ref[start : start + YS, at] = low
        got = dot_nn(u_high, high_ref[...]) + dot_nn(u_low, high_ref[...])
        got = got + dot_nn(u_high, low_ref[...])
        rows = []
        for g in range(GROUPS):
            main = own_ref[0, chunk * GROUPS + g]
            more = own_ref[1, chunk * GROUPS + g]
            off_z = main[6:7]
            hz = hat(z_row, more[1:2], 1.0 - off_z, off_z)
            value = jnp.sum(hz * got[:, 128 * g : 128 * g + 128], axis=0, keepdims=True)
            rows.append(jnp.where(main[3:4] > 0.0, value, 0.0))
        values = jnp.concatenate(rows, axis=0)
        for q in range(4):
            moved = values if q == 0 else pltpu.roll(values, 128 - 32 * q, 1)
            start = q * groups + chunk * GROUPS
            values_ref[start : start + GROUPS, :] = moved[:, 0:32]


def on_device(shape, point_data, point_cells, send_counts):
    gx, gy, gz = shape
    sources = gx * gy * gz
    slots = point_data.shape[3]
    bricks = 3 * (1 + other_count(gy))
    rows = 8 * -(-(bricks + -(-bricks // 4)) // 4)
    groups = sources // 4
    params = pltpu.CompilerParams(vmem_limit_bytes=VMEM_LIMIT)
    whole = pl.BlockSpec(memory_space=pltpu.VMEM)

    outgoing = pl.pallas_call(
        functools.partial(pack_kernel, shape),
        out_shape=jax.ShapeDtypeStruct((sources, rows, 128), f32),
        in_specs=[whole, whole, whole],
        out_specs=whole,
        scratch_shapes=[
            pltpu.VMEM((sources, 8, slots), f32),
            pltpu.VMEM((sources, 2, slots), f32),
        ],
        compiler_params=params,
        name="pack_points",
    )(
        jnp.transpose(point_data, (0, 2, 1, 3)),
        jnp.transpose(point_cells, (0, 2, 1, 3)),
        send_counts,
    )

    arrived = lax.all_to_all(outgoing, AXES, split_axis=0, concat_axis=0, tiled=True)
    arrived = arrived.reshape(4, groups, rows, 128)

    others = other_count(gy)
    lines = 0
    for planes in (CENTER, LOWER, UPPER):
        for high in (24,) + (8,) * others:
            lines += 3 * 16 * -(-len(planes) * high // 16)
    wide_shape = jax.ShapeDtypeStruct((ROWS, LANES), f32)
    edge_shape = jax.ShapeDtypeStruct((2, HALO, LANES), f32)
    steps = groups // GROUPS
    rhs, density, up, down, own = pl.pallas_call(
        functools.partial(splat_kernel, shape),
        grid=(steps,),
        out_shape=(
            wide_shape, wide_shape, edge_shape, edge_shape,
            jax.ShapeDtypeStruct((2, groups, 8, 128), f32),
        ),
        in_specs=[pl.BlockSpec((4, GROUPS, rows, 128), lambda s: (0, s, 0, 0))],
        out_specs=(
            pl.BlockSpec((ROWS, LANES), lambda s: (0, 0)),
            pl.BlockSpec((ROWS, LANES), lambda s: (0, 0)),
            pl.BlockSpec((2, HALO, LANES), lambda s: (0, 0, 0)),
            pl.BlockSpec((2, HALO, LANES), lambda s: (0, 0, 0)),
            pl.BlockSpec((2, GROUPS, 8, 128), lambda s: (0, s, 0, 0)),
        ),
        scratch_shapes=[
            pltpu.VMEM((rows // 2, GROUPS, 8, 128), f32),
            pltpu.VMEM((2, lines, 128 * GROUPS), bf16),
            pltpu.VMEM((bricks, 2, 128 * GROUPS, 2 * 128), bf16),
            pltpu.VMEM((bricks, 2, len(CENTER), GROUPS, 128), f32),
            pltpu.VMEM((3, XPT * XTILES, 24, 2 * 128), f32),
            pltpu.VMEM((max(others, 1), 3, XPT * XTILES, 8, 2 * 128), f32),
        ],
        compiler_params=params,
        name="splat_points",
    )(arrived)

    from_low = lax.ppermute(up, "gz", [(i, i + 1) for i in range(gz - 1)])
    from_high = lax.ppermute(down, "gz", [(i + 1, i) for i in range(gz - 1)])

    depth = 128 * (END_TILE - FIRST_TILE)
    indicator, values = pl.pallas_call(
        functools.partial(solve_kernel, shape),
        out_shape=(
            jax.ShapeDtypeStruct((CX, CY, CZ), f32),
            jax.ShapeDtypeStruct((sources, slots), f32),
        ),
        in_specs=[whole] * 5,
        out_specs=(whole, whole),
        scratch_shapes=[
            pltpu.VMEM((ROWS + 16, LANES), f32),
            pltpu.VMEM((ROWS + 16, LANES), f32),
            pltpu.VMEM((ROWS, LANES), f32),
            pltpu.VMEM((ROWS, LANES), f32),
            pltpu.VMEM((ROWS, LANES), f32),
            pltpu.VMEM((2, 2, 16, LANES), f32),
            pltpu.VMEM((depth, 128 * GROUPS), bf16),
            pltpu.VMEM((depth, 128 * GROUPS), bf16),
        ],
        compiler_params=params,
        name="solve_and_read",
    )(rhs, density, from_low, from_high, own)

    returned = lax.all_to_all(values, AXES, split_axis=0, concat_axis=0, tiled=True)
    return indicator, returned.reshape(1, sources, slots)


def solution(mesh):
    shape = tuple(mesh.shape[axis] for axis in AXES)
    in_specs = (
        P(AXES, None, None, None),
        P(AXES, None, None, None),
        P(AXES, None),
    )
    out_specs = (P("gx", "gy", "gz"), P(AXES, None, None))
    return jax.shard_map(
        functools.partial(on_device, shape),
        mesh=mesh,
        in_specs=in_specs,
        out_specs=out_specs,
        check_vma=False,
    )
```

```python
import functools

import jax
import jax.numpy as jnp
from jax import lax
from jax.experimental import pallas as pl
from jax.experimental.pallas import tpu as pltpu
from jax.sharding import PartitionSpec as P

CX = 16
CY = 16
CZ = 128
ITERS = 6

base_screen = 0.25
point_screen = 4.0

AXES = ("gx", "gy", "gz")
REACH = ITERS - 1
XO = REACH
YO = 9
ZO = 8
YS = 32
XPT = 128 // YS
XTILES = -(-(CX + 2 * REACH + 1) // XPT)
ROWS = CZ + 16
CENTER = tuple(range(XO - 1, XO + CX + 2))
LOWER = tuple(range(0, XO + 2))
UPPER = tuple(range(XO + CX - 1, XO + CX + REACH + 1))
FIRST_TILE, END_TILE = XO // XPT, (XO + CX) // XPT + 1
WINDOW_LOW = YO - REACH
WINDOW_HIGH = YO + CY - 1
UP_AT = ZO + CZ - REACH
DOWN_AT = ZO - 1
HALO = 8
GROUPS = 8
MIB = 1024 * 1024

f32 = jnp.float32
bf16 = jnp.bfloat16


def split(value):
    high = value.astype(bf16)
    return high, (value - high.astype(f32)).astype(bf16)


def dot_nt(lhs, rhs):
    return lax.dot_general(lhs, rhs, (((1,), (1,)), ((), ())), preferred_element_type=f32)


def dot_nn(lhs, rhs):
    return lax.dot_general(lhs, rhs, (((1,), (0,)), ((), ())), preferred_element_type=f32)


def other_count(gy):
    return min(gy - 1, 2)


def extra_place(brick, bricks):
    return bricks + brick // 4, 2 * (brick % 4)


def pack_kernel(shape, data_ref, cells_ref, counts_ref, out_ref, main, extra):
    gx, gy, gz = shape
    slots = data_ref.shape[3]
    sources = gx * gy * gz
    lane = lax.broadcasted_iota(jnp.int32, (sources, slots), 1)
    at_row = lax.broadcasted_iota(jnp.int32, (sources, sources), 0)
    at_lane = lax.broadcasted_iota(jnp.int32, (sources, sources), 1)
    counts = jnp.where(at_row == at_lane, counts_ref[...], 0).astype(f32)
    counts = jnp.sum(counts, axis=1, keepdims=True).astype(jnp.int32)
    others = other_count(gy)
    bricks = 3 * (1 + others)
    weight = jnp.where(lane < counts, data_ref[0, 3], 0.0)
    for c in range(3):
        main[:, c, :] = data_ref[0, c] * (-0.5 * weight)
    main[:, 3, :] = weight
    for c in range(4, 7):
        main[:, c, :] = data_ref[0, c]
    main[:, 7, :] = cells_ref[0, 0].astype(f32)
    extra[:, 0, :] = cells_ref[0, 1].astype(f32)
    extra[:, 1, :] = cells_ref[0, 2].astype(f32)
    out_ref[...] = jnp.zeros_like(out_ref)
    for d in range(gx * gy * gz):
        x, y, z = d // (gy * gz), (d // gz) % gy, d % gz
        if others == 0:
            ys = (y,)
        elif others == 1:
            ys = (y, 1 - y)
        else:
            ys = (y, y - 1, y + 1)
        for e, by in enumerate(ys):
            for o, bx in enumerate((x, x - 1, x + 1)):
                if not (0 <= bx < gx and 0 <= by < gy):
                    continue
                b = e * 3 + o
                source = (bx * gy + by) * gz + z
                tile, part = b // 4, b % 4
                out_ref[d, 8 * tile : 8 * tile + 8, slots * part : slots * part + slots] = main[source]
                place, row = extra_place(b, bricks)
                tile, part = place // 4, place % 4
                out_ref[
                    d, 8 * tile + row : 8 * tile + row + 2, slots * part : slots * part + slots
                ] = extra[source]


def hat(coordinate, cell, low, high):
    away = coordinate - cell
    return jnp.where(away == 0.0, low, jnp.where(away == 1.0, high, 0.0))


def hat_slope(coordinate, cell, low, high):
    away = coordinate - cell
    rising = jnp.where(away == -1.0, low, jnp.where(away == 0.0, high, 0.0))
    return rising - jnp.where(away == 1.0, low, jnp.where(away == 2.0, high, 0.0))


def row_iota(rows):
    return lax.broadcasted_iota(jnp.int32, (rows, 128), 0).astype(f32)


def stack_rows(parts, multiple):
    have = sum(part.shape[0] for part in parts)
    if have % multiple:
        parts = parts + [jnp.zeros((multiple - have % multiple, 128), f32)]
    return jnp.concatenate(parts, axis=0) if len(parts) > 1 else parts[0]


def splat_kernel(
    shape, recv_ref, fields_ref, up_ref, down_ref, own_ref,
    points, left_ref, right_ref, hx_ref, near, beside,
):
    gx, gy, gz = shape
    mx, my, mz = lax.axis_index("gx"), lax.axis_index("gy"), lax.axis_index("gz")
    step = pl.program_id(0)
    single = recv_ref.shape[1] * 4 == gx * gy * gz
    others = other_count(gy)
    bricks = 3 * (1 + others)
    tiles = recv_ref.shape[2] // 8
    lane_part = lax.broadcasted_iota(jnp.int32, (8, 128), 1) // 32
    span = 128 * GROUPS
    written = set()

    def add(ref, place, value):
        if single and place not in written:
            written.add(place)
            ref[place + (slice(None), slice(0, ROWS))] = value
        else:
            ref[place + (slice(None), slice(0, ROWS))] += value

    if not single:
        @pl.when(step == 0)
        def _():
            near[...] = jnp.zeros_like(near)
            beside[...] = jnp.zeros_like(beside)

    for t in range(tiles):
        for g in range(GROUPS):
            given = [recv_ref[q, g, 8 * t : 8 * t + 8, :] for q in range(4)]
            for k in range(4):
                if 4 * t + k >= bricks + -(-bricks // 4):
                    continue
                merged = None
                for q in range(4):
                    moved = given[q] if q == k else pltpu.roll(given[q], (32 * (q - k)) % 128, 1)
                    merged = moved if merged is None else jnp.where(lane_part == q, moved, merged)
                points[4 * t + k, g] = merged
    own_ref[0] = points[0]
    own_ref[1] = points[bricks]

    z_limit = jnp.where(mz == gz - 1, CZ, CZ + 1).astype(f32)
    z_row = row_iota(ROWS) - float(ZO)
    own_row = row_iota(24) + float(8 - YO)

    def multiply(begin, count, b, e, high, planes):
        lines = slice(begin, begin + 3 * count)
        got = dot_nn(left_ref[0, lines, :], right_ref[b, 0, :, 0:ROWS])
        got = got + dot_nn(left_ref[1, lines, :], right_ref[b, 0, :, 0:ROWS])
        got = got + dot_nn(left_ref[0, lines, :], right_ref[b, 1, :, 0:ROWS])
        for c in range(3):
            for i, plane in enumerate(planes):
                value = got[c * count + i * high : c * count + i * high + high]
                if e == 0:
                    add(near, (c, plane), value)
                else:
                    add(beside, (e - 1, c, plane), value)

    row_at = 0
    waiting = None
    for e in reversed(range(1 + others)):
        if e == 0:
            y_limit = jnp.where(my == gy - 1, CY, CY + 1).astype(f32)
            y_row = own_row
        else:
            above = my == 0 if others == 1 else jnp.bool_(e == 2)
            y_limit = jnp.where(
                jnp.logical_and(above, my + 1 == gy - 1), CY, CY + 1
            ).astype(f32)
            first = jnp.where(above, WINDOW_HIGH - YO - CY, WINDOW_LOW - YO + CY)
            y_row = row_iota(8) + first.astype(f32)
        high = y_row.shape[0]
        for o, shift, planes in ((1, -1, LOWER), (0, 0, CENTER), (2, 1, UPPER)):
            b = e * 3 + o
            place, row = extra_place(b, bricks)
            x_limit = jnp.where(mx + shift == gx - 1, CX, CX + 1).astype(f32)
            cell_x = points[b, :, 7, :]
            off_x = points[b, :, 4, :]
            low_x = 1.0 - off_x
            high_x = jnp.where(cell_x + 1.0 < x_limit, off_x, 0.0)
            for n, plane in enumerate(planes):
                at = float(plane - XO - CX * shift)
                hx_ref[b, 0, n] = hat(at, cell_x, low_x, high_x)
                hx_ref[b, 1, n] = hat_slope(at, cell_x, low_x, high_x)
            y_parts = []
            for g in range(GROUPS):
                main = points[b, g]
                more = points[place, g]
                cell_y, cell_z = more[row : row + 1], more[row + 1 : row + 2]
                off_y, off_z = main[5:6], main[6:7]
                high_z = jnp.where(cell_z + 1.0 < z_limit, off_z, 0.0)
                hz_high, hz_low = split(hat(z_row, cell_z, 1.0 - off_z, high_z))
                at = slice(128 * g, 128 * g + 128)
                right_ref[b, 0, at, 0:ROWS] = hz_high.T
                right_ref[b, 1, at, 0:ROWS] = hz_low.T
                high_y = jnp.where(cell_y + 1.0 < y_limit, off_y, 0.0)
                hy = hat(y_row, cell_y, 1.0 - off_y, high_y)
                dy = hat_slope(y_row, cell_y, 1.0 - off_y, high_y)
                y_parts.append((main[0:1] * hy, main[1:2] * dy, main[2:3] * hy, main[3:4] * hy))
            size = 4 if e == 0 else 12
            for start in range(0, len(planes), size):
                block = range(start, min(start + size, len(planes)))
                count = -(-len(block) * high // 16) * 16
                for c in range(3):
                    for g in range(GROUPS):
                        part_x0, part_y1, part_z, part_w = y_parts[g]
                        at = slice(128 * g, 128 * g + 128)
                        rows = []
                        for n in block:
                            hx = hx_ref[b, 0, n, g : g + 1, :]
                            if c == 0:
                                dx = hx_ref[b, 1, n, g : g + 1, :]
                                rows.append(dx * part_x0 + hx * part_y1)
                            else:
                                rows.append(hx * (part_z if c == 1 else part_w))
                        main_part, rest = split(stack_rows(rows, 16))
                        begin = row_at + c * count
                        left_ref[0, begin : begin + count, at] = main_part
                        left_ref[1, begin : begin + count, at] = rest
                if waiting is not None:
                    waiting()
                waiting = functools.partial(
                    multiply, row_at, count, b, e, high, [planes[n] for n in block]
                )
                row_at += 3 * count
    waiting()

    @pl.when(step == pl.num_programs(0) - 1)
    def _():
        row8 = lax.broadcasted_iota(jnp.int32, (8, 2 * 128), 0)
        zero = jnp.zeros((8, 2 * 128), f32)
        for t in range(XTILES):
            turned = []
            for c in range(3):
                pieces = []
                for plane in range(XPT * t, XPT * t + XPT):
                    if plane > UPPER[-1]:
                        pieces.append(jnp.zeros((YS, 2 * 128), f32))
                        continue
                    parts = [zero] + [near[c, plane, 8 * i : 8 * i + 8, :] for i in range(3)]
                    if others:
                        if others == 1:
                            value = beside[0, c, plane]
                            low_part = jnp.where(my == 0, 0.0, value)
                            high_part = jnp.where(my == 0, value, 0.0)
                        else:
                            low_part, high_part = beside[0, c, plane], beside[1, c, plane]
                        moved = pltpu.roll(low_part, 4, 0)
                        parts[0] = jnp.where(row8 >= 4, moved, 0.0)
                        parts[1] = parts[1] + jnp.where(row8 < 4, moved, 0.0)
                        parts[3] = parts[3] + high_part
                    pieces.extend(parts)
                stacked = jnp.concatenate(pieces, axis=0)
                turned.append(
                    jnp.concatenate([stacked[:, :128].T, stacked[:, 128:].T[: ROWS - 128]], axis=0)
                )
            fields_ref[0, t] = (
                turned[0]
                + pltpu.roll(turned[1], ROWS - 1, 0)
                - pltpu.roll(turned[1], 1, 0)
            )
            fields_ref[1, t] = turned[2]
        for c in range(2):
            up_ref[c] = fields_ref[c, :, UP_AT : UP_AT + HALO, :]
            down_ref[c] = fields_ref[c, :, DOWN_AT : DOWN_AT + HALO, :]


def chebyshev_factors():
    half_width = 6.0 / (6.0 + base_screen)
    sigma_ratio = 1.0 / half_width
    rho_prev = half_width
    factors = []
    for _ in range(ITERS - 1):
        rho_next = 1.0 / (2.0 * sigma_ratio - rho_prev)
        factors.append((rho_next * rho_prev, 2.0 * rho_next / half_width))
        rho_prev = rho_next
    return factors


def solve_kernel(
    shape, fields_ref, from_low_ref, from_high_ref, own_ref,
    indicator_ref, values_ref,
    given, low_halo, high_halo, owned, first, second, scaled, inverse, total,
    hx_ref, high_ref, low_ref, arrivals,
):
    gx, gy, gz = shape
    mx, my, mz = lax.axis_index("gx"), lax.axis_index("gy"), lax.axis_index("gz")
    copies = [
        pltpu.make_async_copy(source, target, arrivals.at[i])
        for i, (source, target) in enumerate(
            ((own_ref, owned), (fields_ref, given), (from_low_ref, low_halo), (from_high_ref, high_halo))
        )
    ]
    for copy in copies:
        copy.start()
    copies[0].wait()
    groups = owned.shape[1]
    y_row = row_iota(24) + float(8 - YO)
    blank = jnp.zeros((8, 128), f32)
    read_planes = range(XPT * FIRST_TILE, XPT * END_TILE)

    def read_operand(chunk):
        span = slice(chunk * GROUPS, chunk * GROUPS + GROUPS)
        cell_x, off_x = owned[0, span, 7, :], owned[0, span, 4, :]
        for plane in read_planes:
            if 0 <= plane - XO <= CX:
                hx_ref[plane] = hat(float(plane - XO), cell_x, 1.0 - off_x, off_x)
        for g in range(GROUPS):
            off_y = owned[0, chunk * GROUPS + g, 5:6, :]
            hy = hat(y_row, owned[1, chunk * GROUPS + g, 0:1, :], 1.0 - off_y, off_y)
            at = slice(128 * g, 128 * g + 128)
            for plane in read_planes:
                start = YS * (plane - XPT * FIRST_TILE)
                if 0 <= plane - XO <= CX:
                    rows = jnp.concatenate([blank, hx_ref[plane, g : g + 1, :] * hy], axis=0)
                    high, low = split(rows)
                else:
                    high = jnp.zeros((YS, 128), bf16)
                    low = high
                high_ref[start : start + YS, at] = high
                low_ref[start : start + YS, at] = low

    read_operand(0)
    for copy in copies[1:]:
        copy.wait()
    low_at, high_at = UP_AT - CZ, DOWN_AT + CZ
    for c in range(2):
        given[c, :, low_at : low_at + HALO, :] += low_halo[c]
        given[c, :, high_at : high_at + HALO, :] += high_halo[c]

    lane = lax.broadcasted_iota(jnp.int32, (8, 128), 1)
    row = lax.broadcasted_iota(jnp.int32, (8, 128), 0)
    y = lane % YS - YO + my * CY
    inside_y = (y >= 0) & (y < gy * CY)
    zero = jnp.zeros((8, 128), f32)
    for t in range(XTILES):
        x = lane // YS + (XPT * t - XO) + mx * CX
        inside_xy = inside_y & (x >= 0) & (x < gx * CX)
        for scratch in (first, second):
            scratch[t, 0:8, :] = zero
            scratch[t, ROWS + 8 : ROWS + 16, :] = zero
        for i in range(ROWS // 8):
            at = slice(8 * i, 8 * i + 8)
            z = row + (8 * i - ZO) + mz * CZ
            inside = inside_xy & (z >= 0) & (z < gz * CZ)
            diagonal = 6.0 + base_screen + point_screen * given[1, t, at, :]
            inv = jnp.where(inside, 1.0 / diagonal, 0.0)
            start = given[0, t, at, :] * inv
            inverse[t, at, :] = inv
            scaled[t, at, :] = start
            first[t, 8 * i + 8 : 8 * i + 16, :] = start
            if FIRST_TILE <= t < END_TILE:
                total[t - FIRST_TILE, at, :] = start

    now, later = first, second
    factors = chebyshev_factors()
    low_part, high_part = lane < YS, lane >= 128 - YS
    for k, (keep, gain) in enumerate(factors, 1):
        last = k == len(factors)
        begin, end = k // XPT, (XO + CX + REACH - k + XPT) // XPT
        for i in range(ROWS // 8):
            at = slice(8 * i, 8 * i + 8)
            here = {t: now[t, 8 * i + 8 : 8 * i + 16, :] for t in range(XTILES)}
            ahead_x = {t: pltpu.roll(here[t], YS, 1) for t in range(XTILES)}
            behind_x = {t: pltpu.roll(here[t], 128 - YS, 1) for t in range(XTILES)}
            for t in range(begin, end):
                mine = here[t]
                near = now[t, 8 * i + 7 : 8 * i + 15, :] + now[t, 8 * i + 9 : 8 * i + 17, :]
                near = near + pltpu.roll(mine, 1, 1) + pltpu.roll(mine, 127, 1)
                before = ahead_x[t]
                if t > 0:
                    before = jnp.where(low_part, ahead_x[t - 1], before)
                after = behind_x[t]
                if t + 1 < XTILES:
                    after = jnp.where(high_part, behind_x[t + 1], after)
                near = near + before + after
                left = scaled[t, at, :] - mine + inverse[t, at, :] * near
                ahead = keep * mine + gain * left
                if FIRST_TILE <= t < END_TILE:
                    total[t - FIRST_TILE, at, :] += ahead
                if not last:
                    scaled[t, at, :] = left
                    later[t, 8 * i + 8 : 8 * i + 16, :] = ahead
        now, later = later, now

    parts = [split(total[t - FIRST_TILE]) for t in range(FIRST_TILE, END_TILE)]
    u_high = jnp.concatenate([part[0] for part in parts], axis=1)
    u_low = jnp.concatenate([part[1] for part in parts], axis=1)
    z_row = row_iota(ROWS) - float(ZO)
    for chunk in range(groups // GROUPS):
        if chunk > 0:
            read_operand(chunk)
        got = dot_nn(u_high, high_ref[...]) + dot_nn(u_low, high_ref[...])
        got = got + dot_nn(u_high, low_ref[...])
        rows = []
        for g in range(GROUPS):
            main = owned[0, chunk * GROUPS + g]
            off_z = main[6:7]
            hz = hat(z_row, owned[1, chunk * GROUPS + g, 1:2, :], 1.0 - off_z, off_z)
            value = jnp.sum(hz * got[:, 128 * g : 128 * g + 128], axis=0, keepdims=True)
            rows.append(jnp.where(main[3:4] > 0.0, value, 0.0))
        values = jnp.concatenate(rows, axis=0)
        for q in range(4):
            moved = values if q == 0 else pltpu.roll(values, 128 - 32 * q, 1)
            start = q * groups + chunk * GROUPS
            values_ref[start : start + GROUPS, :] = moved[:, 0:32]

    for t in range(FIRST_TILE, END_TILE):
        turned = total[t - FIRST_TILE, ZO : ZO + CZ, :].T
        for i in range(XPT):
            plane = XPT * t + i - XO
            if 0 <= plane < CX:
                indicator_ref[plane] = turned[YS * i + YO : YS * i + YO + CY, :]


def on_device(shape, point_data, point_cells, send_counts):
    gx, gy, gz = shape
    sources = gx * gy * gz
    slots = point_data.shape[3]
    bricks = 3 * (1 + other_count(gy))
    rows = 8 * -(-(bricks + -(-bricks // 4)) // 4)
    groups = sources // 4
    whole = pl.BlockSpec(memory_space=pltpu.VMEM)

    outgoing = pl.pallas_call(
        functools.partial(pack_kernel, shape),
        out_shape=jax.ShapeDtypeStruct((sources, rows, 128), f32),
        in_specs=[whole, whole, whole],
        out_specs=whole,
        scratch_shapes=[
            pltpu.VMEM((sources, 8, slots), f32),
            pltpu.VMEM((sources, 2, slots), f32),
        ],
        compiler_params=pltpu.CompilerParams(vmem_limit_bytes=56 * MIB),
        name="pack_points",
    )(
        jnp.transpose(point_data, (0, 2, 1, 3)),
        jnp.transpose(point_cells, (0, 2, 1, 3)),
        send_counts,
    )

    arrived = lax.all_to_all(outgoing, AXES, split_axis=0, concat_axis=0, tiled=True)
    arrived = arrived.reshape(4, groups, rows, 128)

    others = other_count(gy)
    lines = 0
    for planes in (CENTER, LOWER, UPPER):
        for high, size in ((24, 4),) + ((8, 12),) * others:
            for start in range(0, len(planes), size):
                count = min(size, len(planes) - start)
                lines += 3 * 16 * -(-count * high // 16)
    edge_shape = jax.ShapeDtypeStruct((2, XTILES, HALO, 128), f32)
    steps = groups // GROUPS
    fields, up, down, own = pl.pallas_call(
        functools.partial(splat_kernel, shape),
        grid=(steps,),
        out_shape=(
            jax.ShapeDtypeStruct((2, XTILES, ROWS, 128), f32), edge_shape, edge_shape,
            jax.ShapeDtypeStruct((2, groups, 8, 128), f32),
        ),
        in_specs=[pl.BlockSpec((4, GROUPS, rows, 128), lambda s: (0, s, 0, 0))],
        out_specs=(
            pl.BlockSpec((2, XTILES, ROWS, 128), lambda s: (0, 0, 0, 0)),
            pl.BlockSpec((2, XTILES, HALO, 128), lambda s: (0, 0, 0, 0)),
            pl.BlockSpec((2, XTILES, HALO, 128), lambda s: (0, 0, 0, 0)),
            pl.BlockSpec((2, GROUPS, 8, 128), lambda s: (0, s, 0, 0)),
        ),
        scratch_shapes=[
            pltpu.VMEM((rows // 2, GROUPS, 8, 128), f32),
            pltpu.VMEM((2, lines, 128 * GROUPS), bf16),
            pltpu.VMEM((bricks, 2, 128 * GROUPS, 2 * 128), bf16),
            pltpu.VMEM((bricks, 2, len(CENTER), GROUPS, 128), f32),
            pltpu.VMEM((3, XPT * XTILES, 24, 2 * 128), f32),
            pltpu.VMEM((max(others, 1), 3, XPT * XTILES, 8, 2 * 128), f32),
        ],
        compiler_params=pltpu.CompilerParams(vmem_limit_bytes=36 * MIB),
        name="splat_points",
    )(arrived)

    from_low = lax.ppermute(up, "gz", [(i, i + 1) for i in range(gz - 1)])
    from_high = lax.ppermute(down, "gz", [(i + 1, i) for i in range(gz - 1)])

    depth = 128 * (END_TILE - FIRST_TILE)
    indicator, values = pl.pallas_call(
        functools.partial(solve_kernel, shape),
        out_shape=(
            jax.ShapeDtypeStruct((CX, CY, CZ), f32),
            jax.ShapeDtypeStruct((sources, slots), f32),
        ),
        in_specs=[pl.BlockSpec(memory_space=pl.ANY)] * 4,
        out_specs=(whole, whole),
        scratch_shapes=[
            pltpu.VMEM((2, XTILES, ROWS, 128), f32),
            pltpu.VMEM((2, XTILES, HALO, 128), f32),
            pltpu.VMEM((2, XTILES, HALO, 128), f32),
            pltpu.VMEM((2, groups, 8, 128), f32),
            pltpu.VMEM((XTILES, ROWS + 16, 128), f32),
            pltpu.VMEM((XTILES, ROWS + 16, 128), f32),
            pltpu.VMEM((XTILES, ROWS, 128), f32),
            pltpu.VMEM((XTILES, ROWS, 128), f32),
            pltpu.VMEM((END_TILE - FIRST_TILE, ROWS, 128), f32),
            pltpu.VMEM((XPT * END_TILE, GROUPS, 128), f32),
            pltpu.VMEM((depth, 128 * GROUPS), bf16),
            pltpu.VMEM((depth, 128 * GROUPS), bf16),
            pltpu.SemaphoreType.DMA((4,)),
        ],
        compiler_params=pltpu.CompilerParams(vmem_limit_bytes=16 * MIB),
        name="solve_and_read",
    )(fields, from_low, from_high, own)

    returned = lax.all_to_all(values, AXES, split_axis=0, concat_axis=0, tiled=True)
    return indicator, returned.reshape(1, sources, slots)


def solution(mesh):
    shape = tuple(mesh.shape[axis] for axis in AXES)
    in_specs = (
        P(AXES, None, None, None),
        P(AXES, None, None, None),
        P(AXES, None),
    )
    out_specs = (P("gx", "gy", "gz"), P(AXES, None, None))
    return jax.shard_map(
        functools.partial(on_device, shape),
        mesh=mesh,
        in_specs=in_specs,
        out_specs=out_specs,
        check_vma=False,
    )
```

```python
import functools

import jax
import jax.numpy as jnp
from jax import lax
from jax.experimental import pallas as pl
from jax.experimental.pallas import tpu as pltpu
from jax.sharding import PartitionSpec as P

CX = 16
CY = 16
CZ = 128
ITERS = 6

base_screen = 0.25
point_screen = 4.0

AXES = ("gx", "gy", "gz")
REACH = ITERS - 1
XO = REACH
YO = 9
ZO = 8
YS = 32
XPT = 128 // YS
XTILES = -(-(CX + 2 * REACH + 1) // XPT)
ROWS = CZ + 16
CENTER = tuple(range(XO - 1, XO + CX + 2))
LOWER = tuple(range(0, XO + 2))
UPPER = tuple(range(XO + CX - 1, XO + CX + REACH + 1))
FIRST_TILE, END_TILE = XO // XPT, (XO + CX) // XPT + 1
WINDOW_LOW = YO - REACH
WINDOW_HIGH = YO + CY - 1
UP_AT = ZO + CZ - REACH
DOWN_AT = ZO - 1
HALO = 8
GROUPS = 8
MIB = 1024 * 1024

f32 = jnp.float32
bf16 = jnp.bfloat16


def split(value):
    high = value.astype(bf16)
    return high, (value - high.astype(f32)).astype(bf16)


def dot_nt(lhs, rhs):
    return lax.dot_general(lhs, rhs, (((1,), (1,)), ((), ())), preferred_element_type=f32)


def dot_nn(lhs, rhs):
    return lax.dot_general(lhs, rhs, (((1,), (0,)), ((), ())), preferred_element_type=f32)


def other_count(gy):
    return min(gy - 1, 2)


def extra_place(brick, bricks):
    return bricks + brick // 4, 2 * (brick % 4)


def pack_kernel(shape, data_ref, cells_ref, counts_ref, out_ref, main, extra):
    gx, gy, gz = shape
    slots = data_ref.shape[3]
    sources = gx * gy * gz
    lane = lax.broadcasted_iota(jnp.int32, (sources, slots), 1)
    at_row = lax.broadcasted_iota(jnp.int32, (sources, sources), 0)
    at_lane = lax.broadcasted_iota(jnp.int32, (sources, sources), 1)
    counts = jnp.where(at_row == at_lane, counts_ref[...], 0).astype(f32)
    counts = jnp.sum(counts, axis=1, keepdims=True).astype(jnp.int32)
    others = other_count(gy)
    bricks = 3 * (1 + others)
    weight = jnp.where(lane < counts, data_ref[0, 3], 0.0)
    cells = [cells_ref[0, c].astype(f32) for c in range(3)]
    channels = [data_ref[0, c] * (-0.5 * weight) for c in range(3)]
    channels += [weight] + [data_ref[0, c] for c in range(4, 7)] + [cells[0]]

    def placed(value, part):
        pieces = [jnp.zeros((sources, slots * part), f32)] if part else []
        pieces.append(value)
        if part < 3:
            pieces.append(jnp.zeros((sources, 128 - slots * (part + 1)), f32))
        return jnp.concatenate(pieces, axis=1)

    for part in range(min(bricks, 4)):
        for c in range(8):
            main[part, :, c, :] = placed(channels[c], part)
    extra[...] = jnp.zeros_like(extra)
    for b in range(bricks):
        place, row = extra_place(b, bricks)
        for c in range(2):
            extra[b, :, row + c, :] = placed(cells[1 + c], place % 4)
    for d in range(sources):
        x, y, z = d // (gy * gz), (d // gz) % gy, d % gz
        if others == 0:
            ys = (y,)
        elif others == 1:
            ys = (y, 1 - y)
        else:
            ys = (y, y - 1, y + 1)
        sums = [None] * (out_ref.shape[1] // 8)
        for e, by in enumerate(ys):
            for o, bx in enumerate((x, x - 1, x + 1)):
                if not (0 <= bx < gx and 0 <= by < gy):
                    continue
                b = e * 3 + o
                source = (bx * gy + by) * gz + z
                place, _ = extra_place(b, bricks)
                for tile, value in (
                    (b // 4, main[b % 4, source]), (place // 4, extra[b, source])
                ):
                    sums[tile] = value if sums[tile] is None else sums[tile] + value
        for tile, value in enumerate(sums):
            if value is None:
                value = jnp.zeros((8, 128), f32)
            out_ref[d, 8 * tile : 8 * tile + 8, :] = value


def hat(coordinate, cell, low, high):
    away = coordinate - cell
    return jnp.where(away == 0.0, low, jnp.where(away == 1.0, high, 0.0))


def hat_slope(coordinate, cell, low, high):
    away = coordinate - cell
    rising = jnp.where(away == -1.0, low, jnp.where(away == 0.0, high, 0.0))
    return rising - jnp.where(away == 1.0, low, jnp.where(away == 2.0, high, 0.0))


def row_iota(rows):
    return lax.broadcasted_iota(jnp.int32, (rows, 128), 0).astype(f32)


def stack_rows(parts, multiple):
    have = sum(part.shape[0] for part in parts)
    if have % multiple:
        parts = parts + [jnp.zeros((multiple - have % multiple, 128), f32)]
    return jnp.concatenate(parts, axis=0) if len(parts) > 1 else parts[0]


def splat_kernel(
    shape, recv_ref, fields_ref, up_ref, down_ref, own_ref,
    points, left_ref, right_ref, hx_ref, near, beside,
):
    gx, gy, gz = shape
    mx, my, mz = lax.axis_index("gx"), lax.axis_index("gy"), lax.axis_index("gz")
    step = pl.program_id(0)
    single = recv_ref.shape[1] * 4 == gx * gy * gz
    others = other_count(gy)
    bricks = 3 * (1 + others)
    tiles = recv_ref.shape[2] // 8
    lane_part = lax.broadcasted_iota(jnp.int32, (8, 128), 1) // 32
    span = 128 * GROUPS
    written = set()

    def add(ref, place, value):
        if single and place not in written:
            written.add(place)
            ref[place + (slice(None), slice(0, ROWS))] = value
        else:
            ref[place + (slice(None), slice(0, ROWS))] += value

    if not single:
        @pl.when(step == 0)
        def _():
            near[...] = jnp.zeros_like(near)
            beside[...] = jnp.zeros_like(beside)

    for t in range(tiles):
        for g in range(GROUPS):
            given = [recv_ref[q, g, 8 * t : 8 * t + 8, :] for q in range(4)]
            for k in range(4):
                if 4 * t + k >= bricks + -(-bricks // 4):
                    continue
                merged = None
                for q in range(4):
                    moved = given[q] if q == k else pltpu.roll(given[q], (32 * (q - k)) % 128, 1)
                    merged = moved if merged is None else jnp.where(lane_part == q, moved, merged)
                points[4 * t + k, g] = merged
    own_ref[0] = points[0]
    own_ref[1] = points[bricks]

    z_limit = jnp.where(mz == gz - 1, CZ, CZ + 1).astype(f32)
    z_row = row_iota(ROWS) - float(ZO)
    own_row = row_iota(24) + float(8 - YO)

    def multiply(begin, count, b, e, high, planes):
        size = 3 * count
        both = dot_nn(left_ref[begin : begin + 2 * size, :], right_ref[b, 0, :, 0:ROWS])
        got = both[:size] + both[size:]
        got = got + dot_nn(left_ref[begin : begin + size, :], right_ref[b, 1, :, 0:ROWS])
        for c in range(3):
            for i, plane in enumerate(planes):
                value = got[c * count + i * high : c * count + i * high + high]
                if e == 0:
                    add(near, (c, plane), value)
                else:
                    add(beside, (e - 1, c, plane), value)

        if single and e == 0:
            for t in sorted({plane // XPT for plane in planes}):
                unfinished[t] -= 1
                if unfinished[t] == 0:
                    finish(t)

    row8 = lax.broadcasted_iota(jnp.int32, (8, 2 * 128), 0)
    zero = jnp.zeros((8, 2 * 128), f32)

    def finish(t):
        turned = []
        for c in range(3):
            pieces = []
            for plane in range(XPT * t, XPT * t + XPT):
                if plane > UPPER[-1]:
                    pieces.append(jnp.zeros((YS, 2 * 128), f32))
                    continue
                parts = [zero] + [near[c, plane, 8 * i : 8 * i + 8, :] for i in range(3)]
                if others:
                    if others == 1:
                        value = beside[0, c, plane]
                        low_part = jnp.where(my == 0, 0.0, value)
                        high_part = jnp.where(my == 0, value, 0.0)
                    else:
                        low_part, high_part = beside[0, c, plane], beside[1, c, plane]
                    moved = pltpu.roll(low_part, 4, 0)
                    parts[0] = jnp.where(row8 >= 4, moved, 0.0)
                    parts[1] = parts[1] + jnp.where(row8 < 4, moved, 0.0)
                    parts[3] = parts[3] + high_part
                pieces.extend(parts)
            stacked = jnp.concatenate(pieces, axis=0)
            turned.append(
                jnp.concatenate([stacked[:, :128].T, stacked[:, 128:].T[: ROWS - 128]], axis=0)
            )
        fields_ref[0, t] = (
            turned[0] + pltpu.roll(turned[1], ROWS - 1, 0) - pltpu.roll(turned[1], 1, 0)
        )
        fields_ref[1, t] = turned[2]

    unfinished = [
        sum(
            plane // XPT == t and (i == 0 or planes[i - 1] // XPT != t)
            for planes in (CENTER, LOWER, UPPER)
            for i, plane in enumerate(planes)
        )
        for t in range(XTILES)
    ]
    row_at = 0
    waiting = None
    for e in reversed(range(1 + others)):
        if e == 0:
            y_limit = jnp.where(my == gy - 1, CY, CY + 1).astype(f32)
            y_row = own_row
        else:
            above = my == 0 if others == 1 else jnp.bool_(e == 2)
            y_limit = jnp.where(
                jnp.logical_and(above, my + 1 == gy - 1), CY, CY + 1
            ).astype(f32)
            first = jnp.where(above, WINDOW_HIGH - YO - CY, WINDOW_LOW - YO + CY)
            y_row = row_iota(8) + first.astype(f32)
        high = y_row.shape[0]
        for o, shift, planes in ((1, -1, LOWER), (2, 1, UPPER), (0, 0, CENTER)):
            b = e * 3 + o
            place, row = extra_place(b, bricks)
            x_limit = jnp.where(mx + shift == gx - 1, CX, CX + 1).astype(f32)
            cell_x = points[b, :, 7, :]
            off_x = points[b, :, 4, :]
            low_x = 1.0 - off_x
            high_x = jnp.where(cell_x + 1.0 < x_limit, off_x, 0.0)
            for n, plane in enumerate(planes):
                at = float(plane - XO - CX * shift)
                hx_ref[b, 0, n] = hat(at, cell_x, low_x, high_x)
                hx_ref[b, 1, n] = hat_slope(at, cell_x, low_x, high_x)
            y_parts = []
            for g in range(GROUPS):
                main = points[b, g]
                more = points[place, g]
                cell_y, cell_z = more[row : row + 1], more[row + 1 : row + 2]
                off_y, off_z = main[5:6], main[6:7]
                high_z = jnp.where(cell_z + 1.0 < z_limit, off_z, 0.0)
                hz_high, hz_low = split(hat(z_row, cell_z, 1.0 - off_z, high_z))
                at = slice(128 * g, 128 * g + 128)
                right_ref[b, 0, at, 0:ROWS] = hz_high.T
                right_ref[b, 1, at, 0:ROWS] = hz_low.T
                high_y = jnp.where(cell_y + 1.0 < y_limit, off_y, 0.0)
                hy = hat(y_row, cell_y, 1.0 - off_y, high_y)
                dy = hat_slope(y_row, cell_y, 1.0 - off_y, high_y)
                y_parts.append((main[0:1] * hy, main[1:2] * dy, main[2:3] * hy, main[3:4] * hy))
            size = 4 if e == 0 else 12
            for start in range(0, len(planes), size):
                block = range(start, min(start + size, len(planes)))
                count = -(-len(block) * high // 16) * 16
                for c in range(3):
                    for g in range(GROUPS):
                        part_x0, part_y1, part_z, part_w = y_parts[g]
                        at = slice(128 * g, 128 * g + 128)
                        rows = []
                        for n in block:
                            hx = hx_ref[b, 0, n, g : g + 1, :]
                            if c == 0:
                                dx = hx_ref[b, 1, n, g : g + 1, :]
                                rows.append(dx * part_x0 + hx * part_y1)
                            else:
                                rows.append(hx * (part_z if c == 1 else part_w))
                        main_part, rest = split(stack_rows(rows, 16))
                        begin = row_at + c * count
                        left_ref[begin : begin + count, at] = main_part
                        begin = begin + 3 * count
                        left_ref[begin : begin + count, at] = rest
                if waiting is not None:
                    waiting()
                waiting = functools.partial(
                    multiply, row_at, count, b, e, high, [planes[n] for n in block]
                )
                row_at += 6 * count
    waiting()

    if not single:
        @pl.when(step == pl.num_programs(0) - 1)
        def _():
            for t in range(XTILES):
                finish(t)
    for c in range(2):
        up_ref[c] = fields_ref[c, :, UP_AT : UP_AT + HALO, :]
        down_ref[c] = fields_ref[c, :, DOWN_AT : DOWN_AT + HALO, :]


def chebyshev_factors():
    half_width = 6.0 / (6.0 + base_screen)
    sigma_ratio = 1.0 / half_width
    rho_prev = half_width
    factors = []
    for _ in range(ITERS - 1):
        rho_next = 1.0 / (2.0 * sigma_ratio - rho_prev)
        factors.append((rho_next * rho_prev, 2.0 * rho_next / half_width))
        rho_prev = rho_next
    return factors


def solve_kernel(
    shape, fields_ref, from_low_ref, from_high_ref, own_ref,
    indicator_ref, values_ref,
    given, low_halo, high_halo, owned, first, second, scaled, inverse, total,
    hx_ref, high_ref, low_ref, arrivals,
):
    gx, gy, gz = shape
    mx, my, mz = lax.axis_index("gx"), lax.axis_index("gy"), lax.axis_index("gz")
    copies = [
        pltpu.make_async_copy(source, target, arrivals.at[i])
        for i, (source, target) in enumerate(
            ((own_ref, owned), (fields_ref, given), (from_low_ref, low_halo), (from_high_ref, high_halo))
        )
    ]
    for copy in copies:
        copy.start()
    copies[0].wait()
    groups = owned.shape[1]
    y_row = row_iota(24) + float(8 - YO)
    blank = jnp.zeros((8, 128), f32)
    read_planes = range(XPT * FIRST_TILE, XPT * END_TILE)

    def read_operand(chunk):
        span = slice(chunk * GROUPS, chunk * GROUPS + GROUPS)
        cell_x, off_x = owned[0, span, 7, :], owned[0, span, 4, :]
        for plane in read_planes:
            if 0 <= plane - XO <= CX:
                hx_ref[plane] = hat(float(plane - XO), cell_x, 1.0 - off_x, off_x)
        for g in range(GROUPS):
            off_y = owned[0, chunk * GROUPS + g, 5:6, :]
            hy = hat(y_row, owned[1, chunk * GROUPS + g, 0:1, :], 1.0 - off_y, off_y)
            at = slice(128 * g, 128 * g + 128)
            for plane in read_planes:
                start = YS * (plane - XPT * FIRST_TILE)
                if 0 <= plane - XO <= CX:
                    rows = jnp.concatenate([blank, hx_ref[plane, g : g + 1, :] * hy], axis=0)
                    high, low = split(rows)
                else:
                    high = jnp.zeros((YS, 128), bf16)
                    low = high
                high_ref[start : start + YS, at] = high
                low_ref[start : start + YS, at] = low

    read_operand(0)
    for copy in copies[1:]:
        copy.wait()
    low_at, high_at = UP_AT - CZ, DOWN_AT + CZ
    for c in range(2):
        given[c, :, low_at : low_at + HALO, :] += low_halo[c]
        given[c, :, high_at : high_at + HALO, :] += high_halo[c]

    lane = lax.broadcasted_iota(jnp.int32, (8, 128), 1)
    row = lax.broadcasted_iota(jnp.int32, (8, 128), 0)
    y = lane % YS - YO + my * CY
    inside_y = (y >= 0) & (y < gy * CY)
    zero = jnp.zeros((8, 128), f32)
    for t in range(XTILES):
        x = lane // YS + (XPT * t - XO) + mx * CX
        inside_xy = inside_y & (x >= 0) & (x < gx * CX)
        for scratch in (first, second):
            scratch[t, 0:8, :] = zero
            scratch[t, ROWS + 8 : ROWS + 16, :] = zero
        for i in range(ROWS // 8):
            at = slice(8 * i, 8 * i + 8)
            z = row + (8 * i - ZO) + mz * CZ
            inside = inside_xy & (z >= 0) & (z < gz * CZ)
            diagonal = 6.0 + base_screen + point_screen * given[1, t, at, :]
            inv = jnp.where(inside, 1.0 / diagonal, 0.0)
            start = given[0, t, at, :] * inv
            inverse[t, at, :] = inv
            scaled[t, at, :] = start
            first[t, 8 * i + 8 : 8 * i + 16, :] = start
            if FIRST_TILE <= t < END_TILE:
                total[t - FIRST_TILE, at, :] = start

    now, later = first, second
    factors = chebyshev_factors()
    low_part, high_part = lane < YS, lane >= 128 - YS
    for k, (keep, gain) in enumerate(factors, 1):
        last = k == len(factors)
        begin, end = k // XPT, (XO + CX + REACH - k + XPT) // XPT
        for i in range(ROWS // 8):
            at = slice(8 * i, 8 * i + 8)
            here = {t: now[t, 8 * i + 8 : 8 * i + 16, :] for t in range(XTILES)}
            ahead_x = {t: pltpu.roll(here[t], YS, 1) for t in range(XTILES)}
            behind_x = {t: pltpu.roll(here[t], 128 - YS, 1) for t in range(XTILES)}
            for t in range(begin, end):
                mine = here[t]
                near = now[t, 8 * i + 7 : 8 * i + 15, :] + now[t, 8 * i + 9 : 8 * i + 17, :]
                near = near + pltpu.roll(mine, 1, 1) + pltpu.roll(mine, 127, 1)
                before = ahead_x[t]
                if t > 0:
                    before = jnp.where(low_part, ahead_x[t - 1], before)
                after = behind_x[t]
                if t + 1 < XTILES:
                    after = jnp.where(high_part, behind_x[t + 1], after)
                near = near + before + after
                left = scaled[t, at, :] - mine + inverse[t, at, :] * near
                ahead = keep * mine + gain * left
                if FIRST_TILE <= t < END_TILE:
                    total[t - FIRST_TILE, at, :] += ahead
                if not last:
                    scaled[t, at, :] = left
                    later[t, 8 * i + 8 : 8 * i + 16, :] = ahead
        now, later = later, now

    parts = [split(total[t - FIRST_TILE]) for t in range(FIRST_TILE, END_TILE)]
    u_high = jnp.concatenate([part[0] for part in parts], axis=1)
    u_low = jnp.concatenate([part[1] for part in parts], axis=1)
    u_both = jnp.concatenate([u_high, u_low], axis=0)
    z_row = row_iota(ROWS) - float(ZO)
    for chunk in range(groups // GROUPS):
        if chunk > 0:
            read_operand(chunk)
        got = dot_nn(u_both, high_ref[...])
        got = got[:ROWS] + got[ROWS:] + dot_nn(u_high, low_ref[...])
        rows = []
        for g in range(GROUPS):
            main = owned[0, chunk * GROUPS + g]
            off_z = main[6:7]
            hz = hat(z_row, owned[1, chunk * GROUPS + g, 1:2, :], 1.0 - off_z, off_z)
            value = jnp.sum(hz * got[:, 128 * g : 128 * g + 128], axis=0, keepdims=True)
            rows.append(jnp.where(main[3:4] > 0.0, value, 0.0))
        values = jnp.concatenate(rows, axis=0)
        for q in range(4):
            moved = values if q == 0 else pltpu.roll(values, 128 - 32 * q, 1)
            start = q * groups + chunk * GROUPS
            values_ref[start : start + GROUPS, :] = moved[:, 0:32]

    for t in range(FIRST_TILE, END_TILE):
        turned = total[t - FIRST_TILE, ZO : ZO + CZ, :].T
        for i in range(XPT):
            plane = XPT * t + i - XO
            if 0 <= plane < CX:
                indicator_ref[plane] = turned[YS * i + YO : YS * i + YO + CY, :]


def on_device(shape, point_data, point_cells, send_counts):
    gx, gy, gz = shape
    sources = gx * gy * gz
    slots = point_data.shape[3]
    bricks = 3 * (1 + other_count(gy))
    rows = 8 * -(-(bricks + -(-bricks // 4)) // 4)
    groups = sources // 4
    whole = pl.BlockSpec(memory_space=pltpu.VMEM)

    outgoing = pl.pallas_call(
        functools.partial(pack_kernel, shape),
        out_shape=jax.ShapeDtypeStruct((sources, rows, 128), f32),
        in_specs=[whole, whole, whole],
        out_specs=whole,
        scratch_shapes=[
            pltpu.VMEM((4, sources, 8, 128), f32),
            pltpu.VMEM((bricks, sources, 8, 128), f32),
        ],
        compiler_params=pltpu.CompilerParams(vmem_limit_bytes=56 * MIB),
        name="pack_points",
    )(
        jnp.transpose(point_data, (0, 2, 1, 3)),
        jnp.transpose(point_cells, (0, 2, 1, 3)),
        send_counts,
    )

    arrived = lax.all_to_all(outgoing, AXES, split_axis=0, concat_axis=0, tiled=True)
    arrived = arrived.reshape(4, groups, rows, 128)

    others = other_count(gy)
    lines = 0
    for planes in (CENTER, LOWER, UPPER):
        for high, size in ((24, 4),) + ((8, 12),) * others:
            for start in range(0, len(planes), size):
                count = min(size, len(planes) - start)
                lines += 6 * 16 * -(-count * high // 16)
    edge_shape = jax.ShapeDtypeStruct((2, XTILES, HALO, 128), f32)
    steps = groups // GROUPS
    fields, up, down, own = pl.pallas_call(
        functools.partial(splat_kernel, shape),
        grid=(steps,),
        out_shape=(
            jax.ShapeDtypeStruct((2, XTILES, ROWS, 128), f32), edge_shape, edge_shape,
            jax.ShapeDtypeStruct((2, groups, 8, 128), f32),
        ),
        in_specs=[pl.BlockSpec((4, GROUPS, rows, 128), lambda s: (0, s, 0, 0))],
        out_specs=(
            pl.BlockSpec((2, XTILES, ROWS, 128), lambda s: (0, 0, 0, 0)),
            pl.BlockSpec((2, XTILES, HALO, 128), lambda s: (0, 0, 0, 0)),
            pl.BlockSpec((2, XTILES, HALO, 128), lambda s: (0, 0, 0, 0)),
            pl.BlockSpec((2, GROUPS, 8, 128), lambda s: (0, s, 0, 0)),
        ),
        scratch_shapes=[
            pltpu.VMEM((rows // 2, GROUPS, 8, 128), f32),
            pltpu.VMEM((lines, 128 * GROUPS), bf16),
            pltpu.VMEM((bricks, 2, 128 * GROUPS, 2 * 128), bf16),
            pltpu.VMEM((bricks, 2, len(CENTER), GROUPS, 128), f32),
            pltpu.VMEM((3, XPT * XTILES, 24, 2 * 128), f32),
            pltpu.VMEM((max(others, 1), 3, XPT * XTILES, 8, 2 * 128), f32),
        ],
        compiler_params=pltpu.CompilerParams(vmem_limit_bytes=36 * MIB),
        name="splat_points",
    )(arrived)

    from_low = lax.ppermute(up, "gz", [(i, i + 1) for i in range(gz - 1)])
    from_high = lax.ppermute(down, "gz", [(i + 1, i) for i in range(gz - 1)])

    depth = 128 * (END_TILE - FIRST_TILE)
    indicator, values = pl.pallas_call(
        functools.partial(solve_kernel, shape),
        out_shape=(
            jax.ShapeDtypeStruct((CX, CY, CZ), f32),
            jax.ShapeDtypeStruct((sources, slots), f32),
        ),
        in_specs=[pl.BlockSpec(memory_space=pl.ANY)] * 4,
        out_specs=(whole, whole),
        scratch_shapes=[
            pltpu.VMEM((2, XTILES, ROWS, 128), f32),
            pltpu.VMEM((2, XTILES, HALO, 128), f32),
            pltpu.VMEM((2, XTILES, HALO, 128), f32),
            pltpu.VMEM((2, groups, 8, 128), f32),
            pltpu.VMEM((XTILES, ROWS + 16, 128), f32),
            pltpu.VMEM((XTILES, ROWS + 16, 128), f32),
            pltpu.VMEM((XTILES, ROWS, 128), f32),
            pltpu.VMEM((XTILES, ROWS, 128), f32),
            pltpu.VMEM((END_TILE - FIRST_TILE, ROWS, 128), f32),
            pltpu.VMEM((XPT * END_TILE, GROUPS, 128), f32),
            pltpu.VMEM((depth, 128 * GROUPS), bf16),
            pltpu.VMEM((depth, 128 * GROUPS), bf16),
            pltpu.SemaphoreType.DMA((4,)),
        ],
        compiler_params=pltpu.CompilerParams(vmem_limit_bytes=16 * MIB),
        name="solve_and_read",
    )(fields, from_low, from_high, own)

    returned = lax.all_to_all(
        values.reshape(1, sources, slots), AXES, split_axis=1, concat_axis=1, tiled=True
    )
    return indicator, returned


def solution(mesh):
    shape = tuple(mesh.shape[axis] for axis in AXES)
    in_specs = (
        P(AXES, None, None, None),
        P(AXES, None, None, None),
        P(AXES, None),
    )
    out_specs = (P("gx", "gy", "gz"), P(AXES, None, None))
    return jax.shard_map(
        functools.partial(on_device, shape),
        mesh=mesh,
        in_specs=in_specs,
        out_specs=out_specs,
        check_vma=False,
    )
```

```python
import functools

import jax
import jax.numpy as jnp
from jax import lax
from jax.experimental import pallas as pl
from jax.experimental.pallas import tpu as pltpu
from jax.sharding import PartitionSpec as P

CX = 16
CY = 16
CZ = 128
ITERS = 6

base_screen = 0.25
point_screen = 4.0

AXES = ("gx", "gy", "gz")
REACH = ITERS - 1
XO = REACH
YO = 9
ZO = 8
YS = 32
XPT = 128 // YS
XTILES = -(-(CX + 2 * REACH + 1) // XPT)
ROWS = CZ + 16
CENTER = tuple(range(XO - 1, XO + CX + 2))
LOWER = tuple(range(0, XO + 2))
UPPER = tuple(range(XO + CX - 1, XO + CX + REACH + 1))
FIRST_TILE, END_TILE = XO // XPT, (XO + CX) // XPT + 1
WINDOW_LOW = YO - REACH
WINDOW_HIGH = YO + CY - 1
UP_AT = ZO + CZ - REACH
DOWN_AT = ZO - 1
HALO = 8
GROUPS = 8
MIB = 1024 * 1024

f32 = jnp.float32
bf16 = jnp.bfloat16


def split(value):
    high = value.astype(bf16)
    return high, (value - high.astype(f32)).astype(bf16)


def dot_nt(lhs, rhs):
    return lax.dot_general(lhs, rhs, (((1,), (1,)), ((), ())), preferred_element_type=f32)


def dot_nn(lhs, rhs):
    return lax.dot_general(lhs, rhs, (((1,), (0,)), ((), ())), preferred_element_type=f32)


def other_count(gy):
    return min(gy - 1, 2)


def extra_place(brick, bricks):
    return bricks + brick // 4, 2 * (brick % 4)


def pack_kernel(shape, data_ref, cells_ref, counts_ref, out_ref, main, extra):
    gx, gy, gz = shape
    slots = data_ref.shape[3]
    sources = gx * gy * gz
    lane = lax.broadcasted_iota(jnp.int32, (sources, slots), 1)
    at_row = lax.broadcasted_iota(jnp.int32, (sources, sources), 0)
    at_lane = lax.broadcasted_iota(jnp.int32, (sources, sources), 1)
    counts = jnp.where(at_row == at_lane, counts_ref[...], 0).astype(f32)
    counts = jnp.sum(counts, axis=1, keepdims=True).astype(jnp.int32)
    others = other_count(gy)
    bricks = 3 * (1 + others)
    weight = jnp.where(lane < counts, data_ref[0, 3], 0.0)
    cells = [cells_ref[0, c].astype(f32) for c in range(3)]
    channels = [data_ref[0, c] * (-0.5 * weight) for c in range(3)]
    channels += [weight] + [data_ref[0, c] for c in range(4, 7)] + [cells[0]]

    def placed(value, part):
        pieces = [jnp.zeros((sources, slots * part), f32)] if part else []
        pieces.append(value)
        if part < 3:
            pieces.append(jnp.zeros((sources, 128 - slots * (part + 1)), f32))
        return jnp.concatenate(pieces, axis=1)

    for part in range(min(bricks, 4)):
        for c in range(8):
            main[part, :, c, :] = placed(channels[c], part)
    extra[...] = jnp.zeros_like(extra)
    for b in range(bricks):
        place, row = extra_place(b, bricks)
        for c in range(2):
            extra[b, :, row + c, :] = placed(cells[1 + c], place % 4)
    for d in range(sources):
        x, y, z = d // (gy * gz), (d // gz) % gy, d % gz
        if others == 0:
            ys = (y,)
        elif others == 1:
            ys = (y, 1 - y)
        else:
            ys = (y, y - 1, y + 1)
        sums = [None] * (out_ref.shape[1] // 8)
        for e, by in enumerate(ys):
            for o, bx in enumerate((x, x - 1, x + 1)):
                if not (0 <= bx < gx and 0 <= by < gy):
                    continue
                b = e * 3 + o
                source = (bx * gy + by) * gz + z
                place, _ = extra_place(b, bricks)
                for tile, value in (
                    (b // 4, main[b % 4, source]), (place // 4, extra[b, source])
                ):
                    sums[tile] = value if sums[tile] is None else sums[tile] + value
        for tile, value in enumerate(sums):
            if value is None:
                value = jnp.zeros((8, 128), f32)
            out_ref[d, 8 * tile : 8 * tile + 8, :] = value


def hat(coordinate, cell, low, high):
    away = coordinate - cell
    return jnp.where(away == 0.0, low, jnp.where(away == 1.0, high, 0.0))


def hat_slope(coordinate, cell, low, high):
    away = coordinate - cell
    rising = jnp.where(away == -1.0, low, jnp.where(away == 0.0, high, 0.0))
    return rising - jnp.where(away == 1.0, low, jnp.where(away == 2.0, high, 0.0))


def row_iota(rows):
    return lax.broadcasted_iota(jnp.int32, (rows, 128), 0).astype(f32)


def stack_rows(parts, multiple):
    have = sum(part.shape[0] for part in parts)
    if have % multiple:
        parts = parts + [jnp.zeros((multiple - have % multiple, 128), f32)]
    return jnp.concatenate(parts, axis=0) if len(parts) > 1 else parts[0]


def splat_kernel(
    shape, recv_ref, fields_ref, up_ref, down_ref, own_ref,
    points, left_ref, right_ref, hx_ref, near, beside, slope,
):
    gx, gy, gz = shape
    mx, my, mz = lax.axis_index("gx"), lax.axis_index("gy"), lax.axis_index("gz")
    step = pl.program_id(0)
    single = recv_ref.shape[1] * 4 == gx * gy * gz
    others = other_count(gy)
    bricks = 3 * (1 + others)
    tiles = recv_ref.shape[2] // 8
    lane_part = lax.broadcasted_iota(jnp.int32, (8, 128), 1) // 32
    span = 128 * GROUPS
    written = set()

    def add(ref, place, value):
        if single and place not in written:
            written.add(place)
            ref[place] = value
        else:
            ref[place] += value

    if not single:
        @pl.when(step == 0)
        def _():
            near[...] = jnp.zeros_like(near)
            beside[...] = jnp.zeros_like(beside)

    for t in range(tiles):
        for g in range(GROUPS):
            given = [recv_ref[q, g, 8 * t : 8 * t + 8, :] for q in range(4)]
            for k in range(4):
                if 4 * t + k >= bricks + -(-bricks // 4):
                    continue
                merged = None
                for q in range(4):
                    moved = given[q] if q == k else pltpu.roll(given[q], (32 * (q - k)) % 128, 1)
                    merged = moved if merged is None else jnp.where(lane_part == q, moved, merged)
                points[4 * t + k, g] = merged
    own_ref[0] = points[0]
    own_ref[1] = points[bricks]

    z_limit = jnp.where(mz == gz - 1, CZ, CZ + 1).astype(f32)
    z_row = row_iota(CZ)
    own_row = row_iota(24) + float(8 - YO)
    point_lane = lax.broadcasted_iota(jnp.int32, (128, 128), 1)

    def multiply(begin, count, b, e, high, planes):
        size = 3 * count
        both = dot_nn(left_ref[begin : begin + 2 * size, :], right_ref[b, 0])
        got = both[:size] + both[size:]
        got = got + dot_nn(left_ref[begin : begin + size, :], right_ref[b, 1])
        for c in range(3):
            for i, plane in enumerate(planes):
                value = got[c * count + i * high : c * count + i * high + high]
                if e == 0:
                    add(near, (c, plane), value)
                else:
                    add(beside, (e - 1, c, plane), value)

        if single and e == 0:
            for t in sorted({plane // XPT for plane in planes}):
                unfinished[t] -= 1
                if unfinished[t] == 0:
                    finish(t)

    row8 = lax.broadcasted_iota(jnp.int32, (8, 2 * 128), 0)
    zero = jnp.zeros((8, 2 * 128), f32)

    def finish(t):
        turned = []
        for c in range(3):
            pieces = []
            for plane in range(XPT * t, XPT * t + XPT):
                if plane > UPPER[-1]:
                    pieces.append(jnp.zeros((YS, 2 * 128), f32))
                    continue
                parts = [zero] + [near[c, plane, 8 * i : 8 * i + 8, :] for i in range(3)]
                if others:
                    if others == 1:
                        value = beside[0, c, plane]
                        low_part = jnp.where(my == 0, 0.0, value)
                        high_part = jnp.where(my == 0, value, 0.0)
                    else:
                        low_part, high_part = beside[0, c, plane], beside[1, c, plane]
                    moved = pltpu.roll(low_part, 4, 0)
                    parts[0] = jnp.where(row8 >= 4, moved, 0.0)
                    parts[1] = parts[1] + jnp.where(row8 < 4, moved, 0.0)
                    parts[3] = parts[3] + high_part
                pieces.extend(parts)
            stacked = jnp.concatenate(pieces, axis=0)
            turned.append(stacked[:, :CZ].T)
            above = stacked[:, CZ:]
            n, at = divmod(3 * t + c, 128 // GROUPS)
            if at:
                above = pltpu.roll(above, GROUPS * at, 1)
            if tops[n] is not None:
                above = jnp.where(point_lane // GROUPS == at, above, tops[n])
            tops[n] = above
        fields_ref[0, t, ZO : ZO + CZ, :] = turned[0]
        slope[t, ZO + 8 : ZO + 8 + CZ, :] = turned[1]
        fields_ref[1, t, ZO : ZO + CZ, :] = turned[2]

    def finish_all():
        zero = jnp.zeros((8, 128), f32)
        sums = [jnp.sum(top.T.reshape(-1, GROUPS, 128), axis=1, keepdims=True) for top in tops]
        for t in range(XTILES):
            at = [divmod(3 * t + c, 128 // GROUPS) for c in range(3)]
            above = [sums[n][i] for n, i in at]
            below = jnp.concatenate([above[1], jnp.zeros((7, 128), f32)], axis=0)
            slope[t, 0 : ZO + 8, :] = jnp.zeros((ZO + 8, 128), f32)
            slope[t, ZO + 8 + CZ : ZO + 16 + CZ, :] = below
            slope[t, ZO + 16 + CZ : ROWS + 16, :] = zero
            for c in range(2):
                fields_ref[c, t, 0:ZO, :] = zero
                fields_ref[c, t, ZO + CZ : ROWS, :] = jnp.concatenate(
                    [above[2 * c], jnp.zeros((7, 128), f32)], axis=0
                )
            fields_ref[0, t] += slope[t, 9 : ROWS + 9, :] - slope[t, 7 : ROWS + 7, :]

    tops = [None] * -(-3 * XTILES * GROUPS // 128)
    unfinished = [
        sum(
            plane // XPT == t and (i == 0 or planes[i - 1] // XPT != t)
            for planes in (CENTER, LOWER, UPPER)
            for i, plane in enumerate(planes)
        )
        for t in range(XTILES)
    ]
    row_at = 0
    waiting = None
    for e in reversed(range(1 + others)):
        if e == 0:
            y_limit = jnp.where(my == gy - 1, CY, CY + 1).astype(f32)
            y_row = own_row
        else:
            above = my == 0 if others == 1 else jnp.bool_(e == 2)
            y_limit = jnp.where(
                jnp.logical_and(above, my + 1 == gy - 1), CY, CY + 1
            ).astype(f32)
            first = jnp.where(above, WINDOW_HIGH - YO - CY, WINDOW_LOW - YO + CY)
            y_row = row_iota(8) + first.astype(f32)
        high = y_row.shape[0]
        for o, shift, planes in ((1, -1, LOWER), (2, 1, UPPER), (0, 0, CENTER)):
            b = e * 3 + o
            place, row = extra_place(b, bricks)
            x_limit = jnp.where(mx + shift == gx - 1, CX, CX + 1).astype(f32)
            cell_x = points[b, :, 7, :]
            off_x = points[b, :, 4, :]
            low_x = 1.0 - off_x
            high_x = jnp.where(cell_x + 1.0 < x_limit, off_x, 0.0)
            for n, plane in enumerate(planes):
                at = float(plane - XO - CX * shift)
                hx_ref[b, 0, n] = hat(at, cell_x, low_x, high_x)
                hx_ref[b, 1, n] = hat_slope(at, cell_x, low_x, high_x)
            cell_z, off_z = points[place, :, row + 1, :], points[b, :, 6, :]
            top = jnp.where((cell_z + 1.0 == float(CZ)) & (cell_z + 1.0 < z_limit), off_z, 0.0)
            top_columns = jnp.concatenate([top, jnp.zeros((128 - GROUPS, 128), f32)], axis=0).T
            top_high = top_columns.astype(bf16).astype(f32)
            top_low = top_columns - top_high
            y_parts = []
            for g in range(GROUPS):
                main = points[b, g]
                more = points[place, g]
                cell_y, cell_z = more[row : row + 1], more[row + 1 : row + 2]
                off_y, off_z = main[5:6], main[6:7]
                at = slice(128 * g, 128 * g + 128)
                hz_high, hz_low = split(hat(z_row, cell_z, 1.0 - off_z, off_z).T)
                right_ref[b, 0, at, 0:CZ] = hz_high
                right_ref[b, 1, at, 0:CZ] = hz_low
                right_ref[b, 0, at, CZ : CZ + 128] = jnp.where(point_lane == g, top_high, 0.0).astype(bf16)
                right_ref[b, 1, at, CZ : CZ + 128] = jnp.where(point_lane == g, top_low, 0.0).astype(bf16)
                high_y = jnp.where(cell_y + 1.0 < y_limit, off_y, 0.0)
                hy = hat(y_row, cell_y, 1.0 - off_y, high_y)
                dy = hat_slope(y_row, cell_y, 1.0 - off_y, high_y)
                y_parts.append((main[0:1] * hy, main[1:2] * dy, main[2:3] * hy, main[3:4] * hy))
            size = 4 if e == 0 else 12
            for start in range(0, len(planes), size):
                block = range(start, min(start + size, len(planes)))
                count = -(-len(block) * high // 16) * 16
                for c in range(3):
                    for g in range(GROUPS):
                        part_x0, part_y1, part_z, part_w = y_parts[g]
                        at = slice(128 * g, 128 * g + 128)
                        rows = []
                        for n in block:
                            hx = hx_ref[b, 0, n, g : g + 1, :]
                            if c == 0:
                                dx = hx_ref[b, 1, n, g : g + 1, :]
                                rows.append(dx * part_x0 + hx * part_y1)
                            else:
                                rows.append(hx * (part_z if c == 1 else part_w))
                        main_part, rest = split(stack_rows(rows, 16))
                        begin = row_at + c * count
                        left_ref[begin : begin + count, at] = main_part
                        begin = begin + 3 * count
                        left_ref[begin : begin + count, at] = rest
                if waiting is not None:
                    waiting()
                waiting = functools.partial(
                    multiply, row_at, count, b, e, high, [planes[n] for n in block]
                )
                row_at += 6 * count
    waiting()

    if not single:
        @pl.when(step == pl.num_programs(0) - 1)
        def _():
            for t in range(XTILES):
                finish(t)
            finish_all()
    else:
        finish_all()
    for c in range(2):
        up_ref[c] = fields_ref[c, :, UP_AT : UP_AT + HALO, :]
        down_ref[c] = fields_ref[c, :, DOWN_AT : DOWN_AT + HALO, :]


def chebyshev_factors():
    half_width = 6.0 / (6.0 + base_screen)
    sigma_ratio = 1.0 / half_width
    rho_prev = half_width
    factors = []
    for _ in range(ITERS - 1):
        rho_next = 1.0 / (2.0 * sigma_ratio - rho_prev)
        factors.append((rho_next * rho_prev, 2.0 * rho_next / half_width))
        rho_prev = rho_next
    return factors


def solve_kernel(
    shape, fields_ref, from_low_ref, from_high_ref, own_ref,
    indicator_ref, values_ref,
    given, low_halo, high_halo, owned, first, second, scaled, inverse, total,
    hx_ref, high_ref, low_ref, arrivals,
):
    gx, gy, gz = shape
    mx, my, mz = lax.axis_index("gx"), lax.axis_index("gy"), lax.axis_index("gz")
    copies = [
        pltpu.make_async_copy(source, target, arrivals.at[i])
        for i, (source, target) in enumerate(
            ((own_ref, owned), (fields_ref, given), (from_low_ref, low_halo), (from_high_ref, high_halo))
        )
    ]
    for copy in copies:
        copy.start()
    copies[0].wait()
    groups = owned.shape[1]
    y_row = row_iota(24) + float(8 - YO)
    blank = jnp.zeros((8, 128), f32)
    read_planes = range(XPT * FIRST_TILE, XPT * END_TILE)

    def read_operand(chunk):
        span = slice(chunk * GROUPS, chunk * GROUPS + GROUPS)
        cell_x, off_x = owned[0, span, 7, :], owned[0, span, 4, :]
        for plane in read_planes:
            if 0 <= plane - XO <= CX:
                hx_ref[plane] = hat(float(plane - XO), cell_x, 1.0 - off_x, off_x)
        for g in range(GROUPS):
            off_y = owned[0, chunk * GROUPS + g, 5:6, :]
            hy = hat(y_row, owned[1, chunk * GROUPS + g, 0:1, :], 1.0 - off_y, off_y)
            at = slice(128 * g, 128 * g + 128)
            for plane in read_planes:
                start = YS * (plane - XPT * FIRST_TILE)
                if 0 <= plane - XO <= CX:
                    rows = jnp.concatenate([blank, hx_ref[plane, g : g + 1, :] * hy], axis=0)
                    high, low = split(rows)
                else:
                    high = jnp.zeros((YS, 128), bf16)
                    low = high
                high_ref[start : start + YS, at] = high
                low_ref[start : start + YS, at] = low

    read_operand(0)
    for copy in copies[1:]:
        copy.wait()
    low_at, high_at = UP_AT - CZ, DOWN_AT + CZ
    for c in range(2):
        given[c, :, low_at : low_at + HALO, :] += low_halo[c]
        given[c, :, high_at : high_at + HALO, :] += high_halo[c]

    lane = lax.broadcasted_iota(jnp.int32, (8, 128), 1)
    row = lax.broadcasted_iota(jnp.int32, (8, 128), 0)
    y = lane % YS - YO + my * CY
    inside_y = (y >= 0) & (y < gy * CY)
    zero = jnp.zeros((8, 128), f32)
    for t in range(XTILES):
        x = lane // YS + (XPT * t - XO) + mx * CX
        inside_xy = inside_y & (x >= 0) & (x < gx * CX)
        for scratch in (first, second):
            scratch[t, 0:8, :] = zero
            scratch[t, ROWS + 8 : ROWS + 16, :] = zero
        for i in range(ROWS // 8):
            at = slice(8 * i, 8 * i + 8)
            z = row + (8 * i - ZO) + mz * CZ
            inside = inside_xy & (z >= 0) & (z < gz * CZ)
            diagonal = 6.0 + base_screen + point_screen * given[1, t, at, :]
            inv = jnp.where(inside, 1.0 / diagonal, 0.0)
            start = given[0, t, at, :] * inv
            inverse[t, at, :] = inv
            scaled[t, at, :] = start
            first[t, 8 * i + 8 : 8 * i + 16, :] = start
            if FIRST_TILE <= t < END_TILE:
                total[t - FIRST_TILE, at, :] = start

    now, later = first, second
    factors = chebyshev_factors()
    low_part, high_part = lane < YS, lane >= 128 - YS
    for k, (keep, gain) in enumerate(factors, 1):
        last = k == len(factors)
        begin, end = k // XPT, (XO + CX + REACH - k + XPT) // XPT
        for i in range(ROWS // 8):
            at = slice(8 * i, 8 * i + 8)
            here = {t: now[t, 8 * i + 8 : 8 * i + 16, :] for t in range(XTILES)}
            ahead_x = {t: pltpu.roll(here[t], YS, 1) for t in range(XTILES)}
            behind_x = {t: pltpu.roll(here[t], 128 - YS, 1) for t in range(XTILES)}
            for t in range(begin, end):
                mine = here[t]
                near = now[t, 8 * i + 7 : 8 * i + 15, :] + now[t, 8 * i + 9 : 8 * i + 17, :]
                near = near + pltpu.roll(mine, 1, 1) + pltpu.roll(mine, 127, 1)
                before = ahead_x[t]
                if t > 0:
                    before = jnp.where(low_part, ahead_x[t - 1], before)
                after = behind_x[t]
                if t + 1 < XTILES:
                    after = jnp.where(high_part, behind_x[t + 1], after)
                near = near + before + after
                left = scaled[t, at, :] - mine + inverse[t, at, :] * near
                ahead = keep * mine + gain * left
                if FIRST_TILE <= t < END_TILE:
                    total[t - FIRST_TILE, at, :] += ahead
                if not last:
                    scaled[t, at, :] = left
                    later[t, 8 * i + 8 : 8 * i + 16, :] = ahead
        now, later = later, now

    parts = [split(total[t - FIRST_TILE]) for t in range(FIRST_TILE, END_TILE)]
    u_high = jnp.concatenate([part[0] for part in parts], axis=1)
    u_low = jnp.concatenate([part[1] for part in parts], axis=1)
    u_both = jnp.concatenate([u_high, u_low], axis=0)
    z_row = row_iota(ROWS) - float(ZO)
    for chunk in range(groups // GROUPS):
        if chunk > 0:
            read_operand(chunk)
        got = dot_nn(u_both, high_ref[...])
        got = got[:ROWS] + got[ROWS:] + dot_nn(u_high, low_ref[...])
        rows = []
        for g in range(GROUPS):
            main = owned[0, chunk * GROUPS + g]
            off_z = main[6:7]
            hz = hat(z_row, owned[1, chunk * GROUPS + g, 1:2, :], 1.0 - off_z, off_z)
            value = jnp.sum(hz * got[:, 128 * g : 128 * g + 128], axis=0, keepdims=True)
            rows.append(jnp.where(main[3:4] > 0.0, value, 0.0))
        values = jnp.concatenate(rows, axis=0)
        for q in range(4):
            moved = values if q == 0 else pltpu.roll(values, 128 - 32 * q, 1)
            start = q * groups + chunk * GROUPS
            values_ref[start : start + GROUPS, :] = moved[:, 0:32]

    for t in range(FIRST_TILE, END_TILE):
        turned = total[t - FIRST_TILE, ZO : ZO + CZ, :].T
        for i in range(XPT):
            plane = XPT * t + i - XO
            if 0 <= plane < CX:
                indicator_ref[plane] = turned[YS * i + YO : YS * i + YO + CY, :]


def on_device(shape, point_data, point_cells, send_counts):
    gx, gy, gz = shape
    sources = gx * gy * gz
    slots = point_data.shape[3]
    bricks = 3 * (1 + other_count(gy))
    rows = 8 * -(-(bricks + -(-bricks // 4)) // 4)
    groups = sources // 4
    whole = pl.BlockSpec(memory_space=pltpu.VMEM)

    outgoing = pl.pallas_call(
        functools.partial(pack_kernel, shape),
        out_shape=jax.ShapeDtypeStruct((sources, rows, 128), f32),
        in_specs=[whole, whole, whole],
        out_specs=whole,
        scratch_shapes=[
            pltpu.VMEM((4, sources, 8, 128), f32),
            pltpu.VMEM((bricks, sources, 8, 128), f32),
        ],
        compiler_params=pltpu.CompilerParams(vmem_limit_bytes=56 * MIB),
        name="pack_points",
    )(
        jnp.transpose(point_data, (0, 2, 1, 3)),
        jnp.transpose(point_cells, (0, 2, 1, 3)),
        send_counts,
    )

    arrived = lax.all_to_all(outgoing, AXES, split_axis=0, concat_axis=0, tiled=True)
    arrived = arrived.reshape(4, groups, rows, 128)

    others = other_count(gy)
    lines = 0
    for planes in (CENTER, LOWER, UPPER):
        for high, size in ((24, 4),) + ((8, 12),) * others:
            for start in range(0, len(planes), size):
                count = min(size, len(planes) - start)
                lines += 6 * 16 * -(-count * high // 16)
    edge_shape = jax.ShapeDtypeStruct((2, XTILES, HALO, 128), f32)
    steps = groups // GROUPS
    fields, up, down, own = pl.pallas_call(
        functools.partial(splat_kernel, shape),
        grid=(steps,),
        out_shape=(
            jax.ShapeDtypeStruct((2, XTILES, ROWS, 128), f32), edge_shape, edge_shape,
            jax.ShapeDtypeStruct((2, groups, 8, 128), f32),
        ),
        in_specs=[pl.BlockSpec((4, GROUPS, rows, 128), lambda s: (0, s, 0, 0))],
        out_specs=(
            pl.BlockSpec((2, XTILES, ROWS, 128), lambda s: (0, 0, 0, 0)),
            pl.BlockSpec((2, XTILES, HALO, 128), lambda s: (0, 0, 0, 0)),
            pl.BlockSpec((2, XTILES, HALO, 128), lambda s: (0, 0, 0, 0)),
            pl.BlockSpec((2, GROUPS, 8, 128), lambda s: (0, s, 0, 0)),
        ),
        scratch_shapes=[
            pltpu.VMEM((rows // 2, GROUPS, 8, 128), f32),
            pltpu.VMEM((lines, 128 * GROUPS), bf16),
            pltpu.VMEM((bricks, 2, 128 * GROUPS, 2 * 128), bf16),
            pltpu.VMEM((bricks, 2, len(CENTER), GROUPS, 128), f32),
            pltpu.VMEM((3, XPT * XTILES, 24, 2 * 128), f32),
            pltpu.VMEM((max(others, 1), 3, XPT * XTILES, 8, 2 * 128), f32),
            pltpu.VMEM((XTILES, ROWS + 16, 128), f32),
        ],
        compiler_params=pltpu.CompilerParams(vmem_limit_bytes=36 * MIB),
        name="splat_points",
    )(arrived)

    from_low = lax.ppermute(up, "gz", [(i, i + 1) for i in range(gz - 1)])
    from_high = lax.ppermute(down, "gz", [(i + 1, i) for i in range(gz - 1)])

    depth = 128 * (END_TILE - FIRST_TILE)
    indicator, values = pl.pallas_call(
        functools.partial(solve_kernel, shape),
        out_shape=(
            jax.ShapeDtypeStruct((CX, CY, CZ), f32),
            jax.ShapeDtypeStruct((sources, slots), f32),
        ),
        in_specs=[pl.BlockSpec(memory_space=pl.ANY)] * 4,
        out_specs=(whole, whole),
        scratch_shapes=[
            pltpu.VMEM((2, XTILES, ROWS, 128), f32),
            pltpu.VMEM((2, XTILES, HALO, 128), f32),
            pltpu.VMEM((2, XTILES, HALO, 128), f32),
            pltpu.VMEM((2, groups, 8, 128), f32),
            pltpu.VMEM((XTILES, ROWS + 16, 128), f32),
            pltpu.VMEM((XTILES, ROWS + 16, 128), f32),
            pltpu.VMEM((XTILES, ROWS, 128), f32),
            pltpu.VMEM((XTILES, ROWS, 128), f32),
            pltpu.VMEM((END_TILE - FIRST_TILE, ROWS, 128), f32),
            pltpu.VMEM((XPT * END_TILE, GROUPS, 128), f32),
            pltpu.VMEM((depth, 128 * GROUPS), bf16),
            pltpu.VMEM((depth, 128 * GROUPS), bf16),
            pltpu.SemaphoreType.DMA((4,)),
        ],
        compiler_params=pltpu.CompilerParams(vmem_limit_bytes=16 * MIB),
        name="solve_and_read",
    )(fields, from_low, from_high, own)

    returned = lax.all_to_all(
        values.reshape(1, sources, slots), AXES, split_axis=1, concat_axis=1, tiled=True
    )
    return indicator, returned


def solution(mesh):
    shape = tuple(mesh.shape[axis] for axis in AXES)
    in_specs = (
        P(AXES, None, None, None),
        P(AXES, None, None, None),
        P(AXES, None),
    )
    out_specs = (P("gx", "gy", "gz"), P(AXES, None, None))
    return jax.shard_map(
        functools.partial(on_device, shape),
        mesh=mesh,
        in_specs=in_specs,
        out_specs=out_specs,
        check_vma=False,
    )
```

```python
import functools

import jax
import jax.numpy as jnp
from jax import lax
from jax.experimental import pallas as pl
from jax.experimental.pallas import tpu as pltpu
from jax.sharding import PartitionSpec as P

CX = 16
CY = 16
CZ = 128
ITERS = 6

base_screen = 0.25
point_screen = 4.0

AXES = ("gx", "gy", "gz")
REACH = ITERS - 1
XO = REACH
YO = 9
ZO = 8
YS = 32
XPT = 128 // YS
XTILES = -(-(CX + 2 * REACH + 1) // XPT)
ROWS = CZ + 16
CENTER = tuple(range(XO - 1, XO + CX + 2))
LOWER = tuple(range(0, XO + 2))
UPPER = tuple(range(XO + CX - 1, XO + CX + REACH + 1))
PLAIN = {0: CENTER[1:-1], -1: LOWER[:-1], 1: UPPER[1:]}
FIRST_TILE, END_TILE = XO // XPT, (XO + CX) // XPT + 1
WINDOW_LOW = YO - REACH
WINDOW_HIGH = YO + CY - 1
UP_AT = ZO + CZ - REACH
DOWN_AT = ZO - 1
HALO = 8
GROUPS = 8
MIB = 1024 * 1024

f32 = jnp.float32
bf16 = jnp.bfloat16


def split(value):
    high = value.astype(bf16)
    return high, (value - high.astype(f32)).astype(bf16)


def dot_nt(lhs, rhs):
    return lax.dot_general(lhs, rhs, (((1,), (1,)), ((), ())), preferred_element_type=f32)


def dot_nn(lhs, rhs):
    return lax.dot_general(lhs, rhs, (((1,), (0,)), ((), ())), preferred_element_type=f32)


def other_count(gy):
    return min(gy - 1, 2)


def extra_place(brick, bricks):
    return bricks + brick // 4, 2 * (brick % 4)


def pack_kernel(shape, data_ref, cells_ref, counts_ref, out_ref, main, extra):
    gx, gy, gz = shape
    slots = data_ref.shape[3]
    sources = gx * gy * gz
    lane = lax.broadcasted_iota(jnp.int32, (sources, slots), 1)
    at_row = lax.broadcasted_iota(jnp.int32, (sources, sources), 0)
    at_lane = lax.broadcasted_iota(jnp.int32, (sources, sources), 1)
    counts = jnp.where(at_row == at_lane, counts_ref[...], 0).astype(f32)
    counts = jnp.sum(counts, axis=1, keepdims=True).astype(jnp.int32)
    others = other_count(gy)
    bricks = 3 * (1 + others)
    weight = jnp.where(lane < counts, data_ref[0, 3], 0.0)
    cells = [cells_ref[0, c].astype(f32) for c in range(3)]
    channels = [data_ref[0, c] * (-0.5 * weight) for c in range(3)]
    channels += [weight] + [data_ref[0, c] for c in range(4, 7)] + [cells[0]]

    def placed(value, part):
        pieces = [jnp.zeros((sources, slots * part), f32)] if part else []
        pieces.append(value)
        if part < 3:
            pieces.append(jnp.zeros((sources, 128 - slots * (part + 1)), f32))
        return jnp.concatenate(pieces, axis=1)

    for part in range(min(bricks, 4)):
        for c in range(8):
            main[part, :, c, :] = placed(channels[c], part)
    extra[...] = jnp.zeros_like(extra)
    for b in range(bricks):
        place, row = extra_place(b, bricks)
        for c in range(2):
            extra[b, :, row + c, :] = placed(cells[1 + c], place % 4)
    for d in range(sources):
        x, y, z = d // (gy * gz), (d // gz) % gy, d % gz
        if others == 0:
            ys = (y,)
        elif others == 1:
            ys = (y, 1 - y)
        else:
            ys = (y, y - 1, y + 1)
        sums = [None] * (out_ref.shape[1] // 8)
        for e, by in enumerate(ys):
            for o, bx in enumerate((x, x - 1, x + 1)):
                if not (0 <= bx < gx and 0 <= by < gy):
                    continue
                b = e * 3 + o
                source = (bx * gy + by) * gz + z
                place, _ = extra_place(b, bricks)
                for tile, value in (
                    (b // 4, main[b % 4, source]), (place // 4, extra[b, source])
                ):
                    sums[tile] = value if sums[tile] is None else sums[tile] + value
        for tile, value in enumerate(sums):
            if value is None:
                value = jnp.zeros((8, 128), f32)
            out_ref[d, 8 * tile : 8 * tile + 8, :] = value


def hat(coordinate, cell, low, high):
    away = coordinate - cell
    return jnp.where(away == 0.0, low, jnp.where(away == 1.0, high, 0.0))


def hat_slope(coordinate, cell, low, high):
    away = coordinate - cell
    rising = jnp.where(away == -1.0, low, jnp.where(away == 0.0, high, 0.0))
    return rising - jnp.where(away == 1.0, low, jnp.where(away == 2.0, high, 0.0))


def row_iota(rows):
    return lax.broadcasted_iota(jnp.int32, (rows, 128), 0).astype(f32)


def stack_rows(parts, multiple):
    have = sum(part.shape[0] for part in parts)
    if have % multiple:
        parts = parts + [jnp.zeros((multiple - have % multiple, 128), f32)]
    return jnp.concatenate(parts, axis=0) if len(parts) > 1 else parts[0]


def splat_kernel(
    shape, recv_ref, fields_ref, up_ref, down_ref, own_ref,
    points, left_ref, right_ref, hx_ref, near, beside, slope, top_x, top_y, top_sum,
):
    gx, gy, gz = shape
    mx, my, mz = lax.axis_index("gx"), lax.axis_index("gy"), lax.axis_index("gz")
    step = pl.program_id(0)
    single = recv_ref.shape[1] * 4 == gx * gy * gz
    others = other_count(gy)
    bricks = 3 * (1 + others)
    tiles = recv_ref.shape[2] // 8
    lane_part = lax.broadcasted_iota(jnp.int32, (8, 128), 1) // 32
    span = 128 * GROUPS
    written = set()

    def add(ref, place, value):
        if single and place not in written:
            written.add(place)
            ref[place] = value
        else:
            ref[place] += value

    if not single:
        @pl.when(step == 0)
        def _():
            near[...] = jnp.zeros_like(near)
            beside[...] = jnp.zeros_like(beside)

    for t in range(tiles):
        for g in range(GROUPS):
            given = [recv_ref[q, g, 8 * t : 8 * t + 8, :] for q in range(4)]
            for k in range(4):
                if 4 * t + k >= bricks + -(-bricks // 4):
                    continue
                merged = None
                for q in range(4):
                    moved = given[q] if q == k else pltpu.roll(given[q], (32 * (q - k)) % 128, 1)
                    merged = moved if merged is None else jnp.where(lane_part == q, moved, merged)
                points[4 * t + k, g] = merged
    own_ref[0] = points[0]
    own_ref[1] = points[bricks]

    z_limit = jnp.where(mz == gz - 1, CZ, CZ + 1).astype(f32)
    z_row = row_iota(CZ)
    own_row = row_iota(24) + float(8 - YO)

    def multiply(begin, lists, b, e, high):
        counts = [-(-len(planes) * high // 16) * 16 for planes in lists]
        size = sum(counts)
        wide = dot_nn(left_ref[begin : begin + size, :], right_ref[b])
        got = wide[:, :CZ] + wide[:, CZ:]
        got = got + dot_nn(left_ref[begin + size : begin + 2 * size, :], right_ref[b, :, 0:CZ])
        at = 0
        for c in range(3):
            for i, plane in enumerate(lists[c]):
                value = got[at + i * high : at + i * high + high]
                if e == 0:
                    add(near, (c, plane), value)
                else:
                    add(beside, (e - 1, c, plane), value)
            at += counts[c]
        if single and e == 0:
            for t in sorted({plane // XPT for plane in lists[0]}):
                unfinished[t] -= 1
                if unfinished[t] == 0:
                    finish(t)

    row8 = lax.broadcasted_iota(jnp.int32, (8, 128), 0)
    zero = jnp.zeros((8, 128), f32)

    def finish(t):
        turned = []
        for c in range(3):
            pieces = []
            for plane in range(XPT * t, XPT * t + XPT):
                if plane > UPPER[-1]:
                    pieces.append(jnp.zeros((YS, 128), f32))
                    continue
                parts = [zero] + [near[c, plane, 8 * i : 8 * i + 8, :] for i in range(3)]
                if others:
                    if others == 1:
                        value = beside[0, c, plane]
                        low_part = jnp.where(my == 0, 0.0, value)
                        high_part = jnp.where(my == 0, value, 0.0)
                    else:
                        low_part, high_part = beside[0, c, plane], beside[1, c, plane]
                    moved = pltpu.roll(low_part, 4, 0)
                    parts[0] = jnp.where(row8 >= 4, moved, 0.0)
                    parts[1] = parts[1] + jnp.where(row8 < 4, moved, 0.0)
                    parts[3] = parts[3] + high_part
                pieces.extend(parts)
            turned.append(jnp.concatenate(pieces, axis=0).T)
        fields_ref[0, t, ZO : ZO + CZ, :] = turned[0]
        slope[t, ZO + 8 : ZO + 8 + CZ, :] = turned[1]
        fields_ref[1, t, ZO : ZO + CZ, :] = turned[2]

    def finish_all():
        planes = XPT * XTILES
        got = dot_nt(top_x[...], top_y[0])
        got = got[:64] + got[64:] + dot_nt(top_x[0:64, :], top_y[1])
        by_x, by_slope = got[:32], got[32:]
        sums = (by_slope + pltpu.roll(by_x, 128 - YS, 1), pltpu.roll(by_x, 128 - 2 * YS, 1))
        sums += (pltpu.roll(by_x, 128 - 3 * YS, 1),)
        above = []
        for c in range(3):
            if single:
                top_sum[c] = sums[c]
            else:
                top_sum[c] = jnp.where(step == 0, 0.0, top_sum[c]) + sums[c]
            line = None
            for i in range(XPT):
                value = top_sum[c, pl.ds(i, 32 // XPT, stride=XPT), :]
                if i:
                    value = pltpu.roll(value, YS * i, 1)
                    value = jnp.where(row_lane // YS == i, value, line)
                line = value
            above.append(line)
        return above

    def place_all(above):
        for t in range(XTILES):
            first_of = [above[c][t : t + 1, :] for c in range(3)]
            rest = jnp.zeros((7, 128), f32)
            slope[t, 0 : ZO + 8, :] = jnp.zeros((ZO + 8, 128), f32)
            slope[t, ZO + 8 + CZ : ZO + 16 + CZ, :] = jnp.concatenate([first_of[1], rest], axis=0)
            slope[t, ZO + 16 + CZ : ROWS + 16, :] = zero
            for c in range(2):
                fields_ref[c, t, 0:ZO, :] = zero
                fields_ref[c, t, ZO + CZ : ROWS, :] = jnp.concatenate(
                    [first_of[2 * c], rest], axis=0
                )
            fields_ref[0, t] += slope[t, 9 : ROWS + 9, :] - slope[t, 7 : ROWS + 7, :]

    row_lane = lax.broadcasted_iota(jnp.int32, (32 // XPT, 128), 1)
    unfinished = [
        sum(
            plane // XPT == t and (i == 0 or planes[i - 1] // XPT != t)
            for planes in (CENTER, LOWER, UPPER)
            for i, plane in enumerate(planes)
        )
        for t in range(XTILES)
    ]
    row_at = 0
    waiting = None
    for e in reversed(range(1 + others)):
        if e == 0:
            y_limit = jnp.where(my == gy - 1, CY, CY + 1).astype(f32)
            y_row = own_row
        else:
            above_me = my == 0 if others == 1 else jnp.bool_(e == 2)
            y_limit = jnp.where(
                jnp.logical_and(above_me, my + 1 == gy - 1), CY, CY + 1
            ).astype(f32)
            first = jnp.where(above_me, WINDOW_HIGH - YO - CY, WINDOW_LOW - YO + CY)
            y_row = row_iota(8) + first.astype(f32)
            y_shift = jnp.where(above_me, CY, -CY).astype(f32)
        high = y_row.shape[0]
        for o, shift, planes in ((1, -1, LOWER), (2, 1, UPPER), (0, 0, CENTER)):
            b = e * 3 + o
            place, row = extra_place(b, bricks)
            x_limit = jnp.where(mx + shift == gx - 1, CX, CX + 1).astype(f32)
            cell_x = points[b, :, 7, :]
            off_x = points[b, :, 4, :]
            low_x = 1.0 - off_x
            high_x = jnp.where(cell_x + 1.0 < x_limit, off_x, 0.0)
            for n, plane in enumerate(planes):
                at = float(plane - XO - CX * shift)
                hx_ref[b, 0, n] = hat(at, cell_x, low_x, high_x)
                hx_ref[b, 1, n] = hat_slope(at, cell_x, low_x, high_x)
            cell_z, off_z = points[place, :, row + 1, :], points[b, :, 6, :]
            top = jnp.where((cell_z + 1.0 == float(CZ)) & (cell_z + 1.0 < z_limit), off_z, 0.0)
            y_parts = []
            for g in range(GROUPS):
                main = points[b, g]
                more = points[place, g]
                cell_y, cell_z = more[row : row + 1], more[row + 1 : row + 2]
                off_y, off_z = main[5:6], main[6:7]
                at = slice(128 * g, 128 * g + 128)
                hz_high, hz_low = split(hat(z_row, cell_z, 1.0 - off_z, off_z).T)
                right_ref[b, at, 0:CZ] = hz_high
                right_ref[b, at, CZ : 2 * CZ] = hz_low
                high_y = jnp.where(cell_y + 1.0 < y_limit, off_y, 0.0)
                hy = hat(y_row, cell_y, 1.0 - off_y, high_y)
                dy = hat_slope(y_row, cell_y, 1.0 - off_y, high_y)
                y_parts.append((main[0:1] * hy, main[1:2] * dy, main[2:3] * hy, main[3:4] * hy))
                if e == 0:
                    wide_parts = [jnp.concatenate([zero, part], axis=0) for part in y_parts[-1]]
                else:
                    wide_row = row_iota(YS) - (y_shift + float(YO))
                    hy = hat(wide_row, cell_y, 1.0 - off_y, high_y)
                    dy = hat_slope(wide_row, cell_y, 1.0 - off_y, high_y)
                    wide_parts = [main[0:1] * hy, main[1:2] * dy, main[2:3] * hy, main[3:4] * hy]
                at = slice(span * b + 128 * g, span * b + 128 * g + 128)
                high_part, low_part = split(jnp.concatenate(wide_parts, axis=0) * top[g : g + 1])
                top_y[0, :, at] = high_part
                top_y[1, :, at] = low_part
                for n in range(2):
                    rows = [jnp.zeros((planes[0], 128), f32)] if planes[0] else []
                    rows.append(hx_ref[b, n, 0 : len(planes), g, :])
                    rows.append(jnp.zeros((32 - planes[-1] - 1, 128), f32))
                    high_part, low_part = split(jnp.concatenate(rows, axis=0))
                    top_x[32 * n : 32 * n + 32, at] = high_part
                    top_x[64 + 32 * n : 96 + 32 * n, at] = low_part
            size = 4 if e == 0 else 12
            for start in range(0, len(planes), size):
                block = planes[start : start + size]
                lists = [block] + 2 * [tuple(p for p in block if p in PLAIN[shift])]
                counts = [-(-len(each) * high // 16) * 16 for each in lists]
                for c in range(3):
                    begin = row_at + sum(counts[:c])
                    for g in range(GROUPS):
                        part_x0, part_y1, part_z, part_w = y_parts[g]
                        at = slice(128 * g, 128 * g + 128)
                        rows = []
                        for plane in lists[c]:
                            n = plane - planes[0]
                            hx = hx_ref[b, 0, n, g : g + 1, :]
                            if c == 0:
                                dx = hx_ref[b, 1, n, g : g + 1, :]
                                rows.append(dx * part_x0 + hx * part_y1)
                            else:
                                rows.append(hx * (part_z if c == 1 else part_w))
                        main_part, rest = split(stack_rows(rows, 16))
                        left_ref[begin : begin + counts[c], at] = main_part
                        after = begin + sum(counts)
                        left_ref[after : after + counts[c], at] = rest
                if waiting is not None:
                    waiting()
                waiting = functools.partial(multiply, row_at, lists, b, e, high)
                row_at += 2 * sum(counts)
    waiting()

    above = finish_all()
    if not single:
        @pl.when(step == pl.num_programs(0) - 1)
        def _():
            for t in range(XTILES):
                finish(t)
            place_all(above)
    else:
        place_all(above)
    for c in range(2):
        up_ref[c] = fields_ref[c, :, UP_AT : UP_AT + HALO, :]
        down_ref[c] = fields_ref[c, :, DOWN_AT : DOWN_AT + HALO, :]


def chebyshev_factors():
    half_width = 6.0 / (6.0 + base_screen)
    sigma_ratio = 1.0 / half_width
    rho_prev = half_width
    factors = []
    for _ in range(ITERS - 1):
        rho_next = 1.0 / (2.0 * sigma_ratio - rho_prev)
        factors.append((rho_next * rho_prev, 2.0 * rho_next / half_width))
        rho_prev = rho_next
    return factors


def solve_kernel(
    shape, fields_ref, from_low_ref, from_high_ref, own_ref,
    indicator_ref, values_ref,
    given, low_halo, high_halo, owned, first, second, scaled, inverse, total,
    hx_ref, high_ref, low_ref, arrivals,
):
    gx, gy, gz = shape
    mx, my, mz = lax.axis_index("gx"), lax.axis_index("gy"), lax.axis_index("gz")
    copies = [
        pltpu.make_async_copy(source, target, arrivals.at[i])
        for i, (source, target) in enumerate(
            ((own_ref, owned), (fields_ref, given), (from_low_ref, low_halo), (from_high_ref, high_halo))
        )
    ]
    for copy in copies:
        copy.start()
    copies[0].wait()
    groups = owned.shape[1]
    y_row = row_iota(24) + float(8 - YO)
    blank = jnp.zeros((8, 128), f32)
    read_planes = range(XPT * FIRST_TILE, XPT * END_TILE)

    def read_operand(chunk):
        span = slice(chunk * GROUPS, chunk * GROUPS + GROUPS)
        cell_x, off_x = owned[0, span, 7, :], owned[0, span, 4, :]
        for plane in read_planes:
            if 0 <= plane - XO <= CX:
                hx_ref[plane] = hat(float(plane - XO), cell_x, 1.0 - off_x, off_x)
        for g in range(GROUPS):
            off_y = owned[0, chunk * GROUPS + g, 5:6, :]
            hy = hat(y_row, owned[1, chunk * GROUPS + g, 0:1, :], 1.0 - off_y, off_y)
            at = slice(128 * g, 128 * g + 128)
            for plane in read_planes:
                start = YS * (plane - XPT * FIRST_TILE)
                if 0 <= plane - XO <= CX:
                    rows = jnp.concatenate([blank, hx_ref[plane, g : g + 1, :] * hy], axis=0)
                    high, low = split(rows)
                else:
                    high = jnp.zeros((YS, 128), bf16)
                    low = high
                high_ref[start : start + YS, at] = high
                low_ref[start : start + YS, at] = low

    read_operand(0)
    for copy in copies[1:]:
        copy.wait()
    low_at, high_at = UP_AT - CZ, DOWN_AT + CZ
    for c in range(2):
        given[c, :, low_at : low_at + HALO, :] += low_halo[c]
        given[c, :, high_at : high_at + HALO, :] += high_halo[c]

    lane = lax.broadcasted_iota(jnp.int32, (8, 128), 1)
    row = lax.broadcasted_iota(jnp.int32, (8, 128), 0)
    y = lane % YS - YO + my * CY
    inside_y = (y >= 0) & (y < gy * CY)
    zero = jnp.zeros((8, 128), f32)
    for t in range(XTILES):
        x = lane // YS + (XPT * t - XO) + mx * CX
        inside_xy = inside_y & (x >= 0) & (x < gx * CX)
        for scratch in (first, second):
            scratch[t, 0:8, :] = zero
            scratch[t, ROWS + 8 : ROWS + 16, :] = zero
        for i in range(ROWS // 8):
            at = slice(8 * i, 8 * i + 8)
            z = row + (8 * i - ZO) + mz * CZ
            inside = inside_xy & (z >= 0) & (z < gz * CZ)
            diagonal = 6.0 + base_screen + point_screen * given[1, t, at, :]
            inv = jnp.where(inside, 1.0 / diagonal, 0.0)
            start = given[0, t, at, :] * inv
            inverse[t, at, :] = inv
            scaled[t, at, :] = start
            first[t, 8 * i + 8 : 8 * i + 16, :] = start
            if FIRST_TILE <= t < END_TILE:
                total[t - FIRST_TILE, at, :] = start

    now, later = first, second
    factors = chebyshev_factors()
    low_part, high_part = lane < YS, lane >= 128 - YS
    for k, (keep, gain) in enumerate(factors, 1):
        last = k == len(factors)
        begin, end = k // XPT, (XO + CX + REACH - k + XPT) // XPT
        for i in range(ROWS // 8):
            at = slice(8 * i, 8 * i + 8)
            here = {t: now[t, 8 * i + 8 : 8 * i + 16, :] for t in range(XTILES)}
            ahead_x = {t: pltpu.roll(here[t], YS, 1) for t in range(XTILES)}
            behind_x = {t: pltpu.roll(here[t], 128 - YS, 1) for t in range(XTILES)}
            for t in range(begin, end):
                mine = here[t]
                near = now[t, 8 * i + 7 : 8 * i + 15, :] + now[t, 8 * i + 9 : 8 * i + 17, :]
                near = near + pltpu.roll(mine, 1, 1) + pltpu.roll(mine, 127, 1)
                before = ahead_x[t]
                if t > 0:
                    before = jnp.where(low_part, ahead_x[t - 1], before)
                after = behind_x[t]
                if t + 1 < XTILES:
                    after = jnp.where(high_part, behind_x[t + 1], after)
                near = near + before + after
                left = scaled[t, at, :] - mine + inverse[t, at, :] * near
                ahead = keep * mine + gain * left
                if FIRST_TILE <= t < END_TILE:
                    total[t - FIRST_TILE, at, :] += ahead
                if not last:
                    scaled[t, at, :] = left
                    later[t, 8 * i + 8 : 8 * i + 16, :] = ahead
        now, later = later, now

    parts = [split(total[t - FIRST_TILE]) for t in range(FIRST_TILE, END_TILE)]
    u_high = jnp.concatenate([part[0] for part in parts], axis=1)
    u_low = jnp.concatenate([part[1] for part in parts], axis=1)
    u_both = jnp.concatenate([u_high, u_low], axis=0)
    z_row = row_iota(ROWS) - float(ZO)
    for chunk in range(groups // GROUPS):
        if chunk > 0:
            read_operand(chunk)
        got = dot_nn(u_both, high_ref[...])
        got = got[:ROWS] + got[ROWS:] + dot_nn(u_high, low_ref[...])
        rows = []
        for g in range(GROUPS):
            main = owned[0, chunk * GROUPS + g]
            off_z = main[6:7]
            hz = hat(z_row, owned[1, chunk * GROUPS + g, 1:2, :], 1.0 - off_z, off_z)
            value = jnp.sum(hz * got[:, 128 * g : 128 * g + 128], axis=0, keepdims=True)
            rows.append(jnp.where(main[3:4] > 0.0, value, 0.0))
        values = jnp.concatenate(rows, axis=0)
        for q in range(4):
            moved = values if q == 0 else pltpu.roll(values, 128 - 32 * q, 1)
            start = q * groups + chunk * GROUPS
            values_ref[start : start + GROUPS, :] = moved[:, 0:32]

    for t in range(FIRST_TILE, END_TILE):
        turned = total[t - FIRST_TILE, ZO : ZO + CZ, :].T
        for i in range(XPT):
            plane = XPT * t + i - XO
            if 0 <= plane < CX:
                indicator_ref[plane] = turned[YS * i + YO : YS * i + YO + CY, :]


def on_device(shape, point_data, point_cells, send_counts):
    gx, gy, gz = shape
    sources = gx * gy * gz
    slots = point_data.shape[3]
    bricks = 3 * (1 + other_count(gy))
    rows = 8 * -(-(bricks + -(-bricks // 4)) // 4)
    groups = sources // 4
    whole = pl.BlockSpec(memory_space=pltpu.VMEM)

    outgoing = pl.pallas_call(
        functools.partial(pack_kernel, shape),
        out_shape=jax.ShapeDtypeStruct((sources, rows, 128), f32),
        in_specs=[whole, whole, whole],
        out_specs=whole,
        scratch_shapes=[
            pltpu.VMEM((4, sources, 8, 128), f32),
            pltpu.VMEM((bricks, sources, 8, 128), f32),
        ],
        compiler_params=pltpu.CompilerParams(vmem_limit_bytes=56 * MIB),
        name="pack_points",
    )(
        jnp.transpose(point_data, (0, 2, 1, 3)),
        jnp.transpose(point_cells, (0, 2, 1, 3)),
        send_counts,
    )

    arrived = lax.all_to_all(outgoing, AXES, split_axis=0, concat_axis=0, tiled=True)
    arrived = arrived.reshape(4, groups, rows, 128)

    others = other_count(gy)
    lines = 0
    for planes in (CENTER, LOWER, UPPER):
        for high, size in ((24, 4),) + ((8, 12),) * others:
            for start in range(0, len(planes), size):
                count = min(size, len(planes) - start)
                lines += 6 * 16 * -(-count * high // 16)
    edge_shape = jax.ShapeDtypeStruct((2, XTILES, HALO, 128), f32)
    steps = groups // GROUPS
    fields, up, down, own = pl.pallas_call(
        functools.partial(splat_kernel, shape),
        grid=(steps,),
        out_shape=(
            jax.ShapeDtypeStruct((2, XTILES, ROWS, 128), f32), edge_shape, edge_shape,
            jax.ShapeDtypeStruct((2, groups, 8, 128), f32),
        ),
        in_specs=[pl.BlockSpec((4, GROUPS, rows, 128), lambda s: (0, s, 0, 0))],
        out_specs=(
            pl.BlockSpec((2, XTILES, ROWS, 128), lambda s: (0, 0, 0, 0)),
            pl.BlockSpec((2, XTILES, HALO, 128), lambda s: (0, 0, 0, 0)),
            pl.BlockSpec((2, XTILES, HALO, 128), lambda s: (0, 0, 0, 0)),
            pl.BlockSpec((2, GROUPS, 8, 128), lambda s: (0, s, 0, 0)),
        ),
        scratch_shapes=[
            pltpu.VMEM((rows // 2, GROUPS, 8, 128), f32),
            pltpu.VMEM((lines, 128 * GROUPS), bf16),
            pltpu.VMEM((bricks, 128 * GROUPS, 2 * CZ), bf16),
            pltpu.VMEM((bricks, 2, len(CENTER), GROUPS, 128), f32),
            pltpu.VMEM((3, XPT * XTILES, 24, 128), f32),
            pltpu.VMEM((max(others, 1), 3, XPT * XTILES, 8, 128), f32),
            pltpu.VMEM((XTILES, ROWS + 16, 128), f32),
            pltpu.VMEM((4 * 32, bricks * 128 * GROUPS), bf16),
            pltpu.VMEM((2, 4 * YS, bricks * 128 * GROUPS), bf16),
            pltpu.VMEM((3, 32, 128), f32),
        ],
        compiler_params=pltpu.CompilerParams(vmem_limit_bytes=36 * MIB),
        name="splat_points",
    )(arrived)

    from_low = lax.ppermute(up, "gz", [(i, i + 1) for i in range(gz - 1)])
    from_high = lax.ppermute(down, "gz", [(i + 1, i) for i in range(gz - 1)])

    depth = 128 * (END_TILE - FIRST_TILE)
    indicator, values = pl.pallas_call(
        functools.partial(solve_kernel, shape),
        out_shape=(
            jax.ShapeDtypeStruct((CX, CY, CZ), f32),
            jax.ShapeDtypeStruct((sources, slots), f32),
        ),
        in_specs=[pl.BlockSpec(memory_space=pl.ANY)] * 4,
        out_specs=(whole, whole),
        scratch_shapes=[
            pltpu.VMEM((2, XTILES, ROWS, 128), f32),
            pltpu.VMEM((2, XTILES, HALO, 128), f32),
            pltpu.VMEM((2, XTILES, HALO, 128), f32),
            pltpu.VMEM((2, groups, 8, 128), f32),
            pltpu.VMEM((XTILES, ROWS + 16, 128), f32),
            pltpu.VMEM((XTILES, ROWS + 16, 128), f32),
            pltpu.VMEM((XTILES, ROWS, 128), f32),
            pltpu.VMEM((XTILES, ROWS, 128), f32),
            pltpu.VMEM((END_TILE - FIRST_TILE, ROWS, 128), f32),
            pltpu.VMEM((XPT * END_TILE, GROUPS, 128), f32),
            pltpu.VMEM((depth, 128 * GROUPS), bf16),
            pltpu.VMEM((depth, 128 * GROUPS), bf16),
            pltpu.SemaphoreType.DMA((4,)),
        ],
        compiler_params=pltpu.CompilerParams(vmem_limit_bytes=16 * MIB),
        name="solve_and_read",
    )(fields, from_low, from_high, own)

    returned = lax.all_to_all(
        values.reshape(1, sources, slots), AXES, split_axis=1, concat_axis=1, tiled=True
    )
    return indicator, returned


def solution(mesh):
    shape = tuple(mesh.shape[axis] for axis in AXES)
    in_specs = (
        P(AXES, None, None, None),
        P(AXES, None, None, None),
        P(AXES, None),
    )
    out_specs = (P("gx", "gy", "gz"), P(AXES, None, None))
    return jax.shard_map(
        functools.partial(on_device, shape),
        mesh=mesh,
        in_specs=in_specs,
        out_specs=out_specs,
        check_vma=False,
    )
```

```python
import functools

import jax
import jax.numpy as jnp
from jax import lax
from jax.experimental import pallas as pl
from jax.experimental.pallas import tpu as pltpu
from jax.sharding import PartitionSpec as P

CX = 16
CY = 16
CZ = 128
ITERS = 6

base_screen = 0.25
point_screen = 4.0

AXES = ("gx", "gy", "gz")
REACH = ITERS - 1
XO = REACH
YO = 9
ZO = 8
YS = 32
XPT = 128 // YS
XTILES = -(-(CX + 2 * REACH + 1) // XPT)
ROWS = CZ + 16
CENTER = tuple(range(XO - 1, XO + CX + 2))
LOWER = tuple(range(0, XO + 2))
UPPER = tuple(range(XO + CX - 1, XO + CX + REACH + 1))
PLAIN = {0: CENTER[1:-1], -1: LOWER[:-1], 1: UPPER[1:]}
FIRST_TILE, END_TILE = XO // XPT, (XO + CX) // XPT + 1
WINDOW_LOW = YO - REACH
WINDOW_HIGH = YO + CY - 1
UP_AT = ZO + CZ - REACH
DOWN_AT = ZO - 1
HALO = 8
GROUPS = 8
MIB = 1024 * 1024

f32 = jnp.float32
bf16 = jnp.bfloat16


def split(value):
    high = value.astype(bf16)
    return high, (value - high.astype(f32)).astype(bf16)


def dot_nt(lhs, rhs):
    return lax.dot_general(lhs, rhs, (((1,), (1,)), ((), ())), preferred_element_type=f32)


def dot_nn(lhs, rhs):
    return lax.dot_general(lhs, rhs, (((1,), (0,)), ((), ())), preferred_element_type=f32)


def other_count(gy):
    return min(gy - 1, 2)


def extra_place(brick, bricks):
    return bricks + brick // 4, 2 * (brick % 4)


def pack_kernel(shape, data_ref, cells_ref, counts_ref, out_ref, main, extra):
    gx, gy, gz = shape
    slots = data_ref.shape[3]
    sources = gx * gy * gz
    lane = lax.broadcasted_iota(jnp.int32, (sources, slots), 1)
    at_row = lax.broadcasted_iota(jnp.int32, (sources, sources), 0)
    at_lane = lax.broadcasted_iota(jnp.int32, (sources, sources), 1)
    counts = jnp.where(at_row == at_lane, counts_ref[...], 0).astype(f32)
    counts = jnp.sum(counts, axis=1, keepdims=True).astype(jnp.int32)
    others = other_count(gy)
    bricks = 3 * (1 + others)
    weight = jnp.where(lane < counts, data_ref[0, 3], 0.0)
    cells = [cells_ref[0, c].astype(f32) for c in range(3)]
    channels = [data_ref[0, c] * (-0.5 * weight) for c in range(3)]
    channels += [weight] + [data_ref[0, c] for c in range(4, 7)] + [cells[0]]

    def placed(value, part):
        pieces = [jnp.zeros((sources, slots * part), f32)] if part else []
        pieces.append(value)
        if part < 3:
            pieces.append(jnp.zeros((sources, 128 - slots * (part + 1)), f32))
        return jnp.concatenate(pieces, axis=1)

    for part in range(min(bricks, 4)):
        for c in range(8):
            main[part, :, c, :] = placed(channels[c], part)
    extra[...] = jnp.zeros_like(extra)
    for b in range(bricks):
        place, row = extra_place(b, bricks)
        for c in range(2):
            extra[b, :, row + c, :] = placed(cells[1 + c], place % 4)
    for d in range(sources):
        x, y, z = d // (gy * gz), (d // gz) % gy, d % gz
        if others == 0:
            ys = (y,)
        elif others == 1:
            ys = (y, 1 - y)
        else:
            ys = (y, y - 1, y + 1)
        sums = [None] * (out_ref.shape[1] // 8)
        for e, by in enumerate(ys):
            for o, bx in enumerate((x, x - 1, x + 1)):
                if not (0 <= bx < gx and 0 <= by < gy):
                    continue
                b = e * 3 + o
                source = (bx * gy + by) * gz + z
                place, _ = extra_place(b, bricks)
                for tile, value in (
                    (b // 4, main[b % 4, source]), (place // 4, extra[b, source])
                ):
                    sums[tile] = value if sums[tile] is None else sums[tile] + value
        for tile, value in enumerate(sums):
            if value is None:
                value = jnp.zeros((8, 128), f32)
            out_ref[d, 8 * tile : 8 * tile + 8, :] = value


def hat(coordinate, cell, low, high):
    away = coordinate - cell
    return jnp.where(away == 0.0, low, jnp.where(away == 1.0, high, 0.0))


def hat_slope(coordinate, cell, low, high):
    away = coordinate - cell
    rising = jnp.where(away == -1.0, low, jnp.where(away == 0.0, high, 0.0))
    return rising - jnp.where(away == 1.0, low, jnp.where(away == 2.0, high, 0.0))


def split_hat(rows, cell, offset):
    spread = (16, 128)
    fill = rows.shape[0] // 16
    ends = []
    for value in (1.0 - offset, offset):
        ends.extend(split(jnp.broadcast_to(value, spread)))
    low_high, low_low, high_high, high_low = (jnp.concatenate([v] * fill, axis=0) for v in ends)
    cells = jnp.broadcast_to(cell, spread).astype(bf16)
    away = rows - jnp.concatenate([cells] * fill, axis=0)
    here, above = away == 0.0, away == 1.0
    zero = jnp.zeros(rows.shape, bf16)
    return (
        jnp.where(here, low_high, jnp.where(above, high_high, zero)),
        jnp.where(here, low_low, jnp.where(above, high_low, zero)),
    )


def row_iota(rows):
    return lax.broadcasted_iota(jnp.int32, (rows, 128), 0).astype(f32)


def stack_rows(parts, multiple):
    have = sum(part.shape[0] for part in parts)
    if have % multiple:
        parts = parts + [jnp.zeros((multiple - have % multiple, 128), f32)]
    return jnp.concatenate(parts, axis=0) if len(parts) > 1 else parts[0]


def splat_kernel(
    shape, recv_ref, fields_ref, up_ref, down_ref, own_ref,
    points, left_ref, right_ref, hx_ref, near, beside, slope,
):
    gx, gy, gz = shape
    mx, my, mz = lax.axis_index("gx"), lax.axis_index("gy"), lax.axis_index("gz")
    step = pl.program_id(0)
    single = recv_ref.shape[1] * 4 == gx * gy * gz
    others = other_count(gy)
    bricks = 3 * (1 + others)
    tiles = recv_ref.shape[2] // 8
    lane_part = lax.broadcasted_iota(jnp.int32, (8, 128), 1) // 32
    span = 128 * GROUPS
    written = set()

    def add(ref, place, value):
        if single and place not in written:
            written.add(place)
            ref[place] = value
        else:
            ref[place] += value

    if not single:
        @pl.when(step == 0)
        def _():
            near[...] = jnp.zeros_like(near)
            beside[...] = jnp.zeros_like(beside)

    for t in range(tiles):
        for g in range(GROUPS):
            given = [recv_ref[q, g, 8 * t : 8 * t + 8, :] for q in range(4)]
            for k in range(4):
                if 4 * t + k >= bricks + -(-bricks // 4):
                    continue
                merged = None
                for q in range(4):
                    moved = given[q] if q == k else pltpu.roll(given[q], (32 * (q - k)) % 128, 1)
                    merged = moved if merged is None else jnp.where(lane_part == q, moved, merged)
                points[4 * t + k, g] = merged
    own_ref[0] = points[0]
    own_ref[1] = points[bricks]

    z_limit = jnp.where(mz == gz - 1, CZ, CZ + 1).astype(f32)
    z_row = row_iota(CZ).astype(bf16)
    own_row = row_iota(24) + float(8 - YO)
    point_lane = lax.broadcasted_iota(jnp.int32, (128, 128), 1)

    def multiply(begin, lists, b, e, high):
        counts = [-(-len(planes) * high // 16) * 16 for planes in lists]
        size = sum(counts)
        both = dot_nn(left_ref[begin : begin + 2 * size, :], right_ref[b, 0])
        got = both[:size] + both[size:]
        got = got + dot_nn(left_ref[begin : begin + size, :], right_ref[b, 1])
        at = 0
        for c in range(3):
            for i, plane in enumerate(lists[c]):
                value = got[at + i * high : at + i * high + high]
                if e == 0:
                    add(near, (c, plane), value)
                else:
                    add(beside, (e - 1, c, plane), value)
            at += counts[c]
        if single and e == 0:
            for t in sorted({plane // XPT for plane in lists[0]}):
                unfinished[t] -= 1
                if unfinished[t] == 0:
                    finish(t)

    row8 = lax.broadcasted_iota(jnp.int32, (8, 2 * 128), 0)
    zero = jnp.zeros((8, 2 * 128), f32)

    def finish(t):
        turned = []
        for c in range(3):
            pieces = []
            for plane in range(XPT * t, XPT * t + XPT):
                if plane > UPPER[-1]:
                    pieces.append(jnp.zeros((YS, 2 * 128), f32))
                    continue
                parts = [zero] + [near[c, plane, 8 * i : 8 * i + 8, :] for i in range(3)]
                if others:
                    if others == 1:
                        value = beside[0, c, plane]
                        low_part = jnp.where(my == 0, 0.0, value)
                        high_part = jnp.where(my == 0, value, 0.0)
                    else:
                        low_part, high_part = beside[0, c, plane], beside[1, c, plane]
                    moved = pltpu.roll(low_part, 4, 0)
                    parts[0] = jnp.where(row8 >= 4, moved, 0.0)
                    parts[1] = parts[1] + jnp.where(row8 < 4, moved, 0.0)
                    parts[3] = parts[3] + high_part
                pieces.extend(parts)
            stacked = jnp.concatenate(pieces, axis=0)
            turned.append(stacked[:, :CZ].T)
            above = stacked[:, CZ:]
            n, at = divmod(3 * t + c, 128 // GROUPS)
            if at:
                above = pltpu.roll(above, GROUPS * at, 1)
            if tops[n] is not None:
                above = jnp.where(point_lane // GROUPS == at, above, tops[n])
            tops[n] = above
        fields_ref[0, t, ZO : ZO + CZ, :] = turned[0]
        slope[t, ZO + 8 : ZO + 8 + CZ, :] = turned[1]
        fields_ref[1, t, ZO : ZO + CZ, :] = turned[2]

    def finish_all():
        zero = jnp.zeros((8, 128), f32)
        sums = [jnp.sum(top.T.reshape(-1, GROUPS, 128), axis=1, keepdims=True) for top in tops]
        for t in range(XTILES):
            at = [divmod(3 * t + c, 128 // GROUPS) for c in range(3)]
            above = [sums[n][i] for n, i in at]
            below = jnp.concatenate([above[1], jnp.zeros((7, 128), f32)], axis=0)
            slope[t, 0 : ZO + 8, :] = jnp.zeros((ZO + 8, 128), f32)
            slope[t, ZO + 8 + CZ : ZO + 16 + CZ, :] = below
            slope[t, ZO + 16 + CZ : ROWS + 16, :] = zero
            for c in range(2):
                fields_ref[c, t, 0:ZO, :] = zero
                fields_ref[c, t, ZO + CZ : ROWS, :] = jnp.concatenate(
                    [above[2 * c], jnp.zeros((7, 128), f32)], axis=0
                )
            fields_ref[0, t] += slope[t, 9 : ROWS + 9, :] - slope[t, 7 : ROWS + 7, :]

    tops = [None] * -(-3 * XTILES * GROUPS // 128)
    unfinished = [
        sum(
            plane // XPT == t and (i == 0 or planes[i - 1] // XPT != t)
            for planes in (CENTER, LOWER, UPPER)
            for i, plane in enumerate(planes)
        )
        for t in range(XTILES)
    ]
    row_at = 0
    waiting = None
    for e in reversed(range(1 + others)):
        if e == 0:
            y_limit = jnp.where(my == gy - 1, CY, CY + 1).astype(f32)
            y_row = own_row
        else:
            above = my == 0 if others == 1 else jnp.bool_(e == 2)
            y_limit = jnp.where(
                jnp.logical_and(above, my + 1 == gy - 1), CY, CY + 1
            ).astype(f32)
            first = jnp.where(above, WINDOW_HIGH - YO - CY, WINDOW_LOW - YO + CY)
            y_row = row_iota(8) + first.astype(f32)
        high = y_row.shape[0]
        for o, shift, planes in ((1, -1, LOWER), (2, 1, UPPER), (0, 0, CENTER)):
            b = e * 3 + o
            place, row = extra_place(b, bricks)
            x_limit = jnp.where(mx + shift == gx - 1, CX, CX + 1).astype(f32)
            cell_x = points[b, :, 7, :]
            off_x = points[b, :, 4, :]
            low_x = 1.0 - off_x
            high_x = jnp.where(cell_x + 1.0 < x_limit, off_x, 0.0)
            first_x = planes[0] - XO - CX * shift
            hats = [
                hat(float(first_x + n - 1), cell_x, low_x, high_x) for n in range(len(planes) + 2)
            ]
            for n in range(len(planes)):
                hx_ref[b, 0, n] = hats[n + 1]
                hx_ref[b, 1, n] = hats[n + 2] - hats[n]
            cell_z, off_z = points[place, :, row + 1, :], points[b, :, 6, :]
            top = jnp.where((cell_z + 1.0 == float(CZ)) & (cell_z + 1.0 < z_limit), off_z, 0.0)
            top_columns = jnp.concatenate([top, jnp.zeros((128 - GROUPS, 128), f32)], axis=0).T
            top_high = top_columns.astype(bf16).astype(f32)
            top_low = top_columns - top_high
            y_parts = []
            for g in range(GROUPS):
                main = points[b, g]
                more = points[place, g]
                cell_y, cell_z = more[row : row + 1], more[row + 1 : row + 2]
                off_y, off_z = main[5:6], main[6:7]
                at = slice(128 * g, 128 * g + 128)
                hz_high, hz_low = split_hat(z_row, cell_z, off_z)
                right_ref[b, 0, at, 0:CZ] = hz_high.T
                right_ref[b, 1, at, 0:CZ] = hz_low.T
                right_ref[b, 0, at, CZ : CZ + 128] = jnp.where(point_lane == g, top_high, 0.0).astype(bf16)
                right_ref[b, 1, at, CZ : CZ + 128] = jnp.where(point_lane == g, top_low, 0.0).astype(bf16)
                high_y = jnp.where(cell_y + 1.0 < y_limit, off_y, 0.0)
                hy = hat(y_row, cell_y, 1.0 - off_y, high_y)
                dy = hat_slope(y_row, cell_y, 1.0 - off_y, high_y)
                y_parts.append((main[0:1] * hy, main[1:2] * dy, main[2:3] * hy, main[3:4] * hy))
            size = 4 if e == 0 else 12
            for start in range(0, len(planes), size):
                block = planes[start : start + size]
                lists = [block] + 2 * [tuple(p for p in block if p in PLAIN[shift])]
                counts = [-(-len(each) * high // 16) * 16 for each in lists]
                for c in range(3):
                    begin = row_at + sum(counts[:c])
                    for g in range(GROUPS):
                        part_x0, part_y1, part_z, part_w = y_parts[g]
                        at = slice(128 * g, 128 * g + 128)
                        rows = []
                        for plane in lists[c]:
                            n = plane - planes[0]
                            hx = hx_ref[b, 0, n, g : g + 1, :]
                            if c == 0:
                                dx = hx_ref[b, 1, n, g : g + 1, :]
                                rows.append(dx * part_x0 + hx * part_y1)
                            else:
                                rows.append(hx * (part_z if c == 1 else part_w))
                        main_part, rest = split(stack_rows(rows, 16))
                        left_ref[begin : begin + counts[c], at] = main_part
                        after = begin + sum(counts)
                        left_ref[after : after + counts[c], at] = rest
                if waiting is not None:
                    waiting()
                waiting = functools.partial(multiply, row_at, lists, b, e, high)
                row_at += 2 * sum(counts)
    waiting()

    if not single:
        @pl.when(step == pl.num_programs(0) - 1)
        def _():
            for t in range(XTILES):
                finish(t)
            finish_all()
    else:
        finish_all()
    for c in range(2):
        up_ref[c] = fields_ref[c, :, UP_AT : UP_AT + HALO, :]
        down_ref[c] = fields_ref[c, :, DOWN_AT : DOWN_AT + HALO, :]


def chebyshev_factors():
    half_width = 6.0 / (6.0 + base_screen)
    sigma_ratio = 1.0 / half_width
    rho_prev = half_width
    factors = []
    for _ in range(ITERS - 1):
        rho_next = 1.0 / (2.0 * sigma_ratio - rho_prev)
        factors.append((rho_next * rho_prev, 2.0 * rho_next / half_width))
        rho_prev = rho_next
    return factors


READ_PLANES = range(XPT * FIRST_TILE, XPT * END_TILE)


def read_kernel(own_ref, out_ref, hx_ref):
    y_row = row_iota(24) + float(8 - YO)
    blank = jnp.zeros((8, 128), f32)
    for chunk in range(own_ref.shape[1] // GROUPS):
        span = slice(chunk * GROUPS, chunk * GROUPS + GROUPS)
        cell_x, off_x = own_ref[0, span, 7, :], own_ref[0, span, 4, :]
        for plane in READ_PLANES:
            if 0 <= plane - XO <= CX:
                hx_ref[plane] = hat(float(plane - XO), cell_x, 1.0 - off_x, off_x)
        for g in range(GROUPS):
            off_y = own_ref[0, chunk * GROUPS + g, 5:6, :]
            hy = hat(y_row, own_ref[1, chunk * GROUPS + g, 0:1, :], 1.0 - off_y, off_y)
            at = slice(128 * g, 128 * g + 128)
            for plane in READ_PLANES:
                start = YS * (plane - XPT * FIRST_TILE)
                if 0 <= plane - XO <= CX:
                    rows = jnp.concatenate([blank, hx_ref[plane, g : g + 1, :] * hy], axis=0)
                    high, low = split(rows)
                else:
                    high = jnp.zeros((YS, 128), bf16)
                    low = high
                out_ref[chunk, 0, start : start + YS, at] = high
                out_ref[chunk, 1, start : start + YS, at] = low


def solve_kernel(
    shape, fields_ref, from_low_ref, from_high_ref, own_ref, read_ref,
    indicator_ref, values_ref,
    given, low_halo, high_halo, owned, first, second, base, inverse, total,
    operand, arrivals,
):
    gx, gy, gz = shape
    mx, my, mz = lax.axis_index("gx"), lax.axis_index("gy"), lax.axis_index("gz")
    sources = (fields_ref, from_low_ref, from_high_ref, own_ref, read_ref.at[0])
    targets = (given, low_halo, high_halo, owned, operand)
    copies = [
        pltpu.make_async_copy(source, target, arrivals.at[i])
        for i, (source, target) in enumerate(zip(sources, targets))
    ]
    for copy in copies:
        copy.start()
    for copy in copies[:3]:
        copy.wait()
    low_at, high_at = UP_AT - CZ, DOWN_AT + CZ
    for c in range(2):
        given[c, :, low_at : low_at + HALO, :] += low_halo[c]
        given[c, :, high_at : high_at + HALO, :] += high_halo[c]

    lane = lax.broadcasted_iota(jnp.int32, (8, 128), 1)
    row = lax.broadcasted_iota(jnp.int32, (8, 128), 0)
    y = lane % YS - YO + my * CY
    inside_y = (y >= 0) & (y < gy * CY)
    zero = jnp.zeros((8, 128), f32)
    strips = ROWS // 8
    for t in range(XTILES):
        x = lane // YS + (XPT * t - XO) + mx * CX
        inside_xy = inside_y & (x >= 0) & (x < gx * CX)
        for scratch in (first, second):
            scratch[t, 0:8, :] = zero
            scratch[t, ROWS + 8 : ROWS + 16, :] = zero
        for i in range(strips):
            at = slice(8 * i, 8 * i + 8)
            inside = inside_xy
            if 8 * i < ZO or 8 * i + 8 > ZO + CZ:
                z = row + (8 * i - ZO) + mz * CZ
                inside = inside & (z >= 0) & (z < gz * CZ)
            diagonal = 6.0 + base_screen + point_screen * given[1, t, at, :]
            inv = jnp.where(inside, 1.0 / diagonal, 0.0)
            start = given[0, t, at, :] * inv
            inverse[t, at, :] = inv
            base[t, at, :] = start
            first[t, 8 * i + 8 : 8 * i + 16, :] = start

    now, later = first, second
    factors = chebyshev_factors()
    low_part, high_part = lane < YS, lane >= 128 - YS
    for k, (keep, gain) in enumerate(factors, 1):
        last = k == len(factors)
        begin, end = k // XPT, (XO + CX + REACH - k + XPT) // XPT
        if last:
            begin, end = max(begin, FIRST_TILE), min(end, END_TILE)
        for i in range(strips):
            at = slice(8 * i, 8 * i + 8)
            inner = slice(8 * i + 8, 8 * i + 16)
            reach = range(max(begin - 1, 0), min(end + 1, XTILES))
            here = {t: now[t, inner, :] for t in reach}
            ahead_x = {t: pltpu.roll(here[t], YS, 1) for t in reach if t < end}
            behind_x = {t: pltpu.roll(here[t], 128 - YS, 1) for t in reach if t >= begin}
            for t in range(begin, end):
                mine = here[t]
                near = now[t, 8 * i + 7 : 8 * i + 15, :] + now[t, 8 * i + 9 : 8 * i + 17, :]
                near = near + pltpu.roll(mine, 1, 1) + pltpu.roll(mine, 127, 1)
                before = ahead_x[t]
                if t > 0:
                    before = jnp.where(low_part, ahead_x[t - 1], before)
                after = behind_x[t]
                if t + 1 < XTILES:
                    after = jnp.where(high_part, behind_x[t + 1], after)
                near = near + before + after
                ahead = (1.0 + keep - gain) * mine + gain * (base[t, at, :] + inverse[t, at, :] * near)
                if k > 1:
                    ahead = ahead - keep * later[t, inner, :]
                if last:
                    total[t - FIRST_TILE, at, :] = ahead
                else:
                    later[t, inner, :] = ahead
        now, later = later, now

    parts = [split(total[t - FIRST_TILE]) for t in range(FIRST_TILE, END_TILE)]
    u_high = jnp.concatenate([part[0] for part in parts], axis=1)
    u_low = jnp.concatenate([part[1] for part in parts], axis=1)
    u_both = jnp.concatenate([u_high, u_low], axis=0)
    z_row = row_iota(ROWS) - float(ZO)
    for copy in copies[3:]:
        copy.wait()
    groups = owned.shape[1]
    for chunk in range(groups // GROUPS):
        if chunk > 0:
            copy = pltpu.make_async_copy(read_ref.at[chunk], operand, arrivals.at[4])
            copy.start()
            copy.wait()
        got = dot_nn(u_both, operand[0])
        got = got[:ROWS] + got[ROWS:] + dot_nn(u_high, operand[1])
        rows = []
        for g in range(GROUPS):
            main = owned[0, chunk * GROUPS + g]
            off_z = main[6:7]
            hz = hat(z_row, owned[1, chunk * GROUPS + g, 1:2, :], 1.0 - off_z, off_z)
            value = jnp.sum(hz * got[:, 128 * g : 128 * g + 128], axis=0, keepdims=True)
            rows.append(jnp.where(main[3:4] > 0.0, value, 0.0))
        values = jnp.concatenate(rows, axis=0)
        for q in range(4):
            moved = values if q == 0 else pltpu.roll(values, 128 - 32 * q, 1)
            start = q * groups + chunk * GROUPS
            values_ref[start : start + GROUPS, :] = moved[:, 0:32]

    for t in range(FIRST_TILE, END_TILE):
        turned = total[t - FIRST_TILE, ZO : ZO + CZ, :].T
        for i in range(XPT):
            plane = XPT * t + i - XO
            if 0 <= plane < CX:
                indicator_ref[plane] = turned[YS * i + YO : YS * i + YO + CY, :]


def on_device(shape, point_data, point_cells, send_counts):
    gx, gy, gz = shape
    sources = gx * gy * gz
    slots = point_data.shape[3]
    bricks = 3 * (1 + other_count(gy))
    rows = 8 * -(-(bricks + -(-bricks // 4)) // 4)
    groups = sources // 4
    whole = pl.BlockSpec(memory_space=pltpu.VMEM)

    outgoing = pl.pallas_call(
        functools.partial(pack_kernel, shape),
        out_shape=jax.ShapeDtypeStruct((sources, rows, 128), f32),
        in_specs=[whole, whole, whole],
        out_specs=whole,
        scratch_shapes=[
            pltpu.VMEM((4, sources, 8, 128), f32),
            pltpu.VMEM((bricks, sources, 8, 128), f32),
        ],
        compiler_params=pltpu.CompilerParams(vmem_limit_bytes=56 * MIB),
        name="pack_points",
    )(
        jnp.transpose(point_data, (0, 2, 1, 3)),
        jnp.transpose(point_cells, (0, 2, 1, 3)),
        send_counts,
    )

    arrived = lax.all_to_all(outgoing, AXES, split_axis=0, concat_axis=0, tiled=True)
    arrived = arrived.reshape(4, groups, rows, 128)

    others = other_count(gy)
    lines = 0
    for planes in (CENTER, LOWER, UPPER):
        for high, size in ((24, 4),) + ((8, 12),) * others:
            for start in range(0, len(planes), size):
                count = min(size, len(planes) - start)
                lines += 6 * 16 * -(-count * high // 16)
    edge_shape = jax.ShapeDtypeStruct((2, XTILES, HALO, 128), f32)
    steps = groups // GROUPS
    fields, up, down, own = pl.pallas_call(
        functools.partial(splat_kernel, shape),
        grid=(steps,),
        out_shape=(
            jax.ShapeDtypeStruct((2, XTILES, ROWS, 128), f32), edge_shape, edge_shape,
            jax.ShapeDtypeStruct((2, groups, 8, 128), f32),
        ),
        in_specs=[pl.BlockSpec((4, GROUPS, rows, 128), lambda s: (0, s, 0, 0))],
        out_specs=(
            pl.BlockSpec((2, XTILES, ROWS, 128), lambda s: (0, 0, 0, 0)),
            pl.BlockSpec((2, XTILES, HALO, 128), lambda s: (0, 0, 0, 0)),
            pl.BlockSpec((2, XTILES, HALO, 128), lambda s: (0, 0, 0, 0)),
            pl.BlockSpec((2, GROUPS, 8, 128), lambda s: (0, s, 0, 0)),
        ),
        scratch_shapes=[
            pltpu.VMEM((rows // 2, GROUPS, 8, 128), f32),
            pltpu.VMEM((lines, 128 * GROUPS), bf16),
            pltpu.VMEM((bricks, 2, 128 * GROUPS, 2 * 128), bf16),
            pltpu.VMEM((bricks, 2, len(CENTER), GROUPS, 128), f32),
            pltpu.VMEM((3, XPT * XTILES, 24, 2 * 128), f32),
            pltpu.VMEM((max(others, 1), 3, XPT * XTILES, 8, 2 * 128), f32),
            pltpu.VMEM((XTILES, ROWS + 16, 128), f32),
        ],
        compiler_params=pltpu.CompilerParams(vmem_limit_bytes=36 * MIB),
        name="splat_points",
    )(arrived)

    from_low = lax.ppermute(up, "gz", [(i, i + 1) for i in range(gz - 1)])
    from_high = lax.ppermute(down, "gz", [(i + 1, i) for i in range(gz - 1)])

    depth = 128 * (END_TILE - FIRST_TILE)
    read = pl.pallas_call(
        read_kernel,
        out_shape=jax.ShapeDtypeStruct((steps, 2, depth, 128 * GROUPS), bf16),
        in_specs=[whole],
        out_specs=whole,
        scratch_shapes=[pltpu.VMEM((XPT * END_TILE, GROUPS, 128), f32)],
        compiler_params=pltpu.CompilerParams(vmem_limit_bytes=16 * MIB),
        cost_estimate=pl.CostEstimate(
            flops=8 * depth * 128 * groups, bytes_accessed=4 * depth * 128 * groups, transcendentals=0
        ),
        name="read_operand",
    )(own)

    indicator, values = pl.pallas_call(
        functools.partial(solve_kernel, shape),
        out_shape=(
            jax.ShapeDtypeStruct((CX, CY, CZ), f32),
            jax.ShapeDtypeStruct((sources, slots), f32),
        ),
        in_specs=[pl.BlockSpec(memory_space=pl.ANY)] * 5,
        out_specs=(whole, whole),
        scratch_shapes=[
            pltpu.VMEM((2, XTILES, ROWS, 128), f32),
            pltpu.VMEM((2, XTILES, HALO, 128), f32),
            pltpu.VMEM((2, XTILES, HALO, 128), f32),
            pltpu.VMEM((2, groups, 8, 128), f32),
            pltpu.VMEM((XTILES, ROWS + 16, 128), f32),
            pltpu.VMEM((XTILES, ROWS + 16, 128), f32),
            pltpu.VMEM((XTILES, ROWS, 128), f32),
            pltpu.VMEM((XTILES, ROWS, 128), f32),
            pltpu.VMEM((END_TILE - FIRST_TILE, ROWS, 128), f32),
            pltpu.VMEM((2, depth, 128 * GROUPS), bf16),
            pltpu.SemaphoreType.DMA((5,)),
        ],
        compiler_params=pltpu.CompilerParams(vmem_limit_bytes=16 * MIB),
        name="solve_and_read",
    )(fields, from_low, from_high, own, read)

    returned = lax.all_to_all(
        values.reshape(1, sources, slots), AXES, split_axis=1, concat_axis=1, tiled=True
    )
    return indicator, returned


def solution(mesh):
    shape = tuple(mesh.shape[axis] for axis in AXES)
    in_specs = (
        P(AXES, None, None, None),
        P(AXES, None, None, None),
        P(AXES, None),
    )
    out_specs = (P("gx", "gy", "gz"), P(AXES, None, None))
    return jax.shard_map(
        functools.partial(on_device, shape),
        mesh=mesh,
        in_specs=in_specs,
        out_specs=out_specs,
        check_vma=False,
    )
```

```python
import functools

import jax
import jax.numpy as jnp
from jax import lax
from jax.experimental import pallas as pl
from jax.experimental.pallas import tpu as pltpu
from jax.sharding import PartitionSpec as P

CX = 16
CY = 16
CZ = 128
ITERS = 6

base_screen = 0.25
point_screen = 4.0

AXES = ("gx", "gy", "gz")
REACH = ITERS - 1
XO = REACH
YO = 9
ZO = 8
YS = 32
XPT = 128 // YS
XTILES = -(-(CX + 2 * REACH + 1) // XPT)
ROWS = CZ + 16
CENTER = tuple(range(XO - 1, XO + CX + 2))
LOWER = tuple(range(0, XO + 2))
UPPER = tuple(range(XO + CX - 1, XO + CX + REACH + 1))
PLAIN = {0: CENTER[1:-1], -1: LOWER[:-1], 1: UPPER[1:]}
FIRST_TILE, END_TILE = XO // XPT, (XO + CX) // XPT + 1
WINDOW_LOW = YO - REACH
WINDOW_HIGH = YO + CY - 1
UP_AT = ZO + CZ - REACH
DOWN_AT = ZO - 1
HALO = 8
GROUPS = 8
MIB = 1024 * 1024

f32 = jnp.float32
bf16 = jnp.bfloat16


def split(value):
    high = value.astype(bf16)
    return high, (value - high.astype(f32)).astype(bf16)


def dot_nt(lhs, rhs):
    return lax.dot_general(lhs, rhs, (((1,), (1,)), ((), ())), preferred_element_type=f32)


def dot_nn(lhs, rhs):
    return lax.dot_general(lhs, rhs, (((1,), (0,)), ((), ())), preferred_element_type=f32)


def other_count(gy):
    return min(gy - 1, 2)


def extra_place(brick, bricks):
    return bricks + brick // 4, 2 * (brick % 4)


def pack_kernel(
    shape, data_hbm, cells_hbm, counts_hbm, out_ref,
    data_ref, cells_ref, counts_ref, main, extra, arrivals,
):
    gx, gy, gz = shape
    copies = [
        pltpu.make_async_copy(source, target, arrivals.at[i])
        for i, (source, target) in enumerate(
            ((data_hbm, data_ref), (cells_hbm, cells_ref), (counts_hbm, counts_ref))
        )
    ]
    for copy in copies:
        copy.start()
    extra[...] = jnp.zeros_like(extra)
    for copy in copies:
        copy.wait()
    slots = data_ref.shape[3]
    sources = gx * gy * gz
    lane = lax.broadcasted_iota(jnp.int32, (sources, slots), 1)
    at_row = lax.broadcasted_iota(jnp.int32, (sources, sources), 0)
    at_lane = lax.broadcasted_iota(jnp.int32, (sources, sources), 1)
    counts = jnp.where(at_row == at_lane, counts_ref[...], 0).astype(f32)
    counts = jnp.sum(counts, axis=1, keepdims=True).astype(jnp.int32)
    others = other_count(gy)
    bricks = 3 * (1 + others)
    weight = jnp.where(lane < counts, data_ref[0, 3], 0.0)
    cells = [cells_ref[0, c].astype(f32) for c in range(3)]
    channels = [data_ref[0, c] * (-0.5 * weight) for c in range(3)]
    channels += [weight] + [data_ref[0, c] for c in range(4, 7)] + [cells[0]]

    def placed(value, part):
        pieces = [jnp.zeros((sources, slots * part), f32)] if part else []
        pieces.append(value)
        if part < 3:
            pieces.append(jnp.zeros((sources, 128 - slots * (part + 1)), f32))
        return jnp.concatenate(pieces, axis=1)

    for part in range(min(bricks, 4)):
        for c in range(8):
            main[part, :, c, :] = placed(channels[c], part)
    for b in range(bricks):
        place, row = extra_place(b, bricks)
        for c in range(2):
            extra[b, :, row + c, :] = placed(cells[1 + c], place % 4)
    for d in range(sources):
        x, y, z = d // (gy * gz), (d // gz) % gy, d % gz
        if others == 0:
            ys = (y,)
        elif others == 1:
            ys = (y, 1 - y)
        else:
            ys = (y, y - 1, y + 1)
        sums = [None] * (out_ref.shape[1] // 8)
        for e, by in enumerate(ys):
            for o, bx in enumerate((x, x - 1, x + 1)):
                if not (0 <= bx < gx and 0 <= by < gy):
                    continue
                b = e * 3 + o
                source = (bx * gy + by) * gz + z
                place, _ = extra_place(b, bricks)
                for tile, value in (
                    (b // 4, main[b % 4, source]), (place // 4, extra[b, source])
                ):
                    sums[tile] = value if sums[tile] is None else sums[tile] + value
        for tile, value in enumerate(sums):
            if value is None:
                value = jnp.zeros((8, 128), f32)
            out_ref[d, 8 * tile : 8 * tile + 8, :] = value


def hat(coordinate, cell, low, high):
    away = coordinate - cell
    return jnp.where(away == 0.0, low, jnp.where(away == 1.0, high, 0.0))


def hat_slope(coordinate, cell, low, high):
    away = coordinate - cell
    rising = jnp.where(away == -1.0, low, jnp.where(away == 0.0, high, 0.0))
    return rising - jnp.where(away == 1.0, low, jnp.where(away == 2.0, high, 0.0))


def split_hat(rows, cell, offset):
    spread = (16, 128)
    fill = rows.shape[0] // 16
    ends = []
    for value in (1.0 - offset, offset):
        ends.extend(split(jnp.broadcast_to(value, spread)))
    low_high, low_low, high_high, high_low = (jnp.concatenate([v] * fill, axis=0) for v in ends)
    cells = jnp.broadcast_to(cell, spread).astype(bf16)
    away = rows - jnp.concatenate([cells] * fill, axis=0)
    here, above = away == 0.0, away == 1.0
    zero = jnp.zeros(rows.shape, bf16)
    return (
        jnp.where(here, low_high, jnp.where(above, high_high, zero)),
        jnp.where(here, low_low, jnp.where(above, high_low, zero)),
    )


def row_iota(rows):
    return lax.broadcasted_iota(jnp.int32, (rows, 128), 0).astype(f32)


def stack_rows(parts, multiple):
    have = sum(part.shape[0] for part in parts)
    if have % multiple:
        parts = parts + [jnp.zeros((multiple - have % multiple, 128), f32)]
    return jnp.concatenate(parts, axis=0) if len(parts) > 1 else parts[0]


def splat_kernel(
    shape, recv_ref, fields_ref, up_ref, down_ref, own_ref,
    points, left_ref, right_ref, hx_ref, near, beside, slope,
):
    gx, gy, gz = shape
    mx, my, mz = lax.axis_index("gx"), lax.axis_index("gy"), lax.axis_index("gz")
    single = recv_ref.shape[1] * 4 == gx * gy * gz
    step = 0 if single else pl.program_id(0)
    others = other_count(gy)
    bricks = 3 * (1 + others)
    tiles = recv_ref.shape[2] // 8
    lane_part = lax.broadcasted_iota(jnp.int32, (8, 128), 1) // 32
    span = 128 * GROUPS
    written = set()

    def add(ref, place, value):
        if single and place not in written:
            written.add(place)
            ref[place] = value
        else:
            ref[place] += value

    if not single:
        @pl.when(step == 0)
        def _():
            near[...] = jnp.zeros_like(near)
            beside[...] = jnp.zeros_like(beside)

    for t in range(tiles):
        for g in range(GROUPS):
            given = [recv_ref[q, g, 8 * t : 8 * t + 8, :] for q in range(4)]
            for k in range(4):
                if 4 * t + k >= bricks + -(-bricks // 4):
                    continue
                merged = None
                for q in range(4):
                    moved = given[q] if q == k else pltpu.roll(given[q], (32 * (q - k)) % 128, 1)
                    merged = moved if merged is None else jnp.where(lane_part == q, moved, merged)
                points[4 * t + k, g] = merged
    own_ref[0] = points[0]
    own_ref[1] = points[bricks]

    z_limit = jnp.where(mz == gz - 1, CZ, CZ + 1).astype(f32)
    z_row = row_iota(CZ).astype(bf16)
    own_row = row_iota(24) + float(8 - YO)
    point_lane = lax.broadcasted_iota(jnp.int32, (128, 128), 1)

    def multiply(begin, lists, b, e, high):
        counts = [-(-len(planes) * high // 16) * 16 for planes in lists]
        size = sum(counts)
        both = dot_nn(left_ref[begin : begin + 2 * size, :], right_ref[b, 0])
        got = both[:size] + both[size:]
        got = got + dot_nn(left_ref[begin : begin + size, :], right_ref[b, 1])
        at = 0
        for c in range(3):
            for i, plane in enumerate(lists[c]):
                value = got[at + i * high : at + i * high + high]
                if e == 0:
                    add(near, (c, plane), value)
                else:
                    add(beside, (e - 1, c, plane), value)
            at += counts[c]
        if single and e == 0:
            for t in sorted({plane // XPT for plane in lists[0]}):
                unfinished[t] -= 1
                if unfinished[t] == 0:
                    finish(t)

    row8 = lax.broadcasted_iota(jnp.int32, (8, 2 * 128), 0)
    zero = jnp.zeros((8, 2 * 128), f32)

    def finish(t):
        turned = []
        for c in range(3):
            pieces = []
            for plane in range(XPT * t, XPT * t + XPT):
                if plane > UPPER[-1]:
                    pieces.append(jnp.zeros((YS, 2 * 128), f32))
                    continue
                parts = [zero] + [near[c, plane, 8 * i : 8 * i + 8, :] for i in range(3)]
                if others:
                    if others == 1:
                        value = beside[0, c, plane]
                        low_part = jnp.where(my == 0, 0.0, value)
                        high_part = jnp.where(my == 0, value, 0.0)
                    else:
                        low_part, high_part = beside[0, c, plane], beside[1, c, plane]
                    moved = pltpu.roll(low_part, 4, 0)
                    parts[0] = jnp.where(row8 >= 4, moved, 0.0)
                    parts[1] = parts[1] + jnp.where(row8 < 4, moved, 0.0)
                    parts[3] = parts[3] + high_part
                pieces.extend(parts)
            stacked = jnp.concatenate(pieces, axis=0)
            turned.append(stacked[:, :CZ].T)
            above = stacked[:, CZ:]
            n, at = divmod(3 * t + c, 128 // GROUPS)
            if at:
                above = pltpu.roll(above, GROUPS * at, 1)
            if tops[n] is not None:
                above = jnp.where(point_lane // GROUPS == at, above, tops[n])
            tops[n] = above
        fields_ref[0, t, ZO : ZO + CZ, :] = turned[0]
        slope[t, ZO + 8 : ZO + 8 + CZ, :] = turned[1]
        fields_ref[1, t, ZO : ZO + CZ, :] = turned[2]

    def finish_all():
        zero = jnp.zeros((8, 128), f32)
        sums = [jnp.sum(top.T.reshape(-1, GROUPS, 128), axis=1, keepdims=True) for top in tops]
        for t in range(XTILES):
            at = [divmod(3 * t + c, 128 // GROUPS) for c in range(3)]
            above = [sums[n][i] for n, i in at]
            below = jnp.concatenate([above[1], jnp.zeros((7, 128), f32)], axis=0)
            slope[t, 0 : ZO + 8, :] = jnp.zeros((ZO + 8, 128), f32)
            slope[t, ZO + 8 + CZ : ZO + 16 + CZ, :] = below
            slope[t, ZO + 16 + CZ : ROWS + 16, :] = zero
            for c in range(2):
                fields_ref[c, t, 0:ZO, :] = zero
                fields_ref[c, t, ZO + CZ : ROWS, :] = jnp.concatenate(
                    [above[2 * c], jnp.zeros((7, 128), f32)], axis=0
                )
            fields_ref[0, t] += slope[t, 9 : ROWS + 9, :] - slope[t, 7 : ROWS + 7, :]

    tops = [None] * -(-3 * XTILES * GROUPS // 128)
    unfinished = [
        sum(
            plane // XPT == t and (i == 0 or planes[i - 1] // XPT != t)
            for planes in (CENTER, LOWER, UPPER)
            for i, plane in enumerate(planes)
        )
        for t in range(XTILES)
    ]
    row_at = 0
    waiting = None
    for e in reversed(range(1 + others)):
        if e == 0:
            y_limit = jnp.where(my == gy - 1, CY, CY + 1).astype(f32)
            y_row = own_row
        else:
            above = my == 0 if others == 1 else jnp.bool_(e == 2)
            y_limit = jnp.where(
                jnp.logical_and(above, my + 1 == gy - 1), CY, CY + 1
            ).astype(f32)
            first = jnp.where(above, WINDOW_HIGH - YO - CY, WINDOW_LOW - YO + CY)
            y_row = row_iota(8) + first.astype(f32)
        high = y_row.shape[0]
        for o, shift, planes in ((1, -1, LOWER), (2, 1, UPPER), (0, 0, CENTER)):
            b = e * 3 + o
            place, row = extra_place(b, bricks)
            x_limit = jnp.where(mx + shift == gx - 1, CX, CX + 1).astype(f32)
            cell_x = points[b, :, 7, :]
            off_x = points[b, :, 4, :]
            low_x = 1.0 - off_x
            high_x = jnp.where(cell_x + 1.0 < x_limit, off_x, 0.0)
            first_x = planes[0] - XO - CX * shift
            hats = [
                hat(float(first_x + n - 1), cell_x, low_x, high_x) for n in range(len(planes) + 2)
            ]
            for n in range(len(planes)):
                hx_ref[b, 0, n] = hats[n + 1]
                hx_ref[b, 1, n] = hats[n + 2] - hats[n]
            cell_z, off_z = points[place, :, row + 1, :], points[b, :, 6, :]
            top = jnp.where((cell_z + 1.0 == float(CZ)) & (cell_z + 1.0 < z_limit), off_z, 0.0)
            top_columns = jnp.concatenate([top, jnp.zeros((128 - GROUPS, 128), f32)], axis=0).T
            top_high = top_columns.astype(bf16).astype(f32)
            top_low = top_columns - top_high
            y_parts = []
            for g in range(GROUPS):
                main = points[b, g]
                more = points[place, g]
                cell_y, cell_z = more[row : row + 1], more[row + 1 : row + 2]
                off_y, off_z = main[5:6], main[6:7]
                at = slice(128 * g, 128 * g + 128)
                hz_high, hz_low = split_hat(z_row, cell_z, off_z)
                right_ref[b, 0, at, 0:CZ] = hz_high.T
                right_ref[b, 1, at, 0:CZ] = hz_low.T
                right_ref[b, 0, at, CZ : CZ + 128] = jnp.where(point_lane == g, top_high, 0.0).astype(bf16)
                right_ref[b, 1, at, CZ : CZ + 128] = jnp.where(point_lane == g, top_low, 0.0).astype(bf16)
                high_y = jnp.where(cell_y + 1.0 < y_limit, off_y, 0.0)
                hy = hat(y_row, cell_y, 1.0 - off_y, high_y)
                dy = hat_slope(y_row, cell_y, 1.0 - off_y, high_y)
                y_parts.append((main[0:1] * hy, main[1:2] * dy, main[2:3] * hy, main[3:4] * hy))
            size = 4 if e == 0 else 12
            for start in range(0, len(planes), size):
                block = planes[start : start + size]
                lists = [block] + 2 * [tuple(p for p in block if p in PLAIN[shift])]
                counts = [-(-len(each) * high // 16) * 16 for each in lists]
                for c in range(3):
                    begin = row_at + sum(counts[:c])
                    for g in range(GROUPS):
                        part_x0, part_y1, part_z, part_w = y_parts[g]
                        at = slice(128 * g, 128 * g + 128)
                        rows = []
                        for plane in lists[c]:
                            n = plane - planes[0]
                            hx = hx_ref[b, 0, n, g : g + 1, :]
                            if c == 0:
                                dx = hx_ref[b, 1, n, g : g + 1, :]
                                rows.append(dx * part_x0 + hx * part_y1)
                            else:
                                rows.append(hx * (part_z if c == 1 else part_w))
                        main_part, rest = split(stack_rows(rows, 16))
                        left_ref[begin : begin + counts[c], at] = main_part
                        after = begin + sum(counts)
                        left_ref[after : after + counts[c], at] = rest
                if waiting is not None:
                    waiting()
                waiting = functools.partial(multiply, row_at, lists, b, e, high)
                row_at += 2 * sum(counts)
    waiting()

    if not single:
        @pl.when(step == pl.num_programs(0) - 1)
        def _():
            for t in range(XTILES):
                finish(t)
            finish_all()
    else:
        finish_all()
    for c in range(2):
        up_ref[c] = fields_ref[c, :, UP_AT : UP_AT + HALO, :]
        down_ref[c] = fields_ref[c, :, DOWN_AT : DOWN_AT + HALO, :]


def chebyshev_factors():
    half_width = 6.0 / (6.0 + base_screen)
    sigma_ratio = 1.0 / half_width
    rho_prev = half_width
    factors = []
    for _ in range(ITERS - 1):
        rho_next = 1.0 / (2.0 * sigma_ratio - rho_prev)
        factors.append((rho_next * rho_prev, 2.0 * rho_next / half_width))
        rho_prev = rho_next
    return factors


READ_PLANES = range(XPT * FIRST_TILE, XPT * END_TILE)


def read_kernel(own_ref, out_ref, hx_ref):
    y_row = row_iota(24) + float(8 - YO)
    blank = jnp.zeros((8, 128), f32)
    for chunk in range(own_ref.shape[1] // GROUPS):
        span = slice(chunk * GROUPS, chunk * GROUPS + GROUPS)
        cell_x, off_x = own_ref[0, span, 7, :], own_ref[0, span, 4, :]
        for plane in READ_PLANES:
            if 0 <= plane - XO <= CX:
                hx_ref[plane] = hat(float(plane - XO), cell_x, 1.0 - off_x, off_x)
        for g in range(GROUPS):
            off_y = own_ref[0, chunk * GROUPS + g, 5:6, :]
            hy = hat(y_row, own_ref[1, chunk * GROUPS + g, 0:1, :], 1.0 - off_y, off_y)
            at = slice(128 * g, 128 * g + 128)
            for plane in READ_PLANES:
                start = YS * (plane - XPT * FIRST_TILE)
                if 0 <= plane - XO <= CX:
                    rows = jnp.concatenate([blank, hx_ref[plane, g : g + 1, :] * hy], axis=0)
                    high, low = split(rows)
                else:
                    high = jnp.zeros((YS, 128), bf16)
                    low = high
                out_ref[chunk, 0, start : start + YS, at] = high
                out_ref[chunk, 1, start : start + YS, at] = low


def solve_kernel(
    shape, fields_ref, from_low_ref, from_high_ref, own_ref, read_ref,
    indicator_ref, values_ref,
    edge, first, second, base, inverse, total, operand, arrivals,
):
    gx, gy, gz = shape
    mx, my, mz = lax.axis_index("gx"), lax.axis_index("gy"), lax.axis_index("gz")
    copy = pltpu.make_async_copy(read_ref.at[0], operand, arrivals)
    copy.start()
    edge[...] = jnp.zeros_like(edge)
    low_at, high_at = UP_AT - CZ, DOWN_AT + CZ - (ROWS - 16)
    edge[0, :, :, low_at : low_at + HALO, :] = from_low_ref[...]
    edge[1, :, :, high_at : high_at + HALO, :] = from_high_ref[...]

    def given(c, t, i):
        value = fields_ref[c, t, 8 * i : 8 * i + 8, :]
        if i < 2:
            value = value + edge[0, c, t, 8 * i : 8 * i + 8, :]
        from_end = i - (ROWS // 8 - 2)
        if from_end >= 0:
            value = value + edge[1, c, t, 8 * from_end : 8 * from_end + 8, :]
        return value

    lane = lax.broadcasted_iota(jnp.int32, (8, 128), 1)
    row = lax.broadcasted_iota(jnp.int32, (8, 128), 0)
    y = lane % YS - YO + my * CY
    inside_y = (y >= 0) & (y < gy * CY)
    zero = jnp.zeros((8, 128), f32)
    strips = ROWS // 8
    for t in range(XTILES):
        x = lane // YS + (XPT * t - XO) + mx * CX
        inside_xy = inside_y & (x >= 0) & (x < gx * CX)
        for scratch in (first, second):
            scratch[t, 0:8, :] = zero
            scratch[t, ROWS + 8 : ROWS + 16, :] = zero
        for i in range(strips):
            at = slice(8 * i, 8 * i + 8)
            inside = inside_xy
            if 8 * i < ZO or 8 * i + 8 > ZO + CZ:
                z = row + (8 * i - ZO) + mz * CZ
                inside = inside & (z >= 0) & (z < gz * CZ)
            diagonal = 6.0 + base_screen + point_screen * given(1, t, i)
            inv = jnp.where(inside, 1.0 / diagonal, 0.0)
            start = given(0, t, i) * inv
            inverse[t, at, :] = inv
            base[t, at, :] = start
            first[t, 8 * i + 8 : 8 * i + 16, :] = start

    now, later = first, second
    factors = chebyshev_factors()
    low_part, high_part = lane < YS, lane >= 128 - YS
    for k, (keep, gain) in enumerate(factors, 1):
        last = k == len(factors)
        begin, end = k // XPT, (XO + CX + REACH - k + XPT) // XPT
        if last:
            begin, end = max(begin, FIRST_TILE), min(end, END_TILE)
        for i in range(strips):
            at = slice(8 * i, 8 * i + 8)
            inner = slice(8 * i + 8, 8 * i + 16)
            reach = range(max(begin - 1, 0), min(end + 1, XTILES))
            here = {t: now[t, inner, :] for t in reach}
            ahead_x = {t: pltpu.roll(here[t], YS, 1) for t in reach if t < end}
            behind_x = {t: pltpu.roll(here[t], 128 - YS, 1) for t in reach if t >= begin}
            for t in range(begin, end):
                mine = here[t]
                near = now[t, 8 * i + 7 : 8 * i + 15, :] + now[t, 8 * i + 9 : 8 * i + 17, :]
                near = near + pltpu.roll(mine, 1, 1) + pltpu.roll(mine, 127, 1)
                before = ahead_x[t]
                if t > 0:
                    before = jnp.where(low_part, ahead_x[t - 1], before)
                after = behind_x[t]
                if t + 1 < XTILES:
                    after = jnp.where(high_part, behind_x[t + 1], after)
                near = near + before + after
                ahead = (1.0 + keep - gain) * mine + gain * (base[t, at, :] + inverse[t, at, :] * near)
                if k > 1:
                    ahead = ahead - keep * later[t, inner, :]
                if last:
                    total[t - FIRST_TILE, at, :] = ahead
                else:
                    later[t, inner, :] = ahead
        now, later = later, now

    parts = [split(total[t - FIRST_TILE]) for t in range(FIRST_TILE, END_TILE)]
    u_high = jnp.concatenate([part[0] for part in parts], axis=1)
    u_low = jnp.concatenate([part[1] for part in parts], axis=1)
    u_both = jnp.concatenate([u_high, u_low], axis=0)
    z_row = row_iota(ROWS) - float(ZO)
    copy.wait()
    groups = own_ref.shape[1]
    for chunk in range(groups // GROUPS):
        if chunk > 0:
            copy = pltpu.make_async_copy(read_ref.at[chunk], operand, arrivals)
            copy.start()
            copy.wait()
        got = dot_nn(u_both, operand[0])
        got = got[:ROWS] + got[ROWS:] + dot_nn(u_high, operand[1])
        rows = []
        for g in range(GROUPS):
            main = own_ref[0, chunk * GROUPS + g]
            off_z = main[6:7]
            hz = hat(z_row, own_ref[1, chunk * GROUPS + g, 1:2, :], 1.0 - off_z, off_z)
            value = jnp.sum(hz * got[:, 128 * g : 128 * g + 128], axis=0, keepdims=True)
            rows.append(jnp.where(main[3:4] > 0.0, value, 0.0))
        values = jnp.concatenate(rows, axis=0)
        for q in range(4):
            moved = values if q == 0 else pltpu.roll(values, 128 - 32 * q, 1)
            start = q * groups + chunk * GROUPS
            values_ref[start : start + GROUPS, :] = moved[:, 0:32]

    for t in range(FIRST_TILE, END_TILE):
        turned = total[t - FIRST_TILE, ZO : ZO + CZ, :].T
        for i in range(XPT):
            plane = XPT * t + i - XO
            if 0 <= plane < CX:
                indicator_ref[plane] = turned[YS * i + YO : YS * i + YO + CY, :]


def on_device(shape, point_data, point_cells, send_counts):
    gx, gy, gz = shape
    sources = gx * gy * gz
    slots = point_data.shape[3]
    bricks = 3 * (1 + other_count(gy))
    rows = 8 * -(-(bricks + -(-bricks // 4)) // 4)
    groups = sources // 4
    whole = pl.BlockSpec(memory_space=pltpu.VMEM)

    outgoing = pl.pallas_call(
        functools.partial(pack_kernel, shape),
        out_shape=jax.ShapeDtypeStruct((sources, rows, 128), f32),
        in_specs=[pl.BlockSpec(memory_space=pl.ANY)] * 3,
        out_specs=whole,
        scratch_shapes=[
            pltpu.VMEM((1, point_data.shape[2], sources, slots), f32),
            pltpu.VMEM((1, point_cells.shape[2], sources, slots), jnp.int32),
            pltpu.VMEM((1, sources), jnp.int32),
            pltpu.VMEM((4, sources, 8, 128), f32),
            pltpu.VMEM((bricks, sources, 8, 128), f32),
            pltpu.SemaphoreType.DMA((3,)),
        ],
        compiler_params=pltpu.CompilerParams(vmem_limit_bytes=56 * MIB),
        name="pack_points",
    )(
        jnp.transpose(point_data, (0, 2, 1, 3)),
        jnp.transpose(point_cells, (0, 2, 1, 3)),
        send_counts,
    )

    arrived = lax.all_to_all(outgoing, AXES, split_axis=0, concat_axis=0, tiled=True)
    arrived = arrived.reshape(4, groups, rows, 128)

    others = other_count(gy)
    lines = 0
    for planes in (CENTER, LOWER, UPPER):
        for high, size in ((24, 4),) + ((8, 12),) * others:
            for start in range(0, len(planes), size):
                count = min(size, len(planes) - start)
                lines += 6 * 16 * -(-count * high // 16)
    edge_shape = jax.ShapeDtypeStruct((2, XTILES, HALO, 128), f32)
    steps = groups // GROUPS
    if steps == 1:
        blocks = {"in_specs": [whole], "out_specs": (whole,) * 4}
    else:
        blocks = {
            "grid": (steps,),
            "in_specs": [pl.BlockSpec((4, GROUPS, rows, 128), lambda s: (0, s, 0, 0))],
            "out_specs": (
                pl.BlockSpec((2, XTILES, ROWS, 128), lambda s: (0, 0, 0, 0)),
                pl.BlockSpec((2, XTILES, HALO, 128), lambda s: (0, 0, 0, 0)),
                pl.BlockSpec((2, XTILES, HALO, 128), lambda s: (0, 0, 0, 0)),
                pl.BlockSpec((2, GROUPS, 8, 128), lambda s: (0, s, 0, 0)),
            ),
        }
    fields, up, down, own = pl.pallas_call(
        functools.partial(splat_kernel, shape),
        out_shape=(
            jax.ShapeDtypeStruct((2, XTILES, ROWS, 128), f32), edge_shape, edge_shape,
            jax.ShapeDtypeStruct((2, groups, 8, 128), f32),
        ),
        **blocks,
        scratch_shapes=[
            pltpu.VMEM((rows // 2, GROUPS, 8, 128), f32),
            pltpu.VMEM((lines, 128 * GROUPS), bf16),
            pltpu.VMEM((bricks, 2, 128 * GROUPS, 2 * 128), bf16),
            pltpu.VMEM((bricks, 2, len(CENTER), GROUPS, 128), f32),
            pltpu.VMEM((3, XPT * XTILES, 24, 2 * 128), f32),
            pltpu.VMEM((max(others, 1), 3, XPT * XTILES, 8, 2 * 128), f32),
            pltpu.VMEM((XTILES, ROWS + 16, 128), f32),
        ],
        compiler_params=pltpu.CompilerParams(vmem_limit_bytes=36 * MIB),
        name="splat_points",
    )(arrived)

    from_low = lax.ppermute(up, "gz", [(i, i + 1) for i in range(gz - 1)])
    from_high = lax.ppermute(down, "gz", [(i + 1, i) for i in range(gz - 1)])

    depth = 128 * (END_TILE - FIRST_TILE)
    read = pl.pallas_call(
        read_kernel,
        out_shape=jax.ShapeDtypeStruct((steps, 2, depth, 128 * GROUPS), bf16),
        in_specs=[whole],
        out_specs=whole,
        scratch_shapes=[pltpu.VMEM((XPT * END_TILE, GROUPS, 128), f32)],
        compiler_params=pltpu.CompilerParams(vmem_limit_bytes=16 * MIB),
        cost_estimate=pl.CostEstimate(
            flops=8 * depth * 128 * groups, bytes_accessed=4 * depth * 128 * groups, transcendentals=0
        ),
        name="read_operand",
    )(own)

    indicator, values = pl.pallas_call(
        functools.partial(solve_kernel, shape),
        out_shape=(
            jax.ShapeDtypeStruct((CX, CY, CZ), f32),
            jax.ShapeDtypeStruct((sources, slots), f32),
        ),
        in_specs=[whole] * 4 + [pl.BlockSpec(memory_space=pl.ANY)],
        out_specs=(whole, whole),
        scratch_shapes=[
            pltpu.VMEM((2, 2, XTILES, 16, 128), f32),
            pltpu.VMEM((XTILES, ROWS + 16, 128), f32),
            pltpu.VMEM((XTILES, ROWS + 16, 128), f32),
            pltpu.VMEM((XTILES, ROWS, 128), f32),
            pltpu.VMEM((XTILES, ROWS, 128), f32),
            pltpu.VMEM((END_TILE - FIRST_TILE, ROWS, 128), f32),
            pltpu.VMEM((2, depth, 128 * GROUPS), bf16),
            pltpu.SemaphoreType.DMA,
        ],
        compiler_params=pltpu.CompilerParams(vmem_limit_bytes=16 * MIB),
        name="solve_and_read",
    )(fields, from_low, from_high, own, read)

    returned = lax.all_to_all(
        values.reshape(1, sources, slots), AXES, split_axis=1, concat_axis=1, tiled=True
    )
    return indicator, returned


def solution(mesh):
    shape = tuple(mesh.shape[axis] for axis in AXES)
    in_specs = (
        P(AXES, None, None, None),
        P(AXES, None, None, None),
        P(AXES, None),
    )
    out_specs = (P("gx", "gy", "gz"), P(AXES, None, None))
    return jax.shard_map(
        functools.partial(on_device, shape),
        mesh=mesh,
        in_specs=in_specs,
        out_specs=out_specs,
        check_vma=False,
    )
```

```python
import functools

import jax
import jax.numpy as jnp
from jax import lax
from jax.experimental import pallas as pl
from jax.experimental.pallas import tpu as pltpu
from jax.sharding import PartitionSpec as P

CX = 16
CY = 16
CZ = 128
ITERS = 6

base_screen = 0.25
point_screen = 4.0

AXES = ("gx", "gy", "gz")
REACH = ITERS - 1
XO = REACH
YO = 9
ZO = 8
YS = 32
XPT = 128 // YS
XTILES = -(-(CX + 2 * REACH + 1) // XPT)
ROWS = CZ + 16
CENTER = tuple(range(XO - 1, XO + CX + 2))
LOWER = tuple(range(0, XO + 2))
UPPER = tuple(range(XO + CX - 1, XO + CX + REACH + 1))
PLAIN = {0: CENTER[1:-1], -1: LOWER[:-1], 1: UPPER[1:]}
FIRST_TILE, END_TILE = XO // XPT, (XO + CX) // XPT + 1
WINDOW_LOW = YO - REACH
WINDOW_HIGH = YO + CY - 1
UP_AT = ZO + CZ - REACH
DOWN_AT = ZO - 1
HALO = 8
GROUPS = 8
MIB = 1024 * 1024

f32 = jnp.float32
bf16 = jnp.bfloat16


def split(value):
    high = value.astype(bf16)
    return high, (value - high.astype(f32)).astype(bf16)


def dot_nt(lhs, rhs):
    return lax.dot_general(lhs, rhs, (((1,), (1,)), ((), ())), preferred_element_type=f32)


def dot_nn(lhs, rhs):
    return lax.dot_general(lhs, rhs, (((1,), (0,)), ((), ())), preferred_element_type=f32)


def other_count(gy):
    return min(gy - 1, 2)


def extra_place(brick, bricks):
    return bricks + brick // 4, 2 * (brick % 4)


def pack_kernel(shape, data_ref, cells_ref, counts_ref, out_ref):
    gx, gy, gz = shape
    slots = data_ref.shape[3]
    sources = gx * gy * gz
    lane = lax.broadcasted_iota(jnp.int32, (sources, slots), 1)
    at_row = lax.broadcasted_iota(jnp.int32, (sources, sources), 0)
    at_lane = lax.broadcasted_iota(jnp.int32, (sources, sources), 1)
    counts = jnp.where(at_row == at_lane, counts_ref[...], 0).astype(f32)
    counts = jnp.sum(counts, axis=1, keepdims=True).astype(jnp.int32)
    others = other_count(gy)
    bricks = 3 * (1 + others)
    weight = jnp.where(lane < counts, data_ref[0, 3], 0.0)
    cells = [cells_ref[0, c].astype(f32) for c in range(3)]
    channels = [data_ref[0, c] * (-0.5 * weight) for c in range(3)]
    channels += [weight] + [data_ref[0, c] for c in range(4, 7)] + cells
    blank = jnp.zeros((sources, 128 - slots), f32)
    channels = [jnp.concatenate([value, blank], axis=1) for value in channels]
    row = lax.broadcasted_iota(jnp.int32, (sources, 128), 0)
    y = (row // gz) % gy

    def moved(value, by):
        if by == 0:
            return value
        gap = jnp.zeros((abs(by), 128), f32)
        if by > 0:
            return jnp.concatenate([value[by:], gap], axis=0)
        return jnp.concatenate([gap, value[:by]], axis=0)

    def beside(value, e):
        if e == 0:
            return value
        up = jnp.where(y < gy - 1, moved(value, gz), 0.0)
        down = jnp.where(y > 0, moved(value, -gz), 0.0)
        if others == 1:
            return up + down
        return down if e == 1 else up

    by_y = [[beside(value, e) for e in range(1 + others)] for value in channels]
    lines = {}
    for b in range(bricks):
        e, o = divmod(b, 3)
        place, extra_row = extra_place(b, bricks)
        for c in range(10):
            block, line = (b, c) if c < 8 else (place, extra_row + c - 8)
            value = moved(by_y[c][e], (0, -gy * gz, gy * gz)[o])
            if block % 4:
                value = pltpu.roll(value, slots * (block % 4), 1)
            key = 8 * (block // 4) + line
            lines[key] = value if key not in lines else lines[key] + value
    for line in range(out_ref.shape[1]):
        value = lines.get(line)
        out_ref[:, line, :] = jnp.zeros((sources, 128), f32) if value is None else value


def hat(coordinate, cell, low, high):
    away = coordinate - cell
    return jnp.where(away == 0.0, low, jnp.where(away == 1.0, high, 0.0))


def hat_slope(coordinate, cell, low, high):
    away = coordinate - cell
    rising = jnp.where(away == -1.0, low, jnp.where(away == 0.0, high, 0.0))
    return rising - jnp.where(away == 1.0, low, jnp.where(away == 2.0, high, 0.0))


def split_hat(rows, cell, offset):
    spread = (16, 128)
    fill = rows.shape[0] // 16
    ends = []
    for value in (1.0 - offset, offset):
        ends.extend(split(jnp.broadcast_to(value, spread)))
    low_high, low_low, high_high, high_low = (jnp.concatenate([v] * fill, axis=0) for v in ends)
    cells = jnp.broadcast_to(cell, spread).astype(bf16)
    away = rows - jnp.concatenate([cells] * fill, axis=0)
    here, above = away == 0.0, away == 1.0
    zero = jnp.zeros(rows.shape, bf16)
    return (
        jnp.where(here, low_high, jnp.where(above, high_high, zero)),
        jnp.where(here, low_low, jnp.where(above, high_low, zero)),
    )


def row_iota(rows):
    return lax.broadcasted_iota(jnp.int32, (rows, 128), 0).astype(f32)


def stack_rows(parts, multiple):
    have = sum(part.shape[0] for part in parts)
    if have % multiple:
        parts = parts + [jnp.zeros((multiple - have % multiple, 128), f32)]
    return jnp.concatenate(parts, axis=0) if len(parts) > 1 else parts[0]


def splat_kernel(
    shape, recv_ref, fields_ref, edges_ref, own_ref,
    points, left_ref, right_ref, hx_ref, near, beside, slope,
):
    gx, gy, gz = shape
    mx, my, mz = lax.axis_index("gx"), lax.axis_index("gy"), lax.axis_index("gz")
    single = recv_ref.shape[1] * 4 == gx * gy * gz
    step = 0 if single else pl.program_id(0)
    others = other_count(gy)
    bricks = 3 * (1 + others)
    tiles = recv_ref.shape[2] // 8
    lane_part = lax.broadcasted_iota(jnp.int32, (8, 128), 1) // 32
    span = 128 * GROUPS
    written = set()

    def add(ref, place, value):
        if single and place not in written:
            written.add(place)
            ref[place] = value
        else:
            ref[place] += value

    if not single:
        @pl.when(step == 0)
        def _():
            near[...] = jnp.zeros_like(near)
            beside[...] = jnp.zeros_like(beside)

    for t in range(tiles):
        for g in range(GROUPS):
            given = [recv_ref[q, g, 8 * t : 8 * t + 8, :] for q in range(4)]
            for k in range(4):
                if 4 * t + k >= bricks + -(-bricks // 4):
                    continue
                merged = None
                for q in range(4):
                    moved = given[q] if q == k else pltpu.roll(given[q], (32 * (q - k)) % 128, 1)
                    merged = moved if merged is None else jnp.where(lane_part == q, moved, merged)
                points[4 * t + k, g] = merged
    own_ref[0] = points[0]
    own_ref[1] = points[bricks]

    z_limit = jnp.where(mz == gz - 1, CZ, CZ + 1).astype(f32)
    z_row = row_iota(CZ).astype(bf16)
    own_row = row_iota(24) + float(8 - YO)
    point_lane = lax.broadcasted_iota(jnp.int32, (128, 128), 1)

    def multiply(begin, lists, b, e, high):
        counts = [-(-len(planes) * high // 16) * 16 for planes in lists]
        size = sum(counts)
        both = dot_nn(left_ref[begin : begin + 2 * size, :], right_ref[b, 0])
        got = both[:size] + both[size:]
        got = got + dot_nn(left_ref[begin : begin + size, :], right_ref[b, 1])
        at = 0
        for c in range(3):
            for i, plane in enumerate(lists[c]):
                value = got[at + i * high : at + i * high + high]
                if e == 0:
                    add(near, (c, plane), value)
                else:
                    add(beside, (e - 1, c, plane), value)
            at += counts[c]
        if single and e == 0:
            for t in sorted({plane // XPT for plane in lists[0]}):
                unfinished[t] -= 1
                if unfinished[t] == 0:
                    finish(t)

    row8 = lax.broadcasted_iota(jnp.int32, (8, 2 * 128), 0)
    zero = jnp.zeros((8, 2 * 128), f32)

    def finish(t):
        turned = []
        for c in range(3):
            pieces = []
            for plane in range(XPT * t, XPT * t + XPT):
                if plane > UPPER[-1]:
                    pieces.append(jnp.zeros((YS, 2 * 128), f32))
                    continue
                parts = [zero] + [near[c, plane, 8 * i : 8 * i + 8, :] for i in range(3)]
                if others:
                    if others == 1:
                        value = beside[0, c, plane]
                        low_part = jnp.where(my == 0, 0.0, value)
                        high_part = jnp.where(my == 0, value, 0.0)
                    else:
                        low_part, high_part = beside[0, c, plane], beside[1, c, plane]
                    moved = pltpu.roll(low_part, 4, 0)
                    parts[0] = jnp.where(row8 >= 4, moved, 0.0)
                    parts[1] = parts[1] + jnp.where(row8 < 4, moved, 0.0)
                    parts[3] = parts[3] + high_part
                pieces.extend(parts)
            stacked = jnp.concatenate(pieces, axis=0)
            turned.append(stacked[:, :CZ].T)
            above = stacked[:, CZ:]
            n, at = divmod(3 * t + c, 128 // GROUPS)
            if at:
                above = pltpu.roll(above, GROUPS * at, 1)
            if tops[n] is not None:
                above = jnp.where(point_lane // GROUPS == at, above, tops[n])
            tops[n] = above
        fields_ref[0, t, ZO : ZO + CZ, :] = turned[0]
        slope[t, ZO + 8 : ZO + 8 + CZ, :] = turned[1]
        fields_ref[1, t, ZO : ZO + CZ, :] = turned[2]

    def finish_all():
        zero = jnp.zeros((8, 128), f32)
        sums = [jnp.sum(top.T.reshape(-1, GROUPS, 128), axis=1, keepdims=True) for top in tops]
        for t in range(XTILES):
            at = [divmod(3 * t + c, 128 // GROUPS) for c in range(3)]
            above = [sums[n][i] for n, i in at]
            below = jnp.concatenate([above[1], jnp.zeros((7, 128), f32)], axis=0)
            slope[t, 0 : ZO + 8, :] = jnp.zeros((ZO + 8, 128), f32)
            slope[t, ZO + 8 + CZ : ZO + 16 + CZ, :] = below
            slope[t, ZO + 16 + CZ : ROWS + 16, :] = zero
            for c in range(2):
                fields_ref[c, t, 0:ZO, :] = zero
                fields_ref[c, t, ZO + CZ : ROWS, :] = jnp.concatenate(
                    [above[2 * c], jnp.zeros((7, 128), f32)], axis=0
                )
            fields_ref[0, t] += slope[t, 9 : ROWS + 9, :] - slope[t, 7 : ROWS + 7, :]

    tops = [None] * -(-3 * XTILES * GROUPS // 128)
    unfinished = [
        sum(
            plane // XPT == t and (i == 0 or planes[i - 1] // XPT != t)
            for planes in (CENTER, LOWER, UPPER)
            for i, plane in enumerate(planes)
        )
        for t in range(XTILES)
    ]
    row_at = 0
    waiting = None
    for e in reversed(range(1 + others)):
        if e == 0:
            y_limit = jnp.where(my == gy - 1, CY, CY + 1).astype(f32)
            y_row = own_row
        else:
            above = my == 0 if others == 1 else jnp.bool_(e == 2)
            y_limit = jnp.where(
                jnp.logical_and(above, my + 1 == gy - 1), CY, CY + 1
            ).astype(f32)
            first = jnp.where(above, WINDOW_HIGH - YO - CY, WINDOW_LOW - YO + CY)
            y_row = row_iota(8) + first.astype(f32)
        high = y_row.shape[0]
        for o, shift, planes in ((1, -1, LOWER), (2, 1, UPPER), (0, 0, CENTER)):
            b = e * 3 + o
            place, row = extra_place(b, bricks)
            x_limit = jnp.where(mx + shift == gx - 1, CX, CX + 1).astype(f32)
            cell_x = points[b, :, 7, :]
            off_x = points[b, :, 4, :]
            low_x = 1.0 - off_x
            high_x = jnp.where(cell_x + 1.0 < x_limit, off_x, 0.0)
            first_x = planes[0] - XO - CX * shift
            hats = [
                hat(float(first_x + n - 1), cell_x, low_x, high_x) for n in range(len(planes) + 2)
            ]
            for n in range(len(planes)):
                hx_ref[b, 0, n] = hats[n + 1]
                hx_ref[b, 1, n] = hats[n + 2] - hats[n]
            cell_z, off_z = points[place, :, row + 1, :], points[b, :, 6, :]
            top = jnp.where((cell_z + 1.0 == float(CZ)) & (cell_z + 1.0 < z_limit), off_z, 0.0)
            top_columns = jnp.concatenate([top, jnp.zeros((128 - GROUPS, 128), f32)], axis=0).T
            top_high = top_columns.astype(bf16).astype(f32)
            top_low = top_columns - top_high
            y_parts = []
            for g in range(GROUPS):
                main = points[b, g]
                more = points[place, g]
                cell_y, cell_z = more[row : row + 1], more[row + 1 : row + 2]
                off_y, off_z = main[5:6], main[6:7]
                at = slice(128 * g, 128 * g + 128)
                hz_high, hz_low = split_hat(z_row, cell_z, off_z)
                right_ref[b, 0, at, 0:CZ] = hz_high.T
                right_ref[b, 1, at, 0:CZ] = hz_low.T
                right_ref[b, 0, at, CZ : CZ + 128] = jnp.where(point_lane == g, top_high, 0.0).astype(bf16)
                right_ref[b, 1, at, CZ : CZ + 128] = jnp.where(point_lane == g, top_low, 0.0).astype(bf16)
                high_y = jnp.where(cell_y + 1.0 < y_limit, off_y, 0.0)
                hy = hat(y_row, cell_y, 1.0 - off_y, high_y)
                dy = hat_slope(y_row, cell_y, 1.0 - off_y, high_y)
                y_parts.append((main[0:1] * hy, main[1:2] * dy, main[2:3] * hy, main[3:4] * hy))
            size = 4 if e == 0 else 12
            for start in range(0, len(planes), size):
                block = planes[start : start + size]
                lists = [block] + 2 * [tuple(p for p in block if p in PLAIN[shift])]
                counts = [-(-len(each) * high // 16) * 16 for each in lists]
                for c in range(3):
                    begin = row_at + sum(counts[:c])
                    for g in range(GROUPS):
                        part_x0, part_y1, part_z, part_w = y_parts[g]
                        at = slice(128 * g, 128 * g + 128)
                        rows = []
                        for plane in lists[c]:
                            n = plane - planes[0]
                            hx = hx_ref[b, 0, n, g : g + 1, :]
                            if c == 0:
                                dx = hx_ref[b, 1, n, g : g + 1, :]
                                rows.append(dx * part_x0 + hx * part_y1)
                            else:
                                rows.append(hx * (part_z if c == 1 else part_w))
                        main_part, rest = split(stack_rows(rows, 16))
                        left_ref[begin : begin + counts[c], at] = main_part
                        after = begin + sum(counts)
                        left_ref[after : after + counts[c], at] = rest
                if waiting is not None:
                    waiting()
                waiting = functools.partial(multiply, row_at, lists, b, e, high)
                row_at += 2 * sum(counts)
    waiting()

    if not single:
        @pl.when(step == pl.num_programs(0) - 1)
        def _():
            for t in range(XTILES):
                finish(t)
            finish_all()
    else:
        finish_all()
    edges_ref[...] = jnp.zeros_like(edges_ref)

    @pl.when(mz < gz - 1)
    def _():
        for c in range(2):
            edges_ref[mz + 1, c] = fields_ref[c, :, UP_AT : UP_AT + HALO, :]

    @pl.when(mz > 0)
    def _():
        for c in range(2):
            edges_ref[mz - 1, c] = fields_ref[c, :, DOWN_AT : DOWN_AT + HALO, :]


def chebyshev_factors():
    half_width = 6.0 / (6.0 + base_screen)
    sigma_ratio = 1.0 / half_width
    rho_prev = half_width
    factors = []
    for _ in range(ITERS - 1):
        rho_next = 1.0 / (2.0 * sigma_ratio - rho_prev)
        factors.append((rho_next * rho_prev, 2.0 * rho_next / half_width))
        rho_prev = rho_next
    return factors


READ_PLANES = range(XPT * FIRST_TILE, XPT * END_TILE)


def read_kernel(own_ref, out_ref, hx_ref):
    y_row = row_iota(24) + float(8 - YO)
    blank = jnp.zeros((8, 128), f32)
    for chunk in range(own_ref.shape[1] // GROUPS):
        span = slice(chunk * GROUPS, chunk * GROUPS + GROUPS)
        cell_x, off_x = own_ref[0, span, 7, :], own_ref[0, span, 4, :]
        for plane in READ_PLANES:
            if 0 <= plane - XO <= CX:
                hx_ref[plane] = hat(float(plane - XO), cell_x, 1.0 - off_x, off_x)
        for g in range(GROUPS):
            off_y = own_ref[0, chunk * GROUPS + g, 5:6, :]
            hy = hat(y_row, own_ref[1, chunk * GROUPS + g, 0:1, :], 1.0 - off_y, off_y)
            at = slice(128 * g, 128 * g + 128)
            for plane in READ_PLANES:
                start = YS * (plane - XPT * FIRST_TILE)
                if 0 <= plane - XO <= CX:
                    rows = jnp.concatenate([blank, hx_ref[plane, g : g + 1, :] * hy], axis=0)
                    high, low = split(rows)
                else:
                    high = jnp.zeros((YS, 128), bf16)
                    low = high
                out_ref[chunk, 0, start : start + YS, at] = high
                out_ref[chunk, 1, start : start + YS, at] = low


def solve_kernel(
    shape, fields_ref, halos_ref, own_ref, read_ref,
    indicator_ref, values_ref,
    edge, first, second, base, inverse, total, operand, arrivals,
):
    gx, gy, gz = shape
    mx, my, mz = lax.axis_index("gx"), lax.axis_index("gy"), lax.axis_index("gz")
    copy = pltpu.make_async_copy(read_ref.at[0], operand, arrivals)
    copy.start()
    edge[...] = jnp.zeros_like(edge)
    low_at, high_at = UP_AT - CZ, DOWN_AT + CZ - (ROWS - 16)

    @pl.when(mz > 0)
    def _():
        edge[0, :, :, low_at : low_at + HALO, :] = halos_ref[mz - 1]

    @pl.when(mz < gz - 1)
    def _():
        edge[1, :, :, high_at : high_at + HALO, :] = halos_ref[mz + 1]


    def given(c, t, i):
        value = fields_ref[c, t, 8 * i : 8 * i + 8, :]
        if i < 2:
            value = value + edge[0, c, t, 8 * i : 8 * i + 8, :]
        from_end = i - (ROWS // 8 - 2)
        if from_end >= 0:
            value = value + edge[1, c, t, 8 * from_end : 8 * from_end + 8, :]
        return value

    lane = lax.broadcasted_iota(jnp.int32, (8, 128), 1)
    row = lax.broadcasted_iota(jnp.int32, (8, 128), 0)
    y = lane % YS - YO + my * CY
    inside_y = (y >= 0) & (y < gy * CY)
    zero = jnp.zeros((8, 128), f32)
    strips = ROWS // 8
    for t in range(XTILES):
        x = lane // YS + (XPT * t - XO) + mx * CX
        inside_xy = inside_y & (x >= 0) & (x < gx * CX)
        for scratch in (first, second):
            scratch[t, 0:8, :] = zero
            scratch[t, ROWS + 8 : ROWS + 16, :] = zero
        for i in range(strips):
            at = slice(8 * i, 8 * i + 8)
            inside = inside_xy
            if 8 * i < ZO or 8 * i + 8 > ZO + CZ:
                z = row + (8 * i - ZO) + mz * CZ
                inside = inside & (z >= 0) & (z < gz * CZ)
            diagonal = 6.0 + base_screen + point_screen * given(1, t, i)
            inv = jnp.where(inside, 1.0 / diagonal, 0.0)
            start = given(0, t, i) * inv
            inverse[t, at, :] = inv
            base[t, at, :] = start
            first[t, 8 * i + 8 : 8 * i + 16, :] = start

    now, later = first, second
    factors = chebyshev_factors()
    low_part, high_part = lane < YS, lane >= 128 - YS
    for k, (keep, gain) in enumerate(factors, 1):
        last = k == len(factors)
        begin, end = k // XPT, (XO + CX + REACH - k + XPT) // XPT
        if last:
            begin, end = max(begin, FIRST_TILE), min(end, END_TILE)
        for i in range(strips):
            at = slice(8 * i, 8 * i + 8)
            inner = slice(8 * i + 8, 8 * i + 16)
            reach = range(max(begin - 1, 0), min(end + 1, XTILES))
            here = {t: now[t, inner, :] for t in reach}
            ahead_x = {t: pltpu.roll(here[t], YS, 1) for t in reach if t < end}
            behind_x = {t: pltpu.roll(here[t], 128 - YS, 1) for t in reach if t >= begin}
            for t in range(begin, end):
                mine = here[t]
                near = now[t, 8 * i + 7 : 8 * i + 15, :] + now[t, 8 * i + 9 : 8 * i + 17, :]
                near = near + pltpu.roll(mine, 1, 1) + pltpu.roll(mine, 127, 1)
                before = ahead_x[t]
                if t > 0:
                    before = jnp.where(low_part, ahead_x[t - 1], before)
                after = behind_x[t]
                if t + 1 < XTILES:
                    after = jnp.where(high_part, behind_x[t + 1], after)
                near = near + before + after
                ahead = (1.0 + keep - gain) * mine + gain * (base[t, at, :] + inverse[t, at, :] * near)
                if k > 1:
                    ahead = ahead - keep * later[t, inner, :]
                if last:
                    total[t - FIRST_TILE, at, :] = ahead
                else:
                    later[t, inner, :] = ahead
        now, later = later, now

    parts = [split(total[t - FIRST_TILE]) for t in range(FIRST_TILE, END_TILE)]
    u_high = jnp.concatenate([part[0] for part in parts], axis=1)
    u_low = jnp.concatenate([part[1] for part in parts], axis=1)
    u_both = jnp.concatenate([u_high, u_low], axis=0)
    z_row = row_iota(ROWS) - float(ZO)
    copy.wait()
    groups = own_ref.shape[1]
    for chunk in range(groups // GROUPS):
        if chunk > 0:
            copy = pltpu.make_async_copy(read_ref.at[chunk], operand, arrivals)
            copy.start()
            copy.wait()
        got = dot_nn(u_both, operand[0])
        got = got[:ROWS] + got[ROWS:] + dot_nn(u_high, operand[1])
        rows = []
        for g in range(GROUPS):
            main = own_ref[0, chunk * GROUPS + g]
            off_z = main[6:7]
            hz = hat(z_row, own_ref[1, chunk * GROUPS + g, 1:2, :], 1.0 - off_z, off_z)
            value = jnp.sum(hz * got[:, 128 * g : 128 * g + 128], axis=0, keepdims=True)
            rows.append(jnp.where(main[3:4] > 0.0, value, 0.0))
        values = jnp.concatenate(rows, axis=0)
        for q in range(4):
            moved = values if q == 0 else pltpu.roll(values, 128 - 32 * q, 1)
            start = q * groups + chunk * GROUPS
            values_ref[start : start + GROUPS, :] = moved[:, 0:32]

    for t in range(FIRST_TILE, END_TILE):
        turned = total[t - FIRST_TILE, ZO : ZO + CZ, :].T
        for i in range(XPT):
            plane = XPT * t + i - XO
            if 0 <= plane < CX:
                indicator_ref[plane] = turned[YS * i + YO : YS * i + YO + CY, :]


def on_device(shape, point_data, point_cells, send_counts):
    gx, gy, gz = shape
    sources = gx * gy * gz
    slots = point_data.shape[3]
    bricks = 3 * (1 + other_count(gy))
    rows = 8 * -(-(bricks + -(-bricks // 4)) // 4)
    groups = sources // 4
    whole = pl.BlockSpec(memory_space=pltpu.VMEM)

    outgoing = pl.pallas_call(
        functools.partial(pack_kernel, shape),
        out_shape=jax.ShapeDtypeStruct((sources, rows, 128), f32),
        in_specs=[whole] * 3,
        out_specs=whole,
        compiler_params=pltpu.CompilerParams(vmem_limit_bytes=56 * MIB),
        name="pack_points",
    )(
        jnp.transpose(point_data, (0, 2, 1, 3)),
        jnp.transpose(point_cells, (0, 2, 1, 3)),
        send_counts,
    )

    arrived = lax.all_to_all(outgoing, AXES, split_axis=0, concat_axis=0, tiled=True)
    arrived = arrived.reshape(4, groups, rows, 128)

    others = other_count(gy)
    lines = 0
    for planes in (CENTER, LOWER, UPPER):
        for high, size in ((24, 4),) + ((8, 12),) * others:
            for start in range(0, len(planes), size):
                count = min(size, len(planes) - start)
                lines += 6 * 16 * -(-count * high // 16)
    edge_shape = jax.ShapeDtypeStruct((gz, 2, XTILES, HALO, 128), f32)
    steps = groups // GROUPS
    if steps == 1:
        blocks = {"in_specs": [whole], "out_specs": (whole,) * 3}
    else:
        blocks = {
            "grid": (steps,),
            "in_specs": [pl.BlockSpec((4, GROUPS, rows, 128), lambda s: (0, s, 0, 0))],
            "out_specs": (
                pl.BlockSpec((2, XTILES, ROWS, 128), lambda s: (0, 0, 0, 0)),
                pl.BlockSpec((gz, 2, XTILES, HALO, 128), lambda s: (0, 0, 0, 0, 0)),
                pl.BlockSpec((2, GROUPS, 8, 128), lambda s: (0, s, 0, 0)),
            ),
        }
    fields, edges, own = pl.pallas_call(
        functools.partial(splat_kernel, shape),
        out_shape=(
            jax.ShapeDtypeStruct((2, XTILES, ROWS, 128), f32), edge_shape,
            jax.ShapeDtypeStruct((2, groups, 8, 128), f32),
        ),
        **blocks,
        scratch_shapes=[
            pltpu.VMEM((rows // 2, GROUPS, 8, 128), f32),
            pltpu.VMEM((lines, 128 * GROUPS), bf16),
            pltpu.VMEM((bricks, 2, 128 * GROUPS, 2 * 128), bf16),
            pltpu.VMEM((bricks, 2, len(CENTER), GROUPS, 128), f32),
            pltpu.VMEM((3, XPT * XTILES, 24, 2 * 128), f32),
            pltpu.VMEM((max(others, 1), 3, XPT * XTILES, 8, 2 * 128), f32),
            pltpu.VMEM((XTILES, ROWS + 16, 128), f32),
        ],
        compiler_params=pltpu.CompilerParams(vmem_limit_bytes=36 * MIB),
        name="splat_points",
    )(arrived)

    halos = lax.all_to_all(edges, "gz", split_axis=0, concat_axis=0, tiled=True)

    depth = 128 * (END_TILE - FIRST_TILE)
    read = pl.pallas_call(
        read_kernel,
        out_shape=jax.ShapeDtypeStruct((steps, 2, depth, 128 * GROUPS), bf16),
        in_specs=[whole],
        out_specs=whole,
        scratch_shapes=[pltpu.VMEM((XPT * END_TILE, GROUPS, 128), f32)],
        compiler_params=pltpu.CompilerParams(vmem_limit_bytes=16 * MIB),
        cost_estimate=pl.CostEstimate(
            flops=8 * depth * 128 * groups, bytes_accessed=4 * depth * 128 * groups, transcendentals=0
        ),
        name="read_operand",
    )(own)

    indicator, values = pl.pallas_call(
        functools.partial(solve_kernel, shape),
        out_shape=(
            jax.ShapeDtypeStruct((CX, CY, CZ), f32),
            jax.ShapeDtypeStruct((sources, slots), f32),
        ),
        in_specs=[whole] * 3 + [pl.BlockSpec(memory_space=pl.ANY)],
        out_specs=(whole, whole),
        scratch_shapes=[
            pltpu.VMEM((2, 2, XTILES, 16, 128), f32),
            pltpu.VMEM((XTILES, ROWS + 16, 128), f32),
            pltpu.VMEM((XTILES, ROWS + 16, 128), f32),
            pltpu.VMEM((XTILES, ROWS, 128), f32),
            pltpu.VMEM((XTILES, ROWS, 128), f32),
            pltpu.VMEM((END_TILE - FIRST_TILE, ROWS, 128), f32),
            pltpu.VMEM((2, depth, 128 * GROUPS), bf16),
            pltpu.SemaphoreType.DMA,
        ],
        compiler_params=pltpu.CompilerParams(vmem_limit_bytes=16 * MIB),
        name="solve_and_read",
    )(fields, halos, own, read)

    returned = lax.all_to_all(
        values.reshape(1, sources, slots), AXES, split_axis=1, concat_axis=1, tiled=True
    )
    return indicator, returned


def solution(mesh):
    shape = tuple(mesh.shape[axis] for axis in AXES)
    in_specs = (
        P(AXES, None, None, None),
        P(AXES, None, None, None),
        P(AXES, None),
    )
    out_specs = (P("gx", "gy", "gz"), P(AXES, None, None))
    return jax.shard_map(
        functools.partial(on_device, shape),
        mesh=mesh,
        in_specs=in_specs,
        out_specs=out_specs,
        check_vma=False,
    )
```

```python
import functools

import jax
import jax.numpy as jnp
from jax import lax
from jax.experimental import pallas as pl
from jax.experimental.pallas import tpu as pltpu
from jax.sharding import PartitionSpec as P

CX = 16
CY = 16
CZ = 128
ITERS = 6

base_screen = 0.25
point_screen = 4.0

AXES = ("gx", "gy", "gz")
REACH = ITERS - 1
XO = REACH
YO = 9
ZO = 8
YS = 32
XPT = 128 // YS
XTILES = -(-(CX + 2 * REACH + 1) // XPT)
ROWS = CZ + 16
CENTER = tuple(range(XO - 1, XO + CX + 2))
LOWER = tuple(range(0, XO + 2))
UPPER = tuple(range(XO + CX - 1, XO + CX + REACH + 1))
PLAIN = {0: CENTER[1:-1], -1: LOWER[:-1], 1: UPPER[1:]}
FIRST_TILE, END_TILE = XO // XPT, (XO + CX) // XPT + 1
WINDOW_LOW = YO - REACH
WINDOW_HIGH = YO + CY - 1
UP_AT = ZO + CZ - REACH
DOWN_AT = ZO - 1
HALO = 8
GROUPS = 8
MIB = 1024 * 1024

f32 = jnp.float32
bf16 = jnp.bfloat16


def split(value):
    high = value.astype(bf16)
    return high, (value - high.astype(f32)).astype(bf16)


def dot_nt(lhs, rhs):
    return lax.dot_general(lhs, rhs, (((1,), (1,)), ((), ())), preferred_element_type=f32)


def dot_nn(lhs, rhs):
    return lax.dot_general(lhs, rhs, (((1,), (0,)), ((), ())), preferred_element_type=f32)


def other_count(gy):
    return min(gy - 1, 2)


def extra_place(brick, bricks):
    return bricks + brick // 4, 2 * (brick % 4)


def pack_kernel(shape, data_ref, cells_ref, counts_ref, out_ref):
    gx, gy, gz = shape
    slots = data_ref.shape[3]
    sources = gx * gy * gz
    lane = lax.broadcasted_iota(jnp.int32, (sources, slots), 1)
    at_row = lax.broadcasted_iota(jnp.int32, (sources, sources), 0)
    at_lane = lax.broadcasted_iota(jnp.int32, (sources, sources), 1)
    counts = jnp.where(at_row == at_lane, counts_ref[...], 0).astype(f32)
    counts = jnp.sum(counts, axis=1, keepdims=True).astype(jnp.int32)
    others = other_count(gy)
    bricks = 3 * (1 + others)
    weight = jnp.where(lane < counts, data_ref[0, 3], 0.0)
    cells = [cells_ref[0, c].astype(f32) for c in range(3)]
    channels = [data_ref[0, c] * (-0.5 * weight) for c in range(3)]
    channels += [weight] + [data_ref[0, c] for c in range(4, 7)] + cells
    blank = jnp.zeros((sources, 128 - slots), f32)
    channels = [jnp.concatenate([value, blank], axis=1) for value in channels]
    row = lax.broadcasted_iota(jnp.int32, (sources, 128), 0)
    y = (row // gz) % gy

    def moved(value, by):
        if by == 0:
            return value
        gap = jnp.zeros((abs(by), 128), f32)
        if by > 0:
            return jnp.concatenate([value[by:], gap], axis=0)
        return jnp.concatenate([gap, value[:by]], axis=0)

    def beside(value, e):
        if e == 0:
            return value
        up = jnp.where(y < gy - 1, moved(value, gz), 0.0)
        down = jnp.where(y > 0, moved(value, -gz), 0.0)
        if others == 1:
            return up + down
        return down if e == 1 else up

    by_y = [[beside(value, e) for e in range(1 + others)] for value in channels]
    lines = {}
    for b in range(bricks):
        e, o = divmod(b, 3)
        place, extra_row = extra_place(b, bricks)
        for c in range(10):
            block, line = (b, c) if c < 8 else (place, extra_row + c - 8)
            value = moved(by_y[c][e], (0, -gy * gz, gy * gz)[o])
            if block % 4:
                value = pltpu.roll(value, slots * (block % 4), 1)
            key = 8 * (block // 4) + line
            lines[key] = value if key not in lines else lines[key] + value
    for line in range(out_ref.shape[1]):
        value = lines.get(line)
        out_ref[:, line, :] = jnp.zeros((sources, 128), f32) if value is None else value


def hat(coordinate, cell, low, high):
    away = coordinate - cell
    return jnp.where(away == 0.0, low, jnp.where(away == 1.0, high, 0.0))


def hat_slope(coordinate, cell, low, high):
    away = coordinate - cell
    rising = jnp.where(away == -1.0, low, jnp.where(away == 0.0, high, 0.0))
    return rising - jnp.where(away == 1.0, low, jnp.where(away == 2.0, high, 0.0))


def split_hat(rows, cell, offset):
    spread = (16, 128)
    fill = rows.shape[0] // 16
    ends = []
    for value in (1.0 - offset, offset):
        ends.extend(split(jnp.broadcast_to(value, spread)))
    low_high, low_low, high_high, high_low = (jnp.concatenate([v] * fill, axis=0) for v in ends)
    cells = jnp.broadcast_to(cell, spread).astype(bf16)
    away = rows - jnp.concatenate([cells] * fill, axis=0)
    here, above = away == 0.0, away == 1.0
    zero = jnp.zeros(rows.shape, bf16)
    return (
        jnp.where(here, low_high, jnp.where(above, high_high, zero)),
        jnp.where(here, low_low, jnp.where(above, high_low, zero)),
    )


def row_iota(rows):
    return lax.broadcasted_iota(jnp.int32, (rows, 128), 0).astype(f32)


def stack_rows(parts, multiple):
    have = sum(part.shape[0] for part in parts)
    if have % multiple:
        parts = parts + [jnp.zeros((multiple - have % multiple, 128), f32)]
    return jnp.concatenate(parts, axis=0) if len(parts) > 1 else parts[0]


def splat_kernel(
    shape, recv_ref, fields_ref, up_ref, down_ref, own_ref,
    points, left_ref, right_ref, hx_ref, near, beside, slope,
):
    gx, gy, gz = shape
    mx, my, mz = lax.axis_index("gx"), lax.axis_index("gy"), lax.axis_index("gz")
    single = recv_ref.shape[1] * 4 == gx * gy * gz
    step = 0 if single else pl.program_id(0)
    others = other_count(gy)
    bricks = 3 * (1 + others)
    tiles = recv_ref.shape[2] // 8
    lane_part = lax.broadcasted_iota(jnp.int32, (8, 128), 1) // 32
    span = 128 * GROUPS
    written = set()

    def add(ref, place, value):
        if single and place not in written:
            written.add(place)
            ref[place] = value
        else:
            ref[place] += value

    if not single:
        @pl.when(step == 0)
        def _():
            near[...] = jnp.zeros_like(near)
            beside[...] = jnp.zeros_like(beside)

    for t in range(tiles):
        for g in range(GROUPS):
            given = [recv_ref[q, g, 8 * t : 8 * t + 8, :] for q in range(4)]
            for k in range(4):
                if 4 * t + k >= bricks + -(-bricks // 4):
                    continue
                merged = None
                for q in range(4):
                    moved = given[q] if q == k else pltpu.roll(given[q], (32 * (q - k)) % 128, 1)
                    merged = moved if merged is None else jnp.where(lane_part == q, moved, merged)
                points[4 * t + k, g] = merged
    own_ref[0] = points[0]
    own_ref[1] = points[bricks]

    z_limit = jnp.where(mz == gz - 1, CZ, CZ + 1).astype(f32)
    z_row = row_iota(CZ).astype(bf16)
    own_row = row_iota(24) + float(8 - YO)
    point_lane = lax.broadcasted_iota(jnp.int32, (128, 128), 1)

    def multiply(begin, lists, b, e, high):
        counts = [-(-len(planes) * high // 16) * 16 for planes in lists]
        size = sum(counts)
        both = dot_nn(left_ref[begin : begin + 2 * size, :], right_ref[b, 0])
        got = both[:size] + both[size:]
        got = got + dot_nn(left_ref[begin : begin + size, :], right_ref[b, 1])
        at = 0
        for c in range(3):
            for i, plane in enumerate(lists[c]):
                value = got[at + i * high : at + i * high + high]
                if e == 0:
                    add(near, (c, plane), value)
                else:
                    add(beside, (e - 1, c, plane), value)
            at += counts[c]
        if single and e == 0:
            for t in sorted({plane // XPT for plane in lists[0]}):
                unfinished[t] -= 1
                if unfinished[t] == 0:
                    finish(t)

    row8 = lax.broadcasted_iota(jnp.int32, (8, 2 * 128), 0)
    zero = jnp.zeros((8, 2 * 128), f32)

    def finish(t):
        turned = []
        for c in range(3):
            pieces = []
            for plane in range(XPT * t, XPT * t + XPT):
                if plane > UPPER[-1]:
                    pieces.append(jnp.zeros((YS, 2 * 128), f32))
                    continue
                parts = [zero] + [near[c, plane, 8 * i : 8 * i + 8, :] for i in range(3)]
                if others:
                    if others == 1:
                        value = beside[0, c, plane]
                        low_part = jnp.where(my == 0, 0.0, value)
                        high_part = jnp.where(my == 0, value, 0.0)
                    else:
                        low_part, high_part = beside[0, c, plane], beside[1, c, plane]
                    moved = pltpu.roll(low_part, 4, 0)
                    parts[0] = jnp.where(row8 >= 4, moved, 0.0)
                    parts[1] = parts[1] + jnp.where(row8 < 4, moved, 0.0)
                    parts[3] = parts[3] + high_part
                pieces.extend(parts)
            stacked = jnp.concatenate(pieces, axis=0)
            turned.append(stacked[:, :CZ].T)
            above = stacked[:, CZ:]
            n, at = divmod(3 * t + c, 128 // GROUPS)
            if at:
                above = pltpu.roll(above, GROUPS * at, 1)
            if tops[n] is not None:
                above = jnp.where(point_lane // GROUPS == at, above, tops[n])
            tops[n] = above
        fields_ref[0, t, ZO : ZO + CZ, :] = turned[0]
        slope[t, ZO + 8 : ZO + 8 + CZ, :] = turned[1]
        fields_ref[1, t, ZO : ZO + CZ, :] = turned[2]

    def finish_all():
        zero = jnp.zeros((8, 128), f32)
        sums = [jnp.sum(top.T.reshape(-1, GROUPS, 128), axis=1, keepdims=True) for top in tops]
        for t in range(XTILES):
            at = [divmod(3 * t + c, 128 // GROUPS) for c in range(3)]
            above = [sums[n][i] for n, i in at]
            below = jnp.concatenate([above[1], jnp.zeros((7, 128), f32)], axis=0)
            slope[t, 0 : ZO + 8, :] = jnp.zeros((ZO + 8, 128), f32)
            slope[t, ZO + 8 + CZ : ZO + 16 + CZ, :] = below
            slope[t, ZO + 16 + CZ : ROWS + 16, :] = zero
            for c in range(2):
                fields_ref[c, t, 0:ZO, :] = zero
                fields_ref[c, t, ZO + CZ : ROWS, :] = jnp.concatenate(
                    [above[2 * c], jnp.zeros((7, 128), f32)], axis=0
                )
            fields_ref[0, t] += slope[t, 9 : ROWS + 9, :] - slope[t, 7 : ROWS + 7, :]

    tops = [None] * -(-3 * XTILES * GROUPS // 128)
    unfinished = [
        sum(
            plane // XPT == t and (i == 0 or planes[i - 1] // XPT != t)
            for planes in (CENTER, LOWER, UPPER)
            for i, plane in enumerate(planes)
        )
        for t in range(XTILES)
    ]
    row_at = 0
    waiting = None
    for e in reversed(range(1 + others)):
        if e == 0:
            y_limit = jnp.where(my == gy - 1, CY, CY + 1).astype(f32)
            y_row = own_row
        else:
            above = my == 0 if others == 1 else jnp.bool_(e == 2)
            y_limit = jnp.where(
                jnp.logical_and(above, my + 1 == gy - 1), CY, CY + 1
            ).astype(f32)
            first = jnp.where(above, WINDOW_HIGH - YO - CY, WINDOW_LOW - YO + CY)
            y_row = row_iota(8) + first.astype(f32)
        high = y_row.shape[0]
        for o, shift, planes in ((1, -1, LOWER), (2, 1, UPPER), (0, 0, CENTER)):
            b = e * 3 + o
            place, row = extra_place(b, bricks)
            x_limit = jnp.where(mx + shift == gx - 1, CX, CX + 1).astype(f32)
            cell_x = points[b, :, 7, :]
            off_x = points[b, :, 4, :]
            low_x = 1.0 - off_x
            high_x = jnp.where(cell_x + 1.0 < x_limit, off_x, 0.0)
            first_x = planes[0] - XO - CX * shift
            hats = [
                hat(float(first_x + n - 1), cell_x, low_x, high_x) for n in range(len(planes) + 2)
            ]
            for n in range(len(planes)):
                hx_ref[b, 0, n] = hats[n + 1]
                hx_ref[b, 1, n] = hats[n + 2] - hats[n]
            cell_z, off_z = points[place, :, row + 1, :], points[b, :, 6, :]
            top = jnp.where((cell_z + 1.0 == float(CZ)) & (cell_z + 1.0 < z_limit), off_z, 0.0)
            top_columns = jnp.concatenate([top, jnp.zeros((128 - GROUPS, 128), f32)], axis=0).T
            top_high = top_columns.astype(bf16).astype(f32)
            top_low = top_columns - top_high
            y_parts = []
            for g in range(GROUPS):
                main = points[b, g]
                more = points[place, g]
                cell_y, cell_z = more[row : row + 1], more[row + 1 : row + 2]
                off_y, off_z = main[5:6], main[6:7]
                at = slice(128 * g, 128 * g + 128)
                hz_high, hz_low = split_hat(z_row, cell_z, off_z)
                right_ref[b, 0, at, 0:CZ] = hz_high.T
                right_ref[b, 1, at, 0:CZ] = hz_low.T
                right_ref[b, 0, at, CZ : CZ + 128] = jnp.where(point_lane == g, top_high, 0.0).astype(bf16)
                right_ref[b, 1, at, CZ : CZ + 128] = jnp.where(point_lane == g, top_low, 0.0).astype(bf16)
                high_y = jnp.where(cell_y + 1.0 < y_limit, off_y, 0.0)
                hy = hat(y_row, cell_y, 1.0 - off_y, high_y)
                dy = hat_slope(y_row, cell_y, 1.0 - off_y, high_y)
                y_parts.append((main[0:1] * hy, main[1:2] * dy, main[2:3] * hy, main[3:4] * hy))
            size = 4 if e == 0 else 12
            for start in range(0, len(planes), size):
                block = planes[start : start + size]
                lists = [block] + 2 * [tuple(p for p in block if p in PLAIN[shift])]
                counts = [-(-len(each) * high // 16) * 16 for each in lists]
                for c in range(3):
                    begin = row_at + sum(counts[:c])
                    for g in range(GROUPS):
                        part_x0, part_y1, part_z, part_w = y_parts[g]
                        at = slice(128 * g, 128 * g + 128)
                        rows = []
                        for plane in lists[c]:
                            n = plane - planes[0]
                            hx = hx_ref[b, 0, n, g : g + 1, :]
                            if c == 0:
                                dx = hx_ref[b, 1, n, g : g + 1, :]
                                rows.append(dx * part_x0 + hx * part_y1)
                            else:
                                rows.append(hx * (part_z if c == 1 else part_w))
                        main_part, rest = split(stack_rows(rows, 16))
                        left_ref[begin : begin + counts[c], at] = main_part
                        after = begin + sum(counts)
                        left_ref[after : after + counts[c], at] = rest
                if waiting is not None:
                    waiting()
                waiting = functools.partial(multiply, row_at, lists, b, e, high)
                row_at += 2 * sum(counts)
    waiting()

    if not single:
        @pl.when(step == pl.num_programs(0) - 1)
        def _():
            for t in range(XTILES):
                finish(t)
            finish_all()
    else:
        finish_all()
    for c in range(2):
        up_ref[c] = fields_ref[c, :, UP_AT : UP_AT + HALO, :]
        down_ref[c] = fields_ref[c, :, DOWN_AT : DOWN_AT + HALO, :]


def chebyshev_factors():
    half_width = 6.0 / (6.0 + base_screen)
    sigma_ratio = 1.0 / half_width
    rho_prev = half_width
    factors = []
    for _ in range(ITERS - 1):
        rho_next = 1.0 / (2.0 * sigma_ratio - rho_prev)
        factors.append((rho_next * rho_prev, 2.0 * rho_next / half_width))
        rho_prev = rho_next
    return factors


READ_PLANES = range(XPT * FIRST_TILE, XPT * END_TILE)
STRIPS = ROWS // 8
INNER = range((UP_AT - CZ + HALO + REACH + 7) // 8, (DOWN_AT + CZ - REACH) // 8)
LOW_ZONE = range(0, INNER[0] + 1)
HIGH_ZONE = range(INNER[-1], STRIPS)


def relax(shape, given, zone, wanted, work, store):
    gx, gy, gz = shape
    mx, my, mz = lax.axis_index("gx"), lax.axis_index("gy"), lax.axis_index("gz")
    first, second, base, inverse = work
    lane = lax.broadcasted_iota(jnp.int32, (8, 128), 1)
    row = lax.broadcasted_iota(jnp.int32, (8, 128), 0)
    y = lane % YS - YO + my * CY
    inside_y = (y >= 0) & (y < gy * CY)
    zero = jnp.zeros((8, 128), f32)
    end_row = 8 * len(zone) + 8
    for t in range(XTILES):
        x = lane // YS + (XPT * t - XO) + mx * CX
        inside_xy = inside_y & (x >= 0) & (x < gx * CX)
        for scratch in (first, second):
            scratch[t, 0:8, :] = zero
            scratch[t, end_row : end_row + 8, :] = zero
        for j, i in enumerate(zone):
            inside = inside_xy
            if 8 * i < ZO or 8 * i + 8 > ZO + CZ:
                z = row + (8 * i - ZO) + mz * CZ
                inside = inside & (z >= 0) & (z < gz * CZ)
            diagonal = 6.0 + base_screen + point_screen * given(1, t, i)
            inv = jnp.where(inside, 1.0 / diagonal, 0.0)
            start = given(0, t, i) * inv
            inverse[t, 8 * j : 8 * j + 8, :] = inv
            base[t, 8 * j : 8 * j + 8, :] = start
            first[t, 8 * j + 8 : 8 * j + 16, :] = start

    now, later = first, second
    factors = chebyshev_factors()
    low_part, high_part = lane < YS, lane >= 128 - YS
    for k, (keep, gain) in enumerate(factors, 1):
        last = k == len(factors)
        begin, end = k // XPT, (XO + CX + REACH - k + XPT) // XPT
        if last:
            begin, end = max(begin, FIRST_TILE), min(end, END_TILE)
        for j, i in enumerate(zone):
            if last and i not in wanted:
                continue
            at = slice(8 * j, 8 * j + 8)
            inner = slice(8 * j + 8, 8 * j + 16)
            reach = range(max(begin - 1, 0), min(end + 1, XTILES))
            here = {t: now[t, inner, :] for t in reach}
            ahead_x = {t: pltpu.roll(here[t], YS, 1) for t in reach if t < end}
            behind_x = {t: pltpu.roll(here[t], 128 - YS, 1) for t in reach if t >= begin}
            for t in range(begin, end):
                mine = here[t]
                near = now[t, 8 * j + 7 : 8 * j + 15, :] + now[t, 8 * j + 9 : 8 * j + 17, :]
                near = near + pltpu.roll(mine, 1, 1) + pltpu.roll(mine, 127, 1)
                before = ahead_x[t]
                if t > 0:
                    before = jnp.where(low_part, ahead_x[t - 1], before)
                after = behind_x[t]
                if t + 1 < XTILES:
                    after = jnp.where(high_part, behind_x[t + 1], after)
                near = near + before + after
                if k == 1:
                    ahead = (1.0 + keep) * mine + gain * (inverse[t, at, :] * near)
                else:
                    ahead = gain * (base[t, at, :] + inverse[t, at, :] * near)
                    ahead = ahead + (1.0 + keep - gain) * mine - keep * later[t, inner, :]
                if last:
                    store(t - FIRST_TILE, i, ahead)
                else:
                    later[t, inner, :] = ahead
        now, later = later, now


def inner_kernel(shape, fields_ref, own_ref, out_ref, inner_ref, hx_ref, *work):
    y_row = row_iota(24) + float(8 - YO)
    blank = jnp.zeros((8, 128), f32)
    for chunk in range(own_ref.shape[1] // GROUPS):
        span = slice(chunk * GROUPS, chunk * GROUPS + GROUPS)
        cell_x, off_x = own_ref[0, span, 7, :], own_ref[0, span, 4, :]
        for plane in READ_PLANES:
            if 0 <= plane - XO <= CX:
                hx_ref[plane] = hat(float(plane - XO), cell_x, 1.0 - off_x, off_x)
        for g in range(GROUPS):
            off_y = own_ref[0, chunk * GROUPS + g, 5:6, :]
            hy = hat(y_row, own_ref[1, chunk * GROUPS + g, 0:1, :], 1.0 - off_y, off_y)
            at = slice(128 * g, 128 * g + 128)
            for plane in READ_PLANES:
                start = YS * (plane - XPT * FIRST_TILE)
                if 0 <= plane - XO <= CX:
                    rows = jnp.concatenate([blank, hx_ref[plane, g : g + 1, :] * hy], axis=0)
                    high, low = split(rows)
                else:
                    high = jnp.zeros((YS, 128), bf16)
                    low = high
                out_ref[chunk, 0, start : start + YS, at] = high
                out_ref[chunk, 1, start : start + YS, at] = low

    def given(c, t, i):
        return fields_ref[c, t, 8 * i : 8 * i + 8, :]

    def store(t, i, value):
        at = 8 * (i - INNER[0])
        inner_ref[t, at : at + 8, :] = value

    relax(shape, given, range(INNER[0] - 1, INNER[-1] + 2), INNER, work, store)


def solve_kernel(
    shape, fields_ref, from_low_ref, from_high_ref, own_ref, inner_ref, read_ref,
    indicator_ref, values_ref,
    edge, total, first, second, base, inverse, first_high, second_high, base_high, inverse_high,
):
    edge[...] = jnp.zeros_like(edge)
    low_at, high_at = UP_AT - CZ, DOWN_AT + CZ - (ROWS - 16)
    edge[0, :, :, low_at : low_at + HALO, :] = from_low_ref[...]
    edge[1, :, :, high_at : high_at + HALO, :] = from_high_ref[...]

    def given(c, t, i):
        value = fields_ref[c, t, 8 * i : 8 * i + 8, :]
        if i < 2:
            value = value + edge[0, c, t, 8 * i : 8 * i + 8, :]
        from_end = i - (STRIPS - 2)
        if from_end >= 0:
            value = value + edge[1, c, t, 8 * from_end : 8 * from_end + 8, :]
        return value

    def store(t, i, value):
        total[t, 8 * i : 8 * i + 8, :] = value

    inner_rows = slice(8 * INNER[0], 8 * INNER[-1] + 8)
    for t in range(END_TILE - FIRST_TILE):
        total[t, 0:8, :] = jnp.zeros((8, 128), f32)
        total[t, inner_rows, :] = inner_ref[t]
    low_wanted = range(1, INNER[0])
    high_wanted = range(INNER[-1] + 1, STRIPS)
    relax(shape, given, LOW_ZONE, low_wanted, (first, second, base, inverse), store)
    relax(
        shape, given, HIGH_ZONE, high_wanted,
        (first_high, second_high, base_high, inverse_high), store,
    )

    parts = [split(total[t - FIRST_TILE]) for t in range(FIRST_TILE, END_TILE)]
    u_high = jnp.concatenate([part[0] for part in parts], axis=1)
    u_low = jnp.concatenate([part[1] for part in parts], axis=1)
    u_both = jnp.concatenate([u_high, u_low], axis=0)
    z_row = row_iota(ROWS) - float(ZO)
    groups = own_ref.shape[1]
    for chunk in range(groups // GROUPS):
        got = dot_nn(u_both, read_ref[chunk, 0])
        got = got[:ROWS] + got[ROWS:] + dot_nn(u_high, read_ref[chunk, 1])
        rows = []
        for g in range(GROUPS):
            main = own_ref[0, chunk * GROUPS + g]
            off_z = main[6:7]
            hz = hat(z_row, own_ref[1, chunk * GROUPS + g, 1:2, :], 1.0 - off_z, off_z)
            value = jnp.sum(hz * got[:, 128 * g : 128 * g + 128], axis=0, keepdims=True)
            rows.append(jnp.where(main[3:4] > 0.0, value, 0.0))
        values = jnp.concatenate(rows, axis=0)
        for q in range(4):
            moved = values if q == 0 else pltpu.roll(values, 128 - 32 * q, 1)
            start = q * groups + chunk * GROUPS
            values_ref[start : start + GROUPS, :] = moved[:, 0:32]

    for t in range(FIRST_TILE, END_TILE):
        turned = total[t - FIRST_TILE, ZO : ZO + CZ, :].T
        for i in range(XPT):
            plane = XPT * t + i - XO
            if 0 <= plane < CX:
                indicator_ref[plane] = turned[YS * i + YO : YS * i + YO + CY, :]


def work_shapes(strips):
    padded = pltpu.VMEM((XTILES, 8 * strips + 16, 128), f32)
    return [padded, padded] + 2 * [pltpu.VMEM((XTILES, 8 * strips, 128), f32)]


def on_device(shape, point_data, point_cells, send_counts):
    gx, gy, gz = shape
    sources = gx * gy * gz
    slots = point_data.shape[3]
    bricks = 3 * (1 + other_count(gy))
    rows = 8 * -(-(bricks + -(-bricks // 4)) // 4)
    groups = sources // 4
    whole = pl.BlockSpec(memory_space=pltpu.VMEM)

    outgoing = pl.pallas_call(
        functools.partial(pack_kernel, shape),
        out_shape=jax.ShapeDtypeStruct((sources, rows, 128), f32),
        in_specs=[whole] * 3,
        out_specs=whole,
        compiler_params=pltpu.CompilerParams(vmem_limit_bytes=56 * MIB),
        name="pack_points",
    )(
        jnp.transpose(point_data, (0, 2, 1, 3)),
        jnp.transpose(point_cells, (0, 2, 1, 3)),
        send_counts,
    )

    arrived = lax.all_to_all(outgoing, AXES, split_axis=0, concat_axis=0, tiled=True)
    arrived = arrived.reshape(4, groups, rows, 128)

    others = other_count(gy)
    lines = 0
    for planes in (CENTER, LOWER, UPPER):
        for high, size in ((24, 4),) + ((8, 12),) * others:
            for start in range(0, len(planes), size):
                count = min(size, len(planes) - start)
                lines += 6 * 16 * -(-count * high // 16)
    edge_shape = jax.ShapeDtypeStruct((2, XTILES, HALO, 128), f32)
    steps = groups // GROUPS
    if steps == 1:
        blocks = {"in_specs": [whole], "out_specs": (whole,) * 4}
    else:
        blocks = {
            "grid": (steps,),
            "in_specs": [pl.BlockSpec((4, GROUPS, rows, 128), lambda s: (0, s, 0, 0))],
            "out_specs": (
                pl.BlockSpec((2, XTILES, ROWS, 128), lambda s: (0, 0, 0, 0)),
                pl.BlockSpec((2, XTILES, HALO, 128), lambda s: (0, 0, 0, 0)),
                pl.BlockSpec((2, XTILES, HALO, 128), lambda s: (0, 0, 0, 0)),
                pl.BlockSpec((2, GROUPS, 8, 128), lambda s: (0, s, 0, 0)),
            ),
        }
    fields, up, down, own = pl.pallas_call(
        functools.partial(splat_kernel, shape),
        out_shape=(
            jax.ShapeDtypeStruct((2, XTILES, ROWS, 128), f32), edge_shape, edge_shape,
            jax.ShapeDtypeStruct((2, groups, 8, 128), f32),
        ),
        **blocks,
        scratch_shapes=[
            pltpu.VMEM((rows // 2, GROUPS, 8, 128), f32),
            pltpu.VMEM((lines, 128 * GROUPS), bf16),
            pltpu.VMEM((bricks, 2, 128 * GROUPS, 2 * 128), bf16),
            pltpu.VMEM((bricks, 2, len(CENTER), GROUPS, 128), f32),
            pltpu.VMEM((3, XPT * XTILES, 24, 2 * 128), f32),
            pltpu.VMEM((max(others, 1), 3, XPT * XTILES, 8, 2 * 128), f32),
            pltpu.VMEM((XTILES, ROWS + 16, 128), f32),
        ],
        compiler_params=pltpu.CompilerParams(vmem_limit_bytes=36 * MIB),
        name="splat_points",
    )(arrived)

    from_low = lax.ppermute(up, "gz", [(i, i + 1) for i in range(gz - 1)])
    from_high = lax.ppermute(down, "gz", [(i + 1, i) for i in range(gz - 1)])

    depth = 128 * (END_TILE - FIRST_TILE)
    tiles = END_TILE - FIRST_TILE
    read, inner = pl.pallas_call(
        functools.partial(inner_kernel, shape),
        out_shape=(
            jax.ShapeDtypeStruct((steps, 2, depth, 128 * GROUPS), bf16),
            jax.ShapeDtypeStruct((tiles, 8 * len(INNER), 128), f32),
        ),
        in_specs=[whole, whole],
        out_specs=(whole, whole),
        scratch_shapes=[pltpu.VMEM((XPT * END_TILE, GROUPS, 128), f32)]
        + work_shapes(len(INNER) + 2),
        compiler_params=pltpu.CompilerParams(vmem_limit_bytes=24 * MIB),
        cost_estimate=pl.CostEstimate(
            flops=8 * depth * 128 * groups, bytes_accessed=4 * depth * 128 * groups, transcendentals=0
        ),
        name="solve_inner",
    )(fields, own)

    indicator, values = pl.pallas_call(
        functools.partial(solve_kernel, shape),
        out_shape=(
            jax.ShapeDtypeStruct((CX, CY, CZ), f32),
            jax.ShapeDtypeStruct((sources, slots), f32),
        ),
        in_specs=[whole] * 6,
        out_specs=(whole, whole),
        scratch_shapes=[
            pltpu.VMEM((2, 2, XTILES, 16, 128), f32),
            pltpu.VMEM((tiles, ROWS, 128), f32),
        ]
        + work_shapes(len(LOW_ZONE))
        + work_shapes(len(HIGH_ZONE)),
        compiler_params=pltpu.CompilerParams(vmem_limit_bytes=24 * MIB),
        name="solve_and_read",
    )(fields, from_low, from_high, own, inner, read)

    returned = lax.all_to_all(
        values.reshape(1, sources, slots), AXES, split_axis=1, concat_axis=1, tiled=True
    )
    return indicator, returned


def solution(mesh):
    shape = tuple(mesh.shape[axis] for axis in AXES)
    in_specs = (
        P(AXES, None, None, None),
        P(AXES, None, None, None),
        P(AXES, None),
    )
    out_specs = (P("gx", "gy", "gz"), P(AXES, None, None))
    return jax.shard_map(
        functools.partial(on_device, shape),
        mesh=mesh,
        in_specs=in_specs,
        out_specs=out_specs,
        check_vma=False,
    )
```

```python
import functools

import jax
import jax.numpy as jnp
from jax import lax
from jax.experimental import pallas as pl
from jax.experimental.pallas import tpu as pltpu
from jax.sharding import PartitionSpec as P

CX = 16
CY = 16
CZ = 128
ITERS = 6

base_screen = 0.25
point_screen = 4.0

AXES = ("gx", "gy", "gz")
REACH = ITERS - 1
XO = REACH
YO = 9
ZO = 8
YS = 32
XPT = 128 // YS
XTILES = -(-(CX + 2 * REACH + 1) // XPT)
ROWS = CZ + 16
CENTER = tuple(range(XO - 1, XO + CX + 2))
LOWER = tuple(range(0, XO + 2))
UPPER = tuple(range(XO + CX - 1, XO + CX + REACH + 1))
PLAIN = {0: CENTER[1:-1], -1: LOWER[:-1], 1: UPPER[1:]}
FIRST_TILE, END_TILE = XO // XPT, (XO + CX) // XPT + 1
WINDOW_LOW = YO - REACH
WINDOW_HIGH = YO + CY - 1
UP_AT = ZO + CZ - REACH
DOWN_AT = ZO - 1
HALO = 8
GROUPS = 8
MIB = 1024 * 1024

f32 = jnp.float32
bf16 = jnp.bfloat16


def split(value):
    high = value.astype(bf16)
    return high, (value - high.astype(f32)).astype(bf16)


def dot_nt(lhs, rhs):
    return lax.dot_general(lhs, rhs, (((1,), (1,)), ((), ())), preferred_element_type=f32)


def dot_nn(lhs, rhs):
    return lax.dot_general(lhs, rhs, (((1,), (0,)), ((), ())), preferred_element_type=f32)


def other_count(gy):
    return min(gy - 1, 2)


def extra_place(brick, bricks):
    return bricks + brick // 4, 2 * (brick % 4)


def pack_kernel(shape, data_ref, cells_ref, counts_ref, out_ref):
    gx, gy, gz = shape
    slots = data_ref.shape[3]
    sources = gx * gy * gz
    lane = lax.broadcasted_iota(jnp.int32, (sources, slots), 1)
    at_row = lax.broadcasted_iota(jnp.int32, (sources, sources), 0)
    at_lane = lax.broadcasted_iota(jnp.int32, (sources, sources), 1)
    counts = jnp.where(at_row == at_lane, counts_ref[...], 0).astype(f32)
    counts = jnp.sum(counts, axis=1, keepdims=True).astype(jnp.int32)
    others = other_count(gy)
    bricks = 3 * (1 + others)
    weight = jnp.where(lane < counts, data_ref[0, 3], 0.0)
    cells = [cells_ref[0, c].astype(f32) for c in range(3)]
    channels = [data_ref[0, c] * (-0.5 * weight) for c in range(3)]
    channels += [weight] + [data_ref[0, c] for c in range(4, 7)] + cells
    blank = jnp.zeros((sources, 128 - slots), f32)
    channels = [jnp.concatenate([value, blank], axis=1) for value in channels]
    row = lax.broadcasted_iota(jnp.int32, (sources, 128), 0)
    y = (row // gz) % gy

    def moved(value, by):
        if by == 0:
            return value
        gap = jnp.zeros((abs(by), 128), f32)
        if by > 0:
            return jnp.concatenate([value[by:], gap], axis=0)
        return jnp.concatenate([gap, value[:by]], axis=0)

    def beside(value, e):
        if e == 0:
            return value
        up = jnp.where(y < gy - 1, moved(value, gz), 0.0)
        down = jnp.where(y > 0, moved(value, -gz), 0.0)
        if others == 1:
            return up + down
        return down if e == 1 else up

    by_y = [[beside(value, e) for e in range(1 + others)] for value in channels]
    lines = {}
    for b in range(bricks):
        e, o = divmod(b, 3)
        place, extra_row = extra_place(b, bricks)
        for c in range(10):
            block, line = (b, c) if c < 8 else (place, extra_row + c - 8)
            value = moved(by_y[c][e], (0, -gy * gz, gy * gz)[o])
            if block % 4:
                value = pltpu.roll(value, slots * (block % 4), 1)
            key = 8 * (block // 4) + line
            lines[key] = value if key not in lines else lines[key] + value
    for line in range(out_ref.shape[1]):
        value = lines.get(line)
        out_ref[:, line, :] = jnp.zeros((sources, 128), f32) if value is None else value


def hat(coordinate, cell, low, high):
    away = coordinate - cell
    return jnp.where(away == 0.0, low, jnp.where(away == 1.0, high, 0.0))


def hat_slope(coordinate, cell, low, high):
    away = coordinate - cell
    rising = jnp.where(away == -1.0, low, jnp.where(away == 0.0, high, 0.0))
    return rising - jnp.where(away == 1.0, low, jnp.where(away == 2.0, high, 0.0))


def split_hat(rows, cell, offset):
    spread = (16, 128)
    fill = rows.shape[0] // 16
    ends = []
    for value in (1.0 - offset, offset):
        ends.extend(split(jnp.broadcast_to(value, spread)))
    low_high, low_low, high_high, high_low = (jnp.concatenate([v] * fill, axis=0) for v in ends)
    cells = jnp.broadcast_to(cell, spread).astype(bf16)
    away = rows - jnp.concatenate([cells] * fill, axis=0)
    here, above = away == 0.0, away == 1.0
    zero = jnp.zeros(rows.shape, bf16)
    return (
        jnp.where(here, low_high, jnp.where(above, high_high, zero)),
        jnp.where(here, low_low, jnp.where(above, high_low, zero)),
    )


def row_iota(rows):
    return lax.broadcasted_iota(jnp.int32, (rows, 128), 0).astype(f32)


def stack_rows(parts, multiple):
    have = sum(part.shape[0] for part in parts)
    if have % multiple:
        parts = parts + [jnp.zeros((multiple - have % multiple, 128), f32)]
    return jnp.concatenate(parts, axis=0) if len(parts) > 1 else parts[0]


def splat_kernel(
    shape, recv_ref, fields_ref, first_ref, second_ref, own_ref,
    points, left_ref, right_ref, hx_ref, near, beside, slope,
):
    gx, gy, gz = shape
    mx, my, mz = lax.axis_index("gx"), lax.axis_index("gy"), lax.axis_index("gz")
    single = recv_ref.shape[1] * 4 == gx * gy * gz
    step = 0 if single else pl.program_id(0)
    others = other_count(gy)
    bricks = 3 * (1 + others)
    tiles = recv_ref.shape[2] // 8
    lane_part = lax.broadcasted_iota(jnp.int32, (8, 128), 1) // 32
    span = 128 * GROUPS
    written = set()

    def add(ref, place, value):
        if single and place not in written:
            written.add(place)
            ref[place] = value
        else:
            ref[place] += value

    if not single:
        @pl.when(step == 0)
        def _():
            near[...] = jnp.zeros_like(near)
            beside[...] = jnp.zeros_like(beside)

    for t in range(tiles):
        for g in range(GROUPS):
            given = [recv_ref[q, g, 8 * t : 8 * t + 8, :] for q in range(4)]
            for k in range(4):
                if 4 * t + k >= bricks + -(-bricks // 4):
                    continue
                merged = None
                for q in range(4):
                    moved = given[q] if q == k else pltpu.roll(given[q], (32 * (q - k)) % 128, 1)
                    merged = moved if merged is None else jnp.where(lane_part == q, moved, merged)
                points[4 * t + k, g] = merged
    own_ref[0] = points[0]
    own_ref[1] = points[bricks]

    z_limit = jnp.where(mz == gz - 1, CZ, CZ + 1).astype(f32)
    z_row = row_iota(CZ).astype(bf16)
    own_row = row_iota(24) + float(8 - YO)
    point_lane = lax.broadcasted_iota(jnp.int32, (128, 128), 1)
    lane_number = point_lane.astype(f32).astype(bf16)
    no_top = jnp.zeros((128, 128), bf16)

    def multiply(begin, lists, b, e, high):
        counts = [-(-len(planes) * high // 16) * 16 for planes in lists]
        size = sum(counts)
        both = dot_nn(left_ref[begin : begin + 2 * size, :], right_ref[b, 0])
        got = both[:size] + both[size:]
        got = got + dot_nn(left_ref[begin : begin + size, :], right_ref[b, 1])
        at = 0
        for c in range(3):
            for i, plane in enumerate(lists[c]):
                value = got[at + i * high : at + i * high + high]
                if e == 0:
                    add(near, (c, plane), value)
                else:
                    add(beside, (e - 1, c, plane), value)
            at += counts[c]
        if single and e == 0:
            for t in sorted({plane // XPT for plane in lists[0]}):
                unfinished[t] -= 1
                if unfinished[t] == 0:
                    finish(t)

    row8 = lax.broadcasted_iota(jnp.int32, (8, 2 * 128), 0)
    zero = jnp.zeros((8, 2 * 128), f32)

    def finish(t):
        turned = []
        for c in range(3):
            pieces = []
            for plane in range(XPT * t, XPT * t + XPT):
                if plane > UPPER[-1]:
                    pieces.append(jnp.zeros((YS, 2 * 128), f32))
                    continue
                parts = [zero] + [near[c, plane, 8 * i : 8 * i + 8, :] for i in range(3)]
                if others:
                    if others == 1:
                        value = beside[0, c, plane]
                        low_part = jnp.where(my == 0, 0.0, value)
                        high_part = jnp.where(my == 0, value, 0.0)
                    else:
                        low_part, high_part = beside[0, c, plane], beside[1, c, plane]
                    moved = pltpu.roll(low_part, 4, 0)
                    parts[0] = jnp.where(row8 >= 4, moved, 0.0)
                    parts[1] = parts[1] + jnp.where(row8 < 4, moved, 0.0)
                    parts[3] = parts[3] + high_part
                pieces.extend(parts)
            stacked = jnp.concatenate(pieces, axis=0)
            turned.append(stacked[:, :CZ].T)
            above = stacked[:, CZ:]
            n, at = divmod(3 * t + c, 128 // GROUPS)
            if at:
                above = pltpu.roll(above, GROUPS * at, 1)
            if tops[n] is not None:
                above = jnp.where(point_lane // GROUPS == at, above, tops[n])
            tops[n] = above
        fields_ref[0, t, ZO : ZO + CZ, :] = turned[0]
        slope[t, ZO + 8 : ZO + 8 + CZ, :] = turned[1]
        fields_ref[1, t, ZO : ZO + CZ, :] = turned[2]

    def finish_all():
        zero = jnp.zeros((8, 128), f32)
        sums = [jnp.sum(top.T.reshape(-1, GROUPS, 128), axis=1, keepdims=True) for top in tops]
        for t in range(XTILES):
            at = [divmod(3 * t + c, 128 // GROUPS) for c in range(3)]
            above = [sums[n][i] for n, i in at]
            below = jnp.concatenate([above[1], jnp.zeros((7, 128), f32)], axis=0)
            slope[t, 0 : ZO + 8, :] = jnp.zeros((ZO + 8, 128), f32)
            slope[t, ZO + 8 + CZ : ZO + 16 + CZ, :] = below
            slope[t, ZO + 16 + CZ : ROWS + 16, :] = zero
            for c in range(2):
                fields_ref[c, t, 0:ZO, :] = zero
                fields_ref[c, t, ZO + CZ : ROWS, :] = jnp.concatenate(
                    [above[2 * c], jnp.zeros((7, 128), f32)], axis=0
                )
            fields_ref[0, t] += slope[t, 9 : ROWS + 9, :] - slope[t, 7 : ROWS + 7, :]

    tops = [None] * -(-3 * XTILES * GROUPS // 128)
    unfinished = [
        sum(
            plane // XPT == t and (i == 0 or planes[i - 1] // XPT != t)
            for planes in (CENTER, LOWER, UPPER)
            for i, plane in enumerate(planes)
        )
        for t in range(XTILES)
    ]
    row_at = 0
    waiting = None
    for e in reversed(range(1 + others)):
        if e == 0:
            y_limit = jnp.where(my == gy - 1, CY, CY + 1).astype(f32)
            y_row = own_row
        else:
            above = my == 0 if others == 1 else jnp.bool_(e == 2)
            y_limit = jnp.where(
                jnp.logical_and(above, my + 1 == gy - 1), CY, CY + 1
            ).astype(f32)
            first = jnp.where(above, WINDOW_HIGH - YO - CY, WINDOW_LOW - YO + CY)
            y_row = row_iota(8) + first.astype(f32)
        high = y_row.shape[0]
        for o, shift, planes in ((1, -1, LOWER), (2, 1, UPPER), (0, 0, CENTER)):
            b = e * 3 + o
            place, row = extra_place(b, bricks)
            x_limit = jnp.where(mx + shift == gx - 1, CX, CX + 1).astype(f32)
            cell_x = points[b, :, 7, :]
            off_x = points[b, :, 4, :]
            low_x = 1.0 - off_x
            high_x = jnp.where(cell_x + 1.0 < x_limit, off_x, 0.0)
            first_x = planes[0] - XO - CX * shift
            hats = [
                hat(float(first_x + n - 1), cell_x, low_x, high_x) for n in range(len(planes) + 2)
            ]
            for n in range(len(planes)):
                hx_ref[b, 0, n] = hats[n + 1]
                hx_ref[b, 1, n] = hats[n + 2] - hats[n]
            cell_z, off_z = points[place, :, row + 1, :], points[b, :, 6, :]
            top = jnp.where((cell_z + 1.0 == float(CZ)) & (cell_z + 1.0 < z_limit), off_z, 0.0)
            top_columns = jnp.concatenate([top, jnp.zeros((128 - GROUPS, 128), f32)], axis=0).T
            top_high, top_low = split(top_columns)
            y_parts = []
            for g in range(GROUPS):
                main = points[b, g]
                more = points[place, g]
                cell_y, cell_z = more[row : row + 1], more[row + 1 : row + 2]
                off_y, off_z = main[5:6], main[6:7]
                at = slice(128 * g, 128 * g + 128)
                hz_high, hz_low = split_hat(z_row, cell_z, off_z)
                right_ref[b, 0, at, 0:CZ] = hz_high.T
                right_ref[b, 1, at, 0:CZ] = hz_low.T
                column = lane_number == float(g)
                right_ref[b, 0, at, CZ : CZ + 128] = jnp.where(column, top_high, no_top)
                right_ref[b, 1, at, CZ : CZ + 128] = jnp.where(column, top_low, no_top)
                high_y = jnp.where(cell_y + 1.0 < y_limit, off_y, 0.0)
                hy = hat(y_row, cell_y, 1.0 - off_y, high_y)
                dy = hat_slope(y_row, cell_y, 1.0 - off_y, high_y)
                y_parts.append((main[0:1] * hy, main[1:2] * dy, main[2:3] * hy, main[3:4] * hy))
            size = 4 if e == 0 else 12
            for start in range(0, len(planes), size):
                block = planes[start : start + size]
                lists = [block] + 2 * [tuple(p for p in block if p in PLAIN[shift])]
                counts = [-(-len(each) * high // 16) * 16 for each in lists]
                for c in range(3):
                    begin = row_at + sum(counts[:c])
                    for g in range(GROUPS):
                        part_x0, part_y1, part_z, part_w = y_parts[g]
                        at = slice(128 * g, 128 * g + 128)
                        rows = []
                        for plane in lists[c]:
                            n = plane - planes[0]
                            hx = hx_ref[b, 0, n, g : g + 1, :]
                            if c == 0:
                                dx = hx_ref[b, 1, n, g : g + 1, :]
                                rows.append(dx * part_x0 + hx * part_y1)
                            else:
                                rows.append(hx * (part_z if c == 1 else part_w))
                        main_part, rest = split(stack_rows(rows, 16))
                        left_ref[begin : begin + counts[c], at] = main_part
                        after = begin + sum(counts)
                        left_ref[after : after + counts[c], at] = rest
                if waiting is not None:
                    waiting()
                waiting = functools.partial(multiply, row_at, lists, b, e, high)
                row_at += 2 * sum(counts)
    waiting()

    if not single:
        @pl.when(step == pl.num_programs(0) - 1)
        def _():
            for t in range(XTILES):
                finish(t)
            finish_all()
    else:
        finish_all()
    for c in range(2):
        up = fields_ref[c, :, UP_AT : UP_AT + HALO, :]
        down = fields_ref[c, :, DOWN_AT : DOWN_AT + HALO, :]
        first_ref[c] = jnp.where(mz % 2 == 0, up, down)
        second_ref[c] = jnp.where(mz % 2 == 0, down, up)


def chebyshev_factors():
    half_width = 6.0 / (6.0 + base_screen)
    sigma_ratio = 1.0 / half_width
    rho_prev = half_width
    factors = []
    for _ in range(ITERS - 1):
        rho_next = 1.0 / (2.0 * sigma_ratio - rho_prev)
        factors.append((rho_next * rho_prev, 2.0 * rho_next / half_width))
        rho_prev = rho_next
    return factors


READ_PLANES = range(XPT * FIRST_TILE, XPT * END_TILE)
STRIPS = ROWS // 8
INNER = range((UP_AT - CZ + HALO + REACH + 7) // 8, (DOWN_AT + CZ - REACH) // 8)
LOW_ZONE = range(0, INNER[0] + 1)
HIGH_ZONE = range(INNER[-1], STRIPS)


def relax(shape, given, zone, wanted, work, store):
    gx, gy, gz = shape
    mx, my, mz = lax.axis_index("gx"), lax.axis_index("gy"), lax.axis_index("gz")
    first, second, base, inverse = work
    lane = lax.broadcasted_iota(jnp.int32, (8, 128), 1)
    row = lax.broadcasted_iota(jnp.int32, (8, 128), 0)
    y = lane % YS - YO + my * CY
    inside_y = (y >= 0) & (y < gy * CY)
    zero = jnp.zeros((8, 128), f32)
    end_row = 8 * len(zone) + 8
    for t in range(XTILES):
        x = lane // YS + (XPT * t - XO) + mx * CX
        inside_xy = inside_y & (x >= 0) & (x < gx * CX)
        for scratch in (first, second):
            scratch[t, 0:8, :] = zero
            scratch[t, end_row : end_row + 8, :] = zero
        for j, i in enumerate(zone):
            inside = inside_xy
            if 8 * i < ZO or 8 * i + 8 > ZO + CZ:
                z = row + (8 * i - ZO) + mz * CZ
                inside = inside & (z >= 0) & (z < gz * CZ)
            diagonal = 6.0 + base_screen + point_screen * given(1, t, i)
            inv = jnp.where(inside, 1.0 / diagonal, 0.0)
            start = given(0, t, i) * inv
            inverse[t, 8 * j : 8 * j + 8, :] = inv
            base[t, 8 * j : 8 * j + 8, :] = start
            first[t, 8 * j + 8 : 8 * j + 16, :] = start

    now, later = first, second
    factors = chebyshev_factors()
    low_part, high_part = lane < YS, lane >= 128 - YS
    for k, (keep, gain) in enumerate(factors, 1):
        last = k == len(factors)
        begin, end = k // XPT, (XO + CX + REACH - k + XPT) // XPT
        if last:
            begin, end = max(begin, FIRST_TILE), min(end, END_TILE)
        for j, i in enumerate(zone):
            if last and i not in wanted:
                continue
            at = slice(8 * j, 8 * j + 8)
            inner = slice(8 * j + 8, 8 * j + 16)
            reach = range(max(begin - 1, 0), min(end + 1, XTILES))
            here = {t: now[t, inner, :] for t in reach}
            ahead_x = {t: pltpu.roll(here[t], YS, 1) for t in reach if t < end}
            behind_x = {t: pltpu.roll(here[t], 128 - YS, 1) for t in reach if t >= begin}
            for t in range(begin, end):
                mine = here[t]
                near = now[t, 8 * j + 7 : 8 * j + 15, :] + now[t, 8 * j + 9 : 8 * j + 17, :]
                near = near + pltpu.roll(mine, 1, 1) + pltpu.roll(mine, 127, 1)
                before = ahead_x[t]
                if t > 0:
                    before = jnp.where(low_part, ahead_x[t - 1], before)
                after = behind_x[t]
                if t + 1 < XTILES:
                    after = jnp.where(high_part, behind_x[t + 1], after)
                near = near + before + after
                if k == 1:
                    ahead = (1.0 + keep) * mine + gain * (inverse[t, at, :] * near)
                else:
                    ahead = gain * (base[t, at, :] + inverse[t, at, :] * near)
                    ahead = ahead + (1.0 + keep - gain) * mine - keep * later[t, inner, :]
                if last:
                    store(t - FIRST_TILE, i, ahead)
                else:
                    later[t, inner, :] = ahead
        now, later = later, now


def inner_kernel(shape, fields_ref, own_ref, out_ref, inner_ref, hx_ref, *work):
    y_row = row_iota(24) + float(8 - YO)
    blank = jnp.zeros((8, 128), f32)
    for chunk in range(own_ref.shape[1] // GROUPS):
        span = slice(chunk * GROUPS, chunk * GROUPS + GROUPS)
        cell_x, off_x = own_ref[0, span, 7, :], own_ref[0, span, 4, :]
        for plane in READ_PLANES:
            if 0 <= plane - XO <= CX:
                hx_ref[plane] = hat(float(plane - XO), cell_x, 1.0 - off_x, off_x)
        for g in range(GROUPS):
            off_y = own_ref[0, chunk * GROUPS + g, 5:6, :]
            hy = hat(y_row, own_ref[1, chunk * GROUPS + g, 0:1, :], 1.0 - off_y, off_y)
            at = slice(128 * g, 128 * g + 128)
            for plane in READ_PLANES:
                start = YS * (plane - XPT * FIRST_TILE)
                if 0 <= plane - XO <= CX:
                    rows = jnp.concatenate([blank, hx_ref[plane, g : g + 1, :] * hy], axis=0)
                    high, low = split(rows)
                else:
                    high = jnp.zeros((YS, 128), bf16)
                    low = high
                out_ref[chunk, 0, start : start + YS, at] = high
                out_ref[chunk, 1, start : start + YS, at] = low

    def given(c, t, i):
        return fields_ref[c, t, 8 * i : 8 * i + 8, :]

    def store(t, i, value):
        at = 8 * (i - INNER[0])
        inner_ref[t, at : at + 8, :] = value

    relax(shape, given, range(INNER[0] - 1, INNER[-1] + 2), INNER, work, store)


def solve_kernel(
    shape, fields_ref, first_ref, second_ref, own_ref, inner_ref, read_ref,
    indicator_ref, values_ref,
    edge, total, first, second, base, inverse, first_high, second_high, base_high, inverse_high,
):
    edge[...] = jnp.zeros_like(edge)
    low_at, high_at = UP_AT - CZ, DOWN_AT + CZ - (ROWS - 16)
    even = lax.axis_index("gz") % 2 == 0
    got_first, got_second = first_ref[...], second_ref[...]
    edge[0, :, :, low_at : low_at + HALO, :] = jnp.where(even, got_second, got_first)
    edge[1, :, :, high_at : high_at + HALO, :] = jnp.where(even, got_first, got_second)

    def given(c, t, i):
        value = fields_ref[c, t, 8 * i : 8 * i + 8, :]
        if i < 2:
            value = value + edge[0, c, t, 8 * i : 8 * i + 8, :]
        from_end = i - (STRIPS - 2)
        if from_end >= 0:
            value = value + edge[1, c, t, 8 * from_end : 8 * from_end + 8, :]
        return value

    def store(t, i, value):
        total[t, 8 * i : 8 * i + 8, :] = value

    inner_rows = slice(8 * INNER[0], 8 * INNER[-1] + 8)
    for t in range(END_TILE - FIRST_TILE):
        total[t, 0:8, :] = jnp.zeros((8, 128), f32)
        total[t, inner_rows, :] = inner_ref[t]
    low_wanted = range(1, INNER[0])
    high_wanted = range(INNER[-1] + 1, STRIPS)
    relax(shape, given, LOW_ZONE, low_wanted, (first, second, base, inverse), store)
    relax(
        shape, given, HIGH_ZONE, high_wanted,
        (first_high, second_high, base_high, inverse_high), store,
    )

    parts = [split(total[t - FIRST_TILE]) for t in range(FIRST_TILE, END_TILE)]
    u_high = jnp.concatenate([part[0] for part in parts], axis=1)
    u_low = jnp.concatenate([part[1] for part in parts], axis=1)
    u_both = jnp.concatenate([u_high, u_low], axis=0)
    z_row = row_iota(ROWS) - float(ZO)
    groups = own_ref.shape[1]
    for chunk in range(groups // GROUPS):
        got = dot_nn(u_both, read_ref[chunk, 0])
        got = got[:ROWS] + got[ROWS:] + dot_nn(u_high, read_ref[chunk, 1])
        rows = []
        for g in range(GROUPS):
            main = own_ref[0, chunk * GROUPS + g]
            off_z = main[6:7]
            hz = hat(z_row, own_ref[1, chunk * GROUPS + g, 1:2, :], 1.0 - off_z, off_z)
            value = jnp.sum(hz * got[:, 128 * g : 128 * g + 128], axis=0, keepdims=True)
            rows.append(jnp.where(main[3:4] > 0.0, value, 0.0))
        values = jnp.concatenate(rows, axis=0)
        for q in range(4):
            moved = values if q == 0 else pltpu.roll(values, 128 - 32 * q, 1)
            start = q * groups + chunk * GROUPS
            values_ref[start : start + GROUPS, :] = moved[:, 0:32]

    for t in range(FIRST_TILE, END_TILE):
        turned = total[t - FIRST_TILE, ZO : ZO + CZ, :].T
        for i in range(XPT):
            plane = XPT * t + i - XO
            if 0 <= plane < CX:
                indicator_ref[plane] = turned[YS * i + YO : YS * i + YO + CY, :]


def work_shapes(strips):
    padded = pltpu.VMEM((XTILES, 8 * strips + 16, 128), f32)
    return [padded, padded] + 2 * [pltpu.VMEM((XTILES, 8 * strips, 128), f32)]


def on_device(shape, point_data, point_cells, send_counts):
    gx, gy, gz = shape
    sources = gx * gy * gz
    slots = point_data.shape[3]
    bricks = 3 * (1 + other_count(gy))
    rows = 8 * -(-(bricks + -(-bricks // 4)) // 4)
    groups = sources // 4
    whole = pl.BlockSpec(memory_space=pltpu.VMEM)

    outgoing = pl.pallas_call(
        functools.partial(pack_kernel, shape),
        out_shape=jax.ShapeDtypeStruct((sources, rows, 128), f32),
        in_specs=[whole] * 3,
        out_specs=whole,
        compiler_params=pltpu.CompilerParams(vmem_limit_bytes=56 * MIB),
        name="pack_points",
    )(
        jnp.transpose(point_data, (0, 2, 1, 3)),
        jnp.transpose(point_cells, (0, 2, 1, 3)),
        send_counts,
    )

    arrived = lax.all_to_all(outgoing, AXES, split_axis=0, concat_axis=0, tiled=True)
    arrived = arrived.reshape(4, groups, rows, 128)

    others = other_count(gy)
    lines = 0
    for planes in (CENTER, LOWER, UPPER):
        for high, size in ((24, 4),) + ((8, 12),) * others:
            for start in range(0, len(planes), size):
                count = min(size, len(planes) - start)
                lines += 6 * 16 * -(-count * high // 16)
    edge_shape = jax.ShapeDtypeStruct((2, XTILES, HALO, 128), f32)
    steps = groups // GROUPS
    if steps == 1:
        blocks = {"in_specs": [whole], "out_specs": (whole,) * 4}
    else:
        blocks = {
            "grid": (steps,),
            "in_specs": [pl.BlockSpec((4, GROUPS, rows, 128), lambda s: (0, s, 0, 0))],
            "out_specs": (
                pl.BlockSpec((2, XTILES, ROWS, 128), lambda s: (0, 0, 0, 0)),
                pl.BlockSpec((2, XTILES, HALO, 128), lambda s: (0, 0, 0, 0)),
                pl.BlockSpec((2, XTILES, HALO, 128), lambda s: (0, 0, 0, 0)),
                pl.BlockSpec((2, GROUPS, 8, 128), lambda s: (0, s, 0, 0)),
            ),
        }
    fields, first, second, own = pl.pallas_call(
        functools.partial(splat_kernel, shape),
        out_shape=(
            jax.ShapeDtypeStruct((2, XTILES, ROWS, 128), f32), edge_shape, edge_shape,
            jax.ShapeDtypeStruct((2, groups, 8, 128), f32),
        ),
        **blocks,
        scratch_shapes=[
            pltpu.VMEM((rows // 2, GROUPS, 8, 128), f32),
            pltpu.VMEM((lines, 128 * GROUPS), bf16),
            pltpu.VMEM((bricks, 2, 128 * GROUPS, 2 * 128), bf16),
            pltpu.VMEM((bricks, 2, len(CENTER), GROUPS, 128), f32),
            pltpu.VMEM((3, XPT * XTILES, 24, 2 * 128), f32),
            pltpu.VMEM((max(others, 1), 3, XPT * XTILES, 8, 2 * 128), f32),
            pltpu.VMEM((XTILES, ROWS + 16, 128), f32),
        ],
        compiler_params=pltpu.CompilerParams(vmem_limit_bytes=36 * MIB),
        name="splat_points",
    )(arrived)

    def swapped(edge, start):
        pairs = [(i, i + 1) for i in range(start, gz - 1, 2)]
        return lax.ppermute(edge, "gz", pairs + [(j, i) for i, j in pairs])

    got_first, got_second = swapped(first, 0), swapped(second, 1)

    depth = 128 * (END_TILE - FIRST_TILE)
    tiles = END_TILE - FIRST_TILE
    read, inner = pl.pallas_call(
        functools.partial(inner_kernel, shape),
        out_shape=(
            jax.ShapeDtypeStruct((steps, 2, depth, 128 * GROUPS), bf16),
            jax.ShapeDtypeStruct((tiles, 8 * len(INNER), 128), f32),
        ),
        in_specs=[whole, whole],
        out_specs=(whole, whole),
        scratch_shapes=[pltpu.VMEM((XPT * END_TILE, GROUPS, 128), f32)]
        + work_shapes(len(INNER) + 2),
        compiler_params=pltpu.CompilerParams(vmem_limit_bytes=24 * MIB),
        cost_estimate=pl.CostEstimate(
            flops=8 * depth * 128 * groups, bytes_accessed=4 * depth * 128 * groups, transcendentals=0
        ),
        name="solve_inner",
    )(fields, own)

    indicator, values = pl.pallas_call(
        functools.partial(solve_kernel, shape),
        out_shape=(
            jax.ShapeDtypeStruct((CX, CY, CZ), f32),
            jax.ShapeDtypeStruct((sources, slots), f32),
        ),
        in_specs=[whole] * 6,
        out_specs=(whole, whole),
        scratch_shapes=[
            pltpu.VMEM((2, 2, XTILES, 16, 128), f32),
            pltpu.VMEM((tiles, ROWS, 128), f32),
        ]
        + work_shapes(len(LOW_ZONE))
        + work_shapes(len(HIGH_ZONE)),
        compiler_params=pltpu.CompilerParams(vmem_limit_bytes=24 * MIB),
        name="solve_and_read",
    )(fields, got_first, got_second, own, inner, read)

    returned = lax.all_to_all(
        values.reshape(1, sources, slots), AXES, split_axis=1, concat_axis=1, tiled=True
    )
    return indicator, returned


def solution(mesh):
    shape = tuple(mesh.shape[axis] for axis in AXES)
    in_specs = (
        P(AXES, None, None, None),
        P(AXES, None, None, None),
        P(AXES, None),
    )
    out_specs = (P("gx", "gy", "gz"), P(AXES, None, None))
    return jax.shard_map(
        functools.partial(on_device, shape),
        mesh=mesh,
        in_specs=in_specs,
        out_specs=out_specs,
        check_vma=False,
    )
```

```python
import functools

import jax
import jax.numpy as jnp
from jax import lax
from jax.experimental import pallas as pl
from jax.experimental.pallas import tpu as pltpu
from jax.sharding import PartitionSpec as P

CX = 16
CY = 16
CZ = 128
ITERS = 6

base_screen = 0.25
point_screen = 4.0

AXES = ("gx", "gy", "gz")
REACH = ITERS - 1
XO = REACH
YO = 9
ZO = 8
YS = 32
XPT = 128 // YS
XTILES = -(-(CX + 2 * REACH + 1) // XPT)
ROWS = CZ + 16
CENTER = tuple(range(XO - 1, XO + CX + 2))
LOWER = tuple(range(0, XO + 2))
UPPER = tuple(range(XO + CX - 1, XO + CX + REACH + 1))
PLAIN = {0: CENTER[1:-1], -1: LOWER[:-1], 1: UPPER[1:]}
FIRST_TILE, END_TILE = XO // XPT, (XO + CX) // XPT + 1
WINDOW_LOW = YO - REACH
WINDOW_HIGH = YO + CY - 1
UP_AT = ZO + CZ - REACH
DOWN_AT = ZO - 1
HALO = 8
GROUPS = 8
MIB = 1024 * 1024

f32 = jnp.float32
bf16 = jnp.bfloat16


def split(value):
    high = value.astype(bf16)
    return high, (value - high.astype(f32)).astype(bf16)


def dot_nt(lhs, rhs):
    return lax.dot_general(lhs, rhs, (((1,), (1,)), ((), ())), preferred_element_type=f32)


def dot_nn(lhs, rhs):
    return lax.dot_general(lhs, rhs, (((1,), (0,)), ((), ())), preferred_element_type=f32)


def other_count(gy):
    return min(gy - 1, 2)


def extra_place(brick, bricks):
    return bricks + brick // 4, 2 * (brick % 4)


def pack_kernel(shape, data_ref, cells_ref, counts_ref, out_ref):
    gx, gy, gz = shape
    slots = data_ref.shape[3]
    sources = gx * gy * gz
    lane = lax.broadcasted_iota(jnp.int32, (sources, slots), 1)
    at_row = lax.broadcasted_iota(jnp.int32, (sources, sources), 0)
    at_lane = lax.broadcasted_iota(jnp.int32, (sources, sources), 1)
    counts = jnp.where(at_row == at_lane, counts_ref[...], 0).astype(f32)
    counts = jnp.sum(counts, axis=1, keepdims=True).astype(jnp.int32)
    others = other_count(gy)
    bricks = 3 * (1 + others)
    weight = jnp.where(lane < counts, data_ref[0, 3], 0.0)
    cells = [cells_ref[0, c].astype(f32) for c in range(3)]
    channels = [data_ref[0, c] * (-0.5 * weight) for c in range(3)]
    channels += [weight] + [data_ref[0, c] for c in range(4, 7)] + cells
    blank = jnp.zeros((sources, 128 - slots), f32)
    channels = [jnp.concatenate([value, blank], axis=1) for value in channels]
    row = lax.broadcasted_iota(jnp.int32, (sources, 128), 0)
    y = (row // gz) % gy

    def moved(value, by):
        if by == 0:
            return value
        gap = jnp.zeros((abs(by), 128), f32)
        if by > 0:
            return jnp.concatenate([value[by:], gap], axis=0)
        return jnp.concatenate([gap, value[:by]], axis=0)

    def beside(value, e):
        if e == 0:
            return value
        up = jnp.where(y < gy - 1, moved(value, gz), 0.0)
        down = jnp.where(y > 0, moved(value, -gz), 0.0)
        if others == 1:
            return up + down
        return down if e == 1 else up

    by_y = [[beside(value, e) for e in range(1 + others)] for value in channels]
    lines = {}
    for b in range(bricks):
        e, o = divmod(b, 3)
        place, extra_row = extra_place(b, bricks)
        for c in range(10):
            block, line = (b, c) if c < 8 else (place, extra_row + c - 8)
            value = moved(by_y[c][e], (0, -gy * gz, gy * gz)[o])
            if block % 4:
                value = pltpu.roll(value, slots * (block % 4), 1)
            key = 8 * (block // 4) + line
            lines[key] = value if key not in lines else lines[key] + value
    for line in range(out_ref.shape[1]):
        value = lines.get(line)
        out_ref[:, line, :] = jnp.zeros((sources, 128), f32) if value is None else value


def hat(coordinate, cell, low, high):
    away = coordinate - cell
    return jnp.where(away == 0.0, low, jnp.where(away == 1.0, high, 0.0))


def hat_slope(coordinate, cell, low, high):
    away = coordinate - cell
    rising = jnp.where(away == -1.0, low, jnp.where(away == 0.0, high, 0.0))
    return rising - jnp.where(away == 1.0, low, jnp.where(away == 2.0, high, 0.0))


def split_hat(rows, cell, offset):
    spread = (16, 128)
    fill = rows.shape[0] // 16
    ends = []
    for value in (1.0 - offset, offset):
        ends.extend(split(jnp.broadcast_to(value, spread)))
    low_high, low_low, high_high, high_low = (jnp.concatenate([v] * fill, axis=0) for v in ends)
    cells = jnp.broadcast_to(cell, spread).astype(bf16)
    away = rows - jnp.concatenate([cells] * fill, axis=0)
    here, above = away == 0.0, away == 1.0
    zero = jnp.zeros(rows.shape, bf16)
    return (
        jnp.where(here, low_high, jnp.where(above, high_high, zero)),
        jnp.where(here, low_low, jnp.where(above, high_low, zero)),
    )


def row_iota(rows):
    return lax.broadcasted_iota(jnp.int32, (rows, 128), 0).astype(f32)


def stack_rows(parts, multiple):
    have = sum(part.shape[0] for part in parts)
    if have % multiple:
        parts = parts + [jnp.zeros((multiple - have % multiple, 128), f32)]
    return jnp.concatenate(parts, axis=0) if len(parts) > 1 else parts[0]


def splat_kernel(
    shape, recv_ref, fields_ref, first_ref, second_ref, own_ref,
    points, left_ref, right_ref, hx_ref, near, beside, slope,
):
    gx, gy, gz = shape
    mx, my, mz = lax.axis_index("gx"), lax.axis_index("gy"), lax.axis_index("gz")
    single = recv_ref.shape[1] * 4 == gx * gy * gz
    step = 0 if single else pl.program_id(0)
    others = other_count(gy)
    bricks = 3 * (1 + others)
    tiles = recv_ref.shape[2] // 8
    lane_part = lax.broadcasted_iota(jnp.int32, (8, 128), 1) // 32
    span = 128 * GROUPS
    written = set()

    def add(ref, place, value):
        if single and place not in written:
            written.add(place)
            ref[place] = value
        else:
            ref[place] += value

    if not single:
        @pl.when(step == 0)
        def _():
            near[...] = jnp.zeros_like(near)
            beside[...] = jnp.zeros_like(beside)

    for t in range(tiles):
        for g in range(GROUPS):
            given = [recv_ref[q, g, 8 * t : 8 * t + 8, :] for q in range(4)]
            for k in range(4):
                if 4 * t + k >= bricks + -(-bricks // 4):
                    continue
                merged = None
                for q in range(4):
                    moved = given[q] if q == k else pltpu.roll(given[q], (32 * (q - k)) % 128, 1)
                    merged = moved if merged is None else jnp.where(lane_part == q, moved, merged)
                points[4 * t + k, g] = merged
    own_ref[0] = points[0]
    own_ref[1] = points[bricks]

    z_limit = jnp.where(mz == gz - 1, CZ, CZ + 1).astype(f32)
    z_row = row_iota(CZ).astype(bf16)
    own_row = row_iota(24) + float(8 - YO)
    point_lane = lax.broadcasted_iota(jnp.int32, (128, 128), 1)
    lane_number = point_lane.astype(f32).astype(bf16)
    no_top = jnp.zeros((128, 128), bf16)

    def multiply(begin, lists, b, e, high):
        counts = [-(-len(planes) * high // 16) * 16 for planes in lists]
        size = sum(counts)
        both = dot_nn(left_ref[begin : begin + 2 * size, :], right_ref[b, 0])
        got = both[:size] + both[size:]
        got = got + dot_nn(left_ref[begin : begin + size, :], right_ref[b, 1])
        at = 0
        for c in range(3):
            for i, plane in enumerate(lists[c]):
                value = got[at + i * high : at + i * high + high]
                if e == 0:
                    add(near, (c, plane), value)
                else:
                    add(beside, (e - 1, c, plane), value)
            at += counts[c]
        if single and e == 0:
            for t in sorted({plane // XPT for plane in lists[0]}):
                unfinished[t] -= 1
                if unfinished[t] == 0:
                    finish(t)

    row8 = lax.broadcasted_iota(jnp.int32, (8, 2 * 128), 0)
    zero = jnp.zeros((8, 2 * 128), f32)

    def finish(t):
        turned = []
        for c in range(3):
            pieces = []
            for plane in range(XPT * t, XPT * t + XPT):
                if plane > UPPER[-1]:
                    pieces.append(jnp.zeros((YS, 2 * 128), f32))
                    continue
                parts = [zero] + [near[c, plane, 8 * i : 8 * i + 8, :] for i in range(3)]
                if others:
                    if others == 1:
                        value = beside[0, c, plane]
                        low_part = jnp.where(my == 0, 0.0, value)
                        high_part = jnp.where(my == 0, value, 0.0)
                    else:
                        low_part, high_part = beside[0, c, plane], beside[1, c, plane]
                    moved = pltpu.roll(low_part, 4, 0)
                    parts[0] = jnp.where(row8 >= 4, moved, 0.0)
                    parts[1] = parts[1] + jnp.where(row8 < 4, moved, 0.0)
                    parts[3] = parts[3] + high_part
                pieces.extend(parts)
            stacked = jnp.concatenate(pieces, axis=0)
            turned.append(stacked[:, :CZ].T)
            above = stacked[:, CZ:]
            n, at = divmod(3 * t + c, 128 // GROUPS)
            if at:
                above = pltpu.roll(above, GROUPS * at, 1)
            if tops[n] is not None:
                above = jnp.where(point_lane // GROUPS == at, above, tops[n])
            tops[n] = above
        fields_ref[0, t, ZO : ZO + CZ, :] = turned[0]
        slope[t, ZO + 8 : ZO + 8 + CZ, :] = turned[1]
        fields_ref[1, t, ZO : ZO + CZ, :] = turned[2]

    def finish_all():
        zero = jnp.zeros((8, 128), f32)
        sums = [jnp.sum(top.T.reshape(-1, GROUPS, 128), axis=1, keepdims=True) for top in tops]
        for t in range(XTILES):
            at = [divmod(3 * t + c, 128 // GROUPS) for c in range(3)]
            above = [sums[n][i] for n, i in at]
            below = jnp.concatenate([above[1], jnp.zeros((7, 128), f32)], axis=0)
            slope[t, 0 : ZO + 8, :] = jnp.zeros((ZO + 8, 128), f32)
            slope[t, ZO + 8 + CZ : ZO + 16 + CZ, :] = below
            slope[t, ZO + 16 + CZ : ROWS + 16, :] = zero
            for c in range(2):
                fields_ref[c, t, 0:ZO, :] = zero
                fields_ref[c, t, ZO + CZ : ROWS, :] = jnp.concatenate(
                    [above[2 * c], jnp.zeros((7, 128), f32)], axis=0
                )
            fields_ref[0, t] += slope[t, 9 : ROWS + 9, :] - slope[t, 7 : ROWS + 7, :]

    tops = [None] * -(-3 * XTILES * GROUPS // 128)
    unfinished = [
        sum(
            plane // XPT == t and (i == 0 or planes[i - 1] // XPT != t)
            for planes in (CENTER, LOWER, UPPER)
            for i, plane in enumerate(planes)
        )
        for t in range(XTILES)
    ]
    row_at = 0
    waiting = None
    for e in reversed(range(1 + others)):
        if e == 0:
            y_limit = jnp.where(my == gy - 1, CY, CY + 1).astype(f32)
            y_row = own_row
        else:
            above = my == 0 if others == 1 else jnp.bool_(e == 2)
            y_limit = jnp.where(
                jnp.logical_and(above, my + 1 == gy - 1), CY, CY + 1
            ).astype(f32)
            first = jnp.where(above, WINDOW_HIGH - YO - CY, WINDOW_LOW - YO + CY)
            y_row = row_iota(8) + first.astype(f32)
        high = y_row.shape[0]
        for o, shift, planes in ((1, -1, LOWER), (2, 1, UPPER), (0, 0, CENTER)):
            b = e * 3 + o
            place, row = extra_place(b, bricks)
            x_limit = jnp.where(mx + shift == gx - 1, CX, CX + 1).astype(f32)
            cell_x = points[b, :, 7, :]
            off_x = points[b, :, 4, :]
            low_x = 1.0 - off_x
            high_x = jnp.where(cell_x + 1.0 < x_limit, off_x, 0.0)
            first_x = planes[0] - XO - CX * shift
            hats = [
                hat(float(first_x + n - 1), cell_x, low_x, high_x) for n in range(len(planes) + 2)
            ]
            for n in range(len(planes)):
                hx_ref[b, 0, n] = hats[n + 1]
                hx_ref[b, 1, n] = hats[n + 2] - hats[n]
            cell_z, off_z = points[place, :, row + 1, :], points[b, :, 6, :]
            top = jnp.where((cell_z + 1.0 == float(CZ)) & (cell_z + 1.0 < z_limit), off_z, 0.0)
            top_columns = jnp.concatenate([top, jnp.zeros((128 - GROUPS, 128), f32)], axis=0).T
            top_high, top_low = split(top_columns)
            y_parts = []
            for g in range(GROUPS):
                main = points[b, g]
                more = points[place, g]
                cell_y, cell_z = more[row : row + 1], more[row + 1 : row + 2]
                off_y, off_z = main[5:6], main[6:7]
                at = slice(128 * g, 128 * g + 128)
                hz_high, hz_low = split_hat(z_row, cell_z, off_z)
                right_ref[b, 0, at, 0:CZ] = hz_high.T
                right_ref[b, 1, at, 0:CZ] = hz_low.T
                column = lane_number == float(g)
                right_ref[b, 0, at, CZ : CZ + 128] = jnp.where(column, top_high, no_top)
                right_ref[b, 1, at, CZ : CZ + 128] = jnp.where(column, top_low, no_top)
                high_y = jnp.where(cell_y + 1.0 < y_limit, off_y, 0.0)
                hy = hat(y_row, cell_y, 1.0 - off_y, high_y)
                dy = hat_slope(y_row, cell_y, 1.0 - off_y, high_y)
                y_parts.append((main[0:1] * hy, main[1:2] * dy, main[2:3] * hy, main[3:4] * hy))
            size = 4 if e == 0 else 12
            for start in range(0, len(planes), size):
                block = planes[start : start + size]
                lists = [block] + 2 * [tuple(p for p in block if p in PLAIN[shift])]
                counts = [-(-len(each) * high // 16) * 16 for each in lists]
                for c in range(3):
                    begin = row_at + sum(counts[:c])
                    for g in range(GROUPS):
                        part_x0, part_y1, part_z, part_w = y_parts[g]
                        at = slice(128 * g, 128 * g + 128)
                        rows = []
                        for plane in lists[c]:
                            n = plane - planes[0]
                            hx = hx_ref[b, 0, n, g : g + 1, :]
                            if c == 0:
                                dx = hx_ref[b, 1, n, g : g + 1, :]
                                rows.append(dx * part_x0 + hx * part_y1)
                            else:
                                rows.append(hx * (part_z if c == 1 else part_w))
                        main_part, rest = split(stack_rows(rows, 16))
                        left_ref[begin : begin + counts[c], at] = main_part
                        after = begin + sum(counts)
                        left_ref[after : after + counts[c], at] = rest
                if waiting is not None:
                    waiting()
                waiting = functools.partial(multiply, row_at, lists, b, e, high)
                row_at += 2 * sum(counts)
    waiting()

    if not single:
        @pl.when(step == pl.num_programs(0) - 1)
        def _():
            for t in range(XTILES):
                finish(t)
            finish_all()
    else:
        finish_all()
    for c in range(2):
        up = fields_ref[c, :, UP_AT : UP_AT + HALO, :]
        down = fields_ref[c, :, DOWN_AT : DOWN_AT + HALO, :]
        first_ref[c] = jnp.where(mz % 2 == 0, up, down)
        second_ref[c] = jnp.where(mz % 2 == 0, down, up)


def chebyshev_factors():
    half_width = 6.0 / (6.0 + base_screen)
    sigma_ratio = 1.0 / half_width
    rho_prev = half_width
    factors = []
    for _ in range(ITERS - 1):
        rho_next = 1.0 / (2.0 * sigma_ratio - rho_prev)
        factors.append((rho_next * rho_prev, 2.0 * rho_next / half_width))
        rho_prev = rho_next
    return factors


READ_PLANES = range(XPT * FIRST_TILE, XPT * END_TILE)
STRIPS = ROWS // 8
INNER = range((UP_AT - CZ + HALO + REACH + 7) // 8, (DOWN_AT + CZ - REACH) // 8)
LOW_ZONE = range(0, INNER[0] + 1)
HIGH_ZONE = range(INNER[-1], STRIPS)


def relax(shape, given, zone, wanted, work, store):
    gx, gy, gz = shape
    mx, my, mz = lax.axis_index("gx"), lax.axis_index("gy"), lax.axis_index("gz")
    first, second, base, inverse = work
    lane = lax.broadcasted_iota(jnp.int32, (8, 128), 1)
    row = lax.broadcasted_iota(jnp.int32, (8, 128), 0)
    y = lane % YS - YO + my * CY
    inside_y = (y >= 0) & (y < gy * CY)
    zero = jnp.zeros((8, 128), f32)
    end_row = 8 * len(zone) + 8
    for t in range(XTILES):
        x = lane // YS + (XPT * t - XO) + mx * CX
        inside_xy = inside_y & (x >= 0) & (x < gx * CX)
        for scratch in (first, second):
            scratch[t, 0:8, :] = zero
            scratch[t, end_row : end_row + 8, :] = zero
        for j, i in enumerate(zone):
            inside = inside_xy
            if 8 * i < ZO or 8 * i + 8 > ZO + CZ:
                z = row + (8 * i - ZO) + mz * CZ
                inside = inside & (z >= 0) & (z < gz * CZ)
            diagonal = 6.0 + base_screen + point_screen * given(1, t, i)
            inv = jnp.where(inside, 1.0 / diagonal, 0.0)
            start = given(0, t, i) * inv
            inverse[t, 8 * j : 8 * j + 8, :] = inv
            base[t, 8 * j : 8 * j + 8, :] = start
            first[t, 8 * j + 8 : 8 * j + 16, :] = start

    now, later = first, second
    factors = chebyshev_factors()
    low_part, high_part = lane < YS, lane >= 128 - YS
    for k, (keep, gain) in enumerate(factors, 1):
        last = k == len(factors)
        begin, end = k // XPT, (XO + CX + REACH - k + XPT) // XPT
        if last:
            begin, end = max(begin, FIRST_TILE), min(end, END_TILE)
        for j, i in enumerate(zone):
            if last and i not in wanted:
                continue
            at = slice(8 * j, 8 * j + 8)
            inner = slice(8 * j + 8, 8 * j + 16)
            reach = range(max(begin - 1, 0), min(end + 1, XTILES))
            here = {t: now[t, inner, :] for t in reach}
            ahead_x = {t: pltpu.roll(here[t], YS, 1) for t in reach if t < end}
            behind_x = {t: pltpu.roll(here[t], 128 - YS, 1) for t in reach if t >= begin}
            for t in range(begin, end):
                mine = here[t]
                near = now[t, 8 * j + 7 : 8 * j + 15, :] + now[t, 8 * j + 9 : 8 * j + 17, :]
                near = near + pltpu.roll(mine, 1, 1) + pltpu.roll(mine, 127, 1)
                before = ahead_x[t]
                if t > 0:
                    before = jnp.where(low_part, ahead_x[t - 1], before)
                after = behind_x[t]
                if t + 1 < XTILES:
                    after = jnp.where(high_part, behind_x[t + 1], after)
                near = near + before + after
                if k == 1:
                    ahead = (1.0 + keep) * mine + gain * (inverse[t, at, :] * near)
                else:
                    ahead = gain * (base[t, at, :] + inverse[t, at, :] * near)
                    ahead = ahead + (1.0 + keep - gain) * mine - keep * later[t, inner, :]
                if last:
                    store(t - FIRST_TILE, i, ahead)
                else:
                    later[t, inner, :] = ahead
        now, later = later, now


def read_kernel(own_ref, out_ref, hx_ref):
    y_row = row_iota(24) + float(8 - YO)
    blank = jnp.zeros((8, 128), f32)
    for chunk in range(own_ref.shape[1] // GROUPS):
        span = slice(chunk * GROUPS, chunk * GROUPS + GROUPS)
        cell_x, off_x = own_ref[0, span, 7, :], own_ref[0, span, 4, :]
        for plane in READ_PLANES:
            if 0 <= plane - XO <= CX:
                hx_ref[plane] = hat(float(plane - XO), cell_x, 1.0 - off_x, off_x)
        for g in range(GROUPS):
            off_y = own_ref[0, chunk * GROUPS + g, 5:6, :]
            hy = hat(y_row, own_ref[1, chunk * GROUPS + g, 0:1, :], 1.0 - off_y, off_y)
            at = slice(128 * g, 128 * g + 128)
            for plane in READ_PLANES:
                start = YS * (plane - XPT * FIRST_TILE)
                if 0 <= plane - XO <= CX:
                    rows = jnp.concatenate([blank, hx_ref[plane, g : g + 1, :] * hy], axis=0)
                    high, low = split(rows)
                else:
                    high = jnp.zeros((YS, 128), bf16)
                    low = high
                out_ref[chunk, 0, start : start + YS, at] = high
                out_ref[chunk, 1, start : start + YS, at] = low


def inner_kernel(shape, fields_ref, inner_ref, *work):
    def given(c, t, i):
        return fields_ref[c, t, 8 * i : 8 * i + 8, :]

    def store(t, i, value):
        at = 8 * (i - INNER[0])
        inner_ref[t, at : at + 8, :] = value

    relax(shape, given, range(INNER[0] - 1, INNER[-1] + 2), INNER, work, store)


def solve_kernel(
    shape, fields_ref, first_ref, second_ref, own_ref, inner_ref, read_ref,
    indicator_ref, values_ref,
    edge, total, first, second, base, inverse, first_high, second_high, base_high, inverse_high,
):
    edge[...] = jnp.zeros_like(edge)
    low_at, high_at = UP_AT - CZ, DOWN_AT + CZ - (ROWS - 16)
    even = lax.axis_index("gz") % 2 == 0
    got_first, got_second = first_ref[...], second_ref[...]
    edge[0, :, :, low_at : low_at + HALO, :] = jnp.where(even, got_second, got_first)
    edge[1, :, :, high_at : high_at + HALO, :] = jnp.where(even, got_first, got_second)

    def given(c, t, i):
        value = fields_ref[c, t, 8 * i : 8 * i + 8, :]
        if i < 2:
            value = value + edge[0, c, t, 8 * i : 8 * i + 8, :]
        from_end = i - (STRIPS - 2)
        if from_end >= 0:
            value = value + edge[1, c, t, 8 * from_end : 8 * from_end + 8, :]
        return value

    def store(t, i, value):
        total[t, 8 * i : 8 * i + 8, :] = value

    inner_rows = slice(8 * INNER[0], 8 * INNER[-1] + 8)
    for t in range(END_TILE - FIRST_TILE):
        total[t, 0:8, :] = jnp.zeros((8, 128), f32)
        total[t, inner_rows, :] = inner_ref[t]
    low_wanted = range(1, INNER[0])
    high_wanted = range(INNER[-1] + 1, STRIPS)
    relax(shape, given, LOW_ZONE, low_wanted, (first, second, base, inverse), store)
    relax(
        shape, given, HIGH_ZONE, high_wanted,
        (first_high, second_high, base_high, inverse_high), store,
    )

    parts = [split(total[t - FIRST_TILE]) for t in range(FIRST_TILE, END_TILE)]
    u_high = jnp.concatenate([part[0] for part in parts], axis=1)
    u_low = jnp.concatenate([part[1] for part in parts], axis=1)
    u_both = jnp.concatenate([u_high, u_low], axis=0)
    z_row = row_iota(ROWS) - float(ZO)
    groups = own_ref.shape[1]
    for chunk in range(groups // GROUPS):
        got = dot_nn(u_both, read_ref[chunk, 0])
        got = got[:ROWS] + got[ROWS:] + dot_nn(u_high, read_ref[chunk, 1])
        rows = []
        for g in range(GROUPS):
            main = own_ref[0, chunk * GROUPS + g]
            off_z = main[6:7]
            hz = hat(z_row, own_ref[1, chunk * GROUPS + g, 1:2, :], 1.0 - off_z, off_z)
            value = jnp.sum(hz * got[:, 128 * g : 128 * g + 128], axis=0, keepdims=True)
            rows.append(jnp.where(main[3:4] > 0.0, value, 0.0))
        values = jnp.concatenate(rows, axis=0)
        for q in range(4):
            moved = values if q == 0 else pltpu.roll(values, 128 - 32 * q, 1)
            start = q * groups + chunk * GROUPS
            values_ref[start : start + GROUPS, :] = moved[:, 0:32]

    for t in range(FIRST_TILE, END_TILE):
        turned = total[t - FIRST_TILE, ZO : ZO + CZ, :].T
        for i in range(XPT):
            plane = XPT * t + i - XO
            if 0 <= plane < CX:
                indicator_ref[plane] = turned[YS * i + YO : YS * i + YO + CY, :]


def work_shapes(strips):
    padded = pltpu.VMEM((XTILES, 8 * strips + 16, 128), f32)
    return [padded, padded] + 2 * [pltpu.VMEM((XTILES, 8 * strips, 128), f32)]


def on_device(shape, point_data, point_cells, send_counts):
    gx, gy, gz = shape
    sources = gx * gy * gz
    slots = point_data.shape[3]
    bricks = 3 * (1 + other_count(gy))
    rows = 8 * -(-(bricks + -(-bricks // 4)) // 4)
    groups = sources // 4
    whole = pl.BlockSpec(memory_space=pltpu.VMEM)

    outgoing = pl.pallas_call(
        functools.partial(pack_kernel, shape),
        out_shape=jax.ShapeDtypeStruct((sources, rows, 128), f32),
        in_specs=[whole] * 3,
        out_specs=whole,
        compiler_params=pltpu.CompilerParams(vmem_limit_bytes=56 * MIB),
        name="pack_points",
    )(
        jnp.transpose(point_data, (0, 2, 1, 3)),
        jnp.transpose(point_cells, (0, 2, 1, 3)),
        send_counts,
    )

    arrived = lax.all_to_all(outgoing, AXES, split_axis=0, concat_axis=0, tiled=True)
    arrived = arrived.reshape(4, groups, rows, 128)

    others = other_count(gy)
    lines = 0
    for planes in (CENTER, LOWER, UPPER):
        for high, size in ((24, 4),) + ((8, 12),) * others:
            for start in range(0, len(planes), size):
                count = min(size, len(planes) - start)
                lines += 6 * 16 * -(-count * high // 16)
    edge_shape = jax.ShapeDtypeStruct((2, XTILES, HALO, 128), f32)
    steps = groups // GROUPS
    if steps == 1:
        blocks = {"in_specs": [whole], "out_specs": (whole,) * 4}
    else:
        blocks = {
            "grid": (steps,),
            "in_specs": [pl.BlockSpec((4, GROUPS, rows, 128), lambda s: (0, s, 0, 0))],
            "out_specs": (
                pl.BlockSpec((2, XTILES, ROWS, 128), lambda s: (0, 0, 0, 0)),
                pl.BlockSpec((2, XTILES, HALO, 128), lambda s: (0, 0, 0, 0)),
                pl.BlockSpec((2, XTILES, HALO, 128), lambda s: (0, 0, 0, 0)),
                pl.BlockSpec((2, GROUPS, 8, 128), lambda s: (0, s, 0, 0)),
            ),
        }
    fields, first, second, own = pl.pallas_call(
        functools.partial(splat_kernel, shape),
        out_shape=(
            jax.ShapeDtypeStruct((2, XTILES, ROWS, 128), f32), edge_shape, edge_shape,
            jax.ShapeDtypeStruct((2, groups, 8, 128), f32),
        ),
        **blocks,
        scratch_shapes=[
            pltpu.VMEM((rows // 2, GROUPS, 8, 128), f32),
            pltpu.VMEM((lines, 128 * GROUPS), bf16),
            pltpu.VMEM((bricks, 2, 128 * GROUPS, 2 * 128), bf16),
            pltpu.VMEM((bricks, 2, len(CENTER), GROUPS, 128), f32),
            pltpu.VMEM((3, XPT * XTILES, 24, 2 * 128), f32),
            pltpu.VMEM((max(others, 1), 3, XPT * XTILES, 8, 2 * 128), f32),
            pltpu.VMEM((XTILES, ROWS + 16, 128), f32),
        ],
        compiler_params=pltpu.CompilerParams(vmem_limit_bytes=36 * MIB),
        name="splat_points",
    )(arrived)

    def swapped(edge, start):
        pairs = [(i, i + 1) for i in range(start, gz - 1, 2)]
        return lax.ppermute(edge, "gz", pairs + [(j, i) for i, j in pairs])

    depth = 128 * (END_TILE - FIRST_TILE)
    tiles = END_TILE - FIRST_TILE
    got_first = swapped(first, 0)
    read = pl.pallas_call(
        read_kernel,
        out_shape=jax.ShapeDtypeStruct((steps, 2, depth, 128 * GROUPS), bf16),
        in_specs=[whole],
        out_specs=whole,
        scratch_shapes=[pltpu.VMEM((XPT * END_TILE, GROUPS, 128), f32)],
        compiler_params=pltpu.CompilerParams(vmem_limit_bytes=24 * MIB),
        cost_estimate=pl.CostEstimate(
            flops=8 * depth * 128 * groups, bytes_accessed=4 * depth * 128 * groups, transcendentals=0
        ),
        name="read_operand",
    )(own)
    second, read = lax.optimization_barrier((second, read))
    got_second = swapped(second, 1)
    inner = pl.pallas_call(
        functools.partial(inner_kernel, shape),
        out_shape=jax.ShapeDtypeStruct((tiles, 8 * len(INNER), 128), f32),
        in_specs=[whole],
        out_specs=whole,
        scratch_shapes=work_shapes(len(INNER) + 2),
        compiler_params=pltpu.CompilerParams(vmem_limit_bytes=24 * MIB),
        cost_estimate=pl.CostEstimate(
            flops=70 * ROWS * 128 * XTILES, bytes_accessed=8 * ROWS * 128 * XTILES, transcendentals=0
        ),
        name="solve_inner",
    )(fields)

    indicator, values = pl.pallas_call(
        functools.partial(solve_kernel, shape),
        out_shape=(
            jax.ShapeDtypeStruct((CX, CY, CZ), f32),
            jax.ShapeDtypeStruct((sources, slots), f32),
        ),
        in_specs=[whole] * 6,
        out_specs=(whole, whole),
        scratch_shapes=[
            pltpu.VMEM((2, 2, XTILES, 16, 128), f32),
            pltpu.VMEM((tiles, ROWS, 128), f32),
        ]
        + work_shapes(len(LOW_ZONE))
        + work_shapes(len(HIGH_ZONE)),
        compiler_params=pltpu.CompilerParams(vmem_limit_bytes=24 * MIB),
        name="solve_and_read",
    )(fields, got_first, got_second, own, inner, read)

    returned = lax.all_to_all(
        values.reshape(1, sources, slots), AXES, split_axis=1, concat_axis=1, tiled=True
    )
    return indicator, returned


def solution(mesh):
    shape = tuple(mesh.shape[axis] for axis in AXES)
    in_specs = (
        P(AXES, None, None, None),
        P(AXES, None, None, None),
        P(AXES, None),
    )
    out_specs = (P("gx", "gy", "gz"), P(AXES, None, None))
    return jax.shard_map(
        functools.partial(on_device, shape),
        mesh=mesh,
        in_specs=in_specs,
        out_specs=out_specs,
        check_vma=False,
    )
```

```python
import functools

import jax
import jax.numpy as jnp
from jax import lax
from jax.experimental import pallas as pl
from jax.experimental.pallas import tpu as pltpu
from jax.sharding import PartitionSpec as P

CX = 16
CY = 16
CZ = 128
ITERS = 6

base_screen = 0.25
point_screen = 4.0

AXES = ("gx", "gy", "gz")
REACH = ITERS - 1
XO = REACH
YO = 9
ZO = 8
YS = 32
XPT = 128 // YS
XTILES = -(-(CX + 2 * REACH + 1) // XPT)
ROWS = CZ + 16
CENTER = tuple(range(XO - 1, XO + CX + 2))
LOWER = tuple(range(0, XO + 2))
UPPER = tuple(range(XO + CX - 1, XO + CX + REACH + 1))
PLAIN = {0: CENTER[1:-1], -1: LOWER[:-1], 1: UPPER[1:]}
FIRST_TILE, END_TILE = XO // XPT, (XO + CX) // XPT + 1
WINDOW_LOW = YO - REACH
WINDOW_HIGH = YO + CY - 1
UP_AT = ZO + CZ - REACH
DOWN_AT = ZO - 1
HALO = 8
GROUPS = 8
MIB = 1024 * 1024

f32 = jnp.float32
bf16 = jnp.bfloat16


def split(value):
    high = value.astype(bf16)
    return high, (value - high.astype(f32)).astype(bf16)


def dot_nt(lhs, rhs):
    return lax.dot_general(lhs, rhs, (((1,), (1,)), ((), ())), preferred_element_type=f32)


def dot_nn(lhs, rhs):
    return lax.dot_general(lhs, rhs, (((1,), (0,)), ((), ())), preferred_element_type=f32)


def other_count(gy):
    return min(gy - 1, 2)


def extra_place(brick, bricks):
    return bricks + brick // 4, 2 * (brick % 4)


def pack_kernel(shape, data_ref, cells_ref, counts_ref, out_ref):
    gx, gy, gz = shape
    slots = data_ref.shape[3]
    sources = gx * gy * gz
    lane = lax.broadcasted_iota(jnp.int32, (sources, slots), 1)
    at_row = lax.broadcasted_iota(jnp.int32, (sources, sources), 0)
    at_lane = lax.broadcasted_iota(jnp.int32, (sources, sources), 1)
    counts = jnp.where(at_row == at_lane, counts_ref[...], 0).astype(f32)
    counts = jnp.sum(counts, axis=1, keepdims=True).astype(jnp.int32)
    others = other_count(gy)
    bricks = 3 * (1 + others)
    weight = jnp.where(lane < counts, data_ref[0, 3], 0.0)
    cells = [cells_ref[0, c].astype(f32) for c in range(3)]
    channels = [data_ref[0, c] * (-0.5 * weight) for c in range(3)]
    channels += [weight] + [data_ref[0, c] for c in range(4, 7)] + cells
    blank = jnp.zeros((sources, 128 - slots), f32)
    channels = [jnp.concatenate([value, blank], axis=1) for value in channels]
    row = lax.broadcasted_iota(jnp.int32, (sources, 128), 0)
    y = (row // gz) % gy

    def moved(value, by):
        if by == 0:
            return value
        gap = jnp.zeros((abs(by), 128), f32)
        if by > 0:
            return jnp.concatenate([value[by:], gap], axis=0)
        return jnp.concatenate([gap, value[:by]], axis=0)

    def beside(value, e):
        if e == 0:
            return value
        up = jnp.where(y < gy - 1, moved(value, gz), 0.0)
        down = jnp.where(y > 0, moved(value, -gz), 0.0)
        if others == 1:
            return up + down
        return down if e == 1 else up

    by_y = [[beside(value, e) for e in range(1 + others)] for value in channels]
    lines = {}
    for b in range(bricks):
        e, o = divmod(b, 3)
        place, extra_row = extra_place(b, bricks)
        for c in range(10):
            block, line = (b, c) if c < 8 else (place, extra_row + c - 8)
            value = moved(by_y[c][e], (0, -gy * gz, gy * gz)[o])
            if block % 4:
                value = pltpu.roll(value, slots * (block % 4), 1)
            key = 8 * (block // 4) + line
            lines[key] = value if key not in lines else lines[key] + value
    for line in range(out_ref.shape[1]):
        value = lines.get(line)
        out_ref[:, line, :] = jnp.zeros((sources, 128), f32) if value is None else value


def hat(coordinate, cell, low, high):
    away = coordinate - cell
    return jnp.where(away == 0.0, low, jnp.where(away == 1.0, high, 0.0))


def hat_slope(coordinate, cell, low, high):
    away = coordinate - cell
    rising = jnp.where(away == -1.0, low, jnp.where(away == 0.0, high, 0.0))
    return rising - jnp.where(away == 1.0, low, jnp.where(away == 2.0, high, 0.0))


def split_hat(rows, cell, offset):
    spread = (16, 128)
    fill = rows.shape[0] // 16
    ends = []
    for value in (1.0 - offset, offset):
        ends.extend(split(jnp.broadcast_to(value, spread)))
    low_high, low_low, high_high, high_low = (jnp.concatenate([v] * fill, axis=0) for v in ends)
    cells = jnp.broadcast_to(cell, spread).astype(bf16)
    away = rows - jnp.concatenate([cells] * fill, axis=0)
    here, above = away == 0.0, away == 1.0
    zero = jnp.zeros(rows.shape, bf16)
    return (
        jnp.where(here, low_high, jnp.where(above, high_high, zero)),
        jnp.where(here, low_low, jnp.where(above, high_low, zero)),
    )


def row_iota(rows):
    return lax.broadcasted_iota(jnp.int32, (rows, 128), 0).astype(f32)


def stack_rows(parts, multiple):
    have = sum(part.shape[0] for part in parts)
    if have % multiple:
        parts = parts + [jnp.zeros((multiple - have % multiple, 128), f32)]
    return jnp.concatenate(parts, axis=0) if len(parts) > 1 else parts[0]


def splat_kernel(
    shape, recv_ref, fields_ref, first_ref, second_ref, own_ref,
    points, left_ref, right_ref, hx_ref, near, beside, slope,
):
    gx, gy, gz = shape
    mx, my, mz = lax.axis_index("gx"), lax.axis_index("gy"), lax.axis_index("gz")
    single = recv_ref.shape[1] * 4 == gx * gy * gz
    step = 0 if single else pl.program_id(0)
    others = other_count(gy)
    bricks = 3 * (1 + others)
    tiles = recv_ref.shape[2] // 8
    lane_part = lax.broadcasted_iota(jnp.int32, (8, 128), 1) // 32
    span = 128 * GROUPS
    written = set()

    def add(ref, place, value):
        if single and place not in written:
            written.add(place)
            ref[place] = value
        else:
            ref[place] += value

    if not single:
        @pl.when(step == 0)
        def _():
            near[...] = jnp.zeros_like(near)
            beside[...] = jnp.zeros_like(beside)

    for t in range(tiles):
        for g in range(GROUPS):
            given = [recv_ref[q, g, 8 * t : 8 * t + 8, :] for q in range(4)]
            for k in range(4):
                if 4 * t + k >= bricks + -(-bricks // 4):
                    continue
                merged = None
                for q in range(4):
                    moved = given[q] if q == k else pltpu.roll(given[q], (32 * (q - k)) % 128, 1)
                    merged = moved if merged is None else jnp.where(lane_part == q, moved, merged)
                points[4 * t + k, g] = merged
    own_ref[0] = points[0]
    own_ref[1] = points[bricks]

    z_limit = jnp.where(mz == gz - 1, CZ, CZ + 1).astype(f32)
    z_row = row_iota(CZ).astype(bf16)
    own_row = row_iota(24) + float(8 - YO)
    point_lane = lax.broadcasted_iota(jnp.int32, (128, 128), 1)
    lane_number = point_lane.astype(f32).astype(bf16)
    no_top = jnp.zeros((128, 128), bf16)

    def multiply(begin, lists, b, e, high):
        counts = [-(-len(planes) * high // 16) * 16 for planes in lists]
        size = sum(counts)
        both = dot_nn(left_ref[begin : begin + 2 * size, :], right_ref[b, 0])
        got = both[:size] + both[size:]
        got = got + dot_nn(left_ref[begin : begin + size, :], right_ref[b, 1])
        at = 0
        for c in range(3):
            for i, plane in enumerate(lists[c]):
                value = got[at + i * high : at + i * high + high]
                if e == 0:
                    add(near, (c, plane), value)
                else:
                    add(beside, (e - 1, c, plane), value)
            at += counts[c]
        if single and e == 0:
            for t in sorted({plane // XPT for plane in lists[0]}):
                unfinished[t] -= 1
                if unfinished[t] == 0:
                    finish(t)

    row8 = lax.broadcasted_iota(jnp.int32, (8, 2 * 128), 0)
    zero = jnp.zeros((8, 2 * 128), f32)

    def finish(t):
        turned = []
        for c in range(3):
            pieces = []
            for plane in range(XPT * t, XPT * t + XPT):
                if plane > UPPER[-1]:
                    pieces.append(jnp.zeros((YS, 2 * 128), f32))
                    continue
                parts = [zero] + [near[c, plane, 8 * i : 8 * i + 8, :] for i in range(3)]
                if others:
                    if others == 1:
                        value = beside[0, c, plane]
                        low_part = jnp.where(my == 0, 0.0, value)
                        high_part = jnp.where(my == 0, value, 0.0)
                    else:
                        low_part, high_part = beside[0, c, plane], beside[1, c, plane]
                    moved = pltpu.roll(low_part, 4, 0)
                    parts[0] = jnp.where(row8 >= 4, moved, 0.0)
                    parts[1] = parts[1] + jnp.where(row8 < 4, moved, 0.0)
                    parts[3] = parts[3] + high_part
                pieces.extend(parts)
            stacked = jnp.concatenate(pieces, axis=0)
            turned.append(stacked[:, :CZ].T)
            above = stacked[:, CZ:]
            n, at = divmod(3 * t + c, 128 // GROUPS)
            if at:
                above = pltpu.roll(above, GROUPS * at, 1)
            if tops[n] is not None:
                above = jnp.where(point_lane // GROUPS == at, above, tops[n])
            tops[n] = above
        fields_ref[0, t, ZO : ZO + CZ, :] = turned[0]
        slope[t, ZO + 8 : ZO + 8 + CZ, :] = turned[1]
        fields_ref[1, t, ZO : ZO + CZ, :] = turned[2]

    def finish_all():
        zero = jnp.zeros((8, 128), f32)
        sums = [jnp.sum(top.T.reshape(-1, GROUPS, 128), axis=1, keepdims=True) for top in tops]
        for t in range(XTILES):
            at = [divmod(3 * t + c, 128 // GROUPS) for c in range(3)]
            above = [sums[n][i] for n, i in at]
            below = jnp.concatenate([above[1], jnp.zeros((7, 128), f32)], axis=0)
            slope[t, 0 : ZO + 8, :] = jnp.zeros((ZO + 8, 128), f32)
            slope[t, ZO + 8 + CZ : ZO + 16 + CZ, :] = below
            slope[t, ZO + 16 + CZ : ROWS + 16, :] = zero
            for c in range(2):
                fields_ref[c, t, 0:ZO, :] = zero
                fields_ref[c, t, ZO + CZ : ROWS, :] = jnp.concatenate(
                    [above[2 * c], jnp.zeros((7, 128), f32)], axis=0
                )
            fields_ref[0, t] += slope[t, 9 : ROWS + 9, :] - slope[t, 7 : ROWS + 7, :]

    tops = [None] * -(-3 * XTILES * GROUPS // 128)
    unfinished = [
        sum(
            plane // XPT == t and (i == 0 or planes[i - 1] // XPT != t)
            for planes in (CENTER, LOWER, UPPER)
            for i, plane in enumerate(planes)
        )
        for t in range(XTILES)
    ]
    row_at = 0
    waiting = None
    for e in reversed(range(1 + others)):
        if e == 0:
            y_limit = jnp.where(my == gy - 1, CY, CY + 1).astype(f32)
            y_row = own_row
        else:
            above = my == 0 if others == 1 else jnp.bool_(e == 2)
            y_limit = jnp.where(
                jnp.logical_and(above, my + 1 == gy - 1), CY, CY + 1
            ).astype(f32)
            first = jnp.where(above, WINDOW_HIGH - YO - CY, WINDOW_LOW - YO + CY)
            y_row = row_iota(8) + first.astype(f32)
        high = y_row.shape[0]
        for o, shift, planes in ((1, -1, LOWER), (2, 1, UPPER), (0, 0, CENTER)):
            b = e * 3 + o
            place, row = extra_place(b, bricks)
            x_limit = jnp.where(mx + shift == gx - 1, CX, CX + 1).astype(f32)
            cell_x = points[b, :, 7, :]
            off_x = points[b, :, 4, :]
            low_x = 1.0 - off_x
            high_x = jnp.where(cell_x + 1.0 < x_limit, off_x, 0.0)
            first_x = planes[0] - XO - CX * shift
            hats = [
                hat(float(first_x + n - 1), cell_x, low_x, high_x) for n in range(len(planes) + 2)
            ]
            for n in range(len(planes)):
                hx_ref[b, 0, n] = hats[n + 1]
                hx_ref[b, 1, n] = hats[n + 2] - hats[n]
            cell_z, off_z = points[place, :, row + 1, :], points[b, :, 6, :]
            top = jnp.where((cell_z + 1.0 == float(CZ)) & (cell_z + 1.0 < z_limit), off_z, 0.0)
            top_columns = jnp.concatenate([top, jnp.zeros((128 - GROUPS, 128), f32)], axis=0).T
            top_high, top_low = split(top_columns)
            y_parts = []
            for g in range(GROUPS):
                main = points[b, g]
                more = points[place, g]
                cell_y, cell_z = more[row : row + 1], more[row + 1 : row + 2]
                off_y, off_z = main[5:6], main[6:7]
                at = slice(128 * g, 128 * g + 128)
                hz_high, hz_low = split_hat(z_row, cell_z, off_z)
                right_ref[b, 0, at, 0:CZ] = hz_high.T
                right_ref[b, 1, at, 0:CZ] = hz_low.T
                column = lane_number == float(g)
                right_ref[b, 0, at, CZ : CZ + 128] = jnp.where(column, top_high, no_top)
                right_ref[b, 1, at, CZ : CZ + 128] = jnp.where(column, top_low, no_top)
                high_y = jnp.where(cell_y + 1.0 < y_limit, off_y, 0.0)
                hy = hat(y_row, cell_y, 1.0 - off_y, high_y)
                dy = hat_slope(y_row, cell_y, 1.0 - off_y, high_y)
                y_parts.append((main[0:1] * hy, main[1:2] * dy, main[2:3] * hy, main[3:4] * hy))
            size = 4 if e == 0 else 12
            for start in range(0, len(planes), size):
                block = planes[start : start + size]
                lists = [block] + 2 * [tuple(p for p in block if p in PLAIN[shift])]
                counts = [-(-len(each) * high // 16) * 16 for each in lists]
                for c in range(3):
                    begin = row_at + sum(counts[:c])
                    for g in range(GROUPS):
                        part_x0, part_y1, part_z, part_w = y_parts[g]
                        at = slice(128 * g, 128 * g + 128)
                        rows = []
                        for plane in lists[c]:
                            n = plane - planes[0]
                            hx = hx_ref[b, 0, n, g : g + 1, :]
                            if c == 0:
                                dx = hx_ref[b, 1, n, g : g + 1, :]
                                rows.append(dx * part_x0 + hx * part_y1)
                            else:
                                rows.append(hx * (part_z if c == 1 else part_w))
                        main_part, rest = split(stack_rows(rows, 16))
                        left_ref[begin : begin + counts[c], at] = main_part
                        after = begin + sum(counts)
                        left_ref[after : after + counts[c], at] = rest
                if waiting is not None:
                    waiting()
                waiting = functools.partial(multiply, row_at, lists, b, e, high)
                row_at += 2 * sum(counts)
    waiting()

    if not single:
        @pl.when(step == pl.num_programs(0) - 1)
        def _():
            for t in range(XTILES):
                finish(t)
            finish_all()
    else:
        finish_all()
    for c in range(2):
        up = fields_ref[c, :, UP_AT : UP_AT + HALO, :]
        down = fields_ref[c, :, DOWN_AT : DOWN_AT + HALO, :]
        first_ref[c] = jnp.where(mz % 2 == 0, up, down)
        second_ref[c] = jnp.where(mz % 2 == 0, down, up)


def chebyshev_factors():
    half_width = 6.0 / (6.0 + base_screen)
    sigma_ratio = 1.0 / half_width
    rho_prev = half_width
    factors = []
    for _ in range(ITERS - 1):
        rho_next = 1.0 / (2.0 * sigma_ratio - rho_prev)
        factors.append((rho_next * rho_prev, 2.0 * rho_next / half_width))
        rho_prev = rho_next
    return factors


READ_PLANES = range(XPT * FIRST_TILE, XPT * END_TILE)
STRIPS = ROWS // 8
INNER = range((UP_AT - CZ + HALO + REACH + 7) // 8, (DOWN_AT + CZ - REACH) // 8)
LOW_ZONE = range(0, INNER[0] + 1)
HIGH_ZONE = range(INNER[-1], STRIPS)


def relax(shape, given, zone, wanted, work, store):
    gx, gy, gz = shape
    mx, my, mz = lax.axis_index("gx"), lax.axis_index("gy"), lax.axis_index("gz")
    first, second, base, inverse = work
    lane = lax.broadcasted_iota(jnp.int32, (8, 128), 1)
    row = lax.broadcasted_iota(jnp.int32, (8, 128), 0)
    y = lane % YS - YO + my * CY
    inside_y = (y >= 0) & (y < gy * CY)
    zero = jnp.zeros((8, 128), f32)
    end_row = 8 * len(zone) + 8
    for t in range(XTILES):
        x = lane // YS + (XPT * t - XO) + mx * CX
        inside_xy = inside_y & (x >= 0) & (x < gx * CX)
        for scratch in (first, second):
            scratch[t, 0:8, :] = zero
            scratch[t, end_row : end_row + 8, :] = zero
        for j, i in enumerate(zone):
            inside = inside_xy
            if 8 * i < ZO or 8 * i + 8 > ZO + CZ:
                z = row + (8 * i - ZO) + mz * CZ
                inside = inside & (z >= 0) & (z < gz * CZ)
            diagonal = 6.0 + base_screen + point_screen * given(1, t, i)
            inv = jnp.where(inside, 1.0 / diagonal, 0.0)
            start = given(0, t, i) * inv
            inverse[t, 8 * j : 8 * j + 8, :] = inv
            base[t, 8 * j : 8 * j + 8, :] = start
            first[t, 8 * j + 8 : 8 * j + 16, :] = start

    now, later = first, second
    factors = chebyshev_factors()
    low_part, high_part = lane < YS, lane >= 128 - YS
    for k, (keep, gain) in enumerate(factors, 1):
        last = k == len(factors)
        begin, end = k // XPT, (XO + CX + REACH - k + XPT) // XPT
        if last:
            begin, end = max(begin, FIRST_TILE), min(end, END_TILE)
        for j, i in enumerate(zone):
            if last and i not in wanted:
                continue
            at = slice(8 * j, 8 * j + 8)
            inner = slice(8 * j + 8, 8 * j + 16)
            reach = range(max(begin - 1, 0), min(end + 1, XTILES))
            here = {t: now[t, inner, :] for t in reach}
            ahead_x = {t: pltpu.roll(here[t], YS, 1) for t in reach if t < end}
            behind_x = {t: pltpu.roll(here[t], 128 - YS, 1) for t in reach if t >= begin}
            for t in range(begin, end):
                mine = here[t]
                near = now[t, 8 * j + 7 : 8 * j + 15, :] + now[t, 8 * j + 9 : 8 * j + 17, :]
                near = near + pltpu.roll(mine, 1, 1) + pltpu.roll(mine, 127, 1)
                before = ahead_x[t]
                if t > 0:
                    before = jnp.where(low_part, ahead_x[t - 1], before)
                after = behind_x[t]
                if t + 1 < XTILES:
                    after = jnp.where(high_part, behind_x[t + 1], after)
                near = near + before + after
                if k == 1:
                    ahead = (1.0 + keep) * mine + gain * (inverse[t, at, :] * near)
                else:
                    ahead = gain * (base[t, at, :] + inverse[t, at, :] * near)
                    ahead = ahead + (1.0 + keep - gain) * mine - keep * later[t, inner, :]
                if last:
                    store(t - FIRST_TILE, i, ahead)
                else:
                    later[t, inner, :] = ahead
        now, later = later, now


def inner_kernel(shape, fields_ref, own_ref, out_ref, inner_ref, hx_ref, *work):
    y_row = row_iota(24) + float(8 - YO)
    blank = jnp.zeros((8, 128), f32)
    for chunk in range(own_ref.shape[1] // GROUPS):
        span = slice(chunk * GROUPS, chunk * GROUPS + GROUPS)
        cell_x, off_x = own_ref[0, span, 7, :], own_ref[0, span, 4, :]
        for plane in READ_PLANES:
            if 0 <= plane - XO <= CX:
                hx_ref[plane] = hat(float(plane - XO), cell_x, 1.0 - off_x, off_x)
        for g in range(GROUPS):
            off_y = own_ref[0, chunk * GROUPS + g, 5:6, :]
            hy = hat(y_row, own_ref[1, chunk * GROUPS + g, 0:1, :], 1.0 - off_y, off_y)
            at = slice(128 * g, 128 * g + 128)
            for plane in READ_PLANES:
                start = YS * (plane - XPT * FIRST_TILE)
                if 0 <= plane - XO <= CX:
                    rows = jnp.concatenate([blank, hx_ref[plane, g : g + 1, :] * hy], axis=0)
                    high, low = split(rows)
                else:
                    high = jnp.zeros((YS, 128), bf16)
                    low = high
                out_ref[chunk, 0, start : start + YS, at] = high
                out_ref[chunk, 1, start : start + YS, at] = low

    def given(c, t, i):
        return fields_ref[c, t, 8 * i : 8 * i + 8, :]

    def store(t, i, value):
        at = 8 * (i - INNER[0])
        inner_ref[t, at : at + 8, :] = value

    relax(shape, given, range(INNER[0] - 1, INNER[-1] + 2), INNER, work, store)


def solve_kernel(
    shape, fields_ref, first_ref, second_ref, own_ref, inner_ref, read_ref,
    indicator_ref, values_ref,
    edge, total, first, second, base, inverse, first_high, second_high, base_high, inverse_high,
):
    edge[...] = jnp.zeros_like(edge)
    low_at, high_at = UP_AT - CZ, DOWN_AT + CZ - (ROWS - 16)
    mz = lax.axis_index("gz")
    even = mz % 2 == 0
    got_first, got_second = first_ref[...], second_ref[...]
    from_low = jnp.where(even, got_second, got_first)
    from_high = jnp.where(even, got_first, got_second)
    edge[0, :, :, low_at : low_at + HALO, :] = jnp.where(mz > 0, from_low, 0.0)
    edge[1, :, :, high_at : high_at + HALO, :] = jnp.where(mz < shape[2] - 1, from_high, 0.0)

    def given(c, t, i):
        value = fields_ref[c, t, 8 * i : 8 * i + 8, :]
        if i < 2:
            value = value + edge[0, c, t, 8 * i : 8 * i + 8, :]
        from_end = i - (STRIPS - 2)
        if from_end >= 0:
            value = value + edge[1, c, t, 8 * from_end : 8 * from_end + 8, :]
        return value

    def store(t, i, value):
        total[t, 8 * i : 8 * i + 8, :] = value

    inner_rows = slice(8 * INNER[0], 8 * INNER[-1] + 8)
    for t in range(END_TILE - FIRST_TILE):
        total[t, 0:8, :] = jnp.zeros((8, 128), f32)
        total[t, inner_rows, :] = inner_ref[t]
    low_wanted = range(1, INNER[0])
    high_wanted = range(INNER[-1] + 1, STRIPS)
    relax(shape, given, LOW_ZONE, low_wanted, (first, second, base, inverse), store)
    relax(
        shape, given, HIGH_ZONE, high_wanted,
        (first_high, second_high, base_high, inverse_high), store,
    )

    parts = [split(total[t - FIRST_TILE]) for t in range(FIRST_TILE, END_TILE)]
    u_high = jnp.concatenate([part[0] for part in parts], axis=1)
    u_low = jnp.concatenate([part[1] for part in parts], axis=1)
    u_both = jnp.concatenate([u_high, u_low], axis=0)
    z_row = row_iota(ROWS) - float(ZO)
    groups = own_ref.shape[1]
    for chunk in range(groups // GROUPS):
        got = dot_nn(u_both, read_ref[chunk, 0])
        got = got[:ROWS] + got[ROWS:] + dot_nn(u_high, read_ref[chunk, 1])
        rows = []
        for g in range(GROUPS):
            main = own_ref[0, chunk * GROUPS + g]
            off_z = main[6:7]
            hz = hat(z_row, own_ref[1, chunk * GROUPS + g, 1:2, :], 1.0 - off_z, off_z)
            value = jnp.sum(hz * got[:, 128 * g : 128 * g + 128], axis=0, keepdims=True)
            rows.append(jnp.where(main[3:4] > 0.0, value, 0.0))
        values = jnp.concatenate(rows, axis=0)
        for q in range(4):
            moved = values if q == 0 else pltpu.roll(values, 128 - 32 * q, 1)
            start = q * groups + chunk * GROUPS
            values_ref[start : start + GROUPS, :] = moved[:, 0:32]

    for t in range(FIRST_TILE, END_TILE):
        turned = total[t - FIRST_TILE, ZO : ZO + CZ, :].T
        for i in range(XPT):
            plane = XPT * t + i - XO
            if 0 <= plane < CX:
                indicator_ref[plane] = turned[YS * i + YO : YS * i + YO + CY, :]


def work_shapes(strips):
    padded = pltpu.VMEM((XTILES, 8 * strips + 16, 128), f32)
    return [padded, padded] + 2 * [pltpu.VMEM((XTILES, 8 * strips, 128), f32)]


def on_device(shape, point_data, point_cells, send_counts):
    gx, gy, gz = shape
    sources = gx * gy * gz
    slots = point_data.shape[3]
    bricks = 3 * (1 + other_count(gy))
    rows = 8 * -(-(bricks + -(-bricks // 4)) // 4)
    groups = sources // 4
    whole = pl.BlockSpec(memory_space=pltpu.VMEM)

    outgoing = pl.pallas_call(
        functools.partial(pack_kernel, shape),
        out_shape=jax.ShapeDtypeStruct((sources, rows, 128), f32),
        in_specs=[whole] * 3,
        out_specs=whole,
        compiler_params=pltpu.CompilerParams(vmem_limit_bytes=56 * MIB),
        name="pack_points",
    )(
        jnp.transpose(point_data, (0, 2, 1, 3)),
        jnp.transpose(point_cells, (0, 2, 1, 3)),
        send_counts,
    )

    arrived = lax.all_to_all(outgoing, AXES, split_axis=0, concat_axis=0, tiled=True)
    arrived = arrived.reshape(4, groups, rows, 128)

    others = other_count(gy)
    lines = 0
    for planes in (CENTER, LOWER, UPPER):
        for high, size in ((24, 4),) + ((8, 12),) * others:
            for start in range(0, len(planes), size):
                count = min(size, len(planes) - start)
                lines += 6 * 16 * -(-count * high // 16)
    edge_shape = jax.ShapeDtypeStruct((2, XTILES, HALO, 128), f32)
    steps = groups // GROUPS
    if steps == 1:
        blocks = {"in_specs": [whole], "out_specs": (whole,) * 4}
    else:
        blocks = {
            "grid": (steps,),
            "in_specs": [pl.BlockSpec((4, GROUPS, rows, 128), lambda s: (0, s, 0, 0))],
            "out_specs": (
                pl.BlockSpec((2, XTILES, ROWS, 128), lambda s: (0, 0, 0, 0)),
                pl.BlockSpec((2, XTILES, HALO, 128), lambda s: (0, 0, 0, 0)),
                pl.BlockSpec((2, XTILES, HALO, 128), lambda s: (0, 0, 0, 0)),
                pl.BlockSpec((2, GROUPS, 8, 128), lambda s: (0, s, 0, 0)),
            ),
        }
    fields, first, second, own = pl.pallas_call(
        functools.partial(splat_kernel, shape),
        out_shape=(
            jax.ShapeDtypeStruct((2, XTILES, ROWS, 128), f32), edge_shape, edge_shape,
            jax.ShapeDtypeStruct((2, groups, 8, 128), f32),
        ),
        **blocks,
        scratch_shapes=[
            pltpu.VMEM((rows // 2, GROUPS, 8, 128), f32),
            pltpu.VMEM((lines, 128 * GROUPS), bf16),
            pltpu.VMEM((bricks, 2, 128 * GROUPS, 2 * 128), bf16),
            pltpu.VMEM((bricks, 2, len(CENTER), GROUPS, 128), f32),
            pltpu.VMEM((3, XPT * XTILES, 24, 2 * 128), f32),
            pltpu.VMEM((max(others, 1), 3, XPT * XTILES, 8, 2 * 128), f32),
            pltpu.VMEM((XTILES, ROWS + 16, 128), f32),
        ],
        compiler_params=pltpu.CompilerParams(vmem_limit_bytes=36 * MIB),
        name="splat_points",
    )(arrived)

    def swapped(edge, start):
        pairs = [(i, i + 1) for i in range(start, gz - 1, 2)]
        if start == 1 and gz % 2 == 0:
            pairs.append((gz - 1, 0))
        return lax.ppermute(edge, "gz", pairs + [(j, i) for i, j in pairs])

    got_first, got_second = swapped(first, 0), swapped(second, 1)

    depth = 128 * (END_TILE - FIRST_TILE)
    tiles = END_TILE - FIRST_TILE
    read, inner = pl.pallas_call(
        functools.partial(inner_kernel, shape),
        out_shape=(
            jax.ShapeDtypeStruct((steps, 2, depth, 128 * GROUPS), bf16),
            jax.ShapeDtypeStruct((tiles, 8 * len(INNER), 128), f32),
        ),
        in_specs=[whole, whole],
        out_specs=(whole, whole),
        scratch_shapes=[pltpu.VMEM((XPT * END_TILE, GROUPS, 128), f32)]
        + work_shapes(len(INNER) + 2),
        compiler_params=pltpu.CompilerParams(vmem_limit_bytes=24 * MIB),
        cost_estimate=pl.CostEstimate(
            flops=8 * depth * 128 * groups, bytes_accessed=4 * depth * 128 * groups, transcendentals=0
        ),
        name="solve_inner",
    )(fields, own)

    indicator, values = pl.pallas_call(
        functools.partial(solve_kernel, shape),
        out_shape=(
            jax.ShapeDtypeStruct((CX, CY, CZ), f32),
            jax.ShapeDtypeStruct((sources, slots), f32),
        ),
        in_specs=[whole] * 6,
        out_specs=(whole, whole),
        scratch_shapes=[
            pltpu.VMEM((2, 2, XTILES, 16, 128), f32),
            pltpu.VMEM((tiles, ROWS, 128), f32),
        ]
        + work_shapes(len(LOW_ZONE))
        + work_shapes(len(HIGH_ZONE)),
        compiler_params=pltpu.CompilerParams(vmem_limit_bytes=24 * MIB),
        name="solve_and_read",
    )(fields, got_first, got_second, own, inner, read)

    returned = lax.all_to_all(
        values.reshape(1, sources, slots), AXES, split_axis=1, concat_axis=1, tiled=True
    )
    return indicator, returned


def solution(mesh):
    shape = tuple(mesh.shape[axis] for axis in AXES)
    in_specs = (
        P(AXES, None, None, None),
        P(AXES, None, None, None),
        P(AXES, None),
    )
    out_specs = (P("gx", "gy", "gz"), P(AXES, None, None))
    return jax.shard_map(
        functools.partial(on_device, shape),
        mesh=mesh,
        in_specs=in_specs,
        out_specs=out_specs,
        check_vma=False,
    )
```

```python
import functools

import jax
import jax.numpy as jnp
from jax import lax
from jax.experimental import pallas as pl
from jax.experimental.pallas import tpu as pltpu
from jax.sharding import PartitionSpec as P

CX = 16
CY = 16
CZ = 128
ITERS = 6

base_screen = 0.25
point_screen = 4.0

AXES = ("gx", "gy", "gz")
REACH = ITERS - 1
XO = REACH
YO = 9
ZO = 8
YS = 32
XPT = 128 // YS
XTILES = -(-(CX + 2 * REACH + 1) // XPT)
ROWS = CZ + 16
CENTER = tuple(range(XO - 1, XO + CX + 2))
LOWER = tuple(range(0, XO + 2))
UPPER = tuple(range(XO + CX - 1, XO + CX + REACH + 1))
PLAIN = {0: CENTER[1:-1], -1: LOWER[:-1], 1: UPPER[1:]}
FIRST_TILE, END_TILE = XO // XPT, (XO + CX) // XPT + 1
WINDOW_LOW = YO - REACH
WINDOW_HIGH = YO + CY - 1
UP_AT = ZO + CZ - REACH
DOWN_AT = ZO - 1
HALO = 8
GROUPS = 8
MIB = 1024 * 1024

f32 = jnp.float32
bf16 = jnp.bfloat16


def split(value):
    high = value.astype(bf16)
    return high, (value - high.astype(f32)).astype(bf16)


def dot_nt(lhs, rhs):
    return lax.dot_general(lhs, rhs, (((1,), (1,)), ((), ())), preferred_element_type=f32)


def dot_nn(lhs, rhs):
    return lax.dot_general(lhs, rhs, (((1,), (0,)), ((), ())), preferred_element_type=f32)


def other_count(gy):
    return min(gy - 1, 2)


def extra_place(brick, bricks):
    return bricks + brick // 4, 2 * (brick % 4)


def pack_kernel(shape, data_ref, cells_ref, counts_ref, out_ref):
    gx, gy, gz = shape
    slots = data_ref.shape[3]
    sources = gx * gy * gz
    lane = lax.broadcasted_iota(jnp.int32, (sources, slots), 1)
    at_row = lax.broadcasted_iota(jnp.int32, (sources, sources), 0)
    at_lane = lax.broadcasted_iota(jnp.int32, (sources, sources), 1)
    counts = jnp.where(at_row == at_lane, counts_ref[...], 0).astype(f32)
    counts = jnp.sum(counts, axis=1, keepdims=True).astype(jnp.int32)
    others = other_count(gy)
    bricks = 3 * (1 + others)
    weight = jnp.where(lane < counts, data_ref[0, 3], 0.0)
    cells = [cells_ref[0, c].astype(f32) for c in range(3)]
    channels = [data_ref[0, c] * (-0.5 * weight) for c in range(3)]
    channels += [weight] + [data_ref[0, c] for c in range(4, 7)] + cells
    blank = jnp.zeros((sources, 128 - slots), f32)
    channels = [jnp.concatenate([value, blank], axis=1) for value in channels]
    row = lax.broadcasted_iota(jnp.int32, (sources, 128), 0)
    y = (row // gz) % gy

    def moved(value, by):
        if by == 0:
            return value
        gap = jnp.zeros((abs(by), 128), f32)
        if by > 0:
            return jnp.concatenate([value[by:], gap], axis=0)
        return jnp.concatenate([gap, value[:by]], axis=0)

    def beside(value, e):
        if e == 0:
            return value
        up = jnp.where(y < gy - 1, moved(value, gz), 0.0)
        down = jnp.where(y > 0, moved(value, -gz), 0.0)
        if others == 1:
            return up + down
        return down if e == 1 else up

    by_y = [[beside(value, e) for e in range(1 + others)] for value in channels]
    lines = {}
    for b in range(bricks):
        e, o = divmod(b, 3)
        place, extra_row = extra_place(b, bricks)
        for c in range(10):
            block, line = (b, c) if c < 8 else (place, extra_row + c - 8)
            value = moved(by_y[c][e], (0, -gy * gz, gy * gz)[o])
            if block % 4:
                value = pltpu.roll(value, slots * (block % 4), 1)
            key = 8 * (block // 4) + line
            lines[key] = value if key not in lines else lines[key] + value
    for line in range(out_ref.shape[1]):
        value = lines.get(line)
        out_ref[:, line, :] = jnp.zeros((sources, 128), f32) if value is None else value


def hat(coordinate, cell, low, high):
    away = coordinate - cell
    return jnp.where(away == 0.0, low, jnp.where(away == 1.0, high, 0.0))


def hat_slope(coordinate, cell, low, high):
    away = coordinate - cell
    rising = jnp.where(away == -1.0, low, jnp.where(away == 0.0, high, 0.0))
    return rising - jnp.where(away == 1.0, low, jnp.where(away == 2.0, high, 0.0))


def split_hat(rows, cell, offset):
    spread = (16, 128)
    fill = rows.shape[0] // 16
    ends = []
    for value in (1.0 - offset, offset):
        ends.extend(split(jnp.broadcast_to(value, spread)))
    low_high, low_low, high_high, high_low = (jnp.concatenate([v] * fill, axis=0) for v in ends)
    cells = jnp.broadcast_to(cell, spread).astype(bf16)
    away = rows - jnp.concatenate([cells] * fill, axis=0)
    here, above = away == 0.0, away == 1.0
    zero = jnp.zeros(rows.shape, bf16)
    return (
        jnp.where(here, low_high, jnp.where(above, high_high, zero)),
        jnp.where(here, low_low, jnp.where(above, high_low, zero)),
    )


def row_iota(rows):
    return lax.broadcasted_iota(jnp.int32, (rows, 128), 0).astype(f32)


def stack_rows(parts, multiple):
    have = sum(part.shape[0] for part in parts)
    if have % multiple:
        parts = parts + [jnp.zeros((multiple - have % multiple, 128), f32)]
    return jnp.concatenate(parts, axis=0) if len(parts) > 1 else parts[0]


def splat_kernel(
    shape, recv_ref, fields_ref, first_ref, second_ref, own_ref,
    points, left_ref, right_ref, hx_ref, near, beside, slope,
):
    gx, gy, gz = shape
    mx, my, mz = lax.axis_index("gx"), lax.axis_index("gy"), lax.axis_index("gz")
    single = recv_ref.shape[1] * 4 == gx * gy * gz
    step = 0 if single else pl.program_id(0)
    others = other_count(gy)
    bricks = 3 * (1 + others)
    tiles = recv_ref.shape[2] // 8
    lane_part = lax.broadcasted_iota(jnp.int32, (8, 128), 1) // 32
    span = 128 * GROUPS
    written = set()

    def add(ref, place, value):
        if single and place not in written:
            written.add(place)
            ref[place] = value
        else:
            ref[place] += value

    if not single:
        @pl.when(step == 0)
        def _():
            near[...] = jnp.zeros_like(near)
            beside[...] = jnp.zeros_like(beside)

    for t in range(tiles):
        for g in range(GROUPS):
            given = [recv_ref[q, g, 8 * t : 8 * t + 8, :] for q in range(4)]
            for k in range(4):
                if 4 * t + k >= bricks + -(-bricks // 4):
                    continue
                merged = None
                for q in range(4):
                    moved = given[q] if q == k else pltpu.roll(given[q], (32 * (q - k)) % 128, 1)
                    merged = moved if merged is None else jnp.where(lane_part == q, moved, merged)
                points[4 * t + k, g] = merged
    own_ref[0] = points[0]
    own_ref[1] = points[bricks]

    z_limit = jnp.where(mz == gz - 1, CZ, CZ + 1).astype(f32)
    z_row = row_iota(CZ).astype(bf16)
    own_row = row_iota(24) + float(8 - YO)
    point_lane = lax.broadcasted_iota(jnp.int32, (128, 128), 1)
    lane_number = point_lane.astype(f32).astype(bf16)
    no_top = jnp.zeros((128, 128), bf16)

    def multiply(begin, lists, b, e, high):
        counts = [-(-len(planes) * high // 16) * 16 for planes in lists]
        size = sum(counts)
        both = dot_nn(left_ref[begin : begin + 2 * size, :], right_ref[b, 0])
        got = both[:size] + both[size:]
        got = got + dot_nn(left_ref[begin : begin + size, :], right_ref[b, 1])
        at = 0
        for c in range(3):
            for i, plane in enumerate(lists[c]):
                value = got[at + i * high : at + i * high + high]
                if e == 0:
                    add(near, (c, plane), value)
                else:
                    add(beside, (e - 1, c, plane), value)
            at += counts[c]
        if single and e == 0:
            for t in sorted({plane // XPT for plane in lists[0]}):
                unfinished[t] -= 1
                if unfinished[t] == 0:
                    finish(t)

    row8 = lax.broadcasted_iota(jnp.int32, (8, 2 * 128), 0)
    zero = jnp.zeros((8, 2 * 128), f32)

    def finish(t):
        turned = []
        for c in range(3):
            pieces = []
            for plane in range(XPT * t, XPT * t + XPT):
                if plane > UPPER[-1]:
                    pieces.append(jnp.zeros((YS, 2 * 128), f32))
                    continue
                parts = [zero] + [near[c, plane, 8 * i : 8 * i + 8, :] for i in range(3)]
                if others:
                    if others == 1:
                        value = beside[0, c, plane]
                        low_part = jnp.where(my == 0, 0.0, value)
                        high_part = jnp.where(my == 0, value, 0.0)
                    else:
                        low_part, high_part = beside[0, c, plane], beside[1, c, plane]
                    moved = pltpu.roll(low_part, 4, 0)
                    parts[0] = jnp.where(row8 >= 4, moved, 0.0)
                    parts[1] = parts[1] + jnp.where(row8 < 4, moved, 0.0)
                    parts[3] = parts[3] + high_part
                pieces.extend(parts)
            stacked = jnp.concatenate(pieces, axis=0)
            turned.append(stacked[:, :CZ].T)
            above = stacked[:, CZ:]
            n, at = divmod(3 * t + c, 128 // GROUPS)
            if at:
                above = pltpu.roll(above, GROUPS * at, 1)
            if tops[n] is not None:
                above = jnp.where(point_lane // GROUPS == at, above, tops[n])
            tops[n] = above
        fields_ref[0, t, ZO : ZO + CZ, :] = turned[0]
        slope[t, ZO + 8 : ZO + 8 + CZ, :] = turned[1]
        fields_ref[1, t, ZO : ZO + CZ, :] = turned[2]

    def finish_all():
        zero = jnp.zeros((8, 128), f32)
        sums = [jnp.sum(top.T.reshape(-1, GROUPS, 128), axis=1, keepdims=True) for top in tops]
        for t in range(XTILES):
            at = [divmod(3 * t + c, 128 // GROUPS) for c in range(3)]
            above = [sums[n][i] for n, i in at]
            below = jnp.concatenate([above[1], jnp.zeros((7, 128), f32)], axis=0)
            slope[t, 0 : ZO + 8, :] = jnp.zeros((ZO + 8, 128), f32)
            slope[t, ZO + 8 + CZ : ZO + 16 + CZ, :] = below
            slope[t, ZO + 16 + CZ : ROWS + 16, :] = zero
            for c in range(2):
                fields_ref[c, t, 0:ZO, :] = zero
                fields_ref[c, t, ZO + CZ : ROWS, :] = jnp.concatenate(
                    [above[2 * c], jnp.zeros((7, 128), f32)], axis=0
                )
            fields_ref[0, t] += slope[t, 9 : ROWS + 9, :] - slope[t, 7 : ROWS + 7, :]

    tops = [None] * -(-3 * XTILES * GROUPS // 128)
    unfinished = [
        sum(
            plane // XPT == t and (i == 0 or planes[i - 1] // XPT != t)
            for planes in (CENTER, LOWER, UPPER)
            for i, plane in enumerate(planes)
        )
        for t in range(XTILES)
    ]
    row_at = 0
    waiting = None
    for e in reversed(range(1 + others)):
        if e == 0:
            y_limit = jnp.where(my == gy - 1, CY, CY + 1).astype(f32)
            y_row = own_row
        else:
            above = my == 0 if others == 1 else jnp.bool_(e == 2)
            y_limit = jnp.where(
                jnp.logical_and(above, my + 1 == gy - 1), CY, CY + 1
            ).astype(f32)
            first = jnp.where(above, WINDOW_HIGH - YO - CY, WINDOW_LOW - YO + CY)
            y_row = row_iota(8) + first.astype(f32)
        high = y_row.shape[0]
        for o, shift, planes in ((1, -1, LOWER), (2, 1, UPPER), (0, 0, CENTER)):
            b = e * 3 + o
            place, row = extra_place(b, bricks)
            x_limit = jnp.where(mx + shift == gx - 1, CX, CX + 1).astype(f32)
            cell_x = points[b, :, 7, :]
            off_x = points[b, :, 4, :]
            low_x = 1.0 - off_x
            high_x = jnp.where(cell_x + 1.0 < x_limit, off_x, 0.0)
            first_x = planes[0] - XO - CX * shift
            hats = [
                hat(float(first_x + n - 1), cell_x, low_x, high_x) for n in range(len(planes) + 2)
            ]
            for n in range(len(planes)):
                hx_ref[b, 0, n] = hats[n + 1]
                hx_ref[b, 1, n] = hats[n + 2] - hats[n]
            cell_z, off_z = points[place, :, row + 1, :], points[b, :, 6, :]
            top = jnp.where((cell_z + 1.0 == float(CZ)) & (cell_z + 1.0 < z_limit), off_z, 0.0)
            top_columns = jnp.concatenate([top, jnp.zeros((128 - GROUPS, 128), f32)], axis=0).T
            top_high, top_low = split(top_columns)
            y_parts = []
            for g in range(GROUPS):
                main = points[b, g]
                more = points[place, g]
                cell_y, cell_z = more[row : row + 1], more[row + 1 : row + 2]
                off_y, off_z = main[5:6], main[6:7]
                at = slice(128 * g, 128 * g + 128)
                hz_high, hz_low = split_hat(z_row, cell_z, off_z)
                right_ref[b, 0, at, 0:CZ] = hz_high.T
                right_ref[b, 1, at, 0:CZ] = hz_low.T
                column = lane_number == float(g)
                right_ref[b, 0, at, CZ : CZ + 128] = jnp.where(column, top_high, no_top)
                right_ref[b, 1, at, CZ : CZ + 128] = jnp.where(column, top_low, no_top)
                high_y = jnp.where(cell_y + 1.0 < y_limit, off_y, 0.0)
                hy = hat(y_row, cell_y, 1.0 - off_y, high_y)
                dy = hat_slope(y_row, cell_y, 1.0 - off_y, high_y)
                y_parts.append((main[0:1] * hy, main[1:2] * dy, main[2:3] * hy, main[3:4] * hy))
            size = 4 if e == 0 else 12
            for start in range(0, len(planes), size):
                block = planes[start : start + size]
                lists = [block] + 2 * [tuple(p for p in block if p in PLAIN[shift])]
                counts = [-(-len(each) * high // 16) * 16 for each in lists]
                for c in range(3):
                    begin = row_at + sum(counts[:c])
                    for g in range(GROUPS):
                        part_x0, part_y1, part_z, part_w = y_parts[g]
                        at = slice(128 * g, 128 * g + 128)
                        rows = []
                        for plane in lists[c]:
                            n = plane - planes[0]
                            hx = hx_ref[b, 0, n, g : g + 1, :]
                            if c == 0:
                                dx = hx_ref[b, 1, n, g : g + 1, :]
                                rows.append(dx * part_x0 + hx * part_y1)
                            else:
                                rows.append(hx * (part_z if c == 1 else part_w))
                        main_part, rest = split(stack_rows(rows, 16))
                        left_ref[begin : begin + counts[c], at] = main_part
                        after = begin + sum(counts)
                        left_ref[after : after + counts[c], at] = rest
                if waiting is not None:
                    waiting()
                waiting = functools.partial(multiply, row_at, lists, b, e, high)
                row_at += 2 * sum(counts)
    waiting()

    if not single:
        @pl.when(step == pl.num_programs(0) - 1)
        def _():
            for t in range(XTILES):
                finish(t)
            finish_all()
    else:
        finish_all()
    for c in range(2):
        up = fields_ref[c, :, UP_AT : UP_AT + HALO, :]
        down = fields_ref[c, :, DOWN_AT : DOWN_AT + HALO, :]
        first_ref[c] = jnp.where(mz % 2 == 0, up, down)
        second_ref[c] = jnp.where(mz % 2 == 0, down, up)


def chebyshev_factors():
    half_width = 6.0 / (6.0 + base_screen)
    sigma_ratio = 1.0 / half_width
    rho_prev = half_width
    factors = []
    for _ in range(ITERS - 1):
        rho_next = 1.0 / (2.0 * sigma_ratio - rho_prev)
        factors.append((rho_next * rho_prev, 2.0 * rho_next / half_width))
        rho_prev = rho_next
    return factors


READ_PLANES = range(XPT * FIRST_TILE, XPT * END_TILE)
STRIPS = ROWS // 8
INNER = range((UP_AT - CZ + HALO + REACH + 7) // 8, (DOWN_AT + CZ - REACH) // 8)
LOW_ZONE = range(0, INNER[0] + 1)
HIGH_ZONE = range(INNER[-1], STRIPS)


def relax(shape, given, zone, wanted, work, store):
    gx, gy, gz = shape
    mx, my, mz = lax.axis_index("gx"), lax.axis_index("gy"), lax.axis_index("gz")
    first, second, base, inverse = work
    lane = lax.broadcasted_iota(jnp.int32, (8, 128), 1)
    row = lax.broadcasted_iota(jnp.int32, (8, 128), 0)
    y = lane % YS - YO + my * CY
    inside_y = (y >= 0) & (y < gy * CY)
    zero = jnp.zeros((8, 128), f32)
    end_row = 8 * len(zone) + 8
    for t in range(XTILES):
        x = lane // YS + (XPT * t - XO) + mx * CX
        inside_xy = inside_y & (x >= 0) & (x < gx * CX)
        for scratch in (first, second):
            scratch[t, 0:8, :] = zero
            scratch[t, end_row : end_row + 8, :] = zero
        for j, i in enumerate(zone):
            inside = inside_xy
            if 8 * i < ZO or 8 * i + 8 > ZO + CZ:
                z = row + (8 * i - ZO) + mz * CZ
                inside = inside & (z >= 0) & (z < gz * CZ)
            diagonal = 6.0 + base_screen + point_screen * given(1, t, i)
            inv = jnp.where(inside, 1.0 / diagonal, 0.0)
            start = given(0, t, i) * inv
            inverse[t, 8 * j : 8 * j + 8, :] = inv
            base[t, 8 * j : 8 * j + 8, :] = start
            first[t, 8 * j + 8 : 8 * j + 16, :] = start

    now, later = first, second
    factors = chebyshev_factors()
    low_part, high_part = lane < YS, lane >= 128 - YS
    for k, (keep, gain) in enumerate(factors, 1):
        last = k == len(factors)
        begin, end = k // XPT, (XO + CX + REACH - k + XPT) // XPT
        if last:
            begin, end = max(begin, FIRST_TILE), min(end, END_TILE)
        for j, i in enumerate(zone):
            if last and i not in wanted:
                continue
            at = slice(8 * j, 8 * j + 8)
            inner = slice(8 * j + 8, 8 * j + 16)
            reach = range(max(begin - 1, 0), min(end + 1, XTILES))
            here = {t: now[t, inner, :] for t in reach}
            ahead_x = {t: pltpu.roll(here[t], YS, 1) for t in reach if t < end}
            behind_x = {t: pltpu.roll(here[t], 128 - YS, 1) for t in reach if t >= begin}
            for t in range(begin, end):
                mine = here[t]
                near = now[t, 8 * j + 7 : 8 * j + 15, :] + now[t, 8 * j + 9 : 8 * j + 17, :]
                near = near + pltpu.roll(mine, 1, 1) + pltpu.roll(mine, 127, 1)
                before = ahead_x[t]
                if t > 0:
                    before = jnp.where(low_part, ahead_x[t - 1], before)
                after = behind_x[t]
                if t + 1 < XTILES:
                    after = jnp.where(high_part, behind_x[t + 1], after)
                near = near + before + after
                if k == 1:
                    ahead = (1.0 + keep) * mine + gain * (inverse[t, at, :] * near)
                else:
                    ahead = gain * (base[t, at, :] + inverse[t, at, :] * near)
                    ahead = ahead + (1.0 + keep - gain) * mine - keep * later[t, inner, :]
                if last:
                    store(t - FIRST_TILE, i, ahead)
                else:
                    later[t, inner, :] = ahead
        now, later = later, now


def inner_kernel(shape, fields_ref, own_ref, out_ref, inner_ref, hx_ref, *work):
    y_row = row_iota(24) + float(8 - YO)
    blank = jnp.zeros((8, 128), f32)
    for chunk in range(own_ref.shape[1] // GROUPS):
        span = slice(chunk * GROUPS, chunk * GROUPS + GROUPS)
        cell_x, off_x = own_ref[0, span, 7, :], own_ref[0, span, 4, :]
        for plane in READ_PLANES:
            if 0 <= plane - XO <= CX:
                hx_ref[plane] = hat(float(plane - XO), cell_x, 1.0 - off_x, off_x)
        for g in range(GROUPS):
            off_y = own_ref[0, chunk * GROUPS + g, 5:6, :]
            hy = hat(y_row, own_ref[1, chunk * GROUPS + g, 0:1, :], 1.0 - off_y, off_y)
            at = slice(128 * g, 128 * g + 128)
            for plane in READ_PLANES:
                start = YS * (plane - XPT * FIRST_TILE)
                if 0 <= plane - XO <= CX:
                    rows = jnp.concatenate([blank, hx_ref[plane, g : g + 1, :] * hy], axis=0)
                    high, low = split(rows)
                else:
                    high = jnp.zeros((YS, 128), bf16)
                    low = high
                out_ref[chunk, 0, start : start + YS, at] = high
                out_ref[chunk, 1, start : start + YS, at] = low

    def given(c, t, i):
        return fields_ref[c, t, 8 * i : 8 * i + 8, :]

    def store(t, i, value):
        at = 8 * (i - INNER[0])
        inner_ref[t, at : at + 8, :] = value

    relax(shape, given, range(INNER[0] - 1, INNER[-1] + 2), INNER, work, store)


def solve_kernel(
    shape, fields_ref, first_ref, second_ref, own_ref, inner_ref, read_ref,
    indicator_ref, values_ref,
    edge, total, first, second, base, inverse, first_high, second_high, base_high, inverse_high,
):
    edge[...] = jnp.zeros_like(edge)
    low_at, high_at = UP_AT - CZ, DOWN_AT + CZ - (ROWS - 16)
    mz = lax.axis_index("gz")
    even = mz % 2 == 0
    got_first, got_second = first_ref[...], second_ref[...]
    from_low = jnp.where(even, got_second, got_first)
    from_high = jnp.where(even, got_first, got_second)
    edge[0, :, :, low_at : low_at + HALO, :] = jnp.where(mz > 0, from_low, 0.0)
    edge[1, :, :, high_at : high_at + HALO, :] = jnp.where(mz < shape[2] - 1, from_high, 0.0)

    def given(c, t, i):
        value = fields_ref[c, t, 8 * i : 8 * i + 8, :]
        if i < 2:
            value = value + edge[0, c, t, 8 * i : 8 * i + 8, :]
        from_end = i - (STRIPS - 2)
        if from_end >= 0:
            value = value + edge[1, c, t, 8 * from_end : 8 * from_end + 8, :]
        return value

    def store(t, i, value):
        total[t, 8 * i : 8 * i + 8, :] = value

    inner_rows = slice(8 * INNER[0], 8 * INNER[-1] + 8)
    for t in range(END_TILE - FIRST_TILE):
        total[t, 0:8, :] = jnp.zeros((8, 128), f32)
        total[t, inner_rows, :] = inner_ref[t]
    low_wanted = range(1, INNER[0])
    high_wanted = range(INNER[-1] + 1, STRIPS)
    relax(shape, given, LOW_ZONE, low_wanted, (first, second, base, inverse), store)
    relax(
        shape, given, HIGH_ZONE, high_wanted,
        (first_high, second_high, base_high, inverse_high), store,
    )

    parts = [split(total[t - FIRST_TILE]) for t in range(FIRST_TILE, END_TILE)]
    u_high = jnp.concatenate([part[0] for part in parts], axis=1)
    u_low = jnp.concatenate([part[1] for part in parts], axis=1)
    u_both = jnp.concatenate([u_high, u_low], axis=0)
    z_row = row_iota(ROWS) - float(ZO)
    groups = own_ref.shape[1]
    for chunk in range(groups // GROUPS):
        got = dot_nn(u_both, read_ref[chunk, 0])
        got = got[:ROWS] + got[ROWS:] + dot_nn(u_high, read_ref[chunk, 1])
        rows = []
        for g in range(GROUPS):
            main = own_ref[0, chunk * GROUPS + g]
            off_z = main[6:7]
            hz = hat(z_row, own_ref[1, chunk * GROUPS + g, 1:2, :], 1.0 - off_z, off_z)
            value = jnp.sum(hz * got[:, 128 * g : 128 * g + 128], axis=0, keepdims=True)
            rows.append(jnp.where(main[3:4] > 0.0, value, 0.0))
        values = jnp.concatenate(rows, axis=0)
        for q in range(4):
            moved = values if q == 0 else pltpu.roll(values, 128 - 32 * q, 1)
            start = q * groups + chunk * GROUPS
            values_ref[start : start + GROUPS, :] = moved[:, 0:32]

    for t in range(FIRST_TILE, END_TILE):
        turned = total[t - FIRST_TILE, ZO : ZO + CZ, :].T
        for i in range(XPT):
            plane = XPT * t + i - XO
            if 0 <= plane < CX:
                indicator_ref[plane] = turned[YS * i + YO : YS * i + YO + CY, :]


def work_shapes(strips):
    padded = pltpu.VMEM((XTILES, 8 * strips + 16, 128), f32)
    return [padded, padded] + 2 * [pltpu.VMEM((XTILES, 8 * strips, 128), f32)]


def on_device(shape, point_data, point_cells, send_counts):
    gx, gy, gz = shape
    sources = gx * gy * gz
    slots = point_data.shape[3]
    bricks = 3 * (1 + other_count(gy))
    rows = 8 * -(-(bricks + -(-bricks // 4)) // 4)
    groups = sources // 4
    whole = pl.BlockSpec(memory_space=pltpu.VMEM)

    outgoing = pl.pallas_call(
        functools.partial(pack_kernel, shape),
        out_shape=jax.ShapeDtypeStruct((sources, rows, 128), f32),
        in_specs=[whole] * 3,
        out_specs=whole,
        compiler_params=pltpu.CompilerParams(vmem_limit_bytes=56 * MIB),
        name="pack_points",
    )(
        jnp.transpose(point_data, (0, 2, 1, 3)),
        jnp.transpose(point_cells, (0, 2, 1, 3)),
        send_counts,
    )

    arrived = lax.all_to_all(outgoing, AXES, split_axis=0, concat_axis=0, tiled=True)
    arrived = arrived.reshape(4, groups, rows, 128)

    others = other_count(gy)
    lines = 0
    for planes in (CENTER, LOWER, UPPER):
        for high, size in ((24, 4),) + ((8, 12),) * others:
            for start in range(0, len(planes), size):
                count = min(size, len(planes) - start)
                lines += 6 * 16 * -(-count * high // 16)
    edge_shape = jax.ShapeDtypeStruct((2, XTILES, HALO, 128), f32)
    steps = groups // GROUPS
    if steps == 1:
        blocks = {"in_specs": [whole], "out_specs": (whole,) * 4}
    else:
        blocks = {
            "grid": (steps,),
            "in_specs": [pl.BlockSpec((4, GROUPS, rows, 128), lambda s: (0, s, 0, 0))],
            "out_specs": (
                pl.BlockSpec((2, XTILES, ROWS, 128), lambda s: (0, 0, 0, 0)),
                pl.BlockSpec((2, XTILES, HALO, 128), lambda s: (0, 0, 0, 0)),
                pl.BlockSpec((2, XTILES, HALO, 128), lambda s: (0, 0, 0, 0)),
                pl.BlockSpec((2, GROUPS, 8, 128), lambda s: (0, s, 0, 0)),
            ),
        }
    fields, first, second, own = pl.pallas_call(
        functools.partial(splat_kernel, shape),
        out_shape=(
            jax.ShapeDtypeStruct((2, XTILES, ROWS, 128), f32), edge_shape, edge_shape,
            jax.ShapeDtypeStruct((2, groups, 8, 128), f32),
        ),
        **blocks,
        scratch_shapes=[
            pltpu.VMEM((rows // 2, GROUPS, 8, 128), f32),
            pltpu.VMEM((lines, 128 * GROUPS), bf16),
            pltpu.VMEM((bricks, 2, 128 * GROUPS, 2 * 128), bf16),
            pltpu.VMEM((bricks, 2, len(CENTER), GROUPS, 128), f32),
            pltpu.VMEM((3, XPT * XTILES, 24, 2 * 128), f32),
            pltpu.VMEM((max(others, 1), 3, XPT * XTILES, 8, 2 * 128), f32),
            pltpu.VMEM((XTILES, ROWS + 16, 128), f32),
        ],
        compiler_params=pltpu.CompilerParams(vmem_limit_bytes=36 * MIB),
        name="splat_points",
    )(arrived)

    def swapped(edge, start):
        pairs = [(i, i + 1) for i in range(start, gz - 1, 2)]
        pairs += [(j, i) for i, j in pairs]
        alone = set(range(gz)) - {i for i, _ in pairs}
        return lax.ppermute(edge, "gz", pairs + [(i, i) for i in sorted(alone)])

    got_first, got_second = swapped(first, 0), swapped(second, 1)

    depth = 128 * (END_TILE - FIRST_TILE)
    tiles = END_TILE - FIRST_TILE
    read, inner = pl.pallas_call(
        functools.partial(inner_kernel, shape),
        out_shape=(
            jax.ShapeDtypeStruct((steps, 2, depth, 128 * GROUPS), bf16),
            jax.ShapeDtypeStruct((tiles, 8 * len(INNER), 128), f32),
        ),
        in_specs=[whole, whole],
        out_specs=(whole, whole),
        scratch_shapes=[pltpu.VMEM((XPT * END_TILE, GROUPS, 128), f32)]
        + work_shapes(len(INNER) + 2),
        compiler_params=pltpu.CompilerParams(vmem_limit_bytes=24 * MIB),
        cost_estimate=pl.CostEstimate(
            flops=8 * depth * 128 * groups, bytes_accessed=4 * depth * 128 * groups, transcendentals=0
        ),
        name="solve_inner",
    )(fields, own)

    indicator, values = pl.pallas_call(
        functools.partial(solve_kernel, shape),
        out_shape=(
            jax.ShapeDtypeStruct((CX, CY, CZ), f32),
            jax.ShapeDtypeStruct((sources, slots), f32),
        ),
        in_specs=[whole] * 6,
        out_specs=(whole, whole),
        scratch_shapes=[
            pltpu.VMEM((2, 2, XTILES, 16, 128), f32),
            pltpu.VMEM((tiles, ROWS, 128), f32),
        ]
        + work_shapes(len(LOW_ZONE))
        + work_shapes(len(HIGH_ZONE)),
        compiler_params=pltpu.CompilerParams(vmem_limit_bytes=24 * MIB),
        name="solve_and_read",
    )(fields, got_first, got_second, own, inner, read)

    returned = lax.all_to_all(
        values.reshape(1, sources, slots), AXES, split_axis=1, concat_axis=1, tiled=True
    )
    return indicator, returned


def solution(mesh):
    shape = tuple(mesh.shape[axis] for axis in AXES)
    in_specs = (
        P(AXES, None, None, None),
        P(AXES, None, None, None),
        P(AXES, None),
    )
    out_specs = (P("gx", "gy", "gz"), P(AXES, None, None))
    return jax.shard_map(
        functools.partial(on_device, shape),
        mesh=mesh,
        in_specs=in_specs,
        out_specs=out_specs,
        check_vma=False,
    )
```
